32 devices in a mesh: dp: 4 (over y, x), seq: 4 (over z), dir: 2 (over core).
Axes of the slice: x: 2, y: 2, z: 4, core: 2. Of those that a mesh axis runs over, the one named last changes fastest.
Arguments:
- tokens: bfloat16 [8, 1280, 768], P('dp', ('seq', 'dir')), may hold values from -6 to 6
- starts: int32 [8, 4], P('dp'), may hold values from 0 to 1279, as said below
- pad_len: int32 [8], P('dp'), may hold values from 0 to 160
- norm_gain: float32 [768], replicated, may hold values from 0.5 to 1.5
- w_in: bfloat16 [768, 3328], P(('dp', 'seq', 'dir')), may hold values from -0.21875 to 0.21875
- w_dt: bfloat16 [768, 48], P(('dp', 'seq', 'dir')), may hold values from -0.21875 to 0.21875
- conv_w: float32 [4, 1792], replicated, may hold values from -3 to 3
- conv_b: float32 [1792], replicated, may hold values from -1 to 1
- dt_bias: float32 [48], replicated, may hold values from -4 to 0
- a_log: float32 [48], replicated, may hold values from -5 to -1
- skip: float32 [24], replicated, may hold values from 0.5 to 1.5
- gate_gain: float32 [1536], replicated, may hold values from 0.5 to 1.5
- w_out: bfloat16 [768, 1536], P(('dp', 'seq', 'dir')), may hold values from -0.15625 to 0.15625
- cotangent: bfloat16 [8, 1280, 768], P('dp', ('seq', 'dir')), may hold values from -6 to 6
Outputs:
- mixed: bfloat16 [8, 1280, 768], P('dp', ('seq', 'dir'))
- tokens_grad: bfloat16 [8, 1280, 768], P('dp', ('seq', 'dir'))
- norm_gain_grad: float32 [768], replicated
- w_in_grad: float32 [768, 3328], P(('dp', 'seq', 'dir'))
- w_dt_grad: float32 [768, 48], P(('dp', 'seq', 'dir'))
- conv_w_grad: float32 [4, 1792], replicated
- conv_b_grad: float32 [1792], replicated
- dt_bias_grad: float32 [48], replicated
- a_log_grad: float32 [48], replicated
- skip_grad: float32 [24], replicated
- gate_gain_grad: float32 [1536], replicated
- w_out_grad: float32 [768, 1536], P(('dp', 'seq', 'dir'))
The draws below stay inside these ranges and needn't reach their ends.
Inputs may be any that keep to these rules, and one draw needn't show every extreme that they name: `starts`: entry 0 of every row is 0; a position is the first token of a sequence where it equals some entry of its row.
All inputs are finite; a program needn't handle non-finite values.
Results may differ from the reference program's by a relative error of at most 0.012.
Values may be sent and summed in bfloat16 or wider, within the bound.
A program may use at most 128 MiB of HBM per device.

```python
import jax
import jax.numpy as jnp
from jax import lax

D = 768
HEADS = 24
HEAD_DIM = 64
STATE = 64
KERNEL = 4
BLOCK = 160
ROW_LEN = 1280
STARTS = 4
PAD_MOST = 160
INNER = 1536
XBC_WIDTH = 1792
PROJ_WIDTH = 3328
ROWS = 8


def whole_row(key):
    return jax.random.randint(key, (), 0, ROWS)


def drawn_field(key, shape, spread, limit):
    values = jax.random.normal(key, shape, jnp.float32) * spread
    return jnp.clip(values, -limit, limit)


def draw_tokens(key, part):
    key = jax.random.fold_in(key, 31)
    return drawn_field(key, (ROWS, ROW_LEN, D), 1.0, 6.0).astype(jnp.bfloat16)


def draw_cotangent(key, part):
    key = jax.random.fold_in(key, 37)
    return drawn_field(key, (ROWS, ROW_LEN, D), 1.0, 6.0).astype(jnp.bfloat16)


def draw_conv_b(key, part):
    key = jax.random.fold_in(key, 41)
    return drawn_field(key, (XBC_WIDTH,), 0.3, 1.0)


def draw_starts(key, part):
    chosen = whole_row(key)
    key = jax.random.fold_in(key, 11)
    picked = jax.random.randint(key, (ROWS, STARTS), 1, ROW_LEN)
    col_ids = lax.broadcasted_iota(jnp.int32, (ROWS, STARTS), 1)
    row_ids = lax.broadcasted_iota(jnp.int32, (ROWS, STARTS), 0)
    picked = jnp.where(col_ids == 0, 0, picked)
    picked = jnp.where(row_ids == chosen, 0, picked)
    other_row = (chosen + 1) % ROWS
    picked = jnp.where((row_ids == other_row) & (col_ids == STARTS - 1), ROW_LEN - 1, picked)
    return picked.astype(jnp.int32)


def draw_pad_len(key, part):
    chosen = whole_row(key)
    key = jax.random.fold_in(key, 23)
    pad_vals = jax.random.randint(key, (ROWS,), 0, PAD_MOST + 1)
    row_ids = lax.broadcasted_iota(jnp.int32, (ROWS,), 0)
    pad_vals = jnp.where(row_ids == chosen, 0, pad_vals)
    pad_vals = jnp.where(row_ids == (chosen + 1) % ROWS, PAD_MOST, pad_vals)
    return pad_vals.astype(jnp.int32)


def steps_of(rng, shape, cuts, smallest, top_value):
    loudness = 1.0
    for position, blocks in cuts:
        draws = jax.random.uniform(jax.random.fold_in(jax.random.fold_in(rng, 6), position), (blocks,), jnp.float32, smallest / len(cuts), top_value / len(cuts))
        loudness = loudness * jnp.repeat(jnp.exp(draws), shape[position] // blocks).reshape((-1,) + (1,) * (len(shape) - 1 - position))
    return loudness


def centred(own_key, dims, scale, bound, split=(), kind=jnp.bfloat16):
    loudness = steps_of(own_key, dims, split, -0.22, 0.18) if split else 1.0
    entries = jax.random.normal(own_key, dims, jnp.float32) * scale * loudness
    return jnp.minimum(jnp.maximum(entries, -bound), bound).astype(kind)


def setup_inputs(seed: int = 0) -> dict:
    arg_keys = jax.random.split(jax.random.key(seed), 15)
    tokens = draw_tokens(jax.random.fold_in(arg_keys[14], 71), 0)
    starts = draw_starts(jax.random.fold_in(arg_keys[14], 71), 0)
    pad_len = draw_pad_len(jax.random.fold_in(arg_keys[14], 71), 0)
    norm_gain = jnp.clip(1.0 + 0.1 * jax.random.normal(arg_keys[3], (D,), jnp.float32), 0.5, 1.5)
    w_in = centred(arg_keys[4], (D, PROJ_WIDTH), D ** -0.5, 0.21875, ((0, 32),))
    w_dt = centred(arg_keys[5], (D, 2 * HEADS), D ** -0.5, 0.21875, ((0, 32),))
    conv_w = centred(arg_keys[6], (KERNEL, XBC_WIDTH), KERNEL ** -0.5, 3.0, (), jnp.float32)
    conv_b = draw_conv_b(jax.random.fold_in(arg_keys[14], 71), 0)
    dt_bias = jnp.clip(jax.random.uniform(arg_keys[8], (2 * HEADS,), jnp.float32, -4.0, 0.0), -4.0, 0.0)
    a_log = jnp.clip(jax.random.uniform(arg_keys[9], (2 * HEADS,), jnp.float32, -5.0, -1.0), -5.0, -1.0)
    skip = jnp.clip(jax.random.uniform(arg_keys[10], (HEADS,), jnp.float32, 0.5, 1.5), 0.5, 1.5)
    gate_gain = jnp.clip(1.0 + 0.1 * jax.random.normal(arg_keys[11], (INNER,), jnp.float32), 0.5, 1.5)
    w_out = centred(arg_keys[12], (D, INNER), INNER ** -0.5, 0.15625, ((0, 32),))
    cotangent = draw_cotangent(jax.random.fold_in(arg_keys[14], 71), 0)
    return dict(tokens=tokens, starts=starts, pad_len=pad_len, norm_gain=norm_gain, w_in=w_in, w_dt=w_dt, conv_w=conv_w, conv_b=conv_b, dt_bias=dt_bias, a_log=a_log, skip=skip, gate_gain=gate_gain, w_out=w_out, cotangent=cotangent)


EPSILON = 1e-05
HIGHEST_PREC = lax.Precision.HIGHEST

@jax.custom_vjp
def low(v):
    return lax.optimization_barrier(v.astype(jnp.bfloat16)).astype(jnp.float32)

@jax.custom_vjp
def low_back(v):
    return v

def low_keep(v):
    return (low(v), None)

def low_pass(kept, grad):
    return (grad,)

def back_keep(v):
    return (v, None)

def back_low(kept, grad):
    return (low(grad),)
low.defvjp(low_keep, low_pass)
low_back.defvjp(back_keep, back_low)

def norm_rows(values, norm_gain):
    return values * lax.rsqrt(lax.optimization_barrier(jnp.mean(values * values, axis=-1, keepdims=True)) + EPSILON) * norm_gain

def gated_norm(values, gate_z, gate_gain):
    return norm_rows(values * jax.nn.silu(gate_z), gate_gain)

def conv_silu(extended, conv_w, conv_b, tap_ok, valid):
    conv_len = conv_w.shape[0]
    out_len = extended.shape[-2] - conv_len + 1
    summed = conv_b
    for tap_id in range(conv_len):
        summed = summed + extended[..., tap_id:tap_id + out_len, :] * conv_w[tap_id] * tap_ok[..., tap_id:tap_id + 1]
    return jax.nn.silu(summed) * valid[..., None]

def block_weights(raw_dt, dt_bias, a_log, b_mat, c_mat, scores, doc_ids, prev_doc):
    dt_step = jnp.swapaxes(jax.nn.softplus(raw_dt + dt_bias), 1, 2)
    cum_log = jnp.cumsum(-dt_step * jnp.exp(a_log)[:, None], axis=2)
    block_len = doc_ids.shape[1]
    lower_mask = lax.broadcasted_iota(jnp.int32, (block_len, block_len), 0) > lax.broadcasted_iota(jnp.int32, (block_len, block_len), 1)
    same_doc = ((doc_ids[:, :, None] == doc_ids[:, None, :]) & lower_mask)[:, None]
    gap_log = jnp.where(same_doc, cum_log[:, :, :, None] - cum_log[:, :, None, :], -jnp.inf)
    mixing = jnp.exp(gap_log) * scores[:, None] * dt_step[:, :, None, :]
    last_log = cum_log[:, :, -1:]
    tail_w = jnp.exp(last_log - cum_log) * (doc_ids == doc_ids[:, -1:])[:, None].astype(jnp.float32) * dt_step
    into_w = tail_w[:, :, None, :] * jnp.swapaxes(b_mat, 1, 2)[:, None]
    reach_mask = (doc_ids == prev_doc[:, None])[:, None].astype(jnp.float32)
    out_weight = (jnp.exp(cum_log) * reach_mask)[:, :, None, :] * jnp.swapaxes(c_mat, 1, 2)[:, None]
    carry_decay = jnp.exp(last_log[:, :, 0]) * (doc_ids[:, -1] == prev_doc)[:, None].astype(jnp.float32)
    return (mixing, into_w, out_weight, carry_decay)

def doc_index(starts_row, positions):
    return lax.optimization_barrier(jnp.sum((starts_row <= positions[..., None]).astype(jnp.int32), axis=-1)).astype(jnp.int32)

def direction(u_vals, b_mat, c_mat, raw_dt, dt_bias, a_log, doc_ids):
    row_len = u_vals.shape[0]
    blocks = row_len // BLOCK
    u_blk = u_vals.reshape(blocks, BLOCK, HEADS, HEAD_DIM)
    b_blk = b_mat.reshape(blocks, BLOCK, STATE)
    c_blk = c_mat.reshape(blocks, BLOCK, STATE)
    raw_blk = raw_dt.reshape(blocks, BLOCK, HEADS)
    doc_blk = doc_ids.reshape(blocks, BLOCK)
    prev_doc = jnp.concatenate([doc_ids[:1], doc_blk[:-1, -1]]).astype(jnp.int32)
    scores = low_back(jnp.einsum('gtn,gsn->gts', c_blk, b_blk, precision=HIGHEST_PREC))
    mixing, into_w, out_weight, carry_decay = block_weights(raw_blk, dt_bias, a_log, b_blk, c_blk, scores, doc_blk, prev_doc)
    mixing = low(mixing)
    into_w = low(into_w)
    out_weight = low(out_weight)
    inner_y = jnp.einsum('ghts,gshp->gthp', mixing, u_blk, precision=HIGHEST_PREC)
    local_state = low_back(jnp.einsum('ghns,gshp->ghnp', into_w, u_blk, precision=HIGHEST_PREC))

    def chain(state_now, item):
        decay_now, local_now = item
        return (decay_now[:, None, None] * state_now + local_now, state_now)
    start_state = jnp.zeros((HEADS, STATE, HEAD_DIM), jnp.float32)
    _, incoming = lax.scan(chain, start_state, (carry_decay, local_state))
    outer_y = jnp.einsum('ghnt,ghnp->gthp', out_weight, low(incoming), precision=HIGHEST_PREC)
    return (inner_y + outer_y).reshape(row_len, INNER)

def row_forward(params, x_row, starts_row, pad_row):
    norm_gain, w_in, w_dt, conv_w, conv_b, dt_bias, a_log, skip, gate_gain, w_out = params
    row_len = x_row.shape[0]
    places = jnp.arange(row_len, dtype=jnp.int32)
    doc_ids = doc_index(starts_row, places)
    valid = (places < row_len - pad_row).astype(jnp.float32)
    normed = low(norm_rows(x_row, norm_gain))
    projected = low_back(jnp.dot(normed, w_in, precision=HIGHEST_PREC))
    raw_dt = low(low_back(jnp.dot(normed, w_dt, precision=HIGHEST_PREC)))
    gate_z = projected[:, :INNER]
    pre_conv = low(projected[:, INNER:])
    conv_len = conv_w.shape[0]
    extended = jnp.concatenate([jnp.zeros((conv_len - 1, pre_conv.shape[1]), jnp.float32), pre_conv], axis=0)
    beside_all = places[:, None] - (conv_len - 1) + jnp.arange(conv_len, dtype=jnp.int32)[None, :]
    tap_ok = (doc_index(starts_row, beside_all) == doc_ids[:, None]).astype(jnp.float32)
    xbc = low(conv_silu(extended, conv_w, conv_b, tap_ok, valid))
    u_vals = xbc[:, :INNER]
    b_fwd = xbc[:, INNER:INNER + STATE]
    b_bwd = xbc[:, INNER + STATE:INNER + 2 * STATE]
    c_fwd = xbc[:, INNER + 2 * STATE:INNER + 3 * STATE]
    c_bwd = xbc[:, INNER + 3 * STATE:INNER + 4 * STATE]
    y_fwd = direction(u_vals, b_fwd, c_fwd, raw_dt[:, :HEADS], dt_bias[:HEADS], a_log[:HEADS], doc_ids)
    y_bwd = direction(u_vals[::-1], b_bwd[::-1], c_bwd[::-1], raw_dt[::-1, HEADS:], dt_bias[HEADS:], a_log[HEADS:], doc_ids[::-1])[::-1]
    diag_y = (u_vals.reshape(row_len, HEADS, HEAD_DIM) * skip[:, None]).reshape(row_len, INNER)
    y_sum = low_back(y_fwd + diag_y + y_bwd)
    gated = low(gated_norm(y_sum, gate_z, gate_gain))
    out_branch = jnp.dot(gated, w_out.T, precision=HIGHEST_PREC)
    return x_row + valid[:, None] * out_branch

def reference(tokens, starts, pad_len, norm_gain, w_in, w_dt, conv_w, conv_b, dt_bias, a_log, skip, gate_gain, w_out, cotangent):

    def forward_all(x_all, *params):

        def one_row(item):
            return row_forward(params, item[0], item[1], item[2])
        return lax.map(jax.checkpoint(one_row), (x_all, starts, pad_len))
    params = (norm_gain.astype(jnp.float32), w_in.astype(jnp.float32), w_dt.astype(jnp.float32), conv_w.astype(jnp.float32), conv_b.astype(jnp.float32), dt_bias.astype(jnp.float32), a_log.astype(jnp.float32), skip.astype(jnp.float32), gate_gain.astype(jnp.float32), w_out.astype(jnp.float32))
    mixed, pull_back = jax.vjp(forward_all, tokens.astype(jnp.float32), *params)
    grads = pull_back(cotangent.astype(jnp.float32))
    return (mixed.astype(jnp.bfloat16), grads[0].astype(jnp.bfloat16), grads[1], grads[2], grads[3], grads[4], grads[5], grads[6], grads[7], grads[8], grads[9], grads[10])
```

```python
import functools

import jax
import jax.numpy as jnp
from jax import lax
from jax.experimental import pallas as pl
from jax.experimental.pallas import tpu as pltpu
from jax.sharding import PartitionSpec as P

BLOCK = 160
HALO = 16
LANES = 128
CARRY = 16
EPSILON = 1e-05
BF = jnp.bfloat16
F32 = jnp.float32
FAR = -1e30
VMEM_BYTES = 58 * 1024 * 1024


def dot(a, b):
    return lax.dot_general(a, b, (((1,), (0,)), ((), ())), preferred_element_type=F32)


def dot_nt(a, b):
    return lax.dot_general(a, b, (((1,), (1,)), ((), ())), preferred_element_type=F32)


def dot_tn(a, b):
    return lax.dot_general(a, b, (((0,), (0,)), ((), ())), preferred_element_type=F32)


def pieces(values, count):
    parts = []
    for _ in range(count - 1):
        part = values.astype(BF)
        parts.append(part)
        values = values - part.astype(F32)
    parts.append(values.astype(BF))
    return parts


def exact(op, values, ones, count):
    total = None
    for part in pieces(values, count):
        term = op(part, ones)
        total = term if total is None else total + term
    return total


def head_map(first, width, head_dim):
    lane = lax.broadcasted_iota(jnp.int32, (LANES, width), 0)
    head = lax.broadcasted_iota(jnp.int32, (LANES, width), 1) // head_dim
    return jnp.where(lane == head + first, 1.0, 0.0).astype(BF)


def head_maps(heads, width, head_dim):
    return head_map(0, width, head_dim), head_map(heads, width, head_dim)


def triangles():
    row = lax.broadcasted_iota(jnp.int32, (BLOCK, BLOCK), 0)
    col = lax.broadcasted_iota(jnp.int32, (BLOCK, BLOCK), 1)
    return (
        jnp.where(row >= col, 1.0, 0.0).astype(BF),
        jnp.where(row <= col, 1.0, 0.0).astype(BF),
    )


def doc_of(places, starts_ref, row):
    total = (starts_ref[row, 0] <= places).astype(jnp.int32)
    for j in range(1, starts_ref.shape[1]):
        total = total + (starts_ref[row, j] <= places).astype(jnp.int32)
    return total


def column_places(count, first):
    return lax.broadcasted_iota(jnp.int32, (count, 1), 0) + first


def front(dims, info, starts, pads, halo, own, other, gain, w_pre, conv_w, conv_b, bias, a_log,
          normed_o, pre_o, xbc_o, dsil_o, tab_o, cumt_o, v_o, local_o, decay_o, send_o, xs, ps):
    heads, head_dim, state, row_len = dims
    width = heads * head_dim
    row = pl.program_id(0)
    base, core = info[0, 0], info[0, 1]
    half = own.shape[1]
    span = 2 * half
    blocks = span // BLOCK
    conv_len = conv_w.shape[0]
    conv_width = conv_w.shape[1]
    xs[0:HALO] = halo[0].astype(F32)
    xs[pl.ds(pl.multiple_of(HALO + core * half, 16), half)] = own[0].astype(F32)
    xs[pl.ds(pl.multiple_of(HALO + (1 - core) * half, 16), half)] = other[0].astype(F32)
    x = xs[...]
    scale = lax.rsqrt(jnp.mean(x * x, axis=-1, keepdims=True) + EPSILON)
    normed = (x * scale * gain[...]).astype(BF)
    normed_o[0] = normed
    projected = dot(normed, w_pre[...])
    pre = projected[:, :conv_width].astype(BF)
    pre_o[0] = pre
    ps[...] = pre.astype(F32)
    raw = projected[HALO:, conv_width:].astype(BF).astype(F32)
    places = column_places(span, base)
    doc = doc_of(places, starts, row)
    valid = (places < row_len - pads[row, 0]).astype(F32)
    summed = conv_b[...]
    for k in range(conv_len):
        back = conv_len - 1 - k
        ok = (doc_of(places - back, starts, row) == doc).astype(F32)
        summed = summed + ps[HALO - back : HALO - back + span] * conv_w[k : k + 1] * ok
    gate = 1.0 / (1.0 + jnp.exp(-summed))
    xbc = (summed * gate * valid).astype(BF)
    xbc_o[0] = xbc
    dsil_o[0] = gate * (1.0 + summed * (1.0 - gate)) * valid
    u = xbc[:, :width].astype(F32)
    map_f, map_b = head_maps(heads, width, head_dim)
    lower, upper = triangles()
    forward = lax.broadcasted_iota(jnp.int32, (1, LANES), 1) < heads
    shifted_raw = raw + bias[...]
    step = jnp.maximum(shifted_raw, 0.0) + jnp.log1p(jnp.exp(-jnp.abs(shifted_raw)))
    slope = 1.0 / (1.0 + jnp.exp(-shifted_raw))
    logs = -step * jnp.exp(a_log[...])
    tab_o[0, 0] = step
    tab_o[0, 4] = slope
    locals_f, locals_b, decays_f, decays_b = [], [], [], []
    for b in range(blocks):
        at = slice(b * BLOCK, (b + 1) * BLOCK)
        step_b, logs_b, doc_b = step[at], logs[at], doc[at]
        cum = jnp.where(
            forward,
            exact(lambda p, m: dot(m, p), logs_b, lower, 3),
            exact(lambda p, m: dot(m, p), logs_b, upper, 3),
        )
        turned = jnp.where(
            lax.broadcasted_iota(jnp.int32, (LANES, 1), 0) < heads,
            exact(lambda p, m: dot_tn(p, m), logs_b, upper, 3),
            exact(lambda p, m: dot_tn(p, m), logs_b, lower, 3),
        )
        cumt_o[0, b] = turned[: cumt_o.shape[2]]
        first_place = base + b * BLOCK
        end_f = doc_of(first_place + BLOCK - 1, starts, row)
        end_b = doc_of(first_place, starts, row)
        near_f = doc_of(first_place - 1, starts, row)
        near_b = doc_of(first_place + BLOCK, starts, row)
        final = jnp.where(forward, cum[BLOCK - 1 : BLOCK], cum[0:1])
        tail = jnp.exp(final - cum) * (
            doc_b == jnp.where(forward, end_f, end_b)
        ).astype(F32)
        reach = jnp.exp(cum) * (doc_b == jnp.where(forward, near_f, near_b)).astype(F32)
        tab_o[0, 1, at] = cum
        tab_o[0, 2, at] = tail
        tab_o[0, 3, at] = reach
        decay = jnp.broadcast_to(
            jnp.where(forward, reach[BLOCK - 1 : BLOCK], reach[0:1]), (8, LANES)
        )
        for d, head_ones, kept, rates in (
            (0, map_f, locals_f, decays_f),
            (1, map_b, locals_b, decays_b),
        ):
            u_b = u[at]
            v_o[0, d, at] = (exact(dot, step_b, head_ones, 2) * u_b).astype(BF)
            tailed = (exact(dot, tail * step_b, head_ones, 2) * u_b).astype(BF)
            b_mat = xbc[at, width + d * state : width + (d + 1) * state]
            local = dot_tn(b_mat, tailed)
            rate = exact(dot, decay, head_ones, 3)
            local_o[0, b, d] = local
            decay_o[0, b, d] = rate
            kept.append(local)
            rates.append(rate[0:1])
    for d, kept, rates, order in (
        (0, locals_f, decays_f, range(blocks)),
        (1, locals_b, decays_b, reversed(range(blocks))),
    ):
        total, rate = None, None
        for b in order:
            total = kept[b] if total is None else rates[b] * total + kept[b]
            rate = rates[b] if rate is None else rate * rates[b]
        send_o[d, 0, 0:state] = total.astype(BF)
        send_o[d, 0, state:] = carried_rows(rate)


def carried_rows(rate):
    coarse = rate.astype(BF)
    fine = (rate - coarse.astype(F32)).astype(BF)
    row = lax.broadcasted_iota(jnp.int32, (CARRY, rate.shape[1]), 0)
    return jnp.where(
        row == 0, coarse.astype(F32), jnp.where(row == 1, fine.astype(F32), 0.0)
    ).astype(BF)


def compose(received, place, count, state, up):
    total, rate = None, None
    for k in range(1, count):
        part = received[(k - 1) if up else (count - k - 1)]
        there = (place - k >= 0) if up else (place + k < count)
        there = there.astype(F32)
        term = part[0:state].astype(F32) * there
        total = term if total is None else total + rate * term
        hop = part[state : state + 1].astype(F32) + part[state + 1 : state + 2].astype(F32)
        rate = hop if rate is None else rate * hop
    return total


def pair_masks(first_place, starts, row):
    rows = lax.broadcasted_iota(jnp.int32, (BLOCK, BLOCK), 0)
    cols = lax.broadcasted_iota(jnp.int32, (BLOCK, BLOCK), 1)
    doc_rows = doc_of(column_places(BLOCK, first_place), starts, row)
    row_places = lax.broadcasted_iota(jnp.int32, (1, BLOCK), 1) + first_place
    same = doc_rows == doc_of(row_places, starts, row)
    return (
        jnp.where(same & (rows > cols), 0.0, FAR),
        jnp.where(same & (rows < cols), 0.0, FAR),
    )


def inner(dims, info, starts, xbc, tab, cumt, v, y_o):
    heads, head_dim, state, _ = dims
    width = heads * head_dim
    row, block = pl.program_id(0), pl.program_id(1)
    masks = pair_masks(info[0, 0] + block * BLOCK, starts, row)
    low_half = lax.broadcasted_iota(jnp.int32, (1, LANES), 1) < head_dim
    for d in range(2):
        b_mat = xbc[0, :, width + d * state : width + (d + 1) * state]
        c_mat = xbc[0, :, width + (2 + d) * state : width + (3 + d) * state]
        scores = dot_nt(c_mat, b_mat)
        for pair in range(heads // 2):
            at = slice(pair * LANES, (pair + 1) * LANES)
            values = v[0, d, :, at]
            outs = []
            for h in (2 * pair, 2 * pair + 1):
                lane = d * heads + h
                gap = tab[0, 0, :, lane : lane + 1] - cumt[0, 0, lane : lane + 1, :]
                mixing = (jnp.exp(gap + masks[d]) * scores).astype(BF)
                outs.append(dot(mixing, values))
            y_o[0, d, :, at] = jnp.where(low_half, outs[0], outs[1])


def outer(dims, count, info, starts, pads, received, local, decay, xbc, tab, y_in, normed, cot_own,
          cot_other, skip, gate_gain, w_gate, w_out, y_o, inc_o, sum_o, z_o, dg_o, dout_o, cs):
    heads, head_dim, state, row_len = dims
    width = heads * head_dim
    row = pl.program_id(0)
    base, core, place = info[0, 0], info[0, 1], info[0, 2]
    half = cot_own.shape[1]
    span = 2 * half
    blocks = span // BLOCK
    parts = [received[k, 0] for k in range(count - 1)]
    entering = [[None] * 2 for _ in range(blocks)]
    now = compose(parts, place, count, state, True)
    for b in range(blocks):
        entering[b][0] = now
        now = decay[0, b, 0, 0:1] * now + local[0, b, 0]
    now = compose(parts, place, count, state, False)
    for b in reversed(range(blocks)):
        entering[b][1] = now
        now = decay[0, b, 1, 0:1] * now + local[0, b, 1]
    maps = head_maps(heads, width, head_dim)
    for b in range(blocks):
        at = slice(b * BLOCK, (b + 1) * BLOCK)
        for d in range(2):
            inc_o[0, b, d] = entering[b][d]
            c_mat = xbc[0, at, width + (2 + d) * state : width + (3 + d) * state]
            raw = dot(c_mat, entering[b][d].astype(BF))
            y_o[0, d, at] = y_in[0, d, at] + exact(dot, tab[0, 0, at], maps[d], 2) * raw
    u = xbc[0, :, :width].astype(F32)
    y = y_o[0, 0] + skip[...] * u + y_o[0, 1]
    z = dot(normed[0, HALO:], w_gate[...])
    v = y * z * (1.0 / (1.0 + jnp.exp(-z)))
    cs[pl.ds(pl.multiple_of(core * half, 16), half)] = cot_own[0].astype(F32)
    cs[pl.ds(pl.multiple_of((1 - core) * half, 16), half)] = cot_other[0].astype(F32)
    places = column_places(span, base)
    valid = (places < row_len - pads[row, 0]).astype(F32)
    d_out = (cs[...] * valid).astype(BF)
    dout_o[0] = d_out
    d_gated = dot(d_out, w_out[...])
    lane = lax.broadcasted_iota(jnp.int32, (1, LANES), 1)
    squares = jnp.sum(v * v, axis=-1, keepdims=True)
    against = jnp.sum(d_gated * gate_gain[...] * v, axis=-1, keepdims=True)
    sum_o[0] = jnp.where(lane == 0, squares, jnp.where(lane == 1, against, 0.0))
    z_o[0] = z
    dg_o[0] = d_gated


def turn(dims, inner_width, sums, others, xbc, tab, y_in, z_in, dg_in, dout, normed, decay, skip,
         gate_gain, w_out, dy_o, dz_o, enter_o, send_o, branch_o, grad_out_o, grad_gate_o, gain_o,
         skip_o, acc_out, acc_gate):
    heads, head_dim, state, _ = dims
    width = heads * head_dim
    row = pl.program_id(0)
    span = dout.shape[1]
    blocks = span // BLOCK
    total = sums[0] + others[0]
    scale = lax.rsqrt(total[:, 0:1] * (1.0 / inner_width) + EPSILON)
    against = total[:, 1:2]
    u = xbc[0, :, :width].astype(F32)
    y = y_in[0, 0] + skip[...] * u + y_in[0, 1]
    z = z_in[0]
    gate = 1.0 / (1.0 + jnp.exp(-z))
    silu = z * gate
    v = y * silu
    unit = v * scale
    gated = (unit * gate_gain[...]).astype(BF)
    d_gated = dg_in[0]
    d_v = scale * (d_gated * gate_gain[...]) - unit * (
        scale * scale * against * (1.0 / inner_width)
    )
    dy = (d_v * silu).astype(BF)
    dz = (d_v * y * gate * (1.0 + z * (1.0 - gate))).astype(BF)
    dy_o[0] = dy
    dz_o[0] = dz
    dy_f = dy.astype(F32)
    branch_o[0] = dot_nt(gated, w_out[...])

    @pl.when(row == 0)
    def _():
        acc_out[...] = jnp.zeros_like(acc_out)
        acc_gate[...] = jnp.zeros_like(acc_gate)
        gain_o[...] = jnp.zeros_like(gain_o)
        skip_o[...] = jnp.zeros_like(skip_o)

    acc_out[...] += dot_tn(dout[0], gated)
    acc_gate[...] += dot_tn(normed[0, HALO:], dz)
    gain_o[...] += jnp.sum(d_gated * unit, axis=0, keepdims=True)
    skip_o[...] += jnp.sum(dy_f * u, axis=0, keepdims=True)

    @pl.when(row == pl.num_programs(0) - 1)
    def _():
        grad_out_o[...] = acc_out[...].astype(BF)
        grad_gate_o[...] = acc_gate[...].astype(BF)

    maps = head_maps(heads, width, head_dim)
    for d in range(2):
        gone, rate = None, None
        for b in reversed(range(blocks)) if d == 0 else range(blocks):
            at = slice(b * BLOCK, (b + 1) * BLOCK)
            c_mat = xbc[0, at, width + (2 + d) * state : width + (3 + d) * state]
            weighed = (exact(dot, tab[0, 0, at], maps[d], 2) * dy_f[at]).astype(BF)
            enter = dot_tn(c_mat, weighed)
            enter_o[0, b, d] = enter
            own = decay[0, b, d, 0:1]
            gone = enter if gone is None else enter + own * gone
            rate = own if rate is None else rate * own
        send_o[d, 0, 0:state] = gone.astype(BF)
        send_o[d, 0, state:] = carried_rows(rate)


def inner_back(dims, info, starts, xbc, tab, cumt, v, dy, y_in, inc, dv_o, dbc_o, along_o):
    heads, head_dim, state, _ = dims
    width = heads * head_dim
    row, block = pl.program_id(0), pl.program_id(1)
    masks = pair_masks(info[0, 0] + block * BLOCK, starts, row)
    low_half = lax.broadcasted_iota(jnp.int32, (1, LANES), 1) < head_dim
    maps = head_maps(heads, width, head_dim)
    dy_all = dy[0].astype(F32)
    along = None
    for d in range(2):
        b_mat = xbc[0, :, width + d * state : width + (d + 1) * state]
        c_mat = xbc[0, :, width + (2 + d) * state : width + (3 + d) * state]
        scores = dot_nt(c_mat, b_mat)
        d_scores = jnp.zeros((BLOCK, BLOCK), F32)
        for pair in range(heads // 2):
            at = slice(pair * LANES, (pair + 1) * LANES)
            values = v[0, d, :, at]
            grads = dy[0, :, at]
            outs = []
            for h in (2 * pair, 2 * pair + 1):
                lane = d * heads + h
                gap = tab[0, 1, :, lane : lane + 1] - cumt[0, 0, lane : lane + 1, :]
                spread = jnp.exp(gap + masks[d])
                mixing = (spread * scores).astype(BF)
                mine = low_half if h % 2 == 0 else ~low_half
                d_mixing = dot_nt(jnp.where(mine, grads, jnp.zeros_like(grads)), values)
                d_scores = d_scores + d_mixing * spread
                outs.append(dot_tn(mixing, grads))
            dv_o[0, d, :, at] = jnp.where(low_half, outs[0], outs[1])
        d_scores = d_scores.astype(BF)
        weighed = (exact(dot, tab[0, 3], maps[d], 2) * dy_all).astype(BF)
        d_c = dot(d_scores, b_mat) + dot_nt(weighed, inc[0, 0, d].astype(BF))
        d_b = dot_tn(d_scores, c_mat)
        dbc_o[0, :, d * state : (d + 1) * state] = d_b
        dbc_o[0, :, (2 + d) * state : (3 + d) * state] = d_c
        term = exact(dot_nt, dy_all * y_in[0, d], maps[d], 2)
        along = term if along is None else along + term
    along_o[0] = along


def back(dims, count, info, starts, received, enter, decay, inc, xbc, tab, v, dv, dbc, along, dy,
         dsil, pre, normed, dz, skip, a_log, conv_w, w_pre, w_gate, grad_pre_o, dn_o, conv_w_o,
         conv_b_o, small_o, acc, pad, ps):
    heads, head_dim, state, _ = dims
    width = heads * head_dim
    row = pl.program_id(0)
    base, place = info[0, 0], info[0, 2]
    span = dy.shape[1]
    blocks = span // BLOCK
    conv_len, conv_width = conv_w.shape
    parts = [received[k, 0] for k in range(count - 1)]
    leaving = [[None] * 2 for _ in range(blocks)]
    now = compose(parts, place, count, state, False)
    for b in reversed(range(blocks)):
        leaving[b][0] = now
        now = enter[0, b, 0] + decay[0, b, 0, 0:1] * now
    now = compose(parts, place, count, state, True)
    for b in range(blocks):
        leaving[b][1] = now
        now = enter[0, b, 1] + decay[0, b, 1, 0:1] * now
    maps = head_maps(heads, width, head_dim)
    lower, upper = triangles()
    forward = lax.broadcasted_iota(jnp.int32, (1, LANES), 1) < heads
    rate = jnp.exp(a_log[...])
    rows = lax.broadcasted_iota(jnp.int32, (BLOCK, 1), 0)

    @pl.when(row == 0)
    def _():
        acc[...] = jnp.zeros_like(acc)
        conv_w_o[...] = jnp.zeros_like(conv_w_o)
        conv_b_o[...] = jnp.zeros_like(conv_b_o)
        small_o[...] = jnp.zeros_like(small_o)
        pad[0:HALO] = jnp.zeros((HALO, conv_width), F32)
        pad[HALO + span :] = jnp.zeros((pad.shape[0] - HALO - span, conv_width), F32)

    raws = []
    for b in range(blocks):
        at = slice(b * BLOCK, (b + 1) * BLOCK)
        u = xbc[0, at, :width].astype(F32)
        step, tail, slope = tab[0, 0, at], tab[0, 2, at], tab[0, 4, at]
        reach = tab[0, 3, at]
        d_u = skip[...] * dy[0, at].astype(F32)
        through = None
        direct = None
        ended = None
        closing = None
        d_bc = []
        for d in range(2):
            leave = leaving[b][d].astype(BF)
            b_mat = xbc[0, at, width + d * state : width + (d + 1) * state]
            v_d = v[0, d, at].astype(F32)
            dv_state = exact(dot, tail, maps[d], 2) * dot(b_mat, leave)
            dv_all = dv[0, d, at] + dv_state
            tailed = (exact(dot, tail * step, maps[d], 2) * u).astype(BF)
            d_bc.append(dot_nt(tailed, leave))
            d_u = d_u + exact(dot, step, maps[d], 2) * dv_all
            terms = (
                exact(dot_nt, v_d * dv_all, maps[d], 2),
                exact(dot_nt, u * dv_all, maps[d], 2),
                exact(
                    dot_nt,
                    jnp.broadcast_to(jnp.sum(v_d * dv_state, axis=0, keepdims=True), (8, width)),
                    maps[d],
                    3,
                ),
                exact(
                    dot_nt,
                    jnp.broadcast_to(
                        jnp.sum(leaving[b][d] * inc[0, b, d], axis=0, keepdims=True), (8, width)
                    ),
                    maps[d],
                    3,
                ),
            )
            if d == 0:
                through, direct, ended, closing = terms
            else:
                through = through + terms[0]
                direct = direct + terms[1]
                ended = ended + terms[2]
                closing = closing + terms[3]
        final = jnp.where(forward, reach[BLOCK - 1 : BLOCK], reach[0:1])
        at_end = jnp.where(
            forward, (rows == BLOCK - 1).astype(F32), (rows == 0).astype(F32)
        )
        d_cum = along[0, at] - through + at_end * (ended[0:1] + closing[0:1] * final)
        d_logs = jnp.where(
            forward,
            exact(lambda p, m: dot(m, p), d_cum, upper, 3),
            exact(lambda p, m: dot(m, p), d_cum, lower, 3),
        )
        d_step = direct - rate * d_logs
        d_raw = d_step * slope
        raws.append(d_raw.astype(BF))
        small_o[0:1] += jnp.sum(d_raw, axis=0, keepdims=True)
        small_o[1:2] += jnp.sum(-step * rate * d_logs, axis=0, keepdims=True)
        pad[HALO + b * BLOCK : HALO + (b + 1) * BLOCK, 0:width] = d_u * dsil[0, at, 0:width]
        d_bc_all = jnp.concatenate(
            [d_bc[0], d_bc[1], jnp.zeros((BLOCK, 2 * state), F32)], axis=1
        )
        pad[HALO + b * BLOCK : HALO + (b + 1) * BLOCK, width:] = (dbc[0, at] + d_bc_all) * dsil[
            0, at, width:
        ]
    ps[...] = pre[0].astype(F32)
    places = column_places(span, base)
    doc = doc_of(places, starts, row)
    outs = pad[HALO : HALO + span]
    conv_b_o[...] += jnp.sum(outs, axis=0, keepdims=True)
    ext_places = column_places(HALO + span, base - HALO)
    ext_doc = doc_of(ext_places, starts, row)
    d_pre = None
    for k in range(conv_len):
        ahead = conv_len - 1 - k
        ok = (doc_of(places - ahead, starts, row) == doc).astype(F32)
        conv_w_o[k : k + 1] += jnp.sum(
            outs * ok * ps[HALO - ahead : HALO - ahead + span], axis=0, keepdims=True
        )
        ok_ext = (doc_of(ext_places + ahead, starts, row) == ext_doc).astype(F32)
        term = pad[ahead : ahead + HALO + span] * ok_ext * conv_w[k : k + 1]
        d_pre = term if d_pre is None else d_pre + term
    d_raws = jnp.concatenate([jnp.zeros((HALO, LANES), BF)] + raws, axis=0)
    d_all = jnp.concatenate([d_pre.astype(BF), d_raws], axis=1)
    acc[...] += dot_tn(normed[0], d_all)
    dn = dot_nt(d_all, w_pre[...])
    dn_o[0, 0:HALO] = dn[0:HALO]
    dn_o[0, HALO:] = dn[HALO:] + dot_nt(dz[0], w_gate[...])

    @pl.when(row == pl.num_programs(0) - 1)
    def _():
        grad_pre_o[...] = acc[...].astype(BF)


def finish(dims, info, pads, own, cot, gain, dn, dn_other, rim_a, rim_b, branch, branch_other,
           mixed_o, grad_o, gain_o, ds):
    row_len = dims[3]
    row = pl.program_id(0)
    base, core, place, count = info[0, 0], info[0, 1], info[0, 2], info[0, 3]
    half = own.shape[1]
    x = own[0].astype(F32)
    places = column_places(half, base + core * half)
    valid = (places < row_len - pads[row, 0]).astype(F32)
    mixed_o[0] = (x + valid * (branch[0] + branch_other[0].astype(F32))).astype(BF)
    ds[...] = dn[0] + dn_other[0].astype(F32)
    takes = ((core == 1) & (place + 1 < count)).astype(F32)
    ds[half - HALO :] += takes * (rim_a[0].astype(F32) + rim_b[0].astype(F32))
    d_normed = ds[...]
    scale = lax.rsqrt(jnp.mean(x * x, axis=-1, keepdims=True) + EPSILON)
    weighed = d_normed * gain[...]
    along = jnp.mean(weighed * x, axis=-1, keepdims=True)
    dx = scale * weighed - x * (scale * scale * scale * along)
    grad_o[0] = (cot[0].astype(F32) + dx).astype(BF)

    @pl.when(row == 0)
    def _():
        gain_o[...] = jnp.zeros_like(gain_o)

    gain_o[...] += jnp.sum(d_normed * x * scale, axis=0, keepdims=True)


SMEM = pl.BlockSpec(memory_space=pltpu.SMEM)


def whole(*shape):
    return pl.BlockSpec(shape, lambda *_: (0,) * len(shape))


def by_row(*shape):
    return pl.BlockSpec((1,) + shape, lambda r, *_: (r,) + (0,) * len(shape))


def second(*shape):
    return pl.BlockSpec(
        (shape[0], 1) + shape[1:], lambda r, *_: (0, r) + (0,) * (len(shape) - 1)
    )


def run(body, grid, ins, outs, scratch=(), flops=0, name=None):
    arrays = [a for a, _ in ins]
    moved = sum(a.size * a.dtype.itemsize for a in arrays) + sum(
        s.size * s.dtype.itemsize for s, _ in outs
    )
    return pl.pallas_call(
        body,
        grid=grid,
        out_shape=[s for s, _ in outs],
        in_specs=[b for _, b in ins],
        out_specs=[b for _, b in outs],
        scratch_shapes=list(scratch),
        compiler_params=pltpu.CompilerParams(
            vmem_limit_bytes=VMEM_BYTES,
            dimension_semantics=("arbitrary",) * len(grid),
        ),
        cost_estimate=pl.CostEstimate(
            flops=flops, bytes_accessed=moved, transcendentals=flops // 500
        ),
        name=name,
    )(*arrays)


def shape_of(dtype, *dims):
    return jax.ShapeDtypeStruct(dims, dtype)


def swapped(value):
    return lax.ppermute(value, "dir", [(0, 1), (1, 0)])


def rotated(value, steps):
    count = lax.axis_size("seq")
    return lax.ppermute(value, "seq", [(i, (i + steps) % count) for i in range(count)])


def rotated_to(value, steps, cross):
    count = lax.axis_size("seq")
    pairs = []
    for i in range(count):
        for c in range(2):
            pairs.append((i * 2 + c, (i + steps) % count * 2 + (1 - c if cross else c)))
    return lax.ppermute(value, ("seq", "dir"), pairs)


def around(value):
    count, place = lax.axis_size("seq"), lax.axis_index("seq")
    out = []
    for k in range(1, count):
        chosen = jnp.where(place + k < count, value[0], value[1])
        out.append(rotated(chosen, k))
    return jnp.stack(out)


def shards(tokens, starts, pad_len, norm_gain, w_in, w_dt, conv_w, conv_b, dt_bias, a_log, skip,
           gate_gain, w_out, cotangent):
    rows, half, model = tokens.shape
    span = 2 * half
    count = lax.axis_size("seq")
    row_len = span * count
    blocks = span // BLOCK
    inner_width = gate_gain.shape[0]
    all_heads = skip.shape[0]
    heads = all_heads // 2
    head_dim = inner_width // all_heads
    width = heads * head_dim
    xbc_width = conv_w.shape[1]
    state = (xbc_width - inner_width) // 4
    conv_len = conv_w.shape[0]
    conv_width = width + 4 * state
    pre_width = conv_width + LANES
    ext = HALO + span
    dims = (heads, head_dim, state, row_len)
    place, core = lax.axis_index("seq"), lax.axis_index("dir")
    info = jnp.stack([place * span, core, place, jnp.int32(count)]).astype(jnp.int32)[None]
    pads = pad_len[:, None]
    shard = w_in.shape[0]
    pad_dt = jnp.zeros((shard, LANES - 2 * heads), BF)

    def columns(c):
        return (
            jnp.concatenate(
                [
                    w_in[:, inner_width + c * width : inner_width + (c + 1) * width],
                    w_in[:, 2 * inner_width :],
                    w_dt[:, c * heads : (c + 1) * heads],
                    w_dt[:, all_heads + c * heads : all_heads + (c + 1) * heads],
                    pad_dt,
                ],
                axis=1,
            ),
            w_in[:, c * width : (c + 1) * width],
            w_out[:, c * width : (c + 1) * width],
        )

    first, latter = columns(0), columns(1)
    is_late = core == 1

    def both(own, other):
        return jnp.where(
            is_late,
            jnp.concatenate([other, own], axis=0),
            jnp.concatenate([own, other], axis=0),
        )

    def gathered(i):
        keep = jnp.where(is_late, latter[i], first[i])
        give = jnp.where(is_late, first[i], latter[i])
        return lax.all_gather(both(keep, swapped(give)), ("dp", "seq"), axis=0, tiled=True)

    w_pre = gathered(0)
    w_gate = gathered(1)
    w_out_c = gathered(2)
    tokens_other = swapped(tokens)
    cot_other = swapped(cotangent)
    rim = tokens[:, half - HALO :]
    halo = jnp.where(is_late, rotated_to(rim, 1, False), rotated_to(rim, 1, True))

    def mine(vector, size):
        return lax.dynamic_slice_in_dim(vector, core * size, size, axis=-1)

    conv_w_c = jnp.concatenate([mine(conv_w[:, :inner_width], width), conv_w[:, inner_width:]], axis=1)
    conv_b_c = jnp.concatenate([mine(conv_b[:inner_width], width), conv_b[inner_width:]])[None]
    filler = jnp.zeros((LANES - 2 * heads,), F32)
    bias_c = jnp.concatenate([mine(dt_bias[:all_heads], heads), mine(dt_bias[all_heads:], heads), filler])[None]
    a_log_c = jnp.concatenate([mine(a_log[:all_heads], heads), mine(a_log[all_heads:], heads), filler])[None]
    skip_c = jnp.repeat(mine(skip, heads), head_dim)[None]
    gate_gain_c = mine(gate_gain, width)[None]
    gain = norm_gain[None]
    packed = 2 * heads + (-2 * heads) % 8
    tokens_all = rows * span
    scan_flops = 4 * tokens_all * BLOCK * LANES * heads

    normed, pre, xbc, dsil, tab, cumt, v, local, decay, send = run(
        functools.partial(front, dims),
        (rows,),
        [
            (info, SMEM), (starts, SMEM), (pads, SMEM),
            (halo, by_row(HALO, model)), (tokens, by_row(half, model)),
            (tokens_other, by_row(half, model)), (gain, whole(1, model)),
            (w_pre, whole(model, pre_width)), (conv_w_c, whole(conv_len, conv_width)),
            (conv_b_c, whole(1, conv_width)), (bias_c, whole(1, LANES)), (a_log_c, whole(1, LANES)),
        ],
        [
            (shape_of(BF, rows, ext, model), by_row(ext, model)),
            (shape_of(BF, rows, ext, conv_width), by_row(ext, conv_width)),
            (shape_of(BF, rows, span, conv_width), by_row(span, conv_width)),
            (shape_of(F32, rows, span, conv_width), by_row(span, conv_width)),
            (shape_of(F32, rows, 5, span, LANES), by_row(5, span, LANES)),
            (shape_of(F32, rows, blocks, packed, BLOCK), by_row(blocks, packed, BLOCK)),
            (shape_of(BF, rows, 2, span, width), by_row(2, span, width)),
            (shape_of(F32, rows, blocks, 2, state, width), by_row(blocks, 2, state, width)),
            (shape_of(F32, rows, blocks, 2, 8, width), by_row(blocks, 2, 8, width)),
            (shape_of(BF, 2, rows, state + CARRY, width), second(2, state + CARRY, width)),
        ],
        [pltpu.VMEM((ext, model), F32), pltpu.VMEM((ext, conv_width), F32)],
        flops=2 * tokens_all * model * pre_width,
        name="front",
    )
    received = around(send)
    at_block = lambda *shape: pl.BlockSpec((1,) + shape, lambda r, b: (r, b) + (0,) * (len(shape) - 1))
    at_second = lambda *shape: pl.BlockSpec((1, shape[0]) + shape[1:], lambda r, b: (r, 0, b, 0))
    block_tab = lambda i: pl.BlockSpec((1, 1, BLOCK, LANES), lambda r, b: (r, i, b, 0))
    (y_inner,) = run(
        functools.partial(inner, dims),
        (rows, blocks),
        [
            (info, SMEM), (starts, SMEM), (xbc, at_block(BLOCK, conv_width)),
            (tab, block_tab(1)), (cumt, at_block(1, packed, BLOCK)),
            (v, at_second(2, BLOCK, width)),
        ],
        [(shape_of(F32, rows, 2, span, width), at_second(2, BLOCK, width))],
        flops=scan_flops,
        name="inner",
    )
    y_both, inc, sums, z, d_gated, d_out = run(
        functools.partial(outer, dims, count),
        (rows,),
        [
            (info, SMEM), (starts, SMEM), (pads, SMEM),
            (received, second(count - 1, state + CARRY, width)),
            (local, by_row(blocks, 2, state, width)), (decay, by_row(blocks, 2, 8, width)),
            (xbc, by_row(span, conv_width)),
            (tab, pl.BlockSpec((1, 1, span, LANES), lambda r: (r, 3, 0, 0))),
            (y_inner, by_row(2, span, width)), (normed, by_row(ext, model)),
            (cotangent, by_row(half, model)), (cot_other, by_row(half, model)),
            (skip_c, whole(1, width)), (gate_gain_c, whole(1, width)),
            (w_gate, whole(model, width)), (w_out_c, whole(model, width)),
        ],
        [
            (shape_of(F32, rows, 2, span, width), by_row(2, span, width)),
            (shape_of(F32, rows, blocks, 2, state, width), by_row(blocks, 2, state, width)),
            (shape_of(F32, rows, span, LANES), by_row(span, LANES)),
            (shape_of(F32, rows, span, width), by_row(span, width)),
            (shape_of(F32, rows, span, width), by_row(span, width)),
            (shape_of(BF, rows, span, model), by_row(span, model)),
        ],
        [pltpu.VMEM((span, model), F32)],
        flops=4 * tokens_all * model * width,
        name="outer",
    )
    sums_other = swapped(sums)
    dy, dz, enter, back_send, branch, grad_out, grad_gate, gate_sum, skip_sum = run(
        functools.partial(turn, dims, inner_width),
        (rows,),
        [
            (sums, by_row(span, LANES)), (sums_other, by_row(span, LANES)),
            (xbc, by_row(span, conv_width)),
            (tab, pl.BlockSpec((1, 1, span, LANES), lambda r: (r, 3, 0, 0))),
            (y_both, by_row(2, span, width)), (z, by_row(span, width)),
            (d_gated, by_row(span, width)), (d_out, by_row(span, model)),
            (normed, by_row(ext, model)), (decay, by_row(blocks, 2, 8, width)),
            (skip_c, whole(1, width)), (gate_gain_c, whole(1, width)),
            (w_out_c, whole(model, width)),
        ],
        [
            (shape_of(BF, rows, span, width), by_row(span, width)),
            (shape_of(BF, rows, span, width), by_row(span, width)),
            (shape_of(F32, rows, blocks, 2, state, width), by_row(blocks, 2, state, width)),
            (shape_of(BF, 2, rows, state + CARRY, width), second(2, state + CARRY, width)),
            (shape_of(F32, rows, span, model), by_row(span, model)),
            (shape_of(BF, model, width), whole(model, width)),
            (shape_of(BF, model, width), whole(model, width)),
            (shape_of(F32, 1, width), whole(1, width)),
            (shape_of(F32, 1, width), whole(1, width)),
        ],
        [pltpu.VMEM((model, width), F32), pltpu.VMEM((model, width), F32)],
        flops=6 * tokens_all * model * width,
        name="turn",
    )
    back_received = around(back_send[::-1])

    def reduced(grad):
        return lax.psum_scatter(grad, ("dp", "seq"), scatter_dimension=0, tiled=True)

    shard_out = reduced(grad_out)
    shard_gate = reduced(grad_gate)
    dv, dbc, along = run(
        functools.partial(inner_back, dims),
        (rows, blocks),
        [
            (info, SMEM), (starts, SMEM), (xbc, at_block(BLOCK, conv_width)),
            (tab, at_second(5, BLOCK, LANES)), (cumt, at_block(1, packed, BLOCK)),
            (v, at_second(2, BLOCK, width)), (dy, at_block(BLOCK, width)),
            (y_both, at_second(2, BLOCK, width)), (inc, at_block(1, 2, state, width)),
        ],
        [
            (shape_of(F32, rows, 2, span, width), at_second(2, BLOCK, width)),
            (shape_of(F32, rows, span, 4 * state), at_block(BLOCK, 4 * state)),
            (shape_of(F32, rows, span, LANES), at_block(BLOCK, LANES)),
        ],
        flops=2 * scan_flops,
        name="inner_back",
    )
    grad_pre, dn, sum_conv_w, sum_conv_b, small = run(
        functools.partial(back, dims, count),
        (rows,),
        [
            (info, SMEM), (starts, SMEM),
            (back_received, second(count - 1, state + CARRY, width)),
            (enter, by_row(blocks, 2, state, width)), (decay, by_row(blocks, 2, 8, width)),
            (inc, by_row(blocks, 2, state, width)), (xbc, by_row(span, conv_width)),
            (tab, by_row(5, span, LANES)), (v, by_row(2, span, width)),
            (dv, by_row(2, span, width)), (dbc, by_row(span, 4 * state)),
            (along, by_row(span, LANES)), (dy, by_row(span, width)),
            (dsil, by_row(span, conv_width)), (pre, by_row(ext, conv_width)),
            (normed, by_row(ext, model)), (dz, by_row(span, width)),
            (skip_c, whole(1, width)), (a_log_c, whole(1, LANES)),
            (conv_w_c, whole(conv_len, conv_width)), (w_pre, whole(model, pre_width)),
            (w_gate, whole(model, width)),
        ],
        [
            (shape_of(BF, model, pre_width), whole(model, pre_width)),
            (shape_of(F32, rows, ext, model), by_row(ext, model)),
            (shape_of(F32, conv_len, conv_width), whole(conv_len, conv_width)),
            (shape_of(F32, 1, conv_width), whole(1, conv_width)),
            (shape_of(F32, 8, LANES), whole(8, LANES)),
        ],
        [
            pltpu.VMEM((model, pre_width), F32),
            pltpu.VMEM((ext + 8, conv_width), F32),
            pltpu.VMEM((ext, conv_width), F32),
        ],
        flops=6 * tokens_all * model * pre_width,
        name="back",
    )
    shard_pre = reduced(grad_pre)

    def halves(values, first_row):
        keep = lax.dynamic_slice_in_dim(values, first_row + core * half, half, axis=1)
        give = lax.dynamic_slice_in_dim(values, first_row + (1 - core) * half, half, axis=1)
        return keep, swapped(give.astype(BF))

    dn_own, dn_other = halves(dn, HALO)
    branch_own, branch_other = halves(branch, 0)
    edge = dn[:, :HALO].astype(BF)
    rim_a, rim_b = rotated_to(edge, -1, False), rotated_to(edge, -1, True)
    mixed, tokens_grad, gain_sum = run(
        functools.partial(finish, dims),
        (rows,),
        [
            (info, SMEM), (pads, SMEM), (tokens, by_row(half, model)),
            (cotangent, by_row(half, model)), (gain, whole(1, model)),
            (dn_own, by_row(half, model)), (dn_other, by_row(half, model)),
            (rim_a, by_row(HALO, model)), (rim_b, by_row(HALO, model)),
            (branch_own, by_row(half, model)), (branch_other, by_row(half, model)),
        ],
        [
            (shape_of(BF, rows, half, model), by_row(half, model)),
            (shape_of(BF, rows, half, model), by_row(half, model)),
            (shape_of(F32, 1, model), whole(1, model)),
        ],
        [pltpu.VMEM((half, model), F32)],
        name="finish",
    )

    def placed(values, size):
        empty = jnp.zeros_like(values)
        return jnp.where(
            is_late,
            jnp.concatenate([empty, values], axis=-1),
            jnp.concatenate([values, empty], axis=-1),
        )

    def by_heads(values):
        return placed(jnp.sum(values.reshape(heads, head_dim), axis=-1), heads)

    def by_step(values):
        return jnp.concatenate([placed(values[:heads], heads), placed(values[heads : 2 * heads], heads)])

    sum_norm, all_conv_w, all_conv_b, sum_bias, sum_alog, sum_skip, sum_gate = lax.psum(
        (
            gain_sum[0],
            jnp.concatenate([placed(sum_conv_w[:, :width], width), sum_conv_w[:, width:]], axis=1),
            jnp.concatenate([placed(sum_conv_b[0, :width], width), sum_conv_b[0, width:]]),
            by_step(small[0]),
            by_step(small[1]),
            by_heads(skip_sum[0]),
            placed(gate_sum[0], width),
        ),
        ("dp", "seq", "dir"),
    )

    def returned(value):
        own = lax.dynamic_slice_in_dim(value, core * shard, shard, axis=0)
        give = lax.dynamic_slice_in_dim(value, (1 - core) * shard, shard, axis=0)
        other = swapped(give)
        own, other = own.astype(F32), other.astype(F32)
        return jnp.where(is_late, other, own), jnp.where(is_late, own, other)

    out_a, out_b = returned(shard_out)
    gate_a, gate_b = returned(shard_gate)
    pre_a, pre_b = returned(shard_pre)
    owned_out = jnp.concatenate([out_a, out_b], axis=1)
    owned_in = jnp.concatenate(
        [
            gate_a, gate_b, pre_a[:, :width], pre_b[:, :width],
            pre_a[:, width:conv_width] + pre_b[:, width:conv_width],
        ],
        axis=1,
    )
    last = conv_width
    owned_dt = jnp.concatenate(
        [
            pre_a[:, last : last + heads], pre_b[:, last : last + heads],
            pre_a[:, last + heads : last + 2 * heads], pre_b[:, last + heads : last + 2 * heads],
        ],
        axis=1,
    )
    return (
        mixed, tokens_grad, sum_norm, owned_in, owned_dt, all_conv_w, all_conv_b, sum_bias,
        sum_alog, sum_skip, sum_gate, owned_out,
    )


def solution(mesh):
    weight = P(("dp", "seq", "dir"), None)
    values = P("dp", ("seq", "dir"), None)
    return jax.shard_map(
        shards,
        mesh=mesh,
        in_specs=(
            values, P("dp", None), P("dp"), P(), weight, weight, P(), P(), P(), P(), P(), P(),
            weight, values,
        ),
        out_specs=(
            values, values, P(), weight, weight, P(), P(), P(), P(), P(), P(), weight,
        ),
        check_vma=False,
    )
```

```python
import functools

import jax
import jax.numpy as jnp
from jax import lax
from jax.experimental import pallas as pl
from jax.experimental.pallas import tpu as pltpu
from jax.sharding import PartitionSpec as P

BLOCK = 160
HALO = 16
LANES = 128
CARRY = 16
EPSILON = 1e-05
BF = jnp.bfloat16
F32 = jnp.float32
FAR = -1e30
VMEM_BYTES = 58 * 1024 * 1024


def dot(a, b):
    return lax.dot_general(a, b, (((1,), (0,)), ((), ())), preferred_element_type=F32)


def dot_nt(a, b):
    return lax.dot_general(a, b, (((1,), (1,)), ((), ())), preferred_element_type=F32)


def dot_tn(a, b):
    return lax.dot_general(a, b, (((0,), (0,)), ((), ())), preferred_element_type=F32)


def pieces(values, count):
    parts = []
    for _ in range(count - 1):
        part = values.astype(BF)
        parts.append(part)
        values = values - part.astype(F32)
    parts.append(values.astype(BF))
    return parts


def exact(op, values, ones, count):
    total = None
    for part in pieces(values, count):
        term = op(part, ones)
        total = term if total is None else total + term
    return total


def head_map(first, width, head_dim):
    lane = lax.broadcasted_iota(jnp.int32, (LANES, width), 0)
    head = lax.broadcasted_iota(jnp.int32, (LANES, width), 1) // head_dim
    return jnp.where(lane == head + first, 1.0, 0.0).astype(BF)


def head_maps(heads, width, head_dim):
    return head_map(0, width, head_dim), head_map(heads, width, head_dim)


def triangles():
    row = lax.broadcasted_iota(jnp.int32, (BLOCK, BLOCK), 0)
    col = lax.broadcasted_iota(jnp.int32, (BLOCK, BLOCK), 1)
    return (
        jnp.where(row >= col, 1.0, 0.0).astype(BF),
        jnp.where(row <= col, 1.0, 0.0).astype(BF),
    )


def doc_of(places, starts_ref, row):
    total = (starts_ref[row, 0] <= places).astype(jnp.int32)
    for j in range(1, starts_ref.shape[1]):
        total = total + (starts_ref[row, j] <= places).astype(jnp.int32)
    return total


def column_places(count, first):
    return lax.broadcasted_iota(jnp.int32, (count, 1), 0) + first


def front(dims, info, starts, pads, halo, own, other, gain, w_pre, conv_w, conv_b, bias, a_log,
          normed_o, pre_o, xbc_o, dsil_o, tab_o, cumt_o, v_o, local_o, decay_o, send_o, xs, ps):
    heads, head_dim, state, row_len = dims
    width = heads * head_dim
    row = pl.program_id(0)
    base, core = info[0, 0], info[0, 1]
    half = own.shape[1]
    span = 2 * half
    blocks = span // BLOCK
    conv_len = conv_w.shape[0]
    conv_width = conv_w.shape[1]
    xs[0:HALO] = halo[0].astype(F32)
    xs[pl.ds(pl.multiple_of(HALO + core * half, 16), half)] = own[0].astype(F32)
    xs[pl.ds(pl.multiple_of(HALO + (1 - core) * half, 16), half)] = other[0].astype(F32)
    x = xs[...]
    scale = lax.rsqrt(jnp.mean(x * x, axis=-1, keepdims=True) + EPSILON)
    normed = (x * scale * gain[...]).astype(BF)
    normed_o[0] = normed
    projected = dot(normed, w_pre[...])
    pre = projected[:, :conv_width].astype(BF)
    pre_o[0] = pre
    ps[...] = pre.astype(F32)
    raw = projected[HALO:, conv_width:].astype(BF).astype(F32)
    places = column_places(span, base)
    doc = doc_of(places, starts, row)
    valid = (places < row_len - pads[row, 0]).astype(F32)
    summed = conv_b[...]
    for k in range(conv_len):
        back = conv_len - 1 - k
        ok = (doc_of(places - back, starts, row) == doc).astype(F32)
        summed = summed + ps[HALO - back : HALO - back + span] * conv_w[k : k + 1] * ok
    gate = 1.0 / (1.0 + jnp.exp(-summed))
    xbc = (summed * gate * valid).astype(BF)
    xbc_o[0] = xbc
    dsil_o[0] = gate * (1.0 + summed * (1.0 - gate)) * valid
    u = xbc[:, :width].astype(F32)
    map_f, map_b = head_maps(heads, width, head_dim)
    lower, upper = triangles()
    forward = lax.broadcasted_iota(jnp.int32, (1, LANES), 1) < heads
    shifted_raw = raw + bias[...]
    step = jnp.maximum(shifted_raw, 0.0) + jnp.log1p(jnp.exp(-jnp.abs(shifted_raw)))
    slope = 1.0 / (1.0 + jnp.exp(-shifted_raw))
    logs = -step * jnp.exp(a_log[...])
    tab_o[0, 0] = step
    tab_o[0, 4] = slope
    locals_f, locals_b, decays_f, decays_b = [], [], [], []
    for b in range(blocks):
        at = slice(b * BLOCK, (b + 1) * BLOCK)
        step_b, logs_b, doc_b = step[at], logs[at], doc[at]
        cum = jnp.where(
            forward,
            exact(lambda p, m: dot(m, p), logs_b, lower, 3),
            exact(lambda p, m: dot(m, p), logs_b, upper, 3),
        )
        turned = jnp.where(
            lax.broadcasted_iota(jnp.int32, (LANES, 1), 0) < heads,
            exact(lambda p, m: dot_tn(p, m), logs_b, upper, 3),
            exact(lambda p, m: dot_tn(p, m), logs_b, lower, 3),
        )
        cumt_o[0, b] = turned[: cumt_o.shape[2]]
        first_place = base + b * BLOCK
        end_f = doc_of(first_place + BLOCK - 1, starts, row)
        end_b = doc_of(first_place, starts, row)
        near_f = doc_of(first_place - 1, starts, row)
        near_b = doc_of(first_place + BLOCK, starts, row)
        final = jnp.where(forward, cum[BLOCK - 1 : BLOCK], cum[0:1])
        tail = jnp.exp(final - cum) * (
            doc_b == jnp.where(forward, end_f, end_b)
        ).astype(F32)
        reach = jnp.exp(cum) * (doc_b == jnp.where(forward, near_f, near_b)).astype(F32)
        tab_o[0, 1, at] = cum
        tab_o[0, 2, at] = tail
        tab_o[0, 3, at] = reach
        decay = jnp.broadcast_to(
            jnp.where(forward, reach[BLOCK - 1 : BLOCK], reach[0:1]), (8, LANES)
        )
        for d, head_ones, kept, rates in (
            (0, map_f, locals_f, decays_f),
            (1, map_b, locals_b, decays_b),
        ):
            u_b = u[at]
            v_o[0, d, at] = (exact(dot, step_b, head_ones, 2) * u_b).astype(BF)
            tailed = (exact(dot, tail * step_b, head_ones, 2) * u_b).astype(BF)
            b_mat = xbc[at, width + d * state : width + (d + 1) * state]
            local = dot_tn(b_mat, tailed)
            rate = exact(dot, decay, head_ones, 3)
            local_o[0, b, d] = local
            decay_o[0, b, d] = rate
            kept.append(local)
            rates.append(rate[0:1])
    for d, kept, rates, order in (
        (0, locals_f, decays_f, range(blocks)),
        (1, locals_b, decays_b, reversed(range(blocks))),
    ):
        total, rate = None, None
        for b in order:
            total = kept[b] if total is None else rates[b] * total + kept[b]
            rate = rates[b] if rate is None else rate * rates[b]
        send_o[d, 0, 0:state] = total.astype(BF)
        send_o[d, 0, state:] = carried_rows(rate)


def carried_rows(rate):
    coarse = rate.astype(BF)
    fine = (rate - coarse.astype(F32)).astype(BF)
    row = lax.broadcasted_iota(jnp.int32, (CARRY, rate.shape[1]), 0)
    return jnp.where(
        row == 0, coarse.astype(F32), jnp.where(row == 1, fine.astype(F32), 0.0)
    ).astype(BF)


def compose(received, place, count, state, up):
    total, rate = None, None
    for k in range(1, count):
        part = received[(k - 1) if up else (count - k - 1)]
        there = (place - k >= 0) if up else (place + k < count)
        there = there.astype(F32)
        term = part[0:state].astype(F32) * there
        total = term if total is None else total + rate * term
        hop = part[state : state + 1].astype(F32) + part[state + 1 : state + 2].astype(F32)
        rate = hop if rate is None else rate * hop
    return total


def pair_masks(first_place, starts, row):
    rows = lax.broadcasted_iota(jnp.int32, (BLOCK, BLOCK), 0)
    cols = lax.broadcasted_iota(jnp.int32, (BLOCK, BLOCK), 1)
    doc_rows = doc_of(column_places(BLOCK, first_place), starts, row)
    row_places = lax.broadcasted_iota(jnp.int32, (1, BLOCK), 1) + first_place
    same = doc_rows == doc_of(row_places, starts, row)
    return (
        jnp.where(same & (rows > cols), 0.0, FAR),
        jnp.where(same & (rows < cols), 0.0, FAR),
    )


def inner(dims, info, starts, xbc, tab, cumt, v, y_o):
    heads, head_dim, state, _ = dims
    width = heads * head_dim
    row, block = pl.program_id(0), pl.program_id(1)
    masks = pair_masks(info[0, 0] + block * BLOCK, starts, row)
    low_half = lax.broadcasted_iota(jnp.int32, (1, LANES), 1) < head_dim
    for d in range(2):
        b_mat = xbc[0, :, width + d * state : width + (d + 1) * state]
        c_mat = xbc[0, :, width + (2 + d) * state : width + (3 + d) * state]
        scores = dot_nt(c_mat, b_mat)
        for pair in range(heads // 2):
            at = slice(pair * LANES, (pair + 1) * LANES)
            values = v[0, d, :, at]
            outs = []
            for h in (2 * pair, 2 * pair + 1):
                lane = d * heads + h
                gap = tab[0, 0, :, lane : lane + 1] - cumt[0, 0, lane : lane + 1, :]
                mixing = (jnp.exp(gap + masks[d]) * scores).astype(BF)
                outs.append(dot(mixing, values))
            y_o[0, d, :, at] = jnp.where(low_half, outs[0], outs[1])


def outer(dims, count, info, starts, pads, received, local, decay, xbc, tab, y_in, normed, cot_own,
          cot_other, skip, gate_gain, w_gate, w_out, y_o, inc_o, sum_o, z_o, dg_o, dout_o, cs):
    heads, head_dim, state, row_len = dims
    width = heads * head_dim
    row = pl.program_id(0)
    base, core, place = info[0, 0], info[0, 1], info[0, 2]
    half = cot_own.shape[1]
    span = 2 * half
    blocks = span // BLOCK
    parts = [received[k, 0] for k in range(count - 1)]
    entering = [[None] * 2 for _ in range(blocks)]
    now = compose(parts, place, count, state, True)
    for b in range(blocks):
        entering[b][0] = now
        now = decay[0, b, 0, 0:1] * now + local[0, b, 0]
    now = compose(parts, place, count, state, False)
    for b in reversed(range(blocks)):
        entering[b][1] = now
        now = decay[0, b, 1, 0:1] * now + local[0, b, 1]
    maps = head_maps(heads, width, head_dim)
    for b in range(blocks):
        at = slice(b * BLOCK, (b + 1) * BLOCK)
        for d in range(2):
            inc_o[0, b, d] = entering[b][d]
            c_mat = xbc[0, at, width + (2 + d) * state : width + (3 + d) * state]
            raw = dot(c_mat, entering[b][d].astype(BF))
            y_o[0, d, at] = y_in[0, d, at] + exact(dot, tab[0, 0, at], maps[d], 2) * raw
    u = xbc[0, :, :width].astype(F32)
    y = y_o[0, 0] + skip[...] * u + y_o[0, 1]
    z = dot(normed[0, HALO:], w_gate[...])
    v = y * z * (1.0 / (1.0 + jnp.exp(-z)))
    cs[pl.ds(pl.multiple_of(core * half, 16), half)] = cot_own[0].astype(F32)
    cs[pl.ds(pl.multiple_of((1 - core) * half, 16), half)] = cot_other[0].astype(F32)
    places = column_places(span, base)
    valid = (places < row_len - pads[row, 0]).astype(F32)
    d_out = (cs[...] * valid).astype(BF)
    dout_o[0] = d_out
    d_gated = dot(d_out, w_out[...])
    lane = lax.broadcasted_iota(jnp.int32, (1, LANES), 1)
    squares = jnp.sum(v * v, axis=-1, keepdims=True)
    against = jnp.sum(d_gated * gate_gain[...] * v, axis=-1, keepdims=True)
    sum_o[0] = jnp.where(lane == 0, squares, jnp.where(lane == 1, against, 0.0))
    z_o[0] = z
    dg_o[0] = d_gated


def turn(dims, inner_width, sums, others, xbc, tab, y_in, z_in, dg_in, dout, normed, decay, skip,
         gate_gain, w_out, dy_o, dz_o, enter_o, send_o, branch_o, grad_out_o, grad_gate_o, gain_o,
         skip_o, acc_out, acc_gate):
    heads, head_dim, state, _ = dims
    width = heads * head_dim
    row = pl.program_id(0)
    span = dout.shape[1]
    blocks = span // BLOCK
    total = sums[0] + others[0]
    scale = lax.rsqrt(total[:, 0:1] * (1.0 / inner_width) + EPSILON)
    against = total[:, 1:2]
    u = xbc[0, :, :width].astype(F32)
    y = y_in[0, 0] + skip[...] * u + y_in[0, 1]
    z = z_in[0]
    gate = 1.0 / (1.0 + jnp.exp(-z))
    silu = z * gate
    v = y * silu
    unit = v * scale
    gated = (unit * gate_gain[...]).astype(BF)
    d_gated = dg_in[0]
    d_v = scale * (d_gated * gate_gain[...]) - unit * (
        scale * scale * against * (1.0 / inner_width)
    )
    dy = (d_v * silu).astype(BF)
    dz = (d_v * y * gate * (1.0 + z * (1.0 - gate))).astype(BF)
    dy_o[0] = dy
    dz_o[0] = dz
    dy_f = dy.astype(F32)
    branch_o[0] = dot_nt(gated, w_out[...]).astype(BF)

    @pl.when(row == 0)
    def _():
        acc_out[...] = jnp.zeros_like(acc_out)
        acc_gate[...] = jnp.zeros_like(acc_gate)
        gain_o[...] = jnp.zeros_like(gain_o)
        skip_o[...] = jnp.zeros_like(skip_o)

    acc_out[...] += dot_tn(dout[0], gated)
    acc_gate[...] += dot_tn(normed[0, HALO:], dz)
    gain_o[...] += jnp.sum(d_gated * unit, axis=0, keepdims=True)
    skip_o[...] += jnp.sum(dy_f * u, axis=0, keepdims=True)

    @pl.when(row == pl.num_programs(0) - 1)
    def _():
        grad_out_o[...] = acc_out[...].astype(BF)
        grad_gate_o[...] = acc_gate[...].astype(BF)

    maps = head_maps(heads, width, head_dim)
    for d in range(2):
        gone, rate = None, None
        for b in reversed(range(blocks)) if d == 0 else range(blocks):
            at = slice(b * BLOCK, (b + 1) * BLOCK)
            c_mat = xbc[0, at, width + (2 + d) * state : width + (3 + d) * state]
            weighed = (exact(dot, tab[0, 0, at], maps[d], 2) * dy_f[at]).astype(BF)
            enter = dot_tn(c_mat, weighed)
            enter_o[0, b, d] = enter
            own = decay[0, b, d, 0:1]
            gone = enter if gone is None else enter + own * gone
            rate = own if rate is None else rate * own
        send_o[d, 0, 0:state] = gone.astype(BF)
        send_o[d, 0, state:] = carried_rows(rate)


def inner_back(dims, info, starts, xbc, tab, cumt, v, dy, y_in, inc, dv_o, dbc_o, along_o):
    heads, head_dim, state, _ = dims
    width = heads * head_dim
    row, block = pl.program_id(0), pl.program_id(1)
    masks = pair_masks(info[0, 0] + block * BLOCK, starts, row)
    low_half = lax.broadcasted_iota(jnp.int32, (1, LANES), 1) < head_dim
    maps = head_maps(heads, width, head_dim)
    dy_all = dy[0].astype(F32)
    along = None
    for d in range(2):
        b_mat = xbc[0, :, width + d * state : width + (d + 1) * state]
        c_mat = xbc[0, :, width + (2 + d) * state : width + (3 + d) * state]
        scores = dot_nt(c_mat, b_mat)
        d_scores = jnp.zeros((BLOCK, BLOCK), F32)
        for pair in range(heads // 2):
            at = slice(pair * LANES, (pair + 1) * LANES)
            values = v[0, d, :, at]
            grads = dy[0, :, at]
            outs = []
            for h in (2 * pair, 2 * pair + 1):
                lane = d * heads + h
                gap = tab[0, 1, :, lane : lane + 1] - cumt[0, 0, lane : lane + 1, :]
                spread = jnp.exp(gap + masks[d])
                mixing = (spread * scores).astype(BF)
                mine = low_half if h % 2 == 0 else ~low_half
                d_mixing = dot_nt(jnp.where(mine, grads, jnp.zeros_like(grads)), values)
                d_scores = d_scores + d_mixing * spread
                outs.append(dot_tn(mixing, grads))
            dv_o[0, d, :, at] = jnp.where(low_half, outs[0], outs[1])
        d_scores = d_scores.astype(BF)
        weighed = (exact(dot, tab[0, 3], maps[d], 2) * dy_all).astype(BF)
        d_c = dot(d_scores, b_mat) + dot_nt(weighed, inc[0, 0, d].astype(BF))
        d_b = dot_tn(d_scores, c_mat)
        dbc_o[0, :, d * state : (d + 1) * state] = d_b
        dbc_o[0, :, (2 + d) * state : (3 + d) * state] = d_c
        term = exact(dot_nt, dy_all * y_in[0, d], maps[d], 2)
        along = term if along is None else along + term
    along_o[0] = along


def back(dims, count, info, starts, received, enter, decay, inc, xbc, tab, v, dv, dbc, along, dy,
         dsil, pre, normed, dz, skip, a_log, conv_w, w_pre, w_gate, grad_pre_o, dn_o, conv_w_o,
         conv_b_o, small_o, acc, pad, ps):
    heads, head_dim, state, _ = dims
    width = heads * head_dim
    row = pl.program_id(0)
    base, place = info[0, 0], info[0, 2]
    span = dy.shape[1]
    blocks = span // BLOCK
    conv_len, conv_width = conv_w.shape
    parts = [received[k, 0] for k in range(count - 1)]
    leaving = [[None] * 2 for _ in range(blocks)]
    now = compose(parts, place, count, state, False)
    for b in reversed(range(blocks)):
        leaving[b][0] = now
        now = enter[0, b, 0] + decay[0, b, 0, 0:1] * now
    now = compose(parts, place, count, state, True)
    for b in range(blocks):
        leaving[b][1] = now
        now = enter[0, b, 1] + decay[0, b, 1, 0:1] * now
    maps = head_maps(heads, width, head_dim)
    lower, upper = triangles()
    forward = lax.broadcasted_iota(jnp.int32, (1, LANES), 1) < heads
    rate = jnp.exp(a_log[...])
    rows = lax.broadcasted_iota(jnp.int32, (BLOCK, 1), 0)

    @pl.when(row == 0)
    def _():
        acc[...] = jnp.zeros_like(acc)
        conv_w_o[...] = jnp.zeros_like(conv_w_o)
        conv_b_o[...] = jnp.zeros_like(conv_b_o)
        small_o[...] = jnp.zeros_like(small_o)
        pad[0:HALO] = jnp.zeros((HALO, conv_width), F32)
        pad[HALO + span :] = jnp.zeros((pad.shape[0] - HALO - span, conv_width), F32)

    raws = []
    for b in range(blocks):
        at = slice(b * BLOCK, (b + 1) * BLOCK)
        u = xbc[0, at, :width].astype(F32)
        step, tail, slope = tab[0, 0, at], tab[0, 2, at], tab[0, 4, at]
        reach = tab[0, 3, at]
        d_u = skip[...] * dy[0, at].astype(F32)
        through = None
        direct = None
        ended = None
        closing = None
        d_bc = []
        for d in range(2):
            leave = leaving[b][d].astype(BF)
            b_mat = xbc[0, at, width + d * state : width + (d + 1) * state]
            v_d = v[0, d, at].astype(F32)
            dv_state = exact(dot, tail, maps[d], 2) * dot(b_mat, leave)
            dv_all = dv[0, d, at] + dv_state
            tailed = (exact(dot, tail * step, maps[d], 2) * u).astype(BF)
            d_bc.append(dot_nt(tailed, leave))
            d_u = d_u + exact(dot, step, maps[d], 2) * dv_all
            terms = (
                exact(dot_nt, v_d * dv_all, maps[d], 2),
                exact(dot_nt, u * dv_all, maps[d], 2),
                exact(
                    dot_nt,
                    jnp.broadcast_to(jnp.sum(v_d * dv_state, axis=0, keepdims=True), (8, width)),
                    maps[d],
                    3,
                ),
                exact(
                    dot_nt,
                    jnp.broadcast_to(
                        jnp.sum(leaving[b][d] * inc[0, b, d], axis=0, keepdims=True), (8, width)
                    ),
                    maps[d],
                    3,
                ),
            )
            if d == 0:
                through, direct, ended, closing = terms
            else:
                through = through + terms[0]
                direct = direct + terms[1]
                ended = ended + terms[2]
                closing = closing + terms[3]
        final = jnp.where(forward, reach[BLOCK - 1 : BLOCK], reach[0:1])
        at_end = jnp.where(
            forward, (rows == BLOCK - 1).astype(F32), (rows == 0).astype(F32)
        )
        d_cum = along[0, at] - through + at_end * (ended[0:1] + closing[0:1] * final)
        d_logs = jnp.where(
            forward,
            exact(lambda p, m: dot(m, p), d_cum, upper, 3),
            exact(lambda p, m: dot(m, p), d_cum, lower, 3),
        )
        d_step = direct - rate * d_logs
        d_raw = d_step * slope
        raws.append(d_raw.astype(BF))
        small_o[0:1] += jnp.sum(d_raw, axis=0, keepdims=True)
        small_o[1:2] += jnp.sum(-step * rate * d_logs, axis=0, keepdims=True)
        pad[HALO + b * BLOCK : HALO + (b + 1) * BLOCK, 0:width] = d_u * dsil[0, at, 0:width]
        d_bc_all = jnp.concatenate(
            [d_bc[0], d_bc[1], jnp.zeros((BLOCK, 2 * state), F32)], axis=1
        )
        pad[HALO + b * BLOCK : HALO + (b + 1) * BLOCK, width:] = (dbc[0, at] + d_bc_all) * dsil[
            0, at, width:
        ]
    ps[...] = pre[0].astype(F32)
    places = column_places(span, base)
    doc = doc_of(places, starts, row)
    outs = pad[HALO : HALO + span]
    conv_b_o[...] += jnp.sum(outs, axis=0, keepdims=True)
    ext_places = column_places(HALO + span, base - HALO)
    ext_doc = doc_of(ext_places, starts, row)
    d_pre = None
    for k in range(conv_len):
        ahead = conv_len - 1 - k
        ok = (doc_of(places - ahead, starts, row) == doc).astype(F32)
        conv_w_o[k : k + 1] += jnp.sum(
            outs * ok * ps[HALO - ahead : HALO - ahead + span], axis=0, keepdims=True
        )
        ok_ext = (doc_of(ext_places + ahead, starts, row) == ext_doc).astype(F32)
        term = pad[ahead : ahead + HALO + span] * ok_ext * conv_w[k : k + 1]
        d_pre = term if d_pre is None else d_pre + term
    d_raws = jnp.concatenate([jnp.zeros((HALO, LANES), BF)] + raws, axis=0)
    d_all = jnp.concatenate([d_pre.astype(BF), d_raws], axis=1)
    acc[...] += dot_tn(normed[0], d_all)
    dn = dot_nt(d_all, w_pre[...])
    dn_o[0, 0:HALO] = dn[0:HALO].astype(BF)
    dn_o[0, HALO:] = (dn[HALO:] + dot_nt(dz[0], w_gate[...])).astype(BF)

    @pl.when(row == pl.num_programs(0) - 1)
    def _():
        grad_pre_o[...] = acc[...].astype(BF)


def finish(dims, info, pads, own, cot, gain, dn, dn_other, rim_a, rim_b, branch, branch_other,
           mixed_o, grad_o, gain_o, ds):
    row_len = dims[3]
    row = pl.program_id(0)
    base, core, place, count = info[0, 0], info[0, 1], info[0, 2], info[0, 3]
    half = own.shape[1]
    x = own[0].astype(F32)
    places = column_places(half, base + core * half)
    valid = (places < row_len - pads[row, 0]).astype(F32)
    mixed_o[0] = (x + valid * (branch[0].astype(F32) + branch_other[0].astype(F32))).astype(BF)
    ds[...] = dn[0].astype(F32) + dn_other[0].astype(F32)
    takes = ((core == 1) & (place + 1 < count)).astype(F32)
    ds[half - HALO :] += takes * (rim_a[0].astype(F32) + rim_b[0].astype(F32))
    d_normed = ds[...]
    scale = lax.rsqrt(jnp.mean(x * x, axis=-1, keepdims=True) + EPSILON)
    weighed = d_normed * gain[...]
    along = jnp.mean(weighed * x, axis=-1, keepdims=True)
    dx = scale * weighed - x * (scale * scale * scale * along)
    grad_o[0] = (cot[0].astype(F32) + dx).astype(BF)

    @pl.when(row == 0)
    def _():
        gain_o[...] = jnp.zeros_like(gain_o)

    gain_o[...] += jnp.sum(d_normed * x * scale, axis=0, keepdims=True)


MESH = pl.DeviceIdType.MESH


def remote(src, dst, send_sem, recv_sem, device):
    return pltpu.make_async_remote_copy(
        src_ref=src, dst_ref=dst, send_sem=send_sem, recv_sem=recv_sem, device_id=device,
        device_id_type=MESH,
    )


class Sender:
    def __init__(self, send_sems, recv_sems):
        self.send_sems, self.recv_sems = send_sems, recv_sems
        self.sent = 0
        self.slots = 0
        self.pending = []

    def slot(self):
        self.slots += 1
        return self.slots - 1

    def send(self, src, dst, slot, device):
        copy = remote(src, dst, self.send_sems.at[self.sent], self.recv_sems.at[slot], device)
        self.sent += 1
        copy.start()
        self.pending.append(copy)

    def arrive(self, dst, slot, device):
        remote(dst, dst, self.send_sems.at[0], self.recv_sems.at[slot], device).wait_recv()

    def drain(self):
        for copy in self.pending:
            copy.wait_send()
        self.pending = []


class Place:
    def __init__(self, count):
        self.dp, self.seq, self.dir = (lax.axis_index(a) for a in ("dp", "seq", "dir"))
        self.count = count
        self.side = self.dp + 1 - 2 * (self.dp % 2)
        self.below = (self.dp + 2) % 4
        self.across = 3 - self.dp
        self.me = (self.dp, self.seq, self.dir)
        self.sibling = (self.dp, self.seq, 1 - self.dir)
        self.by_x = (self.side, self.seq, self.dir)
        self.by_y = (self.below, self.seq, self.dir)

    def along(self, k, crossed=False):
        core = 1 - self.dir if crossed else self.dir
        return (self.dp, (self.seq + k + self.count) % self.count, core)

    def at(self, k):
        return (self.seq + k + self.count) % self.count

    def chip(self, dp, k=0):
        return dp * self.count + self.at(k)

    def meet(self):
        barrier = pltpu.get_barrier_semaphore()
        others = [self.sibling, self.by_x, self.by_y]
        others += [self.along(k) for k in range(1, self.count)]
        others += [self.along(1, True), self.along(-1, True)]
        for device in others:
            pl.semaphore_signal(barrier, inc=1, device_id=device, device_id_type=MESH)
        pl.semaphore_wait(barrier, len(others))


class Spread:
    def __init__(self, place, sender, slab, cut):
        self.place, self.sender, self.slab, self.cut = place, sender, slab, cut
        count = place.count
        self.z = [None] + [sender.slot() for _ in range(1, count)]
        self.x, self.y, self.xd, self.yd = (
            [sender.slot() for _ in range(count)] for _ in range(4)
        )

    def start(self, mine):
        here, to = self.place, self.sender
        spot = self.slab.at[here.chip(here.dp)]
        to.send(mine, spot, self.x[0], here.by_x)
        to.send(mine, spot, self.y[0], here.by_y)
        for k in range(1, here.count):
            to.send(mine, spot, self.z[k], here.along(k))

    def relay(self, k):
        here, to = self.place, self.sender
        spot = self.slab.at[here.chip(here.dp, -k)]
        to.arrive(spot, self.z[k], here.along(-k))
        to.send(spot, spot, self.x[k], here.by_x)
        to.send(spot, spot, self.y[k], here.by_y)

    def cross(self, k):
        here, to = self.place, self.sender
        from_x = self.slab.at[here.chip(here.side, -k)]
        to.arrive(from_x, self.x[k], here.by_x)
        part = from_x.at[:, : self.cut]
        to.send(part, part, self.yd[k], here.by_y)
        from_y = self.slab.at[here.chip(here.below, -k)]
        to.arrive(from_y, self.y[k], here.by_y)
        part = from_y.at[:, self.cut :]
        to.send(part, part, self.xd[k], here.by_x)

    def end(self, k):
        here, to = self.place, self.sender
        spot = self.slab.at[here.chip(here.across, -k)]
        to.arrive(spot.at[:, : self.cut], self.yd[k], here.by_y)
        to.arrive(spot.at[:, self.cut :], self.xd[k], here.by_x)


def gather_copies(count):
    return 6 + 2 * ((count - 1) + 4 * count)


def gather(dims, count, cuts, w_in, w_dt, w_out, tokens, cot, pre_o, late_o, tokens_o, cot_o, halo_o,
           give_pre, give_late, got_pre, got_late, pre_mine, late_mine, send_sems, recv_sems, own_sems):
    heads, head_dim, state, _ = dims
    width = heads * head_dim
    half = tokens.shape[1]
    here = Place(count)
    to = Sender(send_sems, recv_sems)
    shard = w_in.shape[0]
    late_core = here.dir == 1
    conv_width = width + 4 * state
    source = lax.broadcasted_iota(jnp.int32, (4 * heads, LANES), 0)
    lane = lax.broadcasted_iota(jnp.int32, (4 * heads, LANES), 1)

    def fill(core, pre, late):
        late_side = core == 1
        pick = lambda ref, at: jnp.where(
            late_side, ref[:, at + width : at + 2 * width], ref[:, at : at + width]
        )
        pre[:, 0:width] = pick(w_in, 2 * width).astype(pre.dtype)
        pre[:, width:conv_width] = w_in[:, 4 * width :].astype(pre.dtype)
        column = jnp.where(lane < heads, lane, lane + heads) + core * heads
        ones = jnp.where((source == column) & (lane < 2 * heads), 1.0, 0.0).astype(BF)
        pre[:, conv_width:] = dot(w_dt[...], ones).astype(pre.dtype)
        late[:, 0:width] = pick(w_in, 0).astype(late.dtype)
        late[:, width:] = pick(w_out, 0).astype(late.dtype)

    fill(1 - here.dir, give_pre, give_late)
    here.meet()
    slots = [to.slot() for _ in range(5)]
    to.send(give_pre, got_pre, slots[0], here.sibling)
    to.send(give_late, got_late, slots[1], here.sibling)
    to.send(tokens, tokens_o, slots[2], here.sibling)
    to.send(cot, cot_o, slots[3], here.sibling)
    rim = tokens.at[:, pl.ds(half - HALO, HALO)]
    first_rim, second_rim = to.sent, to.sent + 1
    to.sent += 2

    @pl.when(late_core)
    def _():
        for sem, crossed in ((first_rim, False), (second_rim, True)):
            remote(
                rim, halo_o, send_sems.at[sem], recv_sems.at[slots[4]], here.along(1, crossed)
            ).start()

    pre_spread = Spread(here, to, pre_o, cuts[0])
    late_spread = Spread(here, to, late_o, cuts[1])
    fill(here.dir, pre_mine, late_mine)

    def joined(own, got):
        other = got[...].astype(F32)
        own = own[...]
        return jnp.where(
            late_core,
            jnp.concatenate([other, own], axis=0),
            jnp.concatenate([own, other], axis=0),
        ).astype(BF)

    return here, to, slots, rim, first_rim, second_rim, pre_spread, late_spread, joined


def gather_all(dims, count, cuts, w_in, w_dt, w_out, tokens, cot, pre_o, late_o, tokens_o, cot_o,
               halo_o, give_pre, give_late, got_pre, got_late, pre_mine, late_mine, pre_block,
               late_block, send_sems, recv_sems, own_sems):
    here, to, slots, rim, first_rim, second_rim, pre_spread, late_spread, joined = gather(
        dims, count, cuts, w_in, w_dt, w_out, tokens, cot, pre_o, late_o, tokens_o, cot_o, halo_o,
        give_pre, give_late, got_pre, got_late, pre_mine, late_mine, send_sems, recv_sems, own_sems)
    to.arrive(got_pre, slots[0], here.sibling)
    pre_block[...] = joined(pre_mine, got_pre)
    pre_spread.start(pre_block)
    to.arrive(got_late, slots[1], here.sibling)
    late_block[...] = joined(late_mine, got_late)
    keep = [
        pltpu.make_async_copy(block, slab.at[here.chip(here.dp)], own_sems.at[i])
        for i, (block, slab) in enumerate(((pre_block, pre_o), (late_block, late_o)))
    ]
    for copy in keep:
        copy.start()
    late_spread.start(late_block)
    for spread in (pre_spread, late_spread):
        spread.cross(0)
        for k in range(1, count):
            spread.relay(k)
            spread.cross(k)
    for spread in (pre_spread, late_spread):
        for k in range(count):
            spread.end(k)
    to.arrive(tokens_o, slots[2], here.sibling)
    to.arrive(cot_o, slots[3], here.sibling)
    to.arrive(halo_o, slots[4], here.along(-1))
    for copy in keep:
        copy.wait()
    to.drain()

    @pl.when(here.dir == 1)
    def _():
        for sem, crossed in ((first_rim, False), (second_rim, True)):
            remote(
                rim, halo_o, send_sems.at[sem], recv_sems.at[slots[4]], here.along(1, crossed)
            ).wait_send()


class Reduce:
    def __init__(self, place, sender, grad, cut, first, second, third, out_second, out_third, total):
        self.place, self.sender, self.grad, self.cut = place, sender, grad, cut
        self.first, self.second, self.third = first, second, third
        self.out_second, self.out_third, self.total = out_second, out_third, total
        count = place.count
        self.one = [[[sender.slot() for _ in range(count)] for _ in range(2)] for _ in range(2)]
        self.two = [[sender.slot() for _ in range(count)] for _ in range(2)]
        self.three = [None] + [sender.slot() for _ in range(1, count)]
        self.sides = (slice(0, cut), slice(cut, grad.shape[2]))

    def start(self, k):
        here, to = self.place, self.sender
        for side, device, targets in (
            (0, here.by_x, (here.side, here.across)),
            (1, here.by_y, (here.below, here.across)),
        ):
            at = self.sides[side]
            for q in (1, 0):
                to.send(
                    self.grad.at[here.chip(targets[q], k), :, at],
                    self.first.at[q, k, :, at],
                    self.one[side][q][k], device,
                )

    def pass_on(self, k):
        here, to = self.place, self.sender
        for side, came, device, target in (
            (0, here.by_x, here.by_y, here.below),
            (1, here.by_y, here.by_x, here.side),
        ):
            at = self.sides[side]
            to.arrive(self.first.at[1, k, :, at], self.one[side][1][k], came)
            self.out_second[k, :, at] = (
                self.grad[here.chip(target, k), :, at].astype(F32)
                + self.first[1, k, :, at].astype(F32)
            ).astype(BF)
            to.send(self.out_second.at[k, :, at], self.second.at[k, :, at], self.two[side][k], device)

    def along(self, k):
        here, to = self.place, self.sender
        for side, came, then in ((0, here.by_x, here.by_y), (1, here.by_y, here.by_x)):
            at = self.sides[side]
            to.arrive(self.first.at[0, k, :, at], self.one[side][0][k], came)
            to.arrive(self.second.at[k, :, at], self.two[side][k], then)
            summed = (
                self.grad[here.chip(here.dp, k), :, at].astype(F32)
                + self.first[0, k, :, at].astype(F32)
                + self.second[k, :, at].astype(F32)
            )
            if k == 0:
                self.total[:, at] = summed
            else:
                self.out_third[k - 1, :, at] = summed.astype(BF)
        if k:
            to.send(self.out_third.at[k - 1], self.third.at[k - 1], self.three[k], here.along(k))

    def end(self):
        here, to = self.place, self.sender
        for k in range(1, here.count):
            to.arrive(self.third.at[k - 1], self.three[k], here.along(-k))
            self.total[...] += self.third[k - 1].astype(F32)


def settle_copies(count):
    per_grad = 4 * count + 2 * count + (count - 1)
    return 3 * (per_grad + 1) + 3 + (2 + (count - 1) + 1)


def settle(dims, count, cuts, pads, tokens, cot, gain, dn, branch, g_pre, g_gate, g_out, conv_w, conv_b,
           gate_sum, skip_sum, small, mixed_o, grad_o, in_o, dt_o, out_o, conv_w_o, conv_b_o, gate_o,
           skip_o, small_o, norm_o, *rest):
    heads, head_dim, state, row_len = dims
    width = heads * head_dim
    conv_width = width + 4 * state
    works = [rest[6 * i : 6 * i + 6] for i in range(3)]
    (other_pre, other_gate, other_out, dn_other, branch_other, rims, ds, v_own, v_x, v_y, v_z, v_other,
     send_sems, recv_sems) = rest[18:]
    here = Place(count)
    to = Sender(send_sems, recv_sems)
    rows, half, model = tokens.shape
    here.meet()
    reduces = [
        Reduce(here, to, grad, cut, *work)
        for grad, cut, work in zip((g_pre, g_gate, g_out), cuts, works)
    ]
    for reduce in reduces:
        for k in list(range(1, count)) + [0]:
            reduce.start(k)
    dn_slot, branch_slot, rim_own, rim_cross = (to.slot() for _ in range(4))
    give = pl.multiple_of((1 - here.dir) * half, HALO)
    keep = pl.multiple_of(here.dir * half, HALO)
    to.send(dn.at[:, pl.ds(HALO + give, half)], dn_other, dn_slot, here.sibling)
    to.send(branch.at[:, pl.ds(give, half)], branch_other, branch_slot, here.sibling)
    edge = dn.at[:, pl.ds(0, HALO)]
    rim_sem = to.sent
    to.sent += 1

    @pl.when(here.dir == 1)
    def _():
        remote(edge, rims.at[1], send_sems.at[rim_sem], recv_sems.at[rim_own], here.along(-1)).start()

    @pl.when(here.dir == 0)
    def _():
        remote(
            edge, rims.at[0], send_sems.at[rim_sem], recv_sems.at[rim_cross], here.along(-1, True)
        ).start()

    order = list(range(1, count)) + [0]
    for reduce in reduces:
        for k in order:
            reduce.pass_on(k)
    to.arrive(dn_other, dn_slot, here.sibling)
    to.arrive(branch_other, branch_slot, here.sibling)

    @pl.when(here.dir == 1)
    def _():
        to.arrive(rims.at[1], rim_own, here.along(1))
        to.arrive(rims.at[0], rim_cross, here.along(1, True))

    @pl.when(here.dir == 0)
    def _():
        rims[...] = jnp.zeros_like(rims)

    gain_sum = None
    takes = ((here.dir == 1) & (here.seq + 1 < count)).astype(F32)
    for row in range(rows):
        x = tokens[row].astype(F32)
        places = column_places(half, (here.seq * 2 + here.dir) * half)
        valid = (places < row_len - pads[row, 0]).astype(F32)
        mixed_o[row] = (
            x + valid * (branch[row, pl.ds(keep, half)].astype(F32) + branch_other[row].astype(F32))
        ).astype(BF)
        ds[...] = dn[row, pl.ds(HALO + keep, half)].astype(F32) + dn_other[row].astype(F32)
        ds[half - HALO :] += takes * (rims[0, row].astype(F32) + rims[1, row].astype(F32))
        d_normed = ds[...]
        scale = lax.rsqrt(jnp.mean(x * x, axis=-1, keepdims=True) + EPSILON)
        weighed = d_normed * gain[...]
        along = jnp.mean(weighed * x, axis=-1, keepdims=True)
        dx = scale * weighed - x * (scale * scale * scale * along)
        grad_o[row] = (cot[row].astype(F32) + dx).astype(BF)
        term = jnp.sum(d_normed * x * scale, axis=0, keepdims=True)
        gain_sum = term if gain_sum is None else gain_sum + term
    side = v_own.shape[1] - width
    v_own[0:4] = conv_w[...]
    v_own[4:5] = conv_b[...]
    v_own[5:6] = jnp.concatenate([gate_sum[...], small[0:1], small[1:2]], axis=1)
    v_own[6:7] = jnp.concatenate([skip_sum[...], jnp.zeros((1, side), F32)], axis=1)
    v_own[7:8] = jnp.concatenate([gain_sum, jnp.zeros((1, side), F32)], axis=1)
    v_slots = [to.slot() for _ in range(2 + count)]
    to.send(v_own, v_x.at[0], v_slots[0], here.by_x)
    for reduce in reduces:
        for k in order:
            reduce.along(k)
    to.arrive(v_x.at[0], v_slots[0], here.by_x)
    v_x[1] = v_own[...] + v_x[0]
    to.send(v_x.at[1], v_y.at[0], v_slots[1], here.by_y)
    to.arrive(v_y.at[0], v_slots[1], here.by_y)
    v_y[1] = v_x[1] + v_y[0]
    for k in range(1, count):
        to.send(v_y.at[1], v_z.at[k - 1], v_slots[1 + k], here.along(k))
    swaps = []
    shard = in_o.shape[0]
    for reduce, other in zip(reduces, (other_pre, other_gate, other_out)):
        reduce.end()
        slot = to.slot()
        back_rows = pl.ds(pl.multiple_of((1 - here.dir) * shard, 8), shard)
        to.send(reduce.total.at[back_rows], other, slot, here.sibling)
        swaps.append((other, slot))
    total = v_y[1]
    for k in range(1, count):
        to.arrive(v_z.at[k - 1], v_slots[1 + k], here.along(-k))
        total = total + v_z[k - 1]
    v_x[0] = total
    to.send(v_x.at[0], v_other, v_slots[1 + count], here.sibling)
    late = here.dir == 1
    own_rows = pl.ds(pl.multiple_of(here.dir * shard, 8), shard)
    sorted_parts = []
    for reduce, (other, slot) in zip(reduces, swaps):
        to.arrive(other, slot, here.sibling)
        own, got = reduce.total[own_rows], other[...]
        sorted_parts.append((jnp.where(late, got, own), jnp.where(late, own, got)))
    (pre_a, pre_b), (gate_a, gate_b), (out_a, out_b) = sorted_parts
    in_o[:, 0:width] = gate_a
    in_o[:, width : 2 * width] = gate_b
    in_o[:, 2 * width : 3 * width] = pre_a[:, :width]
    in_o[:, 3 * width : 4 * width] = pre_b[:, :width]
    in_o[:, 4 * width :] = pre_a[:, width:conv_width] + pre_b[:, width:conv_width]
    dt_o[0] = pre_a[:, conv_width:]
    dt_o[1] = pre_b[:, conv_width:]
    out_o[:, 0:width] = out_a
    out_o[:, width:] = out_b
    to.arrive(v_other, v_slots[1 + count], here.sibling)
    got = v_other[...]
    v_a, v_b = jnp.where(late, got, total), jnp.where(late, total, got)
    both = v_a + v_b
    conv_w_o[:, 0:width] = v_a[0:4, :width]
    conv_w_o[:, width : 2 * width] = v_b[0:4, :width]
    conv_w_o[:, 2 * width :] = both[0:4, width:]
    conv_b_o[:, 0:width] = v_a[4:5, :width]
    conv_b_o[:, width : 2 * width] = v_b[4:5, :width]
    conv_b_o[:, 2 * width :] = both[4:5, width:]
    gate_o[:, 0:width] = v_a[5:6, :width]
    gate_o[:, width:] = v_b[5:6, :width]
    small_o[0:1] = v_a[5:6, width : width + LANES]
    small_o[1:2] = v_a[5:6, width + LANES : width + 2 * LANES]
    small_o[2:3] = v_b[5:6, width : width + LANES]
    small_o[3:4] = v_b[5:6, width + LANES : width + 2 * LANES]
    skip_o[:, 0:width] = v_a[6:7, :width]
    skip_o[:, width:] = v_b[6:7, :width]
    norm_o[...] = both[7:8, :model]
    to.drain()

    @pl.when(here.dir == 1)
    def _():
        remote(edge, rims.at[1], send_sems.at[rim_sem], recv_sems.at[rim_own], here.along(-1)).wait_send()

    @pl.when(here.dir == 0)
    def _():
        remote(
            edge, rims.at[0], send_sems.at[rim_sem], recv_sems.at[rim_cross], here.along(-1, True)
        ).wait_send()


SMEM = pl.BlockSpec(memory_space=pltpu.SMEM)
VMEM = pl.BlockSpec(memory_space=pltpu.VMEM)
ANY = pl.BlockSpec(memory_space=pl.ANY)


def whole(*shape):
    return pl.BlockSpec(shape, lambda *_: (0,) * len(shape))


def by_row(*shape):
    return pl.BlockSpec((1,) + shape, lambda r, *_: (r,) + (0,) * len(shape))


def second(*shape):
    return pl.BlockSpec(
        (shape[0], 1) + shape[1:], lambda r, *_: (0, r) + (0,) * (len(shape) - 1)
    )


def run(body, grid, ins, outs, scratch=(), flops=0, name=None, collective_id=None):
    arrays = [a for a, _ in ins]
    moved = sum(a.size * a.dtype.itemsize for a in arrays) + sum(
        s.size * s.dtype.itemsize for s, _ in outs
    )
    return pl.pallas_call(
        body,
        grid=grid,
        out_shape=[s for s, _ in outs],
        in_specs=[b for _, b in ins],
        out_specs=[b for _, b in outs],
        scratch_shapes=list(scratch),
        compiler_params=pltpu.CompilerParams(
            vmem_limit_bytes=VMEM_BYTES,
            dimension_semantics=("arbitrary",) * len(grid),
            collective_id=collective_id,
            has_side_effects=collective_id is not None,
        ),
        cost_estimate=pl.CostEstimate(
            flops=flops, bytes_accessed=moved, transcendentals=flops // 500
        ),
        name=name,
    )(*arrays)


def shape_of(dtype, *dims):
    return jax.ShapeDtypeStruct(dims, dtype)


def swapped(value):
    return lax.ppermute(value, "dir", [(0, 1), (1, 0)])


def rotated(value, steps):
    count = lax.axis_size("seq")
    return lax.ppermute(value, "seq", [(i, (i + steps) % count) for i in range(count)])


def rotated_to(value, steps, cross):
    count = lax.axis_size("seq")
    pairs = []
    for i in range(count):
        for c in range(2):
            pairs.append((i * 2 + c, (i + steps) % count * 2 + (1 - c if cross else c)))
    return lax.ppermute(value, ("seq", "dir"), pairs)


def around(value):
    count, place = lax.axis_size("seq"), lax.axis_index("seq")
    out = []
    for k in range(1, count):
        chosen = jnp.where(place + k < count, value[0], value[1])
        out.append(rotated(chosen, k))
    return jnp.stack(out)


def gathered_apart(w_in, w_dt, w_out, tokens, cotangent, heads, width, inner_width, is_late):
    all_heads = 2 * heads
    half = tokens.shape[1]
    pad_dt = jnp.zeros((w_in.shape[0], LANES - 2 * heads), BF)

    def columns(c):
        return (
            jnp.concatenate(
                [
                    w_in[:, inner_width + c * width : inner_width + (c + 1) * width],
                    w_in[:, 2 * inner_width :],
                    w_dt[:, c * heads : (c + 1) * heads],
                    w_dt[:, all_heads + c * heads : all_heads + (c + 1) * heads],
                    pad_dt,
                ],
                axis=1,
            ),
            jnp.concatenate(
                [w_in[:, c * width : (c + 1) * width], w_out[:, c * width : (c + 1) * width]], axis=1
            ),
        )

    first, latter = columns(0), columns(1)

    def gathered(i):
        keep = jnp.where(is_late, latter[i], first[i])
        give = swapped(jnp.where(is_late, first[i], latter[i]))
        both = jnp.where(
            is_late,
            jnp.concatenate([give, keep], axis=0),
            jnp.concatenate([keep, give], axis=0),
        )
        return lax.all_gather(both, ("dp", "seq"), axis=0, tiled=True)

    rim = tokens[:, half - HALO :]
    halo = jnp.where(is_late, rotated_to(rim, 1, False), rotated_to(rim, 1, True))
    return gathered(0), gathered(1), swapped(tokens), swapped(cotangent), halo


def settled_apart(dims, info, pads, tokens, cotangent, gain, dn, branch, grads, sums, shard):
    heads, head_dim, state, _ = dims
    width = heads * head_dim
    conv_width = width + 4 * state
    rows, half, model = tokens.shape
    core = lax.axis_index("dir")
    is_late = core == 1
    sum_conv_w, sum_conv_b, gate_sum, skip_sum, small = sums

    def reduced(grad):
        return lax.psum_scatter(grad, ("dp", "seq"), scatter_dimension=0, tiled=True)

    def halves(values, first_row):
        keep = lax.dynamic_slice_in_dim(values, first_row + core * half, half, axis=1)
        give = lax.dynamic_slice_in_dim(values, first_row + (1 - core) * half, half, axis=1)
        return keep, swapped(give)

    dn_own, dn_other = halves(dn, HALO)
    branch_own, branch_other = halves(branch, 0)
    edge = dn[:, :HALO]
    rim_a, rim_b = rotated_to(edge, -1, False), rotated_to(edge, -1, True)
    mixed, tokens_grad, gain_sum = run(
        functools.partial(finish, dims),
        (rows,),
        [
            (info, SMEM), (pads, SMEM), (tokens, by_row(half, model)),
            (cotangent, by_row(half, model)), (gain, whole(1, model)),
            (dn_own, by_row(half, model)), (dn_other, by_row(half, model)),
            (rim_a, by_row(HALO, model)), (rim_b, by_row(HALO, model)),
            (branch_own, by_row(half, model)), (branch_other, by_row(half, model)),
        ],
        [
            (shape_of(BF, rows, half, model), by_row(half, model)),
            (shape_of(BF, rows, half, model), by_row(half, model)),
            (shape_of(F32, 1, model), whole(1, model)),
        ],
        [pltpu.VMEM((half, model), F32)],
        name="finish",
    )

    def placed(values):
        empty = jnp.zeros_like(values)
        return jnp.where(
            is_late,
            jnp.concatenate([empty, values], axis=-1),
            jnp.concatenate([values, empty], axis=-1),
        )

    def returned(grad):
        value = reduced(grad)
        own = lax.dynamic_slice_in_dim(value, core * shard, shard, axis=0)
        give = lax.dynamic_slice_in_dim(value, (1 - core) * shard, shard, axis=0)
        other = swapped(give)
        own, other = own.astype(F32), other.astype(F32)
        return jnp.where(is_late, other, own), jnp.where(is_late, own, other)

    small_both = placed(small[:2]).reshape(2, 2, LANES)
    sum_norm, all_conv_w, all_conv_b, small_all, skip_all, gate_all = lax.psum(
        (
            gain_sum,
            jnp.concatenate([placed(sum_conv_w[:, :width]), sum_conv_w[:, width:]], axis=1),
            jnp.concatenate([placed(sum_conv_b[:, :width]), sum_conv_b[:, width:]], axis=1),
            jnp.swapaxes(small_both, 0, 1).reshape(4, LANES),
            placed(skip_sum),
            placed(gate_sum),
        ),
        ("dp", "seq", "dir"),
    )
    (pre_a, pre_b), (gate_a, gate_b), (out_a, out_b) = (returned(grad) for grad in grads)
    owned_out = jnp.concatenate([out_a, out_b], axis=1)
    owned_in = jnp.concatenate(
        [
            gate_a, gate_b, pre_a[:, :width], pre_b[:, :width],
            pre_a[:, width:conv_width] + pre_b[:, width:conv_width],
        ],
        axis=1,
    )
    dt_both = jnp.stack([pre_a[:, conv_width:], pre_b[:, conv_width:]])
    return (
        mixed, tokens_grad, owned_in, dt_both, owned_out, all_conv_w, all_conv_b, gate_all, skip_all,
        small_all, sum_norm,
    )


def shards(tokens, starts, pad_len, norm_gain, w_in, w_dt, conv_w, conv_b, dt_bias, a_log, skip,
           gate_gain, w_out, cotangent):
    rows, half, model = tokens.shape
    span = 2 * half
    count = lax.axis_size("seq")
    row_len = span * count
    blocks = span // BLOCK
    inner_width = gate_gain.shape[0]
    all_heads = skip.shape[0]
    heads = all_heads // 2
    head_dim = inner_width // all_heads
    width = heads * head_dim
    xbc_width = conv_w.shape[1]
    state = (xbc_width - inner_width) // 4
    conv_len = conv_w.shape[0]
    conv_width = width + 4 * state
    pre_width = conv_width + LANES
    ext = HALO + span
    dims = (heads, head_dim, state, row_len)
    place, core = lax.axis_index("seq"), lax.axis_index("dir")
    info = jnp.stack([place * span, core, place, jnp.int32(count)]).astype(jnp.int32)[None]
    pads = pad_len[:, None]
    shard = w_in.shape[0]
    is_late = core == 1
    direct = lax.axis_size("dp") == 4 and 2 * shard % 16 == 0
    if direct:
        chips = 4 * count
        block = (2 * shard, pre_width), (2 * shard, 2 * width)
        slab_pre, slab_late, tokens_other, cot_other, halo = run(
            functools.partial(gather_all, dims, count, (pre_width // 256 * 128 + 128, width)),
            (),
            [(w_in, VMEM), (w_dt, VMEM), (w_out, VMEM), (tokens, ANY), (cotangent, ANY)],
            [
                (shape_of(BF, chips, *block[0]), ANY), (shape_of(BF, chips, *block[1]), ANY),
                (shape_of(BF, *tokens.shape), ANY), (shape_of(BF, *tokens.shape), ANY),
                (shape_of(BF, rows, HALO, model), ANY),
            ],
            [
                pltpu.VMEM((shard, pre_width), BF), pltpu.VMEM((shard, 2 * width), BF),
                pltpu.VMEM((shard, pre_width), BF), pltpu.VMEM((shard, 2 * width), BF),
                pltpu.VMEM((shard, pre_width), F32), pltpu.VMEM((shard, 2 * width), F32),
                pltpu.VMEM(block[0], BF), pltpu.VMEM(block[1], BF),
                pltpu.SemaphoreType.DMA((gather_copies(count),)),
                pltpu.SemaphoreType.DMA((gather_copies(count),)),
                pltpu.SemaphoreType.DMA((2,)),
            ],
            name="gather",
            collective_id=0,
        )
        w_pre = slab_pre.reshape(model, pre_width)
        w_late = slab_late.reshape(model, 2 * width)
    else:
        w_pre, w_late, tokens_other, cot_other, halo = gathered_apart(
            w_in, w_dt, w_out, tokens, cotangent, heads, width, inner_width, is_late
        )

    def mine(vector, size):
        return lax.dynamic_slice_in_dim(vector, core * size, size, axis=-1)

    conv_w_c = jnp.concatenate([mine(conv_w[:, :inner_width], width), conv_w[:, inner_width:]], axis=1)
    conv_b_c = jnp.concatenate([mine(conv_b[:inner_width], width), conv_b[inner_width:]])[None]
    filler = jnp.zeros((LANES - 2 * heads,), F32)
    bias_c = jnp.concatenate([mine(dt_bias[:all_heads], heads), mine(dt_bias[all_heads:], heads), filler])[None]
    a_log_c = jnp.concatenate([mine(a_log[:all_heads], heads), mine(a_log[all_heads:], heads), filler])[None]
    skip_c = jnp.repeat(mine(skip, heads), head_dim)[None]
    gate_gain_c = mine(gate_gain, width)[None]
    gain = norm_gain[None]
    packed = 2 * heads + (-2 * heads) % 8
    tokens_all = rows * span
    scan_flops = 4 * tokens_all * BLOCK * LANES * heads

    normed, pre, xbc, dsil, tab, cumt, v, local, decay, send = run(
        functools.partial(front, dims),
        (rows,),
        [
            (info, SMEM), (starts, SMEM), (pads, SMEM),
            (halo, by_row(HALO, model)), (tokens, by_row(half, model)),
            (tokens_other, by_row(half, model)), (gain, whole(1, model)),
            (w_pre, whole(model, pre_width)), (conv_w_c, whole(conv_len, conv_width)),
            (conv_b_c, whole(1, conv_width)), (bias_c, whole(1, LANES)), (a_log_c, whole(1, LANES)),
        ],
        [
            (shape_of(BF, rows, ext, model), by_row(ext, model)),
            (shape_of(BF, rows, ext, conv_width), by_row(ext, conv_width)),
            (shape_of(BF, rows, span, conv_width), by_row(span, conv_width)),
            (shape_of(F32, rows, span, conv_width), by_row(span, conv_width)),
            (shape_of(F32, rows, 5, span, LANES), by_row(5, span, LANES)),
            (shape_of(F32, rows, blocks, packed, BLOCK), by_row(blocks, packed, BLOCK)),
            (shape_of(BF, rows, 2, span, width), by_row(2, span, width)),
            (shape_of(F32, rows, blocks, 2, state, width), by_row(blocks, 2, state, width)),
            (shape_of(F32, rows, blocks, 2, 8, width), by_row(blocks, 2, 8, width)),
            (shape_of(BF, 2, rows, state + CARRY, width), second(2, state + CARRY, width)),
        ],
        [pltpu.VMEM((ext, model), F32), pltpu.VMEM((ext, conv_width), F32)],
        flops=2 * tokens_all * model * pre_width,
        name="front",
    )
    received = around(send)
    left_half = pl.BlockSpec((model, width), lambda *_: (0, 0))
    right_half = pl.BlockSpec((model, width), lambda *_: (0, 1))
    at_block = lambda *shape: pl.BlockSpec((1,) + shape, lambda r, b: (r, b) + (0,) * (len(shape) - 1))
    at_second = lambda *shape: pl.BlockSpec((1, shape[0]) + shape[1:], lambda r, b: (r, 0, b, 0))
    block_tab = lambda i: pl.BlockSpec((1, 1, BLOCK, LANES), lambda r, b: (r, i, b, 0))
    (y_inner,) = run(
        functools.partial(inner, dims),
        (rows, blocks),
        [
            (info, SMEM), (starts, SMEM), (xbc, at_block(BLOCK, conv_width)),
            (tab, block_tab(1)), (cumt, at_block(1, packed, BLOCK)),
            (v, at_second(2, BLOCK, width)),
        ],
        [(shape_of(F32, rows, 2, span, width), at_second(2, BLOCK, width))],
        flops=scan_flops,
        name="inner",
    )
    y_both, inc, sums, z, d_gated, d_out = run(
        functools.partial(outer, dims, count),
        (rows,),
        [
            (info, SMEM), (starts, SMEM), (pads, SMEM),
            (received, second(count - 1, state + CARRY, width)),
            (local, by_row(blocks, 2, state, width)), (decay, by_row(blocks, 2, 8, width)),
            (xbc, by_row(span, conv_width)),
            (tab, pl.BlockSpec((1, 1, span, LANES), lambda r: (r, 3, 0, 0))),
            (y_inner, by_row(2, span, width)), (normed, by_row(ext, model)),
            (cotangent, by_row(half, model)), (cot_other, by_row(half, model)),
            (skip_c, whole(1, width)), (gate_gain_c, whole(1, width)),
            (w_late, left_half), (w_late, right_half),
        ],
        [
            (shape_of(F32, rows, 2, span, width), by_row(2, span, width)),
            (shape_of(F32, rows, blocks, 2, state, width), by_row(blocks, 2, state, width)),
            (shape_of(F32, rows, span, LANES), by_row(span, LANES)),
            (shape_of(F32, rows, span, width), by_row(span, width)),
            (shape_of(F32, rows, span, width), by_row(span, width)),
            (shape_of(BF, rows, span, model), by_row(span, model)),
        ],
        [pltpu.VMEM((span, model), F32)],
        flops=4 * tokens_all * model * width,
        name="outer",
    )
    sums_other = swapped(sums)
    dy, dz, enter, back_send, branch, grad_out, grad_gate, gate_sum, skip_sum = run(
        functools.partial(turn, dims, inner_width),
        (rows,),
        [
            (sums, by_row(span, LANES)), (sums_other, by_row(span, LANES)),
            (xbc, by_row(span, conv_width)),
            (tab, pl.BlockSpec((1, 1, span, LANES), lambda r: (r, 3, 0, 0))),
            (y_both, by_row(2, span, width)), (z, by_row(span, width)),
            (d_gated, by_row(span, width)), (d_out, by_row(span, model)),
            (normed, by_row(ext, model)), (decay, by_row(blocks, 2, 8, width)),
            (skip_c, whole(1, width)), (gate_gain_c, whole(1, width)),
            (w_late, right_half),
        ],
        [
            (shape_of(BF, rows, span, width), by_row(span, width)),
            (shape_of(BF, rows, span, width), by_row(span, width)),
            (shape_of(F32, rows, blocks, 2, state, width), by_row(blocks, 2, state, width)),
            (shape_of(BF, 2, rows, state + CARRY, width), second(2, state + CARRY, width)),
            (shape_of(BF, rows, span, model), by_row(span, model)),
            (shape_of(BF, model, width), whole(model, width)),
            (shape_of(BF, model, width), whole(model, width)),
            (shape_of(F32, 1, width), whole(1, width)),
            (shape_of(F32, 1, width), whole(1, width)),
        ],
        [pltpu.VMEM((model, width), F32), pltpu.VMEM((model, width), F32)],
        flops=6 * tokens_all * model * width,
        name="turn",
    )
    back_received = around(back_send[::-1])

    dv, dbc, along = run(
        functools.partial(inner_back, dims),
        (rows, blocks),
        [
            (info, SMEM), (starts, SMEM), (xbc, at_block(BLOCK, conv_width)),
            (tab, at_second(5, BLOCK, LANES)), (cumt, at_block(1, packed, BLOCK)),
            (v, at_second(2, BLOCK, width)), (dy, at_block(BLOCK, width)),
            (y_both, at_second(2, BLOCK, width)), (inc, at_block(1, 2, state, width)),
        ],
        [
            (shape_of(F32, rows, 2, span, width), at_second(2, BLOCK, width)),
            (shape_of(F32, rows, span, 4 * state), at_block(BLOCK, 4 * state)),
            (shape_of(F32, rows, span, LANES), at_block(BLOCK, LANES)),
        ],
        flops=2 * scan_flops,
        name="inner_back",
    )
    grad_pre, dn, sum_conv_w, sum_conv_b, small = run(
        functools.partial(back, dims, count),
        (rows,),
        [
            (info, SMEM), (starts, SMEM),
            (back_received, second(count - 1, state + CARRY, width)),
            (enter, by_row(blocks, 2, state, width)), (decay, by_row(blocks, 2, 8, width)),
            (inc, by_row(blocks, 2, state, width)), (xbc, by_row(span, conv_width)),
            (tab, by_row(5, span, LANES)), (v, by_row(2, span, width)),
            (dv, by_row(2, span, width)), (dbc, by_row(span, 4 * state)),
            (along, by_row(span, LANES)), (dy, by_row(span, width)),
            (dsil, by_row(span, conv_width)), (pre, by_row(ext, conv_width)),
            (normed, by_row(ext, model)), (dz, by_row(span, width)),
            (skip_c, whole(1, width)), (a_log_c, whole(1, LANES)),
            (conv_w_c, whole(conv_len, conv_width)), (w_pre, whole(model, pre_width)),
            (w_late, left_half),
        ],
        [
            (shape_of(BF, model, pre_width), whole(model, pre_width)),
            (shape_of(BF, rows, ext, model), by_row(ext, model)),
            (shape_of(F32, conv_len, conv_width), whole(conv_len, conv_width)),
            (shape_of(F32, 1, conv_width), whole(1, conv_width)),
            (shape_of(F32, 8, LANES), whole(8, LANES)),
        ],
        [
            pltpu.VMEM((model, pre_width), F32),
            pltpu.VMEM((ext + 8, conv_width), F32),
            pltpu.VMEM((ext, conv_width), F32),
        ],
        flops=6 * tokens_all * model * pre_width,
        name="back",
    )
    grads = (grad_pre, grad_gate, grad_out)
    sums = (sum_conv_w, sum_conv_b, gate_sum, skip_sum, small)
    if direct:
        widths = (pre_width, width, width)
        scratch = []
        for size in widths:
            scratch += [
                pltpu.VMEM((2, count, 2 * shard, size), BF), pltpu.VMEM((count, 2 * shard, size), BF),
                pltpu.VMEM((count - 1, 2 * shard, size), BF), pltpu.VMEM((count, 2 * shard, size), BF),
                pltpu.VMEM((count - 1, 2 * shard, size), BF), pltpu.VMEM((2 * shard, size), F32),
            ]
        scratch += [pltpu.VMEM((shard, size), F32) for size in widths]
        lanes = conv_width
        scratch += [
            pltpu.VMEM((rows, half, model), BF), pltpu.VMEM((rows, half, model), BF),
            pltpu.VMEM((2, rows, HALO, model), BF), pltpu.VMEM((half, model), F32),
            pltpu.VMEM((8, lanes), F32), pltpu.VMEM((2, 8, lanes), F32), pltpu.VMEM((2, 8, lanes), F32),
            pltpu.VMEM((count - 1, 8, lanes), F32), pltpu.VMEM((8, lanes), F32),
            pltpu.SemaphoreType.DMA((settle_copies(count),)),
            pltpu.SemaphoreType.DMA((settle_copies(count) + 1,)),
        ]
        (mixed, tokens_grad, owned_in, dt_both, owned_out, all_conv_w, all_conv_b, sum_gate, skip_all,
         small_all, sum_norm) = run(
            functools.partial(settle, dims, count, (pre_width // 256 * 128 + 128, width // 2, width // 2)),
            (),
            [
                (pads, SMEM), (tokens, VMEM), (cotangent, VMEM), (gain, VMEM), (dn, VMEM),
                (branch, VMEM),
            ]
            + [
                (grad.reshape(4 * count, 2 * shard, grad.shape[1]), VMEM) for grad in grads
            ]
            + [(value, VMEM) for value in sums],
            [
                (shape_of(BF, rows, half, model), VMEM), (shape_of(BF, rows, half, model), VMEM),
                (shape_of(F32, shard, w_in.shape[1]), VMEM), (shape_of(F32, 2, shard, LANES), VMEM),
                (shape_of(F32, shard, inner_width), VMEM),
                (shape_of(F32, conv_len, xbc_width), VMEM), (shape_of(F32, 1, xbc_width), VMEM),
                (shape_of(F32, 1, inner_width), VMEM), (shape_of(F32, 1, inner_width), VMEM),
                (shape_of(F32, 4, LANES), VMEM), (shape_of(F32, 1, model), VMEM),
            ],
            scratch,
            name="settle",
            collective_id=1,
        )
    else:
        (mixed, tokens_grad, owned_in, dt_both, owned_out, all_conv_w, all_conv_b, sum_gate, skip_all,
         small_all, sum_norm) = settled_apart(
            dims, info, pads, tokens, cotangent, gain, dn, branch, grads, sums, shard
        )

    def by_step(first, second):
        return jnp.concatenate(
            [first[:heads], second[:heads], first[heads : 2 * heads], second[heads : 2 * heads]]
        )

    owned_dt = by_step(dt_both[0].T, dt_both[1].T).T
    return (
        mixed, tokens_grad, sum_norm[0], owned_in, owned_dt, all_conv_w, all_conv_b[0],
        by_step(small_all[0], small_all[2]), by_step(small_all[1], small_all[3]),
        jnp.sum(skip_all.reshape(all_heads, head_dim), axis=-1), sum_gate[0], owned_out,
    )


def solution(mesh):
    weight = P(("dp", "seq", "dir"), None)
    values = P("dp", ("seq", "dir"), None)
    return jax.shard_map(
        shards,
        mesh=mesh,
        in_specs=(
            values, P("dp", None), P("dp"), P(), weight, weight, P(), P(), P(), P(), P(), P(),
            weight, values,
        ),
        out_specs=(
            values, values, P(), weight, weight, P(), P(), P(), P(), P(), P(), weight,
        ),
        check_vma=False,
    )
```

```python
import jax
import jax.numpy as jnp
from jax import lax
from jax.experimental import pallas as pl
from jax.experimental.pallas import tpu as pltpu
from jax.sharding import PartitionSpec as P

BLOCK = 160
HALO = 16
LANES = 128
CARRY = 16
EPSILON = 1e-05
BF = jnp.bfloat16
F32 = jnp.float32
FAR = -1e30
VMEM_BYTES = 62 * 1024 * 1024


class Names:
    def __getattr__(self, name):
        return name


N = Names()


def dot(a, b):
    return lax.dot_general(a, b, (((1,), (0,)), ((), ())), preferred_element_type=F32)


def dot_nt(a, b):
    return lax.dot_general(a, b, (((1,), (1,)), ((), ())), preferred_element_type=F32)


def dot_tn(a, b):
    return lax.dot_general(a, b, (((0,), (0,)), ((), ())), preferred_element_type=F32)


def pieces(values, count):
    parts = []
    for _ in range(count - 1):
        part = values.astype(BF)
        parts.append(part)
        values = values - part.astype(F32)
    parts.append(values.astype(BF))
    return parts


def exact(op, values, ones, count):
    total = None
    for part in pieces(values, count):
        term = op(part, ones)
        total = term if total is None else total + term
    return total


def head_map(first, width, head_dim):
    lane = lax.broadcasted_iota(jnp.int32, (LANES, width), 0)
    head = lax.broadcasted_iota(jnp.int32, (LANES, width), 1) // head_dim
    return jnp.where(lane == head + first, 1.0, 0.0).astype(BF)


def head_maps(heads, width, head_dim):
    return head_map(0, width, head_dim), head_map(heads, width, head_dim)


def triangles():
    row = lax.broadcasted_iota(jnp.int32, (BLOCK, BLOCK), 0)
    col = lax.broadcasted_iota(jnp.int32, (BLOCK, BLOCK), 1)
    return (
        jnp.where(row >= col, 1.0, 0.0).astype(BF),
        jnp.where(row <= col, 1.0, 0.0).astype(BF),
    )


def doc_of(places, starts_ref, row):
    total = (starts_ref[row, 0] <= places).astype(jnp.int32)
    for j in range(1, starts_ref.shape[1]):
        total = total + (starts_ref[row, j] <= places).astype(jnp.int32)
    return total


def column_places(count, first):
    return lax.broadcasted_iota(jnp.int32, (count, 1), 0) + first


class Refs:
    def __init__(self, sizes, names, refs):
        self.__dict__.update(sizes)
        for name, ref in zip(names, refs):
            setattr(self, name, ref)

    def where(self):
        self.core = lax.axis_index("dir")
        self.place = lax.axis_index("seq")
        self.base = self.place * self.span
        return self


def block_rows(block):
    return slice(block * BLOCK, (block + 1) * BLOCK)


def prepare(s):
    late = s.core == 1
    width, heads = s.width, s.heads

    def mine(values, first, size):
        return jnp.where(
            late, values[:, first + size : first + 2 * size], values[:, first : first + size]
        )

    conv_w = s.conv_w[...]
    s.conv_w_c[:, 0:width] = mine(conv_w, 0, width)
    s.conv_w_c[:, width:] = conv_w[:, 2 * width :]
    conv_b = s.conv_b[...][None]
    s.conv_b_c[:, 0:width] = mine(conv_b, 0, width)
    s.conv_b_c[:, width:] = conv_b[:, 2 * width :]
    s.gate_gain_c[...] = mine(s.gate_gain[...][None], 0, width)
    s.gain_c[...] = s.norm_gain[...][None]
    source = lax.broadcasted_iota(jnp.int32, (4 * heads, LANES), 0)
    lane = lax.broadcasted_iota(jnp.int32, (4 * heads, LANES), 1)
    column = jnp.where(lane < heads, lane, lane + heads) + s.core * heads
    picked = jnp.where((source == column) & (lane < 2 * heads), 1.0, 0.0).astype(BF)
    for ref, out in ((s.dt_bias, s.bias_c), (s.a_log, s.a_log_c)):
        rows = jnp.broadcast_to(ref[...][None], (8, 4 * heads))
        out[...] = exact(dot, rows, picked, 3)[0:1]
    head = lax.broadcasted_iota(jnp.int32, (2 * heads, width), 0)
    channel = lax.broadcasted_iota(jnp.int32, (2 * heads, width), 1) // s.head_dim
    spread = jnp.where(head == channel + s.core * heads, 1.0, 0.0).astype(BF)
    rows = jnp.broadcast_to(s.skip[...][None], (8, 2 * heads))
    s.skip_c[...] = exact(dot, rows, spread, 3)[0:1]


def normalise(s, row):
    def norm(part):
        x = part.astype(F32)
        scale = lax.rsqrt(jnp.mean(x * x, axis=-1, keepdims=True) + EPSILON)
        return (x * scale * s.gain_c[...]).astype(BF)

    half = s.half
    s.normed[row, 0:HALO] = norm(s.halo[row])
    own = pl.multiple_of(HALO + s.core * half, HALO)
    other = pl.multiple_of(HALO + (1 - s.core) * half, HALO)
    s.normed[row, pl.ds(own, half)] = norm(s.tokens[row])
    s.normed[row, pl.ds(other, half)] = norm(s.tokens_other[row])


def front(s, row):
    heads, head_dim, state, width, span = s.heads, s.head_dim, s.state, s.width, s.span
    conv_width = s.conv_width
    projected = dot(s.normed[row], flat(s.w_pre))
    pre = projected[:, :conv_width].astype(BF)
    s.pre[row] = pre
    s.pre_f[...] = pre.astype(F32)
    raw = projected[HALO:, conv_width:].astype(BF).astype(F32)
    places = column_places(span, s.base)
    doc = doc_of(places, s.starts, row)
    valid = (places < s.row_len - s.pad_len[row]).astype(F32)
    summed = s.conv_b_c[...]
    for k in range(s.conv_len):
        back = s.conv_len - 1 - k
        ok = (doc_of(places - back, s.starts, row) == doc).astype(F32)
        summed = summed + s.pre_f[HALO - back : HALO - back + span] * s.conv_w_c[k : k + 1] * ok
    gate = 1.0 / (1.0 + jnp.exp(-summed))
    s.xbc[row] = (summed * gate * valid).astype(BF)
    s.dsil[row] = gate * (1.0 + summed * (1.0 - gate)) * valid
    map_f, map_b = head_maps(heads, width, head_dim)
    lower, upper = triangles()
    forward = lax.broadcasted_iota(jnp.int32, (1, LANES), 1) < heads
    shifted_raw = raw + s.bias_c[...]
    step = jnp.maximum(shifted_raw, 0.0) + jnp.log1p(jnp.exp(-jnp.abs(shifted_raw)))
    slope = 1.0 / (1.0 + jnp.exp(-shifted_raw))
    logs = -step * jnp.exp(s.a_log_c[...])
    s.tab[row, 0] = step
    s.tab[row, 4] = slope
    blocks = s.blocks
    kept = ([], [])
    rates = ([], [])
    for b in range(blocks):
        at = block_rows(b)
        step_b, logs_b, doc_b = step[at], logs[at], doc[at]
        cum = jnp.where(
            forward,
            exact(lambda p, m: dot(m, p), logs_b, lower, 3),
            exact(lambda p, m: dot(m, p), logs_b, upper, 3),
        )
        turned = jnp.where(
            lax.broadcasted_iota(jnp.int32, (LANES, 1), 0) < heads,
            exact(lambda p, m: dot_tn(p, m), logs_b, upper, 3),
            exact(lambda p, m: dot_tn(p, m), logs_b, lower, 3),
        )
        s.cumt[row, b] = turned[: s.cumt.shape[2]]
        first_place = s.base + b * BLOCK
        end_f = doc_of(first_place + BLOCK - 1, s.starts, row)
        end_b = doc_of(first_place, s.starts, row)
        near_f = doc_of(first_place - 1, s.starts, row)
        near_b = doc_of(first_place + BLOCK, s.starts, row)
        final = jnp.where(forward, cum[BLOCK - 1 : BLOCK], cum[0:1])
        tail = jnp.exp(final - cum) * (doc_b == jnp.where(forward, end_f, end_b)).astype(F32)
        reach = jnp.exp(cum) * (doc_b == jnp.where(forward, near_f, near_b)).astype(F32)
        s.tab[row, 1, at] = cum
        s.tab[row, 2, at] = tail
        s.tab[row, 3, at] = reach
        decay = jnp.broadcast_to(
            jnp.where(forward, reach[BLOCK - 1 : BLOCK], reach[0:1]), (8, LANES)
        )
        u = s.xbc[row, at, :width].astype(F32)
        for d, head_ones in ((0, map_f), (1, map_b)):
            s.v[row, d, at] = (exact(dot, step_b, head_ones, 2) * u).astype(BF)
            tailed = (exact(dot, tail * step_b, head_ones, 2) * u).astype(BF)
            b_mat = s.xbc[row, at, width + d * state : width + (d + 1) * state]
            local = dot_tn(b_mat, tailed)
            rate = exact(dot, decay, head_ones, 3)
            s.local[row, b, d] = local
            s.decay[row, b, d] = rate
            kept[d].append(local)
            rates[d].append(rate[0:1])
    for d, order in ((0, range(blocks)), (1, reversed(range(blocks)))):
        total, rate = None, None
        for b in order:
            total = kept[d][b] if total is None else rates[d][b] * total + kept[d][b]
            rate = rates[d][b] if rate is None else rate * rates[d][b]
        s.send[d, row, 0:state] = total.astype(BF)
        s.send[d, row, state:] = carried_rows(rate)


def flat(ref, columns=slice(None)):
    if len(ref.shape) == 2:
        return ref[:, columns]
    value = ref[:, :, columns]
    return value.reshape(value.shape[0] * value.shape[1], value.shape[2])


def carried_rows(rate):
    coarse = rate.astype(BF)
    fine = (rate - coarse.astype(F32)).astype(BF)
    row = lax.broadcasted_iota(jnp.int32, (CARRY, rate.shape[1]), 0)
    return jnp.where(
        row == 0, coarse.astype(F32), jnp.where(row == 1, fine.astype(F32), 0.0)
    ).astype(BF)


def compose(received, place, count, state, up):
    total, rate = None, None
    for k in range(1, count):
        part = received[(k - 1) if up else (count - k - 1)]
        there = (place - k >= 0) if up else (place + k < count)
        there = there.astype(F32)
        term = part[0:state].astype(F32) * there
        total = term if total is None else total + rate * term
        hop = part[state : state + 1].astype(F32) + part[state + 1 : state + 2].astype(F32)
        rate = hop if rate is None else rate * hop
    return total


def pair_masks(first_place, starts, row):
    rows = lax.broadcasted_iota(jnp.int32, (BLOCK, BLOCK), 0)
    cols = lax.broadcasted_iota(jnp.int32, (BLOCK, BLOCK), 1)
    doc_rows = doc_of(column_places(BLOCK, first_place), starts, row)
    row_places = lax.broadcasted_iota(jnp.int32, (1, BLOCK), 1) + first_place
    same = doc_rows == doc_of(row_places, starts, row)
    return (
        jnp.where(same & (rows > cols), 0.0, FAR),
        jnp.where(same & (rows < cols), 0.0, FAR),
    )


def inner(s, row, block):
    heads, head_dim, state, width = s.heads, s.head_dim, s.state, s.width
    rows = block_rows(block)
    masks = pair_masks(s.base + block * BLOCK, s.starts, row)
    low_half = lax.broadcasted_iota(jnp.int32, (1, LANES), 1) < head_dim
    for d in range(2):
        b_mat = s.xbc[row, rows, width + d * state : width + (d + 1) * state]
        c_mat = s.xbc[row, rows, width + (2 + d) * state : width + (3 + d) * state]
        scores = dot_nt(c_mat, b_mat)
        for pair in range(heads // 2):
            at = slice(pair * LANES, (pair + 1) * LANES)
            values = s.v[row, d, rows, at]
            outs = []
            for h in (2 * pair, 2 * pair + 1):
                lane = d * heads + h
                gap = s.tab[row, 1, rows, lane : lane + 1] - s.cumt[row, block, lane : lane + 1, :]
                mixing = (jnp.exp(gap + masks[d]) * scores).astype(BF)
                outs.append(dot(mixing, values))
            s.y[row, d, rows, at] = jnp.where(low_half, outs[0], outs[1])


def outer(s, row):
    heads, head_dim, state, width = s.heads, s.head_dim, s.state, s.width
    half, blocks = s.half, s.blocks
    parts = [s.received[k, row] for k in range(s.count - 1)]
    entering = [[None] * 2 for _ in range(blocks)]
    now = compose(parts, s.place, s.count, state, True)
    for b in range(blocks):
        entering[b][0] = now
        now = s.decay[row, b, 0, 0:1] * now + s.local[row, b, 0]
    now = compose(parts, s.place, s.count, state, False)
    for b in reversed(range(blocks)):
        entering[b][1] = now
        now = s.decay[row, b, 1, 0:1] * now + s.local[row, b, 1]
    maps = head_maps(heads, width, head_dim)
    for b in range(blocks):
        at = block_rows(b)
        for d in range(2):
            s.inc[row, b, d] = entering[b][d]
            c_mat = s.xbc[row, at, width + (2 + d) * state : width + (3 + d) * state]
            raw = dot(c_mat, entering[b][d].astype(BF))
            s.y[row, d, at] = s.y[row, d, at] + exact(dot, s.tab[row, 3, at], maps[d], 2) * raw
    u = s.xbc[row, :, :width].astype(F32)
    y = s.y[row, 0] + s.skip_c[...] * u + s.y[row, 1]
    z = dot(s.normed[row, HALO:], flat(s.w_late, slice(0, width)))
    v = y * z * (1.0 / (1.0 + jnp.exp(-z)))
    for cot, core in ((s.cot, s.core), (s.cot_other, 1 - s.core)):
        places = column_places(half, s.base + core * half)
        valid = (places < s.row_len - s.pad_len[row]).astype(F32)
        s.d_out[row, pl.ds(pl.multiple_of(core * half, HALO), half)] = (
            cot[row].astype(F32) * valid
        ).astype(BF)
    d_gated = dot(s.d_out[row], flat(s.w_late, slice(width, None)))
    lane = lax.broadcasted_iota(jnp.int32, (1, LANES), 1)
    squares = jnp.sum(v * v, axis=-1, keepdims=True)
    against = jnp.sum(d_gated * s.gate_gain_c[...] * v, axis=-1, keepdims=True)
    s.sums[row] = jnp.where(lane == 0, squares, jnp.where(lane == 1, against, 0.0))
    s.z[row] = z
    s.dg[row] = d_gated


def turn(s, row):
    heads, head_dim, state, width = s.heads, s.head_dim, s.state, s.width
    blocks = s.blocks
    total = s.sums[row] + s.sums_other[row]
    scale = lax.rsqrt(total[:, 0:1] * (1.0 / s.inner_width) + EPSILON)
    against = total[:, 1:2]
    u = s.xbc[row, :, :width].astype(F32)
    y = s.y[row, 0] + s.skip_c[...] * u + s.y[row, 1]
    z = s.z[row]
    gate = 1.0 / (1.0 + jnp.exp(-z))
    silu = z * gate
    unit = y * silu * scale
    s.gated[row] = (unit * s.gate_gain_c[...]).astype(BF)
    d_gated = s.dg[row]
    d_v = scale * (d_gated * s.gate_gain_c[...]) - unit * (
        scale * scale * against * (1.0 / s.inner_width)
    )
    dy = (d_v * silu).astype(BF)
    s.dy[row] = dy
    s.dz[row] = (d_v * y * gate * (1.0 + z * (1.0 - gate))).astype(BF)
    dy_f = dy.astype(F32)
    gate_term = jnp.sum(d_gated * unit, axis=0, keepdims=True)
    skip_term = jnp.sum(dy_f * u, axis=0, keepdims=True)
    if row:
        gate_term, skip_term = gate_term + s.gate_sum[...], skip_term + s.skip_sum[...]
    s.gate_sum[...] = gate_term
    s.skip_sum[...] = skip_term
    maps = head_maps(heads, width, head_dim)
    for d in range(2):
        gone, rate = None, None
        for b in reversed(range(blocks)) if d == 0 else range(blocks):
            at = block_rows(b)
            c_mat = s.xbc[row, at, width + (2 + d) * state : width + (3 + d) * state]
            weighed = (exact(dot, s.tab[row, 3, at], maps[d], 2) * dy_f[at]).astype(BF)
            enter = dot_tn(c_mat, weighed)
            s.enter[row, b, d] = enter
            own = s.decay[row, b, d, 0:1]
            gone = enter if gone is None else enter + own * gone
            rate = own if rate is None else rate * own
        s.back_send[1 - d, row, 0:state] = gone.astype(BF)
        s.back_send[1 - d, row, state:] = carried_rows(rate)


def branches(s, row):
    s.branch[row] = dot_nt(s.gated[row], flat(s.w_late, slice(s.width, None))).astype(BF)


def weight_grad(s, out, lefts, rights):
    step = 8 * 2 * s.shard if len(out.shape) == 3 else s.model
    for first in range(0, s.model, step):
        total = None
        for left, right in zip(lefts, rights):
            term = dot_tn(left(slice(first, first + step)), right())
            total = term if total is None else total + term
        if len(out.shape) == 2:
            out[...] = total.astype(BF)
        else:
            per = out.shape[1]
            out[first // per : (first + step) // per] = (
                total.astype(BF).reshape(step // per, per, out.shape[2])
            )


def late_grads(s):
    rows = range(s.rows)
    weight_grad(
        s, s.grad_out,
        [lambda at, r=r: s.d_out[r, :, at] for r in rows], [lambda r=r: s.gated[r] for r in rows],
    )
    weight_grad(
        s, s.grad_gate,
        [lambda at, r=r: s.normed[r, HALO:, at] for r in rows], [lambda r=r: s.dz[r] for r in rows],
    )


def pre_grads(s):
    rows = range(s.rows)
    weight_grad(
        s, s.grad_pre,
        [lambda at, r=r: s.normed[r, :, at] for r in rows], [lambda r=r: s.d_all[r] for r in rows],
    )


def inner_back(s, row, block):
    heads, head_dim, state, width = s.heads, s.head_dim, s.state, s.width
    rows = block_rows(block)
    masks = pair_masks(s.base + block * BLOCK, s.starts, row)
    low_half = lax.broadcasted_iota(jnp.int32, (1, LANES), 1) < head_dim
    maps = head_maps(heads, width, head_dim)
    dy_all = s.dy[row, rows].astype(F32)
    along = None
    for d in range(2):
        term = exact(dot_nt, dy_all * s.y[row, d, rows], maps[d], 2)
        along = term if along is None else along + term
        b_mat = s.xbc[row, rows, width + d * state : width + (d + 1) * state]
        c_mat = s.xbc[row, rows, width + (2 + d) * state : width + (3 + d) * state]
        scores = dot_nt(c_mat, b_mat)
        d_scores = jnp.zeros((BLOCK, BLOCK), F32)
        for pair in range(heads // 2):
            at = slice(pair * LANES, (pair + 1) * LANES)
            values = s.v[row, d, rows, at]
            grads = s.dy[row, rows, at]
            outs = []
            for h in (2 * pair, 2 * pair + 1):
                lane = d * heads + h
                gap = s.tab[row, 1, rows, lane : lane + 1] - s.cumt[row, block, lane : lane + 1, :]
                spread = jnp.exp(gap + masks[d])
                mixing = (spread * scores).astype(BF)
                mine = low_half if h % 2 == 0 else ~low_half
                d_mixing = dot_nt(jnp.where(mine, grads, jnp.zeros_like(grads)), values)
                d_scores = d_scores + d_mixing * spread
                outs.append(dot_tn(mixing, grads))
            s.y[row, d, rows, at] = jnp.where(low_half, outs[0], outs[1])
        d_scores = d_scores.astype(BF)
        weighed = (exact(dot, s.tab[row, 3, rows], maps[d], 2) * dy_all).astype(BF)
        d_c = dot(d_scores, b_mat) + dot_nt(weighed, s.inc[row, block, d].astype(BF))
        d_b = dot_tn(d_scores, c_mat)
        s.dbc[row, rows, d * state : (d + 1) * state] = d_b
        s.dbc[row, rows, (2 + d) * state : (3 + d) * state] = d_c
    s.along[row, rows] = along


def back(s, row):
    heads, head_dim, state, width, span = s.heads, s.head_dim, s.state, s.width, s.span
    conv_width, conv_len, blocks = s.conv_width, s.conv_len, s.blocks
    parts = [s.back_received[k, row] for k in range(s.count - 1)]
    leaving = [[None] * 2 for _ in range(blocks)]
    now = compose(parts, s.place, s.count, state, False)
    for b in reversed(range(blocks)):
        leaving[b][0] = now
        now = s.enter[row, b, 0] + s.decay[row, b, 0, 0:1] * now
    now = compose(parts, s.place, s.count, state, True)
    for b in range(blocks):
        leaving[b][1] = now
        now = s.enter[row, b, 1] + s.decay[row, b, 1, 0:1] * now
    maps = head_maps(heads, width, head_dim)
    lower, upper = triangles()
    forward = lax.broadcasted_iota(jnp.int32, (1, LANES), 1) < heads
    rate = jnp.exp(s.a_log_c[...])
    rows = lax.broadcasted_iota(jnp.int32, (BLOCK, 1), 0)
    if row == 0:
        s.pad[0:HALO] = jnp.zeros((HALO, conv_width), F32)
        s.pad[HALO + span :] = jnp.zeros((s.pad.shape[0] - HALO - span, conv_width), F32)
    d_bias, d_rate = None, None
    for b in range(blocks):
        at = block_rows(b)
        inside = slice(HALO + b * BLOCK, HALO + (b + 1) * BLOCK)
        u = s.xbc[row, at, :width].astype(F32)
        step, tail, slope = s.tab[row, 0, at], s.tab[row, 2, at], s.tab[row, 4, at]
        reach = s.tab[row, 3, at]
        d_u = s.skip_c[...] * s.dy[row, at].astype(F32)
        through, direct, ended = None, None, None
        d_bc = []
        for d in range(2):
            leave = leaving[b][d].astype(BF)
            b_mat = s.xbc[row, at, width + d * state : width + (d + 1) * state]
            v_d = s.v[row, d, at].astype(F32)
            dv_state = exact(dot, tail, maps[d], 2) * dot(b_mat, leave)
            dv_all = s.y[row, d, at] + dv_state
            step_wide = exact(dot, step, maps[d], 2)
            tailed = (exact(dot, tail * step, maps[d], 2) * u).astype(BF)
            d_bc.append(dot_nt(tailed, leave))
            d_u = d_u + step_wide * dv_all
            row_id = lax.broadcasted_iota(jnp.int32, (8, width), 0)
            sides = jnp.where(
                row_id == 0,
                jnp.sum(v_d * dv_state, axis=0, keepdims=True),
                jnp.sum(leaving[b][d] * s.inc[row, b, d], axis=0, keepdims=True),
            )
            terms = (
                exact(dot_nt, v_d * dv_all, maps[d], 2),
                exact(dot_nt, u * dv_all, maps[d], 2),
                exact(dot_nt, sides, maps[d], 3),
            )
            if d == 0:
                through, direct, ended = terms
            else:
                through, direct, ended = through + terms[0], direct + terms[1], ended + terms[2]
        final = jnp.where(forward, reach[BLOCK - 1 : BLOCK], reach[0:1])
        at_end = jnp.where(
            forward, (rows == BLOCK - 1).astype(F32), (rows == 0).astype(F32)
        )
        d_cum = s.along[row, at] - through + at_end * (ended[0:1] + ended[1:2] * final)
        d_logs = jnp.where(
            forward,
            exact(lambda p, m: dot(m, p), d_cum, upper, 3),
            exact(lambda p, m: dot(m, p), d_cum, lower, 3),
        )
        d_raw = (direct - rate * d_logs) * slope
        s.d_all[row, inside, conv_width:] = d_raw.astype(BF)
        bias_term = jnp.sum(d_raw, axis=0, keepdims=True)
        rate_term = jnp.sum(-step * rate * d_logs, axis=0, keepdims=True)
        d_bias = bias_term if d_bias is None else d_bias + bias_term
        d_rate = rate_term if d_rate is None else d_rate + rate_term
        s.pad[inside, 0:width] = d_u * s.dsil[row, at, 0:width]
        half_bc = jnp.concatenate(d_bc, axis=1)
        s.pad[inside, width : width + 2 * state] = (
            s.dbc[row, at, : 2 * state] + half_bc
        ) * s.dsil[row, at, width : width + 2 * state]
        s.pad[inside, width + 2 * state :] = (
            s.dbc[row, at, 2 * state :] * s.dsil[row, at, width + 2 * state :]
        )
    s.d_all[row, 0:HALO, conv_width:] = jnp.zeros((HALO, LANES), BF)
    s.pre_f[...] = s.pre[row].astype(F32)
    places = column_places(span, s.base)
    doc = doc_of(places, s.starts, row)
    outs = s.pad[HALO : HALO + span]
    conv_b_term = jnp.sum(outs, axis=0, keepdims=True)
    ext_places = column_places(HALO + span, s.base - HALO)
    ext_doc = doc_of(ext_places, s.starts, row)
    d_pre = None
    conv_w_terms = []
    for k in range(conv_len):
        ahead = conv_len - 1 - k
        ok = (doc_of(places - ahead, s.starts, row) == doc).astype(F32)
        conv_w_terms.append(
            jnp.sum(
                outs * ok * s.pre_f[HALO - ahead : HALO - ahead + span], axis=0, keepdims=True
            )
        )
        ok_ext = (doc_of(ext_places + ahead, s.starts, row) == ext_doc).astype(F32)
        term = s.pad[ahead : ahead + HALO + span] * ok_ext * s.conv_w_c[k : k + 1]
        d_pre = term if d_pre is None else d_pre + term
    s.d_all[row, :, 0:conv_width] = d_pre.astype(BF)
    conv_w_term = jnp.concatenate(conv_w_terms, axis=0)
    small_term = jnp.concatenate([d_bias, d_rate], axis=0)
    if row:
        conv_w_term = conv_w_term + s.sum_conv_w[...]
        conv_b_term = conv_b_term + s.sum_conv_b[...]
        small_term = small_term + s.small[0:2]
    s.sum_conv_w[...] = conv_w_term
    s.sum_conv_b[...] = conv_b_term
    s.small[0:2] = small_term


def d_norms(s, row):
    dn = dot_nt(s.d_all[row], flat(s.w_pre))
    s.dn[row, 0:HALO] = dn[0:HALO].astype(BF)
    s.dn[row, HALO:] = (
        dn[HALO:] + dot_nt(s.dz[row], flat(s.w_late, slice(0, s.width)))
    ).astype(BF)


def finish(s, row):
    half = s.half
    x = s.tokens[row].astype(F32)
    places = column_places(half, s.base + s.core * half)
    valid = (places < s.row_len - s.pad_len[row]).astype(F32)
    keep = pl.ds(pl.multiple_of(s.core * half, HALO), half)
    s.mixed[row] = (
        x + valid * (s.branch[row, keep].astype(F32) + s.branch_other[row].astype(F32))
    ).astype(BF)
    keep = pl.ds(pl.multiple_of(HALO + s.core * half, HALO), half)
    s.ds[...] = s.dn[row, keep].astype(F32) + s.dn_other[row].astype(F32)
    takes = ((s.core == 1) & (s.place + 1 < s.count)).astype(F32)
    s.ds[half - HALO :] += takes * (s.rims[0, row].astype(F32) + s.rims[1, row].astype(F32))
    d_normed = s.ds[...]
    scale = lax.rsqrt(jnp.mean(x * x, axis=-1, keepdims=True) + EPSILON)
    weighed = d_normed * s.norm_gain[...][None]
    along = jnp.mean(weighed * x, axis=-1, keepdims=True)
    dx = scale * weighed - x * (scale * scale * scale * along)
    s.tokens_grad[row] = (s.cot[row].astype(F32) + dx).astype(BF)
    term = jnp.sum(d_normed * x * scale, axis=0, keepdims=True)
    s.gain_sum[...] = term if row == 0 else s.gain_sum[...] + term


MESH = pl.DeviceIdType.MESH


def remote(src, dst, send_sem, recv_sem, device):
    return pltpu.make_async_remote_copy(
        src_ref=src, dst_ref=dst, send_sem=send_sem, recv_sem=recv_sem, device_id=device,
        device_id_type=MESH,
    )


class Sender:
    def __init__(self, send_sems, recv_sems):
        self.send_sems, self.recv_sems = send_sems, recv_sems
        self.sent = 0
        self.slots = 0
        self.pending = []

    def slot(self):
        self.slots += 1
        return self.slots - 1

    def send(self, src, dst, slot, device):
        copy = remote(src, dst, self.send_sems.at[self.sent], self.recv_sems.at[slot], device)
        self.sent += 1
        copy.start()
        self.pending.append(copy)

    def arrive(self, dst, slot, device):
        remote(dst, dst, self.send_sems.at[0], self.recv_sems.at[slot], device).wait_recv()

    def drain(self):
        for copy in self.pending:
            copy.wait_send()
        self.pending = []


class Place:
    def __init__(self, count):
        self.dp, self.seq, self.dir = (lax.axis_index(a) for a in ("dp", "seq", "dir"))
        self.count = count
        self.side = self.dp + 1 - 2 * (self.dp % 2)
        self.below = (self.dp + 2) % 4
        self.across = 3 - self.dp
        self.me = (self.dp, self.seq, self.dir)
        self.sibling = (self.dp, self.seq, 1 - self.dir)
        self.by_x = (self.side, self.seq, self.dir)
        self.by_y = (self.below, self.seq, self.dir)

    def along(self, k, crossed=False):
        core = 1 - self.dir if crossed else self.dir
        return (self.dp, (self.seq + k + self.count) % self.count, core)

    def at(self, k):
        return (self.seq + k + self.count) % self.count

    def chip(self, dp, k=0):
        return dp * self.count + self.at(k)

    def meet(self):
        barrier = pltpu.get_barrier_semaphore()
        others = [self.sibling, self.by_x, self.by_y]
        others += [self.along(k) for k in range(1, self.count)]
        others += [self.along(1, True), self.along(-1, True)]
        for device in others:
            pl.semaphore_signal(barrier, inc=1, device_id=device, device_id_type=MESH)
        pl.semaphore_wait(barrier, len(others))


class Spread:
    def __init__(self, place, sender, slab, cut):
        self.place, self.sender, self.slab, self.cut = place, sender, slab, cut
        count = place.count
        self.z = [None] + [sender.slot() for _ in range(1, count)]
        self.x, self.y, self.xd, self.yd = (
            [sender.slot() for _ in range(count)] for _ in range(4)
        )

    def start(self, mine):
        here, to = self.place, self.sender
        spot = self.slab.at[here.chip(here.dp)]
        to.send(mine, spot, self.x[0], here.by_x)
        to.send(mine, spot, self.y[0], here.by_y)
        for k in range(1, here.count):
            to.send(mine, spot, self.z[k], here.along(k))

    def relay(self, k):
        here, to = self.place, self.sender
        spot = self.slab.at[here.chip(here.dp, -k)]
        to.arrive(spot, self.z[k], here.along(-k))
        to.send(spot, spot, self.x[k], here.by_x)
        to.send(spot, spot, self.y[k], here.by_y)

    def cross(self, k):
        here, to = self.place, self.sender
        from_x = self.slab.at[here.chip(here.side, -k)]
        to.arrive(from_x, self.x[k], here.by_x)
        part = from_x.at[:, : self.cut]
        to.send(part, part, self.yd[k], here.by_y)
        from_y = self.slab.at[here.chip(here.below, -k)]
        to.arrive(from_y, self.y[k], here.by_y)
        part = from_y.at[:, self.cut :]
        to.send(part, part, self.xd[k], here.by_x)

    def end(self, k):
        here, to = self.place, self.sender
        spot = self.slab.at[here.chip(here.across, -k)]
        to.arrive(spot.at[:, : self.cut], self.yd[k], here.by_y)
        to.arrive(spot.at[:, self.cut :], self.xd[k], here.by_x)


class Reduce:
    def __init__(self, place, sender, grad, cut, first, second, third, out_second, out_third, total):
        self.place, self.sender, self.grad, self.cut = place, sender, grad, cut
        self.first, self.second, self.third = first, second, third
        self.out_second, self.out_third, self.total = out_second, out_third, total
        count = place.count
        self.one = [[[sender.slot() for _ in range(count)] for _ in range(2)] for _ in range(2)]
        self.two = [[sender.slot() for _ in range(count)] for _ in range(2)]
        self.three = [None] + [sender.slot() for _ in range(1, count)]
        self.sides = (slice(0, cut), slice(cut, grad.shape[2]))

    def start(self, k):
        here, to = self.place, self.sender
        for side, device, targets in (
            (0, here.by_x, (here.side, here.across)),
            (1, here.by_y, (here.below, here.across)),
        ):
            at = self.sides[side]
            for q in (1, 0):
                to.send(
                    self.grad.at[here.chip(targets[q], k), :, at],
                    self.first.at[q, k, :, at],
                    self.one[side][q][k], device,
                )

    def pass_on(self, k):
        here, to = self.place, self.sender
        for side, came, device, target in (
            (0, here.by_x, here.by_y, here.below),
            (1, here.by_y, here.by_x, here.side),
        ):
            at = self.sides[side]
            to.arrive(self.first.at[1, k, :, at], self.one[side][1][k], came)
            self.out_second[k, :, at] = (
                self.grad[here.chip(target, k), :, at].astype(F32)
                + self.first[1, k, :, at].astype(F32)
            ).astype(BF)
            to.send(self.out_second.at[k, :, at], self.second.at[k, :, at], self.two[side][k], device)

    def along(self, k):
        here, to = self.place, self.sender
        for side, came, then in ((0, here.by_x, here.by_y), (1, here.by_y, here.by_x)):
            at = self.sides[side]
            to.arrive(self.first.at[0, k, :, at], self.one[side][0][k], came)
            to.arrive(self.second.at[k, :, at], self.two[side][k], then)
            summed = (
                self.grad[here.chip(here.dp, k), :, at].astype(F32)
                + self.first[0, k, :, at].astype(F32)
                + self.second[k, :, at].astype(F32)
            )
            if k == 0:
                self.total[:, at] = summed
            else:
                self.out_third[k - 1, :, at] = summed.astype(BF)
        if k:
            to.send(self.out_third.at[k - 1], self.third.at[k - 1], self.three[k], here.along(k))

    def end(self):
        here, to = self.place, self.sender
        for k in range(1, here.count):
            to.arrive(self.third.at[k - 1], self.three[k], here.along(-k))
            self.total[...] += self.third[k - 1].astype(F32)


def fill_columns(s, core, pre, late):
    width, heads, conv_width = s.width, s.heads, s.conv_width
    late_side = core == 1
    pick = lambda ref, at: jnp.where(
        late_side, ref[:, at + width : at + 2 * width], ref[:, at : at + width]
    )
    source = lax.broadcasted_iota(jnp.int32, (4 * heads, LANES), 0)
    lane = lax.broadcasted_iota(jnp.int32, (4 * heads, LANES), 1)
    column = jnp.where(lane < heads, lane, lane + heads) + core * heads
    ones = jnp.where((source == column) & (lane < 2 * heads), 1.0, 0.0).astype(BF)
    pre[:, 0:width] = pick(s.w_in, 2 * width).astype(pre.dtype)
    pre[:, width:conv_width] = s.w_in[:, 4 * width :].astype(pre.dtype)
    pre[:, conv_width:] = dot(s.w_dt[...], ones).astype(pre.dtype)
    late[:, 0:width] = pick(s.w_in, 0).astype(late.dtype)
    late[:, width:] = pick(s.w_out, 0).astype(late.dtype)


class Around:
    def __init__(self, place, sender, values, landed):
        self.place, self.sender, self.values, self.landed = place, sender, values, landed
        self.slots = [None] + [sender.slot() for _ in range(1, place.count)]

    def start(self):
        here, to = self.place, self.sender
        for k in range(1, here.count):
            which = (here.seq + k) // here.count
            to.send(self.values.at[which], self.landed.at[k - 1], self.slots[k], here.along(k))

    def end(self):
        here, to = self.place, self.sender
        for k in range(1, here.count):
            to.arrive(self.landed.at[k - 1], self.slots[k], here.along(-k))


def everything(sizes, names, *refs):
    s = Refs(sizes, names, refs).where()
    count, rows, half, width, heads = s.count, s.rows, s.half, s.width, s.heads
    conv_width, model, shard = s.conv_width, s.model, s.shard
    here = Place(count)
    to = Sender(s.send_sems, s.recv_sems)
    late_core = here.dir == 1
    fill_columns(s, 1 - here.dir, s.give_pre, s.give_late)
    here.meet()

    pair = [to.slot() for _ in range(5)]
    to.send(s.give_pre, s.got_pre, pair[0], here.sibling)
    to.send(s.tokens, s.tokens_other, pair[2], here.sibling)
    rim = s.tokens.at[:, pl.ds(half - HALO, HALO)]
    first_rim, second_rim = to.sent, to.sent + 1
    to.sent += 2

    def rims_out():
        return [
            remote(rim, s.halo, s.send_sems.at[sem], s.recv_sems.at[pair[4]], here.along(1, crossed))
            for sem, crossed in ((first_rim, False), (second_rim, True))
        ]

    @pl.when(late_core)
    def _():
        for copy in rims_out():
            copy.start()

    to.send(s.give_late, s.got_late, pair[1], here.sibling)
    to.send(s.cot, s.cot_other, pair[3], here.sibling)
    fill_columns(s, here.dir, s.pre_mine, s.late_mine)

    def joined(own, got):
        other = got[...].astype(F32)
        own = own[...]
        return jnp.where(
            late_core,
            jnp.concatenate([other, own], axis=0),
            jnp.concatenate([own, other], axis=0),
        ).astype(BF)

    me = here.chip(here.dp)
    spread_pre = Spread(here, to, s.w_pre, s.cuts[0])
    spread_late = Spread(here, to, s.w_late, s.cuts[1])
    to.arrive(s.got_pre, pair[0], here.sibling)
    s.w_pre[me] = joined(s.pre_mine, s.got_pre)
    spread_pre.start(s.w_pre.at[me])
    to.arrive(s.got_late, pair[1], here.sibling)
    s.w_late[me] = joined(s.late_mine, s.got_late)
    prepare(s)
    to.arrive(s.tokens_other, pair[2], here.sibling)
    to.arrive(s.halo, pair[4], here.along(-1))
    spread_pre.cross(0)
    spread_pre.relay(1)
    for row in range(rows):
        normalise(s, row)
    spread_pre.cross(1)
    for k in range(2, count):
        spread_pre.relay(k)
        spread_pre.cross(k)
    spread_late.start(s.w_late.at[me])
    for k in range(count):
        spread_pre.end(k)

    states = Around(here, to, s.send, s.received)
    front(s, 0)
    spread_late.cross(0)
    spread_late.relay(1)
    for row in range(1, rows):
        front(s, row)
    states.start()
    spread_late.cross(1)
    spread_late.relay(2)
    units = [(row, block) for row in range(rows) for block in range(s.blocks)]
    for i, (row, block) in enumerate(units):
        inner(s, row, block)
        if i == 0:
            spread_late.cross(2)
            spread_late.relay(3)
        if i == 1:
            spread_late.cross(3)
    states.end()
    for k in range(count):
        spread_late.end(k)
    to.arrive(s.cot_other, pair[3], here.sibling)
    sum_slots = [to.slot() for _ in range(rows)]
    for row in range(rows):
        outer(s, row)
        to.send(s.sums.at[row], s.sums_other.at[row], sum_slots[row], here.sibling)

    back_states = Around(here, to, s.back_send, s.back_received)
    for row in range(rows):
        to.arrive(s.sums_other.at[row], sum_slots[row], here.sibling)
        turn(s, row)
    back_states.start()
    grads = (s.grad_pre, s.grad_gate, s.grad_out)
    reduces = [Reduce(here, to, g, cut, *work) for g, cut, work in zip(grads, s.grad_cuts, s.works)]
    reduce_pre, reduce_late = reduces[0], reduces[1:]
    late_grads(s)
    order = list(range(1, count)) + [0]
    for k in order:
        for reduce in reduce_late:
            reduce.start(k)
    for row in range(rows):
        branches(s, row)
    branch_slot, dn_slot, rim_own, rim_cross = (to.slot() for _ in range(4))
    give = pl.multiple_of((1 - here.dir) * half, HALO)
    to.send(s.branch.at[:, pl.ds(give, half)], s.branch_other, branch_slot, here.sibling)
    for i, (row, block) in enumerate(units):
        inner_back(s, row, block)
        if i < count:
            for reduce in reduce_late:
                reduce.pass_on(order[i])
    back_states.end()
    back(s, 0)
    for k in order[:2]:
        for reduce in reduce_late:
            reduce.along(k)
    for row in range(1, rows):
        back(s, row)
    for k in order[2:]:
        for reduce in reduce_late:
            reduce.along(k)
    pre_grads(s)
    for k in order:
        reduce_pre.start(k)
    for row in range(rows):
        d_norms(s, row)
    to.send(s.dn.at[:, pl.ds(HALO + give, half)], s.dn_other, dn_slot, here.sibling)
    edge = s.dn.at[:, pl.ds(0, HALO)]
    rim_sem = to.sent
    to.sent += 1

    def edge_out(core):
        return remote(
            edge, s.rims.at[core], s.send_sems.at[rim_sem],
            s.recv_sems.at[(rim_cross, rim_own)[core]], here.along(-1, core == 0),
        )

    for core in range(2):
        @pl.when(here.dir == core)
        def _():
            edge_out(core).start()

    for reduce in reduce_late:
        reduce.end()
    to.arrive(s.branch_other, branch_slot, here.sibling)
    to.arrive(s.dn_other, dn_slot, here.sibling)

    @pl.when(late_core)
    def _():
        to.arrive(s.rims.at[1], rim_own, here.along(1))
        to.arrive(s.rims.at[0], rim_cross, here.along(1, True))

    @pl.when(here.dir == 0)
    def _():
        s.rims[...] = jnp.zeros_like(s.rims)

    for row in range(rows):
        finish(s, row)
    side = conv_width - width
    s.v_own[0:4] = s.sum_conv_w[...]
    s.v_own[4:5] = s.sum_conv_b[...]
    s.v_own[5:6] = jnp.concatenate([s.gate_sum[...], s.small[0:1], s.small[1:2]], axis=1)
    s.v_own[6:7] = jnp.concatenate([s.skip_sum[...], jnp.zeros((1, side), F32)], axis=1)
    s.v_own[7:8] = jnp.concatenate([s.gain_sum[...], jnp.zeros((1, side), F32)], axis=1)
    v_slots = [to.slot() for _ in range(2 + count)]
    to.send(s.v_own, s.v_x.at[0], v_slots[0], here.by_x)
    for k in order:
        reduce_pre.pass_on(k)
    to.arrive(s.v_x.at[0], v_slots[0], here.by_x)
    s.v_x[1] = s.v_own[...] + s.v_x[0]
    to.send(s.v_x.at[1], s.v_y.at[0], v_slots[1], here.by_y)
    for k in order:
        reduce_pre.along(k)
    to.arrive(s.v_y.at[0], v_slots[1], here.by_y)
    s.v_y[1] = s.v_x[1] + s.v_y[0]
    for k in range(1, count):
        to.send(s.v_y.at[1], s.v_z.at[k - 1], v_slots[1 + k], here.along(k))
    swaps = []
    others = s.others
    back_rows = pl.ds(pl.multiple_of((1 - here.dir) * shard, 8), shard)
    own_rows = pl.ds(pl.multiple_of(here.dir * shard, 8), shard)
    for i in (1, 2, 0):
        slot = to.slot()
        if i == 0:
            reduce_pre.end()
        to.send(reduces[i].total.at[back_rows], others[i], slot, here.sibling)
        swaps.append((i, slot))
    total = s.v_y[1]
    for k in range(1, count):
        to.arrive(s.v_z.at[k - 1], v_slots[1 + k], here.along(-k))
        total = total + s.v_z[k - 1]
    s.v_x[0] = total
    to.send(s.v_x.at[0], s.v_other, v_slots[1 + count], here.sibling)
    parts = {}
    for i, slot in swaps:
        to.arrive(others[i], slot, here.sibling)
        own, got = reduces[i].total[own_rows], others[i][...]
        parts[i] = (jnp.where(late_core, got, own), jnp.where(late_core, own, got))
    (pre_a, pre_b), (gate_a, gate_b), (out_a, out_b) = (parts[i] for i in range(3))
    s.o_in[:, 0:width] = gate_a
    s.o_in[:, width : 2 * width] = gate_b
    s.o_in[:, 2 * width : 3 * width] = pre_a[:, :width]
    s.o_in[:, 3 * width : 4 * width] = pre_b[:, :width]
    s.o_in[:, 4 * width :] = pre_a[:, width:conv_width] + pre_b[:, width:conv_width]
    s.o_out[:, 0:width] = out_a
    s.o_out[:, width:] = out_b
    lane = lax.broadcasted_iota(jnp.int32, (LANES, 4 * heads), 0)
    column = lax.broadcasted_iota(jnp.int32, (LANES, 4 * heads), 1)
    first_lane = jnp.where(lane < heads, lane, jnp.where(lane < 2 * heads, lane + heads, -1))
    picks = [
        jnp.where((first_lane >= 0) & (column == first_lane + side_of * heads), 1.0, 0.0).astype(BF)
        for side_of in range(2)
    ]
    by_step = lambda a, b: exact(dot, a, picks[0], 3) + exact(dot, b, picks[1], 3)
    s.o_dt[...] = by_step(pre_a[:, conv_width:], pre_b[:, conv_width:])
    to.arrive(s.v_other, v_slots[1 + count], here.sibling)
    got = s.v_other[...]
    v_a, v_b = jnp.where(late_core, got, total), jnp.where(late_core, total, got)
    both = v_a + v_b
    s.o_conv_w[:, 0:width] = v_a[0:4, :width]
    s.o_conv_w[:, width : 2 * width] = v_b[0:4, :width]
    s.o_conv_w[:, 2 * width :] = both[0:4, width:]
    s.o_conv_b[...] = jnp.concatenate([v_a[4:5, :width], v_b[4:5, :width], both[4:5, width:]], axis=1)[0]
    s.o_gate[...] = jnp.concatenate([v_a[5:6, :width], v_b[5:6, :width]], axis=1)[0]
    steps = by_step(
        jnp.concatenate([v_a[5:6, width : width + LANES], v_a[5:6, width + LANES : width + 2 * LANES]] * 4, axis=0),
        jnp.concatenate([v_b[5:6, width : width + LANES], v_b[5:6, width + LANES : width + 2 * LANES]] * 4, axis=0),
    )
    s.o_bias[...] = steps[0]
    s.o_alog[...] = steps[1]
    head = lax.broadcasted_iota(jnp.int32, (width, 2 * heads), 1)
    channel = lax.broadcasted_iota(jnp.int32, (width, 2 * heads), 0) // s.head_dim
    skips = None
    for side_of, v_side in ((0, v_a), (1, v_b)):
        ones = jnp.where(head == channel + side_of * heads, 1.0, 0.0).astype(BF)
        term = exact(dot, jnp.broadcast_to(v_side[6:7, :width], (8, width)), ones, 3)
        skips = term if skips is None else skips + term
    s.o_skip[...] = skips[0]
    s.o_norm[...] = both[7:8, :model][0]
    to.drain()

    @pl.when(late_core)
    def _():
        for copy in rims_out():
            copy.wait_send()

    for core in range(2):
        @pl.when(here.dir == core)
        def _():
            edge_out(core).wait_send()


SMEM = pl.BlockSpec(memory_space=pltpu.SMEM)
VMEM = pl.BlockSpec(memory_space=pltpu.VMEM)


def call(body, ins, specs, out_shapes, scratch, name, collective_id=None):
    return pl.pallas_call(
        body,
        out_shape=out_shapes,
        in_specs=specs,
        out_specs=[VMEM] * len(out_shapes),
        scratch_shapes=scratch,
        compiler_params=pltpu.CompilerParams(
            vmem_limit_bytes=VMEM_BYTES, collective_id=collective_id,
            has_side_effects=collective_id is not None,
        ),
        name=name,
    )(*ins)


def shape_of(dtype, *dims):
    return jax.ShapeDtypeStruct(dims, dtype)


def buffers(z):
    rows, span, half, model, width, state = z[N.rows], z[N.span], z[N.half], z[N.model], z[N.width], z[N.state]
    blocks, conv_width, pre_width, count = z[N.blocks], z[N.conv_width], z[N.pre_width], z[N.count]
    ext, conv_len, heads = HALO + span, z[N.conv_len], z[N.heads]
    packed = 2 * heads + (-2 * heads) % 8
    carried = (state + CARRY, width)
    table = dict(
        conv_w_c=(F32, conv_len, conv_width), conv_b_c=(F32, 1, conv_width), bias_c=(F32, 1, LANES),
        a_log_c=(F32, 1, LANES), skip_c=(F32, 1, width), gate_gain_c=(F32, 1, width),
        gain_c=(F32, 1, model), halo=(BF, rows, HALO, model), tokens_other=(BF, rows, half, model),
        cot_other=(BF, rows, half, model), normed=(BF, rows, ext, model),
        pre=(BF, rows, ext, conv_width), pre_f=(F32, ext, conv_width),
        xbc=(BF, rows, span, conv_width), dsil=(F32, rows, span, conv_width),
        tab=(F32, rows, 5, span, LANES), cumt=(F32, rows, blocks, packed, BLOCK),
        v=(BF, rows, 2, span, width), local=(F32, rows, blocks, 2, state, width),
        decay=(F32, rows, blocks, 2, 8, width), send=(BF, 2, rows) + carried,
        received=(BF, count - 1, rows) + carried, y=(F32, rows, 2, span, width),
        inc=(F32, rows, blocks, 2, state, width), sums=(F32, rows, span, LANES),
        sums_other=(F32, rows, span, LANES), z=(F32, rows, span, width), dg=(F32, rows, span, width),
        d_out=(BF, rows, span, model), gated=(BF, rows, span, width), dy=(BF, rows, span, width),
        dz=(BF, rows, span, width), enter=(F32, rows, blocks, 2, state, width),
        back_send=(BF, 2, rows) + carried, back_received=(BF, count - 1, rows) + carried,
        branch=(BF, rows, span, model), grad_out=(BF, model, width), grad_gate=(BF, model, width),
        gate_sum=(F32, 1, width), skip_sum=(F32, 1, width), dbc=(F32, rows, span, 4 * state),
        along=(F32, rows, span, LANES), pad=(F32, ext + 8, conv_width),
        d_all=(BF, rows, ext, pre_width), grad_pre=(BF, model, pre_width),
        sum_conv_w=(F32, conv_len, conv_width), sum_conv_b=(F32, 1, conv_width), small=(F32, 8, LANES),
        dn=(BF, rows, ext, model), branch_other=(BF, rows, half, model),
        dn_other=(BF, rows, half, model), rims=(BF, 2, rows, HALO, model), ds=(F32, half, model),
        gain_sum=(F32, 1, model), mixed=(BF, rows, half, model), tokens_grad=(BF, rows, half, model),
    )
    return {name: shape_of(*shape) for name, shape in table.items()}


def together(z, args):
    count, shard, width, conv_width = z[N.count], z[N.shard], z[N.width], z[N.conv_width]
    pre_width, model, rows, half, heads = z[N.pre_width], z[N.model], z[N.rows], z[N.half], z[N.heads]
    chips, pair = 4 * count, 2 * shard
    table = buffers(z)
    for name in (N.grad_out, N.grad_gate, N.grad_pre):
        table[name] = shape_of(BF, chips, pair, table[name].shape[1])
    outs = dict(
        mixed=table.pop(N.mixed), tokens_grad=table.pop(N.tokens_grad), o_norm=shape_of(F32, model),
        o_in=shape_of(F32, shard, 4 * width + 4 * z[N.state]), o_dt=shape_of(F32, shard, 4 * heads),
        o_conv_w=shape_of(F32, z[N.conv_len], conv_width + width),
        o_conv_b=shape_of(F32, conv_width + width), o_bias=shape_of(F32, 4 * heads),
        o_alog=shape_of(F32, 4 * heads), o_skip=shape_of(F32, 2 * heads),
        o_gate=shape_of(F32, 2 * width), o_out=shape_of(F32, shard, 2 * width),
    )
    aliases = {N.enter: N.local}
    scratch = {
        name: pltpu.VMEM(value.shape, value.dtype)
        for name, value in table.items() if name not in aliases
    }
    scratch.update(
        w_pre=pltpu.VMEM((chips, pair, pre_width), BF), w_late=pltpu.VMEM((chips, pair, 2 * width), BF),
        give_pre=pltpu.VMEM((shard, pre_width), BF), give_late=pltpu.VMEM((shard, 2 * width), BF),
        got_pre=pltpu.VMEM((shard, pre_width), BF), got_late=pltpu.VMEM((shard, 2 * width), BF),
        pre_mine=pltpu.VMEM((shard, pre_width), F32), late_mine=pltpu.VMEM((shard, 2 * width), F32),
        v_own=pltpu.VMEM((8, conv_width), F32), v_x=pltpu.VMEM((2, 8, conv_width), F32),
        v_y=pltpu.VMEM((2, 8, conv_width), F32), v_z=pltpu.VMEM((count - 1, 8, conv_width), F32),
        v_other=pltpu.VMEM((8, conv_width), F32),
    )
    widths = dict(pre=pre_width, gate=width, out=width)
    work_names = []
    for name, size in widths.items():
        scratch[name, -1] = pltpu.VMEM((shard, size), F32)
        for i, shape in enumerate(
            ((2, count, pair), (count, pair), (count - 1, pair), (count, pair), (count - 1, pair))
        ):
            scratch[name, i] = pltpu.VMEM(shape + (size,), BF)
        scratch[name, 5] = pltpu.VMEM((pair, size), F32)
        work_names.append([(name, i) for i in range(6)])
    copies = 64 + 16 * count + 3 * (7 * count) + 16
    scratch[N.send_sems] = pltpu.SemaphoreType.DMA((copies,))
    scratch[N.recv_sems] = pltpu.SemaphoreType.DMA((copies,))
    in_names = list(args)
    names = in_names + list(outs) + list(scratch)
    cut = pre_width // 256 * 128 + 128

    def body(*refs):
        sizes = dict(z, cuts=(cut, width), grad_cuts=(cut, width // 2, width // 2))
        by_name = dict(zip(names, refs))
        for name, of in aliases.items():
            by_name[name] = by_name[of]
        sizes[N.works] = [[by_name[n] for n in group] for group in work_names]
        sizes[N.others] = [by_name[name, -1] for name in widths]
        plain = {name: ref for name, ref in by_name.items() if isinstance(name, str)}
        everything(sizes, list(plain), *plain.values())

    specs = [SMEM if name in (N.starts, N.pad_len) else VMEM for name in in_names]
    out = call(
        body, list(args.values()), specs, list(outs.values()), list(scratch.values()), N.layer, 0
    )
    return dict(zip(outs, out))


def swapped(value):
    return lax.ppermute(value, "dir", [(0, 1), (1, 0)])


def rotated_to(value, steps, cross):
    count = lax.axis_size("seq")
    pairs = []
    for i in range(count):
        for c in range(2):
            pairs.append((i * 2 + c, (i + steps) % count * 2 + (1 - c if cross else c)))
    return lax.ppermute(value, ("seq", "dir"), pairs)


def around(value):
    count, place = lax.axis_size("seq"), lax.axis_index("seq")
    out = []
    for k in range(1, count):
        chosen = jnp.where(place + k < count, value[0], value[1])
        out.append(rotated_to(chosen, k, False))
    return jnp.stack(out)


def stage(z, have, phase, ins, outs, scratch=(), units=None):
    table = buffers(z)
    ins = [N.starts, N.pad_len] + list(ins)
    names = ins + list(outs) + list(scratch)
    units = [(row,) for row in range(z[N.rows])] if units is None else units

    def body(*refs):
        s = Refs(z, names, refs).where()
        for unit in units:
            phase(s, *unit)

    results = call(
        body, [have[name] for name in ins],
        [SMEM if name in (N.starts, N.pad_len) else VMEM for name in ins],
        [table[name] for name in outs],
        [pltpu.VMEM(table[name].shape, table[name].dtype) for name in scratch],
        phase.__name__,
    )
    have.update(zip(outs, results))


def apart(z, args):
    heads, width, conv_width, count = z[N.heads], z[N.width], z[N.conv_width], z[N.count]
    half, shard = z[N.half], z[N.shard]
    have = dict(args)
    core = lax.axis_index("dir")
    is_late = core == 1
    w_in, w_dt, w_out, tokens = (args[n] for n in (N.w_in, N.w_dt, N.w_out, N.tokens))
    pad_dt = jnp.zeros((shard, LANES - 2 * heads), BF)

    def columns(c):
        own = slice(c * width, (c + 1) * width)
        return (
            jnp.concatenate(
                [
                    w_in[:, 2 * width :][:, own], w_in[:, 4 * width :],
                    w_dt[:, c * heads : (c + 1) * heads],
                    w_dt[:, (2 + c) * heads : (3 + c) * heads], pad_dt,
                ],
                axis=1,
            ),
            jnp.concatenate([w_in[:, own], w_out[:, own]], axis=1),
        )

    def ordered(own, other, axis):
        return jnp.where(
            is_late, jnp.concatenate([other, own], axis=axis), jnp.concatenate([own, other], axis=axis)
        )

    first, latter = columns(0), columns(1)

    def gathered(i):
        keep = jnp.where(is_late, latter[i], first[i])
        give = swapped(jnp.where(is_late, first[i], latter[i]))
        return lax.all_gather(ordered(keep, give, 0), ("dp", "seq"), axis=0, tiled=True)

    have[N.w_pre], have[N.w_late] = gathered(0), gathered(1)
    have[N.tokens_other], have[N.cot_other] = swapped(tokens), swapped(args[N.cot])
    rim = tokens[:, half - HALO :]
    have[N.halo] = jnp.where(is_late, rotated_to(rim, 1, False), rotated_to(rim, 1, True))
    small = [N.conv_w_c, N.conv_b_c, N.bias_c, N.a_log_c, N.skip_c, N.gate_gain_c, N.gain_c]
    stage(
        z, have, prepare,
        [N.conv_w, N.conv_b, N.dt_bias, N.a_log, N.skip, N.gate_gain, N.norm_gain], small, units=[()],
    )
    stage(z, have, normalise, [N.gain_c, N.halo, N.tokens, N.tokens_other], [N.normed])
    stage(
        z, have, front, [N.normed, N.w_pre, N.conv_w_c, N.conv_b_c, N.bias_c, N.a_log_c],
        [N.pre, N.xbc, N.dsil, N.tab, N.cumt, N.v, N.local, N.decay, N.send], [N.pre_f],
    )
    have[N.received] = around(have[N.send])
    units = [(row, block) for row in range(z[N.rows]) for block in range(z[N.blocks])]

    def forward(s):
        for unit in units:
            inner(s, *unit)
        for row in range(s.rows):
            outer(s, row)

    stage(
        z, have, forward,
        [N.xbc, N.tab, N.cumt, N.v, N.received, N.local, N.decay, N.normed, N.w_late, N.cot,
         N.cot_other, N.skip_c, N.gate_gain_c],
        [N.y, N.inc, N.d_out, N.sums, N.z, N.dg], units=[()],
    )
    have[N.sums_other] = swapped(have[N.sums])

    def turned(s):
        for row in range(s.rows):
            turn(s, row)
            branches(s, row)
        late_grads(s)

    stage(
        z, have, turned,
        [N.sums, N.sums_other, N.xbc, N.y, N.z, N.dg, N.tab, N.decay, N.skip_c, N.gate_gain_c, N.d_out,
         N.normed, N.w_late],
        [N.gated, N.dy, N.dz, N.gate_sum, N.skip_sum, N.enter, N.back_send, N.branch, N.grad_out,
         N.grad_gate],
        units=[()],
    )
    have[N.back_received] = around(have[N.back_send])

    def backward(s):
        for row in range(s.rows):
            for block in range(s.blocks):
                for d in range(2):
                    at = block_rows(block)
                    s.y[row, d, at] = s.y_both[row, d, at]
                inner_back(s, row, block)
            back(s, row)
            d_norms(s, row)
        pre_grads(s)

    have[N.y_both] = have[N.y]
    stage(
        z, have, backward,
        [N.y_both, N.back_received, N.enter, N.decay, N.inc, N.xbc, N.tab, N.cumt, N.v, N.dy, N.dsil, N.pre,
         N.normed, N.dz, N.skip_c, N.a_log_c, N.conv_w_c, N.w_pre, N.w_late],
        [N.dn, N.d_all, N.grad_pre, N.sum_conv_w, N.sum_conv_b, N.small],
        [N.y, N.dbc, N.along, N.pad, N.pre_f], units=[()],
    )

    def give(values, first_row):
        return swapped(
            lax.dynamic_slice_in_dim(values, first_row + (1 - core) * half, half, axis=1)
        )

    edge = have[N.dn][:, :HALO]
    have[N.dn_other], have[N.branch_other] = give(have[N.dn], HALO), give(have[N.branch], 0)
    have[N.rims] = jnp.stack([rotated_to(edge, -1, True), rotated_to(edge, -1, False)])
    stage(
        z, have, finish,
        [N.tokens, N.cot, N.norm_gain, N.dn, N.dn_other, N.branch, N.branch_other, N.rims],
        [N.mixed, N.tokens_grad, N.gain_sum], [N.ds],
    )

    def placed(values):
        empty = jnp.zeros_like(values)
        return ordered(values, empty, -1)

    def sided(values):
        return jnp.concatenate([placed(values[:, :width]), values[:, width:]], axis=1)

    def reduced(name):
        value = lax.psum_scatter(have[name], ("dp", "seq"), scatter_dimension=0, tiled=True)
        own = lax.dynamic_slice_in_dim(value, core * shard, shard, axis=0)
        other = swapped(lax.dynamic_slice_in_dim(value, (1 - core) * shard, shard, axis=0))
        own, other = own.astype(F32), other.astype(F32)
        return jnp.where(is_late, other, own), jnp.where(is_late, own, other)

    def by_step(values):
        return jnp.concatenate(
            [placed(values[:, :heads]), placed(values[:, heads : 2 * heads])], axis=1
        )

    steps = by_step(have[N.small][:2])
    skips = placed(jnp.sum(have[N.skip_sum].reshape(1, heads, z[N.head_dim]), axis=-1))
    gain, all_conv_w, all_conv_b, steps, skips, gates = lax.psum(
        (
            have[N.gain_sum], sided(have[N.sum_conv_w]), sided(have[N.sum_conv_b]), steps, skips,
            placed(have[N.gate_sum]),
        ),
        ("dp", "seq", "dir"),
    )
    (pre_a, pre_b), (gate_a, gate_b), (out_a, out_b) = (
        reduced(name) for name in (N.grad_pre, N.grad_gate, N.grad_out)
    )
    last = conv_width
    return dict(
        mixed=have[N.mixed], tokens_grad=have[N.tokens_grad], o_norm=gain[0],
        o_in=jnp.concatenate(
            [
                gate_a, gate_b, pre_a[:, :width], pre_b[:, :width],
                pre_a[:, width:conv_width] + pre_b[:, width:conv_width],
            ],
            axis=1,
        ),
        o_dt=jnp.concatenate(
            [
                pre_a[:, last : last + heads], pre_b[:, last : last + heads],
                pre_a[:, last + heads : last + 2 * heads], pre_b[:, last + heads : last + 2 * heads],
            ],
            axis=1,
        ),
        o_conv_w=all_conv_w, o_conv_b=all_conv_b[0], o_bias=steps[0], o_alog=steps[1],
        o_skip=skips[0], o_gate=gates[0], o_out=jnp.concatenate([out_a, out_b], axis=1),
    )


def shards(tokens, starts, pad_len, norm_gain, w_in, w_dt, conv_w, conv_b, dt_bias, a_log, skip,
           gate_gain, w_out, cotangent):
    rows, half, model = tokens.shape
    span = 2 * half
    count = lax.axis_size("seq")
    inner_width = gate_gain.shape[0]
    heads = skip.shape[0] // 2
    width = inner_width // 2
    state = (conv_w.shape[1] - inner_width) // 4
    conv_width = width + 4 * state
    shard = w_in.shape[0]
    z = dict(
        rows=rows, half=half, model=model, span=span, count=count, row_len=span * count,
        blocks=span // BLOCK, inner_width=inner_width, heads=heads, head_dim=width // heads,
        width=width, state=state, conv_width=conv_width, conv_len=conv_w.shape[0],
        pre_width=conv_width + LANES, shard=shard,
    )
    args = dict(
        tokens=tokens, starts=starts, pad_len=pad_len, norm_gain=norm_gain, w_in=w_in, w_dt=w_dt,
        conv_w=conv_w, conv_b=conv_b, dt_bias=dt_bias, a_log=a_log, skip=skip, gate_gain=gate_gain,
        w_out=w_out, cot=cotangent,
    )
    direct = lax.axis_size("dp") == 4 and 2 * shard % 16 == 0 and model % (16 * shard) == 0
    out = together(z, args) if direct else apart(z, args)
    order = (
        N.mixed, N.tokens_grad, N.o_norm, N.o_in, N.o_dt, N.o_conv_w, N.o_conv_b, N.o_bias, N.o_alog,
        N.o_skip, N.o_gate, N.o_out,
    )
    return tuple(out[name] for name in order)


def solution(mesh):
    weight = P(("dp", "seq", "dir"), None)
    values = P("dp", ("seq", "dir"), None)
    return jax.shard_map(
        shards,
        mesh=mesh,
        in_specs=(
            values, P("dp", None), P("dp"), P(), weight, weight, P(), P(), P(), P(), P(), P(),
            weight, values,
        ),
        out_specs=(
            values, values, P(), weight, weight, P(), P(), P(), P(), P(), P(), weight,
        ),
        check_vma=False,
    )
```

```python
import jax
import jax.numpy as jnp
from jax import lax
from jax.experimental import pallas as pl
from jax.experimental.pallas import tpu as pltpu
from jax.sharding import PartitionSpec as P

BLOCK = 160
HALO = 16
LANES = 128
CARRY = 16
EPSILON = 1e-05
BF = jnp.bfloat16
F32 = jnp.float32
FAR = -1e30
VMEM_BYTES = 62 * 1024 * 1024


class Names:
    def __getattr__(self, name):
        return name


N = Names()


def dot(a, b):
    return lax.dot_general(a, b, (((1,), (0,)), ((), ())), preferred_element_type=F32)


def dot_nt(a, b):
    return lax.dot_general(a, b, (((1,), (1,)), ((), ())), preferred_element_type=F32)


def dot_tn(a, b):
    return lax.dot_general(a, b, (((0,), (0,)), ((), ())), preferred_element_type=F32)


def pieces(values, count):
    parts = []
    for _ in range(count - 1):
        part = values.astype(BF)
        parts.append(part)
        values = values - part.astype(F32)
    parts.append(values.astype(BF))
    return parts


def exact(op, values, ones, count):
    total = None
    for part in pieces(values, count):
        term = op(part, ones)
        total = term if total is None else total + term
    return total


def head_map(first, width, head_dim):
    lane = lax.broadcasted_iota(jnp.int32, (LANES, width), 0)
    head = lax.broadcasted_iota(jnp.int32, (LANES, width), 1) // head_dim
    return jnp.where(lane == head + first, 1.0, 0.0).astype(BF)


def head_maps(heads, width, head_dim):
    return head_map(0, width, head_dim), head_map(heads, width, head_dim)


def triangles():
    row = lax.broadcasted_iota(jnp.int32, (BLOCK, BLOCK), 0)
    col = lax.broadcasted_iota(jnp.int32, (BLOCK, BLOCK), 1)
    return (
        jnp.where(row >= col, 1.0, 0.0).astype(BF),
        jnp.where(row <= col, 1.0, 0.0).astype(BF),
    )


def doc_of(places, starts_ref, row):
    total = (starts_ref[row, 0] <= places).astype(jnp.int32)
    for j in range(1, starts_ref.shape[1]):
        total = total + (starts_ref[row, j] <= places).astype(jnp.int32)
    return total


def column_places(count, first):
    return lax.broadcasted_iota(jnp.int32, (count, 1), 0) + first


class Refs:
    def __init__(self, sizes, names, refs):
        self.__dict__.update(sizes)
        for name, ref in zip(names, refs):
            setattr(self, name, ref)

    def where(self):
        self.core = lax.axis_index("dir")
        self.place = lax.axis_index("seq")
        self.base = self.place * self.span
        return self


def block_rows(block):
    return slice(block * BLOCK, (block + 1) * BLOCK)


def prepare(s):
    late = s.core == 1
    width, heads = s.width, s.heads

    def mine(values, first, size):
        return jnp.where(
            late, values[:, first + size : first + 2 * size], values[:, first : first + size]
        )

    conv_w = s.conv_w[...]
    s.conv_w_c[:, 0:width] = mine(conv_w, 0, width)
    s.conv_w_c[:, width:] = conv_w[:, 2 * width :]
    conv_b = s.conv_b[...][None]
    s.conv_b_c[:, 0:width] = mine(conv_b, 0, width)
    s.conv_b_c[:, width:] = conv_b[:, 2 * width :]
    s.gate_gain_c[...] = mine(s.gate_gain[...][None], 0, width)
    s.gain_c[...] = s.norm_gain[...][None]
    source = lax.broadcasted_iota(jnp.int32, (4 * heads, LANES), 0)
    lane = lax.broadcasted_iota(jnp.int32, (4 * heads, LANES), 1)
    column = jnp.where(lane < heads, lane, lane + heads) + s.core * heads
    picked = jnp.where((source == column) & (lane < 2 * heads), 1.0, 0.0).astype(BF)
    for ref, out in ((s.dt_bias, s.bias_c), (s.a_log, s.a_log_c)):
        rows = jnp.broadcast_to(ref[...][None], (8, 4 * heads))
        out[...] = exact(dot, rows, picked, 3)[0:1]
    head = lax.broadcasted_iota(jnp.int32, (2 * heads, width), 0)
    channel = lax.broadcasted_iota(jnp.int32, (2 * heads, width), 1) // s.head_dim
    spread = jnp.where(head == channel + s.core * heads, 1.0, 0.0).astype(BF)
    rows = jnp.broadcast_to(s.skip[...][None], (8, 2 * heads))
    s.skip_c[...] = exact(dot, rows, spread, 3)[0:1]


def normalise(s, row):
    def norm(part):
        x = part.astype(F32)
        scale = lax.rsqrt(jnp.mean(x * x, axis=-1, keepdims=True) + EPSILON)
        return (x * scale * s.gain_c[...]).astype(BF)

    half = s.half
    s.normed[row, 0:HALO] = norm(s.halo[row])
    own = pl.multiple_of(HALO + s.core * half, HALO)
    other = pl.multiple_of(HALO + (1 - s.core) * half, HALO)
    s.normed[row, pl.ds(own, half)] = norm(s.tokens[row])
    s.normed[row, pl.ds(other, half)] = norm(s.tokens_other[row])


def front(s, row):
    heads, head_dim, state, width, span = s.heads, s.head_dim, s.state, s.width, s.span
    conv_width = s.conv_width
    projected = dot(s.normed[row], flat(s.w_pre))
    pre = projected[:, :conv_width].astype(BF)
    s.pre[row] = pre
    s.pre_f[...] = pre.astype(F32)
    raw = projected[HALO:, conv_width:].astype(BF).astype(F32)
    places = column_places(span, s.base)
    doc = doc_of(places, s.starts, row)
    valid = (places < s.row_len - s.pad_len[row]).astype(F32)
    summed = s.conv_b_c[...]
    for k in range(s.conv_len):
        back = s.conv_len - 1 - k
        ok = (doc_of(places - back, s.starts, row) == doc).astype(F32)
        summed = summed + s.pre_f[HALO - back : HALO - back + span] * s.conv_w_c[k : k + 1] * ok
    gate = 1.0 / (1.0 + jnp.exp(-summed))
    s.xbc[row] = (summed * gate * valid).astype(BF)
    s.dsil[row] = gate * (1.0 + summed * (1.0 - gate)) * valid
    map_f, map_b = head_maps(heads, width, head_dim)
    lower, upper = triangles()
    forward = lax.broadcasted_iota(jnp.int32, (1, LANES), 1) < heads
    shifted_raw = raw + s.bias_c[...]
    step = jnp.maximum(shifted_raw, 0.0) + jnp.log1p(jnp.exp(-jnp.abs(shifted_raw)))
    slope = 1.0 / (1.0 + jnp.exp(-shifted_raw))
    logs = -step * jnp.exp(s.a_log_c[...])
    s.tab[row, 0] = step
    s.tab[row, 4] = slope
    blocks = s.blocks
    for b in range(blocks):
        at = block_rows(b)
        step_b, logs_b, doc_b = step[at], logs[at], doc[at]
        cum = jnp.where(
            forward,
            exact(lambda p, m: dot(m, p), logs_b, lower, 3),
            exact(lambda p, m: dot(m, p), logs_b, upper, 3),
        )
        turned = jnp.where(
            lax.broadcasted_iota(jnp.int32, (LANES, 1), 0) < heads,
            exact(lambda p, m: dot_tn(p, m), logs_b, upper, 3),
            exact(lambda p, m: dot_tn(p, m), logs_b, lower, 3),
        )
        s.cumt[row, b] = turned[: s.cumt.shape[2]]
        first_place = s.base + b * BLOCK
        end_f = doc_of(first_place + BLOCK - 1, s.starts, row)
        end_b = doc_of(first_place, s.starts, row)
        near_f = doc_of(first_place - 1, s.starts, row)
        near_b = doc_of(first_place + BLOCK, s.starts, row)
        final = jnp.where(forward, cum[BLOCK - 1 : BLOCK], cum[0:1])
        tail = jnp.exp(final - cum) * (doc_b == jnp.where(forward, end_f, end_b)).astype(F32)
        reach = jnp.exp(cum) * (doc_b == jnp.where(forward, near_f, near_b)).astype(F32)
        s.tab[row, 1, at] = cum
        s.tab[row, 2, at] = tail
        s.tab[row, 3, at] = reach
        decay = jnp.broadcast_to(
            jnp.where(forward, reach[BLOCK - 1 : BLOCK], reach[0:1]), (8, LANES)
        )
        u = s.xbc[row, at, :width].astype(F32)
        for d, head_ones in ((0, map_f), (1, map_b)):
            s.v[row, d, at] = (exact(dot, step_b, head_ones, 2) * u).astype(BF)
            tailed = (exact(dot, tail * step_b, head_ones, 2) * u).astype(BF)
            b_mat = s.xbc[row, at, width + d * state : width + (d + 1) * state]
            s.local[row, b, d] = dot_tn(b_mat, tailed)
            s.decay[row, b, d] = exact(dot, decay, head_ones, 3)


def flat(ref, columns=slice(None)):
    if len(ref.shape) == 2:
        return ref[:, columns]
    value = ref[:, :, columns]
    return value.reshape(value.shape[0] * value.shape[1], value.shape[2])


def carried_rows(rate):
    coarse = rate.astype(BF)
    fine = (rate - coarse.astype(F32)).astype(BF)
    row = lax.broadcasted_iota(jnp.int32, (CARRY, rate.shape[1]), 0)
    return jnp.where(
        row == 0, coarse.astype(F32), jnp.where(row == 1, fine.astype(F32), 0.0)
    ).astype(BF)


def compose(received, place, count, state, up):
    total, rate = None, None
    for k in range(1, count):
        part = received[(k - 1) if up else (count - k - 1)]
        there = (place - k >= 0) if up else (place + k < count)
        there = there.astype(F32)
        term = part[0:state].astype(F32) * there
        total = term if total is None else total + rate * term
        hop = part[state : state + 1].astype(F32) + part[state + 1 : state + 2].astype(F32)
        rate = hop if rate is None else rate * hop
    return total


def run_through(s, row, d, now, terms, out, upward):
    for b in range(s.blocks) if upward else reversed(range(s.blocks)):
        here = terms[row, b, d]
        out[row, b, d] = now
        now = s.decay[row, b, d, 0:1] * now + here
    return now


def summarise(s, row, terms, send, downward):
    for d in range(2):
        upward = (d == 0) != downward
        total, rate = None, None
        for b in range(s.blocks) if upward else reversed(range(s.blocks)):
            own = s.decay[row, b, d, 0:1]
            total = terms[row, b, d] if total is None else own * total + terms[row, b, d]
            rate = own if rate is None else rate * own
        send[0 if upward else 1, row, 0 : s.state] = total.astype(BF)
        send[0 if upward else 1, row, s.state :] = carried_rows(rate)


def sent_states(s, row):
    summarise(s, row, s.local, s.send, False)


def back_states(s, row):
    summarise(s, row, s.enter, s.back_send, True)


def received_states(s, row):
    parts = [s.received[k, row] for k in range(s.count - 1)]
    for d in range(2):
        now = compose(parts, s.place, s.count, s.state, d == 0)
        run_through(s, row, d, now, s.local, s.inc, d == 0)


def returned_states(s, row):
    parts = [s.back_received[k, row] for k in range(s.count - 1)]
    for d in range(2):
        now = compose(parts, s.place, s.count, s.state, d == 1)
        run_through(s, row, d, now, s.enter, s.leaving, d == 1)


def pair_masks(first_place, starts, row):
    rows = lax.broadcasted_iota(jnp.int32, (BLOCK, BLOCK), 0)
    cols = lax.broadcasted_iota(jnp.int32, (BLOCK, BLOCK), 1)
    doc_rows = doc_of(column_places(BLOCK, first_place), starts, row)
    row_places = lax.broadcasted_iota(jnp.int32, (1, BLOCK), 1) + first_place
    same = doc_rows == doc_of(row_places, starts, row)
    return (
        jnp.where(same & (rows > cols), 0.0, FAR),
        jnp.where(same & (rows < cols), 0.0, FAR),
    )


def inner(s, row, block):
    heads, head_dim, state, width = s.heads, s.head_dim, s.state, s.width
    rows = block_rows(block)
    masks = pair_masks(s.base + block * BLOCK, s.starts, row)
    low_half = lax.broadcasted_iota(jnp.int32, (1, LANES), 1) < head_dim
    for d in range(2):
        b_mat = s.xbc[row, rows, width + d * state : width + (d + 1) * state]
        c_mat = s.xbc[row, rows, width + (2 + d) * state : width + (3 + d) * state]
        scores = dot_nt(c_mat, b_mat)
        for pair in range(heads // 2):
            at = slice(pair * LANES, (pair + 1) * LANES)
            values = s.v[row, d, rows, at]
            outs = []
            for h in (2 * pair, 2 * pair + 1):
                lane = d * heads + h
                gap = s.tab[row, 1, rows, lane : lane + 1] - s.cumt[row, block, lane : lane + 1, :]
                mixing = (jnp.exp(gap + masks[d]) * scores).astype(BF)
                outs.append(dot(mixing, values))
            s.y[row, d, rows, at] = jnp.where(low_half, outs[0], outs[1])


def gates(s, row):
    half, width = s.half, s.width
    s.z[row] = dot(s.normed[row, HALO:], flat(s.w_late, slice(0, width)))
    for cot, core in ((s.cot, s.core), (s.cot_other, 1 - s.core)):
        places = column_places(half, s.base + core * half)
        valid = (places < s.row_len - s.pad_len[row]).astype(F32)
        s.d_out[row, pl.ds(pl.multiple_of(core * half, HALO), half)] = (
            cot[row].astype(F32) * valid
        ).astype(BF)
    s.dg[row] = dot(s.d_out[row], flat(s.w_late, slice(width, None)))


def outer(s, row):
    heads, head_dim, state, width = s.heads, s.head_dim, s.state, s.width
    maps = head_maps(heads, width, head_dim)
    for b in range(s.blocks):
        at = block_rows(b)
        for d in range(2):
            c_mat = s.xbc[row, at, width + (2 + d) * state : width + (3 + d) * state]
            raw = dot(c_mat, s.inc[row, b, d].astype(BF))
            s.y[row, d, at] = s.y[row, d, at] + exact(dot, s.tab[row, 3, at], maps[d], 2) * raw
    u = s.xbc[row, :, :width].astype(F32)
    y = s.y[row, 0] + s.skip_c[...] * u + s.y[row, 1]
    z = s.z[row]
    v = y * z * (1.0 / (1.0 + jnp.exp(-z)))
    lane = lax.broadcasted_iota(jnp.int32, (1, LANES), 1)
    squares = jnp.sum(v * v, axis=-1, keepdims=True)
    against = jnp.sum(s.dg[row] * s.gate_gain_c[...] * v, axis=-1, keepdims=True)
    s.sums[row] = jnp.where(lane == 0, squares, jnp.where(lane == 1, against, 0.0))


def turn(s, row):
    heads, head_dim, state, width = s.heads, s.head_dim, s.state, s.width
    blocks = s.blocks
    total = s.sums[row] + s.sums_other[row]
    scale = lax.rsqrt(total[:, 0:1] * (1.0 / s.inner_width) + EPSILON)
    against = total[:, 1:2]
    u = s.xbc[row, :, :width].astype(F32)
    y = s.y[row, 0] + s.skip_c[...] * u + s.y[row, 1]
    z = s.z[row]
    gate = 1.0 / (1.0 + jnp.exp(-z))
    silu = z * gate
    unit = y * silu * scale
    s.gated[row] = (unit * s.gate_gain_c[...]).astype(BF)
    d_gated = s.dg[row]
    d_v = scale * (d_gated * s.gate_gain_c[...]) - unit * (
        scale * scale * against * (1.0 / s.inner_width)
    )
    dy = (d_v * silu).astype(BF)
    s.dy[row] = dy
    s.dz[row] = (d_v * y * gate * (1.0 + z * (1.0 - gate))).astype(BF)
    dy_f = dy.astype(F32)
    gate_term = jnp.sum(d_gated * unit, axis=0, keepdims=True)
    skip_term = jnp.sum(dy_f * u, axis=0, keepdims=True)
    if row:
        gate_term, skip_term = gate_term + s.gate_sum[...], skip_term + s.skip_sum[...]
    s.gate_sum[...] = gate_term
    s.skip_sum[...] = skip_term
    maps = head_maps(heads, width, head_dim)
    for d in range(2):
        for b in range(blocks):
            at = block_rows(b)
            c_mat = s.xbc[row, at, width + (2 + d) * state : width + (3 + d) * state]
            weighed = (exact(dot, s.tab[row, 3, at], maps[d], 2) * dy_f[at]).astype(BF)
            s.enter[row, b, d] = dot_tn(c_mat, weighed)


def branches(s, row):
    s.branch[row] = dot_nt(s.gated[row], flat(s.w_late, slice(s.width, None))).astype(BF)


def weight_grad(s, out, lefts, rights):
    step = 8 * 2 * s.shard if len(out.shape) == 3 else s.model
    for first in range(0, s.model, step):
        total = None
        for left, right in zip(lefts, rights):
            term = dot_tn(left(slice(first, first + step)), right())
            total = term if total is None else total + term
        if len(out.shape) == 2:
            out[...] = total.astype(BF)
        else:
            per = out.shape[1]
            out[first // per : (first + step) // per] = (
                total.astype(BF).reshape(step // per, per, out.shape[2])
            )


def late_grads(s):
    rows = range(s.rows)
    weight_grad(
        s, s.grad_out,
        [lambda at, r=r: s.d_out[r, :, at] for r in rows], [lambda r=r: s.gated[r] for r in rows],
    )
    weight_grad(
        s, s.grad_gate,
        [lambda at, r=r: s.normed[r, HALO:, at] for r in rows], [lambda r=r: s.dz[r] for r in rows],
    )


def pre_grads(s):
    rows = range(s.rows)
    weight_grad(
        s, s.grad_pre,
        [lambda at, r=r: s.normed[r, :, at] for r in rows], [lambda r=r: s.d_all[r] for r in rows],
    )


def inner_back(s, row, block):
    heads, head_dim, state, width = s.heads, s.head_dim, s.state, s.width
    rows = block_rows(block)
    masks = pair_masks(s.base + block * BLOCK, s.starts, row)
    low_half = lax.broadcasted_iota(jnp.int32, (1, LANES), 1) < head_dim
    maps = head_maps(heads, width, head_dim)
    dy_all = s.dy[row, rows].astype(F32)
    along = None
    for d in range(2):
        term = exact(dot_nt, dy_all * s.y[row, d, rows], maps[d], 2)
        along = term if along is None else along + term
        b_mat = s.xbc[row, rows, width + d * state : width + (d + 1) * state]
        c_mat = s.xbc[row, rows, width + (2 + d) * state : width + (3 + d) * state]
        scores = dot_nt(c_mat, b_mat)
        d_scores = jnp.zeros((BLOCK, BLOCK), F32)
        for pair in range(heads // 2):
            at = slice(pair * LANES, (pair + 1) * LANES)
            values = s.v[row, d, rows, at]
            grads = s.dy[row, rows, at]
            outs = []
            for h in (2 * pair, 2 * pair + 1):
                lane = d * heads + h
                gap = s.tab[row, 1, rows, lane : lane + 1] - s.cumt[row, block, lane : lane + 1, :]
                spread = jnp.exp(gap + masks[d])
                mixing = (spread * scores).astype(BF)
                mine = low_half if h % 2 == 0 else ~low_half
                d_mixing = dot_nt(jnp.where(mine, grads, jnp.zeros_like(grads)), values)
                d_scores = d_scores + d_mixing * spread
                outs.append(dot_tn(mixing, grads))
            s.y[row, d, rows, at] = jnp.where(low_half, outs[0], outs[1])
        d_scores = d_scores.astype(BF)
        weighed = (exact(dot, s.tab[row, 3, rows], maps[d], 2) * dy_all).astype(BF)
        d_c = dot(d_scores, b_mat) + dot_nt(weighed, s.inc[row, block, d].astype(BF))
        d_b = dot_tn(d_scores, c_mat)
        s.dbc[row, rows, d * state : (d + 1) * state] = d_b
        s.dbc[row, rows, (2 + d) * state : (3 + d) * state] = d_c
    s.along[row, rows] = along


def back(s, row):
    heads, head_dim, state, width, span = s.heads, s.head_dim, s.state, s.width, s.span
    conv_width, conv_len, blocks = s.conv_width, s.conv_len, s.blocks
    maps = head_maps(heads, width, head_dim)
    lower, upper = triangles()
    forward = lax.broadcasted_iota(jnp.int32, (1, LANES), 1) < heads
    rate = jnp.exp(s.a_log_c[...])
    rows = lax.broadcasted_iota(jnp.int32, (BLOCK, 1), 0)
    if row == 0:
        s.pad[0:HALO] = jnp.zeros((HALO, conv_width), F32)
        s.pad[HALO + span :] = jnp.zeros((s.pad.shape[0] - HALO - span, conv_width), F32)
    d_bias, d_rate = None, None
    for b in range(blocks):
        at = block_rows(b)
        inside = slice(HALO + b * BLOCK, HALO + (b + 1) * BLOCK)
        u = s.xbc[row, at, :width].astype(F32)
        step, tail, slope = s.tab[row, 0, at], s.tab[row, 2, at], s.tab[row, 4, at]
        reach = s.tab[row, 3, at]
        d_u = s.skip_c[...] * s.dy[row, at].astype(F32)
        through, direct, ended = None, None, None
        d_bc = []
        for d in range(2):
            leave = s.leaving[row, b, d].astype(BF)
            b_mat = s.xbc[row, at, width + d * state : width + (d + 1) * state]
            v_d = s.v[row, d, at].astype(F32)
            dv_state = exact(dot, tail, maps[d], 2) * dot(b_mat, leave)
            dv_all = s.y[row, d, at] + dv_state
            step_wide = exact(dot, step, maps[d], 2)
            tailed = (exact(dot, tail * step, maps[d], 2) * u).astype(BF)
            d_bc.append(dot_nt(tailed, leave))
            d_u = d_u + step_wide * dv_all
            row_id = lax.broadcasted_iota(jnp.int32, (8, width), 0)
            sides = jnp.where(
                row_id == 0,
                jnp.sum(v_d * dv_state, axis=0, keepdims=True),
                jnp.sum(s.leaving[row, b, d] * s.inc[row, b, d], axis=0, keepdims=True),
            )
            terms = (
                exact(dot_nt, v_d * dv_all, maps[d], 2),
                exact(dot_nt, u * dv_all, maps[d], 2),
                exact(dot_nt, sides, maps[d], 3),
            )
            if d == 0:
                through, direct, ended = terms
            else:
                through, direct, ended = through + terms[0], direct + terms[1], ended + terms[2]
        final = jnp.where(forward, reach[BLOCK - 1 : BLOCK], reach[0:1])
        at_end = jnp.where(
            forward, (rows == BLOCK - 1).astype(F32), (rows == 0).astype(F32)
        )
        d_cum = s.along[row, at] - through + at_end * (ended[0:1] + ended[1:2] * final)
        d_logs = jnp.where(
            forward,
            exact(lambda p, m: dot(m, p), d_cum, upper, 3),
            exact(lambda p, m: dot(m, p), d_cum, lower, 3),
        )
        d_raw = (direct - rate * d_logs) * slope
        s.d_all[row, inside, conv_width:] = d_raw.astype(BF)
        bias_term = jnp.sum(d_raw, axis=0, keepdims=True)
        rate_term = jnp.sum(-step * rate * d_logs, axis=0, keepdims=True)
        d_bias = bias_term if d_bias is None else d_bias + bias_term
        d_rate = rate_term if d_rate is None else d_rate + rate_term
        s.pad[inside, 0:width] = d_u * s.dsil[row, at, 0:width]
        half_bc = jnp.concatenate(d_bc, axis=1)
        s.pad[inside, width : width + 2 * state] = (
            s.dbc[row, at, : 2 * state] + half_bc
        ) * s.dsil[row, at, width : width + 2 * state]
        s.pad[inside, width + 2 * state :] = (
            s.dbc[row, at, 2 * state :] * s.dsil[row, at, width + 2 * state :]
        )
    s.d_all[row, 0:HALO, conv_width:] = jnp.zeros((HALO, LANES), BF)
    s.pre_f[...] = s.pre[row].astype(F32)
    places = column_places(span, s.base)
    doc = doc_of(places, s.starts, row)
    outs = s.pad[HALO : HALO + span]
    conv_b_term = jnp.sum(outs, axis=0, keepdims=True)
    ext_places = column_places(HALO + span, s.base - HALO)
    ext_doc = doc_of(ext_places, s.starts, row)
    d_pre = None
    conv_w_terms = []
    for k in range(conv_len):
        ahead = conv_len - 1 - k
        ok = (doc_of(places - ahead, s.starts, row) == doc).astype(F32)
        conv_w_terms.append(
            jnp.sum(
                outs * ok * s.pre_f[HALO - ahead : HALO - ahead + span], axis=0, keepdims=True
            )
        )
        ok_ext = (doc_of(ext_places + ahead, s.starts, row) == ext_doc).astype(F32)
        term = s.pad[ahead : ahead + HALO + span] * ok_ext * s.conv_w_c[k : k + 1]
        d_pre = term if d_pre is None else d_pre + term
    s.d_all[row, :, 0:conv_width] = d_pre.astype(BF)
    conv_w_term = jnp.concatenate(conv_w_terms, axis=0)
    small_term = jnp.concatenate([d_bias, d_rate], axis=0)
    if row:
        conv_w_term = conv_w_term + s.sum_conv_w[...]
        conv_b_term = conv_b_term + s.sum_conv_b[...]
        small_term = small_term + s.small[0:2]
    s.sum_conv_w[...] = conv_w_term
    s.sum_conv_b[...] = conv_b_term
    s.small[0:2] = small_term


def d_norms(s, row):
    dn = dot_nt(s.d_all[row], flat(s.w_pre))
    s.dn[row, 0:HALO] = dn[0:HALO].astype(BF)
    s.dn[row, HALO:] = (
        dn[HALO:] + dot_nt(s.dz[row], flat(s.w_late, slice(0, s.width)))
    ).astype(BF)


def finish(s, row):
    half = s.half
    x = s.tokens[row].astype(F32)
    places = column_places(half, s.base + s.core * half)
    valid = (places < s.row_len - s.pad_len[row]).astype(F32)
    keep = pl.ds(pl.multiple_of(s.core * half, HALO), half)
    s.mixed[row] = (
        x + valid * (s.branch[row, keep].astype(F32) + s.branch_other[row].astype(F32))
    ).astype(BF)
    keep = pl.ds(pl.multiple_of(HALO + s.core * half, HALO), half)
    s.ds[...] = s.dn[row, keep].astype(F32) + s.dn_other[row].astype(F32)
    takes = ((s.core == 1) & (s.place + 1 < s.count)).astype(F32)
    s.ds[half - HALO :] += takes * (s.rims[0, row].astype(F32) + s.rims[1, row].astype(F32))
    d_normed = s.ds[...]
    scale = lax.rsqrt(jnp.mean(x * x, axis=-1, keepdims=True) + EPSILON)
    weighed = d_normed * s.norm_gain[...][None]
    along = jnp.mean(weighed * x, axis=-1, keepdims=True)
    dx = scale * weighed - x * (scale * scale * scale * along)
    s.tokens_grad[row] = (s.cot[row].astype(F32) + dx).astype(BF)
    term = jnp.sum(d_normed * x * scale, axis=0, keepdims=True)
    s.gain_sum[...] = term if row == 0 else s.gain_sum[...] + term


MESH = pl.DeviceIdType.MESH


def remote(src, dst, send_sem, recv_sem, device):
    return pltpu.make_async_remote_copy(
        src_ref=src, dst_ref=dst, send_sem=send_sem, recv_sem=recv_sem, device_id=device,
        device_id_type=MESH,
    )


class Sender:
    def __init__(self, send_sems, recv_sems):
        self.send_sems, self.recv_sems = send_sems, recv_sems
        self.sent = 0
        self.slots = 0
        self.pending = []

    def slot(self):
        self.slots += 1
        return self.slots - 1

    def send(self, src, dst, slot, device):
        copy = remote(src, dst, self.send_sems.at[self.sent], self.recv_sems.at[slot], device)
        self.sent += 1
        copy.start()
        self.pending.append(copy)

    def arrive(self, dst, slot, device):
        remote(dst, dst, self.send_sems.at[0], self.recv_sems.at[slot], device).wait_recv()

    def drain(self):
        for copy in self.pending:
            copy.wait_send()
        self.pending = []


class Place:
    def __init__(self, count):
        self.dp, self.seq, self.dir = (lax.axis_index(a) for a in ("dp", "seq", "dir"))
        self.count = count
        self.side = self.dp + 1 - 2 * (self.dp % 2)
        self.below = (self.dp + 2) % 4
        self.across = 3 - self.dp
        self.me = (self.dp, self.seq, self.dir)
        self.sibling = (self.dp, self.seq, 1 - self.dir)
        self.by_x = (self.side, self.seq, self.dir)
        self.by_y = (self.below, self.seq, self.dir)

    def along(self, k, crossed=False):
        core = 1 - self.dir if crossed else self.dir
        return (self.dp, (self.seq + k + self.count) % self.count, core)

    def at(self, k):
        return (self.seq + k + self.count) % self.count

    def chip(self, dp, k=0):
        return dp * self.count + self.at(k)

    def meet(self):
        barrier = pltpu.get_barrier_semaphore()
        others = [self.sibling, self.by_x, self.by_y]
        others += [self.along(k) for k in range(1, self.count)]
        others += [self.along(1, True), self.along(-1, True)]
        for device in others:
            pl.semaphore_signal(barrier, inc=1, device_id=device, device_id_type=MESH)
        pl.semaphore_wait(barrier, len(others))


class Spread:
    def __init__(self, place, sender, slab, cut):
        self.place, self.sender, self.slab, self.cut = place, sender, slab, cut
        count = place.count
        self.z = [None] + [sender.slot() for _ in range(1, count)]
        self.x, self.y, self.xd, self.yd = (
            [sender.slot() for _ in range(count)] for _ in range(4)
        )

    def start_z(self):
        here, to = self.place, self.sender
        spot = self.slab.at[here.chip(here.dp)]
        for k in range(1, here.count):
            to.send(spot, spot, self.z[k], here.along(k))

    def start_xy(self):
        here, to = self.place, self.sender
        spot = self.slab.at[here.chip(here.dp)]
        to.send(spot, spot, self.x[0], here.by_x)
        to.send(spot, spot, self.y[0], here.by_y)

    def relay(self, k):
        here, to = self.place, self.sender
        spot = self.slab.at[here.chip(here.dp, -k)]
        to.arrive(spot, self.z[k], here.along(-k))
        to.send(spot, spot, self.x[k], here.by_x)
        to.send(spot, spot, self.y[k], here.by_y)

    def cross(self, k):
        here, to = self.place, self.sender
        from_x = self.slab.at[here.chip(here.side, -k)]
        to.arrive(from_x, self.x[k], here.by_x)
        part = from_x.at[:, : self.cut]
        to.send(part, part, self.yd[k], here.by_y)
        from_y = self.slab.at[here.chip(here.below, -k)]
        to.arrive(from_y, self.y[k], here.by_y)
        part = from_y.at[:, self.cut :]
        to.send(part, part, self.xd[k], here.by_x)

    def end(self, k):
        here, to = self.place, self.sender
        spot = self.slab.at[here.chip(here.across, -k)]
        to.arrive(spot.at[:, : self.cut], self.yd[k], here.by_y)
        to.arrive(spot.at[:, self.cut :], self.xd[k], here.by_x)


class Reduce:
    def __init__(self, place, sender, grad, cut, first, second, third, out_second, out_third, total):
        self.place, self.sender, self.grad, self.cut = place, sender, grad, cut
        self.first, self.second, self.third = first, second, third
        self.out_second, self.out_third, self.total = out_second, out_third, total
        count = place.count
        self.one = [[[sender.slot() for _ in range(count)] for _ in range(2)] for _ in range(2)]
        self.two = [[sender.slot() for _ in range(count)] for _ in range(2)]
        self.three = [None] + [sender.slot() for _ in range(1, count)]
        self.sides = (slice(0, cut), slice(cut, grad.shape[2]))

    def start(self, k):
        here, to = self.place, self.sender
        for side, device, targets in (
            (0, here.by_x, (here.side, here.across)),
            (1, here.by_y, (here.below, here.across)),
        ):
            at = self.sides[side]
            for q in (1, 0):
                to.send(
                    self.grad.at[here.chip(targets[q], k), :, at],
                    self.first.at[q, k, :, at],
                    self.one[side][q][k], device,
                )

    def pass_on(self, k):
        here, to = self.place, self.sender
        for side, came, device, target in (
            (0, here.by_x, here.by_y, here.below),
            (1, here.by_y, here.by_x, here.side),
        ):
            at = self.sides[side]
            to.arrive(self.first.at[1, k, :, at], self.one[side][1][k], came)
            self.out_second[k, :, at] = (
                self.grad[here.chip(target, k), :, at].astype(F32)
                + self.first[1, k, :, at].astype(F32)
            ).astype(BF)
            to.send(self.out_second.at[k, :, at], self.second.at[k, :, at], self.two[side][k], device)

    def along(self, k):
        here, to = self.place, self.sender
        for side, came, then in ((0, here.by_x, here.by_y), (1, here.by_y, here.by_x)):
            at = self.sides[side]
            to.arrive(self.first.at[0, k, :, at], self.one[side][0][k], came)
            to.arrive(self.second.at[k, :, at], self.two[side][k], then)
            summed = (
                self.grad[here.chip(here.dp, k), :, at].astype(F32)
                + self.first[0, k, :, at].astype(F32)
                + self.second[k, :, at].astype(F32)
            )
            if k == 0:
                self.total[:, at] = summed
            else:
                self.out_third[k - 1, :, at] = summed.astype(BF)
        if k:
            to.send(self.out_third.at[k - 1], self.third.at[k - 1], self.three[k], here.along(k))

    def end(self):
        here, to = self.place, self.sender
        for k in range(1, here.count):
            to.arrive(self.third.at[k - 1], self.three[k], here.along(-k))
            self.total[...] += self.third[k - 1].astype(F32)


def fill_columns(s, core, pre, late):
    width, heads, conv_width = s.width, s.heads, s.conv_width
    late_side = core == 1
    pick = lambda ref, at: jnp.where(
        late_side, ref[:, at + width : at + 2 * width], ref[:, at : at + width]
    )
    source = lax.broadcasted_iota(jnp.int32, (4 * heads, LANES), 0)
    lane = lax.broadcasted_iota(jnp.int32, (4 * heads, LANES), 1)
    column = jnp.where(lane < heads, lane, lane + heads) + core * heads
    ones = jnp.where((source == column) & (lane < 2 * heads), 1.0, 0.0).astype(BF)
    pre[:, 0:width] = pick(s.w_in, 2 * width).astype(pre.dtype)
    pre[:, width:conv_width] = s.w_in[:, 4 * width :].astype(pre.dtype)
    pre[:, conv_width:] = dot(s.w_dt[...], ones).astype(pre.dtype)
    late[:, 0:width] = pick(s.w_in, 0).astype(late.dtype)
    late[:, width:] = pick(s.w_out, 0).astype(late.dtype)


class Chain:
    def __init__(self, s, place, sender, upward, terms, out, landed, leaves):
        self.s, self.place, self.sender, self.upward = s, place, sender, upward
        self.terms, self.out, self.landed, self.leaves = terms, out, landed, leaves
        self.slots = [[sender.slot() for _ in range(2)] for _ in range(s.rows)]
        self.sems = [[sender.sent + 2 * row + d for d in range(2)] for row in range(s.rows)]
        sender.sent += 2 * s.rows

    def turn(self, d):
        here = self.place
        return here.seq if self.upward[d] else here.count - 1 - here.seq

    def copy(self, row, d):
        to = self.sender
        return remote(
            self.leaves.at[row, d], self.landed.at[row, d], to.send_sems.at[self.sems[row][d]],
            to.recv_sems.at[self.slots[row][d]], self.place.along(1 if self.upward[d] else -1),
        )

    def step(self, row, at):
        for d in range(2):
            @pl.when(self.turn(d) == at)
            def _():
                if at:
                    self.sender.arrive(
                        self.landed.at[row, d], self.slots[row][d],
                        self.place.along(-1 if self.upward[d] else 1),
                    )
                now = self.landed[row, d].astype(F32)
                now = run_through(self.s, row, d, now, self.terms, self.out, self.upward[d])
                if at < self.place.count - 1:
                    self.leaves[row, d] = now.astype(BF)
                    self.copy(row, d).start()

    def steps(self, level, last=None):
        for now in range(level, (level if last is None else last) + 1):
            for row in range(self.s.rows):
                if 0 <= now - row < self.place.count:
                    self.step(row, now - row)

    def drain(self):
        for row in range(self.s.rows):
            for d in range(2):
                @pl.when(self.turn(d) < self.place.count - 1)
                def _():
                    self.copy(row, d).wait_send()


def everything(sizes, names, *refs):
    s = Refs(sizes, names, refs).where()
    count, rows, half, width, heads = s.count, s.rows, s.half, s.width, s.heads
    conv_width, model, shard = s.conv_width, s.model, s.shard
    here = Place(count)
    to = Sender(s.send_sems, s.recv_sems)
    late_core = here.dir == 1
    fill_columns(s, 1 - here.dir, s.give_pre, s.give_late)
    s.chain_in[...] = jnp.zeros_like(s.chain_in)
    s.back_chain_in[...] = jnp.zeros_like(s.back_chain_in)
    here.meet()

    pair = [to.slot() for _ in range(5)]
    to.send(s.give_pre, s.got_pre, pair[0], here.sibling)
    to.send(s.tokens, s.tokens_other, pair[2], here.sibling)
    rim = s.tokens.at[:, pl.ds(half - HALO, HALO)]
    first_rim, second_rim = to.sent, to.sent + 1
    to.sent += 2

    def rims_out():
        return [
            remote(rim, s.halo, s.send_sems.at[sem], s.recv_sems.at[pair[4]], here.along(1, crossed))
            for sem, crossed in ((first_rim, False), (second_rim, True))
        ]

    @pl.when(late_core)
    def _():
        for copy in rims_out():
            copy.start()

    to.send(s.give_late, s.got_late, pair[1], here.sibling)
    to.send(s.cot, s.cot_other, pair[3], here.sibling)
    fill_columns(s, here.dir, s.pre_mine, s.late_mine)

    def joined(own, got):
        other = got[...].astype(F32)
        own = own[...]
        return jnp.where(
            late_core,
            jnp.concatenate([other, own], axis=0),
            jnp.concatenate([own, other], axis=0),
        ).astype(BF)

    me = here.chip(here.dp)
    spread_pre = Spread(here, to, s.w_pre, s.cuts[0])
    spread_late = Spread(here, to, s.w_late, s.cuts[1])
    to.arrive(s.got_pre, pair[0], here.sibling)
    s.w_pre[me] = joined(s.pre_mine, s.got_pre)
    spread_pre.start_xy()
    spread_pre.start_z()
    to.arrive(s.got_late, pair[1], here.sibling)
    s.w_late[me] = joined(s.late_mine, s.got_late)
    prepare(s)
    to.arrive(s.tokens_other, pair[2], here.sibling)
    to.arrive(s.halo, pair[4], here.along(-1))
    spread_pre.cross(0)
    spread_pre.relay(1)
    for row in range(rows):
        normalise(s, row)
    spread_pre.cross(1)
    for k in range(2, count):
        spread_pre.relay(k)
    spread_late.start_z()
    for k in range(2, count):
        spread_pre.cross(k)
    spread_late.start_xy()
    for k in range(count):
        spread_pre.end(k)

    states = Chain(s, here, to, (True, False), s.local, s.inc, s.chain_in, s.chain_out)
    front(s, 0)
    states.steps(0)
    spread_late.relay(1)
    spread_late.cross(0)
    for row in range(1, rows):
        front(s, row)
        states.steps(row)
    spread_late.relay(2)
    spread_late.relay(3)
    units = [(row, block) for row in range(rows) for block in range(s.blocks)]
    for i, (row, block) in enumerate(units):
        inner(s, row, block)
        if i == 0:
            spread_late.cross(1)
            spread_late.cross(2)
        if block == s.blocks - 1:
            states.steps(rows + row)
        if i == 2:
            spread_late.cross(3)
    for k in range(count):
        spread_late.end(k)
    to.arrive(s.cot_other, pair[3], here.sibling)
    for row in range(rows):
        gates(s, row)
    states.steps(2 * rows, rows + count)
    sum_slots = [to.slot() for _ in range(rows)]
    for row in range(rows):
        outer(s, row)
        to.send(s.sums.at[row], s.sums_other.at[row], sum_slots[row], here.sibling)

    back_chain = Chain(
        s, here, to, (False, True), s.enter, s.leaving, s.back_chain_in, s.back_chain_out
    )
    for row in range(rows):
        to.arrive(s.sums_other.at[row], sum_slots[row], here.sibling)
        turn(s, row)
        back_chain.steps(row)
    grads = (s.grad_pre, s.grad_gate, s.grad_out)
    reduces = [Reduce(here, to, g, cut, *work) for g, cut, work in zip(grads, s.grad_cuts, s.works)]
    reduce_pre, reduce_late = reduces[0], reduces[1:]
    late_grads(s)
    order = list(range(1, count)) + [0]
    for k in order:
        for reduce in reduce_late:
            reduce.start(k)
    back_chain.steps(rows)
    for row in range(rows):
        branches(s, row)
    branch_slot, dn_slot, rim_own, rim_cross = (to.slot() for _ in range(4))
    give = pl.multiple_of((1 - here.dir) * half, HALO)
    to.send(s.branch.at[:, pl.ds(give, half)], s.branch_other, branch_slot, here.sibling)
    for i, (row, block) in enumerate(units):
        inner_back(s, row, block)
        if i == 0:
            back_chain.steps(rows + 1)
        if i == 1:
            back_chain.steps(rows + 2, rows + count)
        if i < count:
            for reduce in reduce_late:
                reduce.pass_on(order[i])
    back(s, 0)
    for k in order[:2]:
        for reduce in reduce_late:
            reduce.along(k)
    for row in range(1, rows):
        back(s, row)
    for k in order[2:]:
        for reduce in reduce_late:
            reduce.along(k)
    pre_grads(s)
    for k in order:
        reduce_pre.start(k)
    for row in range(rows):
        d_norms(s, row)
    to.send(s.dn.at[:, pl.ds(HALO + give, half)], s.dn_other, dn_slot, here.sibling)
    edge = s.dn.at[:, pl.ds(0, HALO)]
    rim_sem = to.sent
    to.sent += 1

    def edge_out(core):
        return remote(
            edge, s.rims.at[core], s.send_sems.at[rim_sem],
            s.recv_sems.at[(rim_cross, rim_own)[core]], here.along(-1, core == 0),
        )

    for core in range(2):
        @pl.when(here.dir == core)
        def _():
            edge_out(core).start()

    for reduce in reduce_late:
        reduce.end()
    to.arrive(s.branch_other, branch_slot, here.sibling)
    to.arrive(s.dn_other, dn_slot, here.sibling)

    @pl.when(late_core)
    def _():
        to.arrive(s.rims.at[1], rim_own, here.along(1))
        to.arrive(s.rims.at[0], rim_cross, here.along(1, True))

    @pl.when(here.dir == 0)
    def _():
        s.rims[...] = jnp.zeros_like(s.rims)

    for row in range(rows):
        finish(s, row)
    side = conv_width - width
    s.v_own[0:4] = s.sum_conv_w[...]
    s.v_own[4:5] = s.sum_conv_b[...]
    s.v_own[5:6] = jnp.concatenate([s.gate_sum[...], s.small[0:1], s.small[1:2]], axis=1)
    s.v_own[6:7] = jnp.concatenate([s.skip_sum[...], jnp.zeros((1, side), F32)], axis=1)
    s.v_own[7:8] = jnp.concatenate([s.gain_sum[...], jnp.zeros((1, side), F32)], axis=1)
    v_slots = [to.slot() for _ in range(2 + count)]
    to.send(s.v_own, s.v_x.at[0], v_slots[0], here.by_x)
    for k in order:
        reduce_pre.pass_on(k)
    to.arrive(s.v_x.at[0], v_slots[0], here.by_x)
    s.v_x[1] = s.v_own[...] + s.v_x[0]
    to.send(s.v_x.at[1], s.v_y.at[0], v_slots[1], here.by_y)
    for k in order:
        reduce_pre.along(k)
    to.arrive(s.v_y.at[0], v_slots[1], here.by_y)
    s.v_y[1] = s.v_x[1] + s.v_y[0]
    for k in range(1, count):
        to.send(s.v_y.at[1], s.v_z.at[k - 1], v_slots[1 + k], here.along(k))
    swaps = []
    others = s.others
    back_rows = pl.ds(pl.multiple_of((1 - here.dir) * shard, 8), shard)
    own_rows = pl.ds(pl.multiple_of(here.dir * shard, 8), shard)
    for i in (1, 2, 0):
        slot = to.slot()
        if i == 0:
            reduce_pre.end()
        to.send(reduces[i].total.at[back_rows], others[i], slot, here.sibling)
        swaps.append((i, slot))
    total = s.v_y[1]
    for k in range(1, count):
        to.arrive(s.v_z.at[k - 1], v_slots[1 + k], here.along(-k))
        total = total + s.v_z[k - 1]
    s.v_x[0] = total
    to.send(s.v_x.at[0], s.v_other, v_slots[1 + count], here.sibling)
    parts = {}
    for i, slot in swaps:
        to.arrive(others[i], slot, here.sibling)
        own, got = reduces[i].total[own_rows], others[i][...]
        parts[i] = (jnp.where(late_core, got, own), jnp.where(late_core, own, got))
    (pre_a, pre_b), (gate_a, gate_b), (out_a, out_b) = (parts[i] for i in range(3))
    s.o_in[:, 0:width] = gate_a
    s.o_in[:, width : 2 * width] = gate_b
    s.o_in[:, 2 * width : 3 * width] = pre_a[:, :width]
    s.o_in[:, 3 * width : 4 * width] = pre_b[:, :width]
    s.o_in[:, 4 * width :] = pre_a[:, width:conv_width] + pre_b[:, width:conv_width]
    s.o_out[:, 0:width] = out_a
    s.o_out[:, width:] = out_b
    lane = lax.broadcasted_iota(jnp.int32, (LANES, 4 * heads), 0)
    column = lax.broadcasted_iota(jnp.int32, (LANES, 4 * heads), 1)
    first_lane = jnp.where(lane < heads, lane, jnp.where(lane < 2 * heads, lane + heads, -1))
    picks = [
        jnp.where((first_lane >= 0) & (column == first_lane + side_of * heads), 1.0, 0.0).astype(BF)
        for side_of in range(2)
    ]
    by_step = lambda a, b: exact(dot, a, picks[0], 3) + exact(dot, b, picks[1], 3)
    s.o_dt[...] = by_step(pre_a[:, conv_width:], pre_b[:, conv_width:])
    to.arrive(s.v_other, v_slots[1 + count], here.sibling)
    got = s.v_other[...]
    v_a, v_b = jnp.where(late_core, got, total), jnp.where(late_core, total, got)
    both = v_a + v_b
    s.o_conv_w[:, 0:width] = v_a[0:4, :width]
    s.o_conv_w[:, width : 2 * width] = v_b[0:4, :width]
    s.o_conv_w[:, 2 * width :] = both[0:4, width:]
    s.o_conv_b[...] = jnp.concatenate([v_a[4:5, :width], v_b[4:5, :width], both[4:5, width:]], axis=1)[0]
    s.o_gate[...] = jnp.concatenate([v_a[5:6, :width], v_b[5:6, :width]], axis=1)[0]
    steps = by_step(
        jnp.concatenate([v_a[5:6, width : width + LANES], v_a[5:6, width + LANES : width + 2 * LANES]] * 4, axis=0),
        jnp.concatenate([v_b[5:6, width : width + LANES], v_b[5:6, width + LANES : width + 2 * LANES]] * 4, axis=0),
    )
    s.o_bias[...] = steps[0]
    s.o_alog[...] = steps[1]
    head = lax.broadcasted_iota(jnp.int32, (width, 2 * heads), 1)
    channel = lax.broadcasted_iota(jnp.int32, (width, 2 * heads), 0) // s.head_dim
    skips = None
    for side_of, v_side in ((0, v_a), (1, v_b)):
        ones = jnp.where(head == channel + side_of * heads, 1.0, 0.0).astype(BF)
        term = exact(dot, jnp.broadcast_to(v_side[6:7, :width], (8, width)), ones, 3)
        skips = term if skips is None else skips + term
    s.o_skip[...] = skips[0]
    s.o_norm[...] = both[7:8, :model][0]
    to.drain()
    states.drain()
    back_chain.drain()

    @pl.when(late_core)
    def _():
        for copy in rims_out():
            copy.wait_send()

    for core in range(2):
        @pl.when(here.dir == core)
        def _():
            edge_out(core).wait_send()


SMEM = pl.BlockSpec(memory_space=pltpu.SMEM)
VMEM = pl.BlockSpec(memory_space=pltpu.VMEM)


def call(body, ins, specs, out_shapes, scratch, name, collective_id=None):
    return pl.pallas_call(
        body,
        out_shape=out_shapes,
        in_specs=specs,
        out_specs=[VMEM] * len(out_shapes),
        scratch_shapes=scratch,
        compiler_params=pltpu.CompilerParams(
            vmem_limit_bytes=VMEM_BYTES, collective_id=collective_id,
            has_side_effects=collective_id is not None,
        ),
        name=name,
    )(*ins)


def shape_of(dtype, *dims):
    return jax.ShapeDtypeStruct(dims, dtype)


def buffers(z):
    rows, span, half, model, width, state = z[N.rows], z[N.span], z[N.half], z[N.model], z[N.width], z[N.state]
    blocks, conv_width, pre_width, count = z[N.blocks], z[N.conv_width], z[N.pre_width], z[N.count]
    ext, conv_len, heads = HALO + span, z[N.conv_len], z[N.heads]
    packed = 2 * heads + (-2 * heads) % 8
    carried = (state + CARRY, width)
    table = dict(
        conv_w_c=(F32, conv_len, conv_width), conv_b_c=(F32, 1, conv_width), bias_c=(F32, 1, LANES),
        a_log_c=(F32, 1, LANES), skip_c=(F32, 1, width), gate_gain_c=(F32, 1, width),
        gain_c=(F32, 1, model), halo=(BF, rows, HALO, model), tokens_other=(BF, rows, half, model),
        cot_other=(BF, rows, half, model), normed=(BF, rows, ext, model),
        pre=(BF, rows, ext, conv_width), pre_f=(F32, ext, conv_width),
        xbc=(BF, rows, span, conv_width), dsil=(F32, rows, span, conv_width),
        tab=(F32, rows, 5, span, LANES), cumt=(F32, rows, blocks, packed, BLOCK),
        v=(BF, rows, 2, span, width), local=(F32, rows, blocks, 2, state, width),
        decay=(F32, rows, blocks, 2, 8, width), send=(BF, 2, rows) + carried,
        received=(BF, count - 1, rows) + carried, y=(F32, rows, 2, span, width),
        inc=(F32, rows, blocks, 2, state, width), sums=(F32, rows, span, LANES),
        sums_other=(F32, rows, span, LANES), z=(F32, rows, span, width), dg=(F32, rows, span, width),
        d_out=(BF, rows, span, model), gated=(BF, rows, span, width), dy=(BF, rows, span, width),
        dz=(BF, rows, span, width), enter=(F32, rows, blocks, 2, state, width),
        back_send=(BF, 2, rows) + carried, back_received=(BF, count - 1, rows) + carried,
        leaving=(F32, rows, blocks, 2, state, width), branch=(BF, rows, span, model), grad_out=(BF, model, width), grad_gate=(BF, model, width),
        gate_sum=(F32, 1, width), skip_sum=(F32, 1, width), dbc=(F32, rows, span, 4 * state),
        along=(F32, rows, span, LANES), pad=(F32, ext + 8, conv_width),
        d_all=(BF, rows, ext, pre_width), grad_pre=(BF, model, pre_width),
        sum_conv_w=(F32, conv_len, conv_width), sum_conv_b=(F32, 1, conv_width), small=(F32, 8, LANES),
        dn=(BF, rows, ext, model), branch_other=(BF, rows, half, model),
        dn_other=(BF, rows, half, model), rims=(BF, 2, rows, HALO, model), ds=(F32, half, model),
        gain_sum=(F32, 1, model), mixed=(BF, rows, half, model), tokens_grad=(BF, rows, half, model),
    )
    return {name: shape_of(*shape) for name, shape in table.items()}


def together(z, args):
    count, shard, width, conv_width = z[N.count], z[N.shard], z[N.width], z[N.conv_width]
    pre_width, model, rows, half, heads = z[N.pre_width], z[N.model], z[N.rows], z[N.half], z[N.heads]
    chips, pair = 4 * count, 2 * shard
    table = buffers(z)
    for name in (N.grad_out, N.grad_gate, N.grad_pre):
        table[name] = shape_of(BF, chips, pair, table[name].shape[1])
    outs = dict(
        mixed=table.pop(N.mixed), tokens_grad=table.pop(N.tokens_grad), o_norm=shape_of(F32, model),
        o_in=shape_of(F32, shard, 4 * width + 4 * z[N.state]), o_dt=shape_of(F32, shard, 4 * heads),
        o_conv_w=shape_of(F32, z[N.conv_len], conv_width + width),
        o_conv_b=shape_of(F32, conv_width + width), o_bias=shape_of(F32, 4 * heads),
        o_alog=shape_of(F32, 4 * heads), o_skip=shape_of(F32, 2 * heads),
        o_gate=shape_of(F32, 2 * width), o_out=shape_of(F32, shard, 2 * width),
    )
    for name in (N.send, N.received, N.back_send, N.back_received):
        table.pop(name)
    aliases = {N.inc: N.local, N.leaving: N.enter}
    scratch = {
        name: pltpu.VMEM(value.shape, value.dtype)
        for name, value in table.items() if name not in aliases
    }
    scratch.update(
        w_pre=pltpu.VMEM((chips, pair, pre_width), BF), w_late=pltpu.VMEM((chips, pair, 2 * width), BF),
        give_pre=pltpu.VMEM((shard, pre_width), BF), give_late=pltpu.VMEM((shard, 2 * width), BF),
        got_pre=pltpu.VMEM((shard, pre_width), BF), got_late=pltpu.VMEM((shard, 2 * width), BF),
        pre_mine=pltpu.VMEM((shard, pre_width), F32), late_mine=pltpu.VMEM((shard, 2 * width), F32),
        **{
            name: pltpu.VMEM((rows, 2, z[N.state], width), BF)
            for name in (N.chain_in, N.chain_out, N.back_chain_in, N.back_chain_out)
        },
        v_own=pltpu.VMEM((8, conv_width), F32), v_x=pltpu.VMEM((2, 8, conv_width), F32),
        v_y=pltpu.VMEM((2, 8, conv_width), F32), v_z=pltpu.VMEM((count - 1, 8, conv_width), F32),
        v_other=pltpu.VMEM((8, conv_width), F32),
    )
    widths = dict(pre=pre_width, gate=width, out=width)
    work_names = []
    for name, size in widths.items():
        scratch[name, -1] = pltpu.VMEM((shard, size), F32)
        for i, shape in enumerate(
            ((2, count, pair), (count, pair), (count - 1, pair), (count, pair), (count - 1, pair))
        ):
            scratch[name, i] = pltpu.VMEM(shape + (size,), BF)
        scratch[name, 5] = pltpu.VMEM((pair, size), F32)
        work_names.append([(name, i) for i in range(6)])
    copies = 64 + 16 * count + 3 * (7 * count) + 16
    scratch[N.send_sems] = pltpu.SemaphoreType.DMA((copies,))
    scratch[N.recv_sems] = pltpu.SemaphoreType.DMA((copies,))
    in_names = list(args)
    names = in_names + list(outs) + list(scratch)
    cut = pre_width // 256 * 128 + 128

    def body(*refs):
        sizes = dict(z, cuts=(cut, width), grad_cuts=(cut, width // 2, width // 2))
        by_name = dict(zip(names, refs))
        for name, of in aliases.items():
            by_name[name] = by_name[of]
        sizes[N.works] = [[by_name[n] for n in group] for group in work_names]
        sizes[N.others] = [by_name[name, -1] for name in widths]
        plain = {name: ref for name, ref in by_name.items() if isinstance(name, str)}
        everything(sizes, list(plain), *plain.values())

    specs = [SMEM if name in (N.starts, N.pad_len) else VMEM for name in in_names]
    out = call(
        body, list(args.values()), specs, list(outs.values()), list(scratch.values()), N.layer, 0
    )
    return dict(zip(outs, delivered(out)))


def delivered(arrays):
    count = len(arrays)

    def body(*refs):
        for source, target in zip(refs[:count], refs[count:]):
            target[...] = source[...]

    return call(
        body, arrays, [VMEM] * count, [shape_of(a.dtype, *a.shape) for a in arrays], (), N.deliver
    )


def swapped(value):
    return lax.ppermute(value, "dir", [(0, 1), (1, 0)])


def rotated_to(value, steps, cross):
    count = lax.axis_size("seq")
    pairs = []
    for i in range(count):
        for c in range(2):
            pairs.append((i * 2 + c, (i + steps) % count * 2 + (1 - c if cross else c)))
    return lax.ppermute(value, ("seq", "dir"), pairs)


def around(value):
    count, place = lax.axis_size("seq"), lax.axis_index("seq")
    out = []
    for k in range(1, count):
        chosen = jnp.where(place + k < count, value[0], value[1])
        out.append(rotated_to(chosen, k, False))
    return jnp.stack(out)


def stage(z, have, phase, ins, outs, scratch=(), units=None):
    table = buffers(z)
    ins = [N.starts, N.pad_len] + list(ins)
    names = ins + list(outs) + list(scratch)
    units = [(row,) for row in range(z[N.rows])] if units is None else units

    def body(*refs):
        s = Refs(z, names, refs).where()
        for unit in units:
            phase(s, *unit)

    results = call(
        body, [have[name] for name in ins],
        [SMEM if name in (N.starts, N.pad_len) else VMEM for name in ins],
        [table[name] for name in outs],
        [pltpu.VMEM(table[name].shape, table[name].dtype) for name in scratch],
        phase.__name__,
    )
    have.update(zip(outs, results))


def apart(z, args):
    heads, width, conv_width, count = z[N.heads], z[N.width], z[N.conv_width], z[N.count]
    half, shard = z[N.half], z[N.shard]
    have = dict(args)
    core = lax.axis_index("dir")
    is_late = core == 1
    w_in, w_dt, w_out, tokens = (args[n] for n in (N.w_in, N.w_dt, N.w_out, N.tokens))
    pad_dt = jnp.zeros((shard, LANES - 2 * heads), BF)

    def columns(c):
        own = slice(c * width, (c + 1) * width)
        return (
            jnp.concatenate(
                [
                    w_in[:, 2 * width :][:, own], w_in[:, 4 * width :],
                    w_dt[:, c * heads : (c + 1) * heads],
                    w_dt[:, (2 + c) * heads : (3 + c) * heads], pad_dt,
                ],
                axis=1,
            ),
            jnp.concatenate([w_in[:, own], w_out[:, own]], axis=1),
        )

    def ordered(own, other, axis):
        return jnp.where(
            is_late, jnp.concatenate([other, own], axis=axis), jnp.concatenate([own, other], axis=axis)
        )

    first, latter = columns(0), columns(1)

    def gathered(i):
        keep = jnp.where(is_late, latter[i], first[i])
        give = swapped(jnp.where(is_late, first[i], latter[i]))
        return lax.all_gather(ordered(keep, give, 0), ("dp", "seq"), axis=0, tiled=True)

    have[N.w_pre], have[N.w_late] = gathered(0), gathered(1)
    have[N.tokens_other], have[N.cot_other] = swapped(tokens), swapped(args[N.cot])
    rim = tokens[:, half - HALO :]
    have[N.halo] = jnp.where(is_late, rotated_to(rim, 1, False), rotated_to(rim, 1, True))
    small = [N.conv_w_c, N.conv_b_c, N.bias_c, N.a_log_c, N.skip_c, N.gate_gain_c, N.gain_c]
    stage(
        z, have, prepare,
        [N.conv_w, N.conv_b, N.dt_bias, N.a_log, N.skip, N.gate_gain, N.norm_gain], small, units=[()],
    )
    stage(z, have, normalise, [N.gain_c, N.halo, N.tokens, N.tokens_other], [N.normed])
    stage(
        z, have, front, [N.normed, N.w_pre, N.conv_w_c, N.conv_b_c, N.bias_c, N.a_log_c],
        [N.pre, N.xbc, N.dsil, N.tab, N.cumt, N.v, N.local, N.decay], [N.pre_f],
    )
    stage(z, have, sent_states, [N.local, N.decay], [N.send])
    have[N.received] = around(have[N.send])
    stage(z, have, received_states, [N.received, N.local, N.decay], [N.inc])
    units = [(row, block) for row in range(z[N.rows]) for block in range(z[N.blocks])]

    def forward(s):
        for unit in units:
            inner(s, *unit)
        for row in range(s.rows):
            gates(s, row)
            outer(s, row)

    stage(
        z, have, forward,
        [N.xbc, N.tab, N.cumt, N.v, N.inc, N.normed, N.w_late, N.cot,
         N.cot_other, N.skip_c, N.gate_gain_c],
        [N.y, N.d_out, N.sums, N.z, N.dg], units=[()],
    )
    have[N.sums_other] = swapped(have[N.sums])

    def turned(s):
        for row in range(s.rows):
            turn(s, row)
            branches(s, row)
        late_grads(s)

    stage(
        z, have, turned,
        [N.sums, N.sums_other, N.xbc, N.y, N.z, N.dg, N.tab, N.decay, N.skip_c, N.gate_gain_c, N.d_out,
         N.normed, N.w_late],
        [N.gated, N.dy, N.dz, N.gate_sum, N.skip_sum, N.enter, N.branch, N.grad_out,
         N.grad_gate],
        units=[()],
    )
    stage(z, have, back_states, [N.enter, N.decay], [N.back_send])
    have[N.back_received] = around(have[N.back_send])
    stage(z, have, returned_states, [N.back_received, N.enter, N.decay], [N.leaving])

    def backward(s):
        for row in range(s.rows):
            for block in range(s.blocks):
                for d in range(2):
                    at = block_rows(block)
                    s.y[row, d, at] = s.y_both[row, d, at]
                inner_back(s, row, block)
            back(s, row)
            d_norms(s, row)
        pre_grads(s)

    have[N.y_both] = have[N.y]
    stage(
        z, have, backward,
        [N.y_both, N.leaving, N.inc, N.xbc, N.tab, N.cumt, N.v, N.dy, N.dsil, N.pre,
         N.normed, N.dz, N.skip_c, N.a_log_c, N.conv_w_c, N.w_pre, N.w_late],
        [N.dn, N.d_all, N.grad_pre, N.sum_conv_w, N.sum_conv_b, N.small],
        [N.y, N.dbc, N.along, N.pad, N.pre_f], units=[()],
    )

    def give(values, first_row):
        return swapped(
            lax.dynamic_slice_in_dim(values, first_row + (1 - core) * half, half, axis=1)
        )

    edge = have[N.dn][:, :HALO]
    have[N.dn_other], have[N.branch_other] = give(have[N.dn], HALO), give(have[N.branch], 0)
    have[N.rims] = jnp.stack([rotated_to(edge, -1, True), rotated_to(edge, -1, False)])
    stage(
        z, have, finish,
        [N.tokens, N.cot, N.norm_gain, N.dn, N.dn_other, N.branch, N.branch_other, N.rims],
        [N.mixed, N.tokens_grad, N.gain_sum], [N.ds],
    )

    def placed(values):
        empty = jnp.zeros_like(values)
        return ordered(values, empty, -1)

    def sided(values):
        return jnp.concatenate([placed(values[:, :width]), values[:, width:]], axis=1)

    def reduced(name):
        value = lax.psum_scatter(have[name], ("dp", "seq"), scatter_dimension=0, tiled=True)
        own = lax.dynamic_slice_in_dim(value, core * shard, shard, axis=0)
        other = swapped(lax.dynamic_slice_in_dim(value, (1 - core) * shard, shard, axis=0))
        own, other = own.astype(F32), other.astype(F32)
        return jnp.where(is_late, other, own), jnp.where(is_late, own, other)

    def by_step(values):
        return jnp.concatenate(
            [placed(values[:, :heads]), placed(values[:, heads : 2 * heads])], axis=1
        )

    steps = by_step(have[N.small][:2])
    skips = placed(jnp.sum(have[N.skip_sum].reshape(1, heads, z[N.head_dim]), axis=-1))
    gain, all_conv_w, all_conv_b, steps, skips, gate_all = lax.psum(
        (
            have[N.gain_sum], sided(have[N.sum_conv_w]), sided(have[N.sum_conv_b]), steps, skips,
            placed(have[N.gate_sum]),
        ),
        ("dp", "seq", "dir"),
    )
    (pre_a, pre_b), (gate_a, gate_b), (out_a, out_b) = (
        reduced(name) for name in (N.grad_pre, N.grad_gate, N.grad_out)
    )
    last = conv_width
    return dict(
        mixed=have[N.mixed], tokens_grad=have[N.tokens_grad], o_norm=gain[0],
        o_in=jnp.concatenate(
            [
                gate_a, gate_b, pre_a[:, :width], pre_b[:, :width],
                pre_a[:, width:conv_width] + pre_b[:, width:conv_width],
            ],
            axis=1,
        ),
        o_dt=jnp.concatenate(
            [
                pre_a[:, last : last + heads], pre_b[:, last : last + heads],
                pre_a[:, last + heads : last + 2 * heads], pre_b[:, last + heads : last + 2 * heads],
            ],
            axis=1,
        ),
        o_conv_w=all_conv_w, o_conv_b=all_conv_b[0], o_bias=steps[0], o_alog=steps[1],
        o_skip=skips[0], o_gate=gate_all[0], o_out=jnp.concatenate([out_a, out_b], axis=1),
    )


def shards(tokens, starts, pad_len, norm_gain, w_in, w_dt, conv_w, conv_b, dt_bias, a_log, skip,
           gate_gain, w_out, cotangent):
    rows, half, model = tokens.shape
    span = 2 * half
    count = lax.axis_size("seq")
    inner_width = gate_gain.shape[0]
    heads = skip.shape[0] // 2
    width = inner_width // 2
    state = (conv_w.shape[1] - inner_width) // 4
    conv_width = width + 4 * state
    shard = w_in.shape[0]
    z = dict(
        rows=rows, half=half, model=model, span=span, count=count, row_len=span * count,
        blocks=span // BLOCK, inner_width=inner_width, heads=heads, head_dim=width // heads,
        width=width, state=state, conv_width=conv_width, conv_len=conv_w.shape[0],
        pre_width=conv_width + LANES, shard=shard,
    )
    args = dict(
        tokens=tokens, starts=starts, pad_len=pad_len, norm_gain=norm_gain, w_in=w_in, w_dt=w_dt,
        conv_w=conv_w, conv_b=conv_b, dt_bias=dt_bias, a_log=a_log, skip=skip, gate_gain=gate_gain,
        w_out=w_out, cot=cotangent,
    )
    direct = lax.axis_size("dp") == 4 and 2 * shard % 16 == 0 and model % (16 * shard) == 0
    out = together(z, args) if direct else apart(z, args)
    order = (
        N.mixed, N.tokens_grad, N.o_norm, N.o_in, N.o_dt, N.o_conv_w, N.o_conv_b, N.o_bias, N.o_alog,
        N.o_skip, N.o_gate, N.o_out,
    )
    return tuple(out[name] for name in order)


def solution(mesh):
    weight = P(("dp", "seq", "dir"), None)
    values = P("dp", ("seq", "dir"), None)
    return jax.shard_map(
        shards,
        mesh=mesh,
        in_specs=(
            values, P("dp", None), P("dp"), P(), weight, weight, P(), P(), P(), P(), P(), P(),
            weight, values,
        ),
        out_specs=(
            values, values, P(), weight, weight, P(), P(), P(), P(), P(), P(), weight,
        ),
        check_vma=False,
    )
```

```python
import jax
import jax.numpy as jnp
from jax import lax
from jax.experimental import pallas as pl
from jax.experimental.pallas import tpu as pltpu
from jax.sharding import PartitionSpec as P

BLOCK = 160
HALO = 16
LANES = 128
CARRY = 16
EPSILON = 1e-05
BF = jnp.bfloat16
F32 = jnp.float32
FAR = -1e30
LOG2E = 1.4426950408889634
VMEM_BYTES = 62 * 1024 * 1024


class Names:
    def __getattr__(self, name):
        return name


N = Names()


def dot(a, b):
    return lax.dot_general(a, b, (((1,), (0,)), ((), ())), preferred_element_type=F32)


def dot_nt(a, b):
    return lax.dot_general(a, b, (((1,), (1,)), ((), ())), preferred_element_type=F32)


def dot_tn(a, b):
    return lax.dot_general(a, b, (((0,), (0,)), ((), ())), preferred_element_type=F32)


def pieces(values, count):
    parts = []
    for _ in range(count - 1):
        part = values.astype(BF)
        parts.append(part)
        values = values - part.astype(F32)
    parts.append(values.astype(BF))
    return parts


def exact(op, values, ones, count):
    total = None
    for part in pieces(values, count):
        term = op(part, ones)
        total = term if total is None else total + term
    return total


def head_map(first, width, head_dim):
    lane = lax.broadcasted_iota(jnp.int32, (LANES, width), 0)
    head = lax.broadcasted_iota(jnp.int32, (LANES, width), 1) // head_dim
    return jnp.where(lane == head + first, 1.0, 0.0).astype(BF)


def expand(s, values, d):
    return dot(jnp.concatenate(pieces(values, 2), axis=1), s.maps[d])


def reduce(s, values, d, count):
    return exact(dot_nt, values, s.maps[d, 0:LANES], count)


def running(s, values):
    parts = pieces(values, 3)
    blocks = range(values.shape[0] // BLOCK)
    wide = jnp.concatenate([part[block_rows(b)] for b in blocks for part in parts], axis=1)
    both = dot(s.tri[...], wide)
    result = []
    for b in blocks:
        first = 3 * b * LANES
        total = (
            both[:, first : first + LANES]
            + both[:, first + LANES : first + 2 * LANES]
            + both[:, first + 2 * LANES : first + 3 * LANES]
        )
        result.append((total[:BLOCK], total[BLOCK:]))
    return result


def doc_of(places, starts_ref, row):
    total = (starts_ref[row, 0] <= places).astype(jnp.int32)
    for j in range(1, starts_ref.shape[1]):
        total = total + (starts_ref[row, j] <= places).astype(jnp.int32)
    return total


def column_places(count, first):
    return lax.broadcasted_iota(jnp.int32, (count, 1), 0) + first


class Refs:
    def __init__(self, sizes, names, refs):
        self.__dict__.update(sizes)
        for name, ref in zip(names, refs):
            setattr(self, name, ref)

    def where(self):
        self.core = lax.axis_index("dir")
        self.place = lax.axis_index("seq")
        self.base = self.place * self.span
        return self


def block_rows(block):
    return slice(block * BLOCK, (block + 1) * BLOCK)


def prepare(s):
    late = s.core == 1
    width, heads = s.width, s.heads

    def mine(values, first, size):
        return jnp.where(
            late, values[:, first + size : first + 2 * size], values[:, first : first + size]
        )

    conv_w = s.conv_w[...]
    s.conv_w_c[:, 0:width] = mine(conv_w, 0, width)
    s.conv_w_c[:, width:] = conv_w[:, 2 * width :]
    conv_b = s.conv_b[...][None]
    s.conv_b_c[:, 0:width] = mine(conv_b, 0, width)
    s.conv_b_c[:, width:] = conv_b[:, 2 * width :]
    s.gate_gain_c[...] = mine(s.gate_gain[...][None], 0, width)
    s.gain_c[...] = s.norm_gain[...][None]
    source = lax.broadcasted_iota(jnp.int32, (4 * heads, LANES), 0)
    lane = lax.broadcasted_iota(jnp.int32, (4 * heads, LANES), 1)
    column = jnp.where(lane < heads, lane, lane + heads) + s.core * heads
    picked = jnp.where((source == column) & (lane < 2 * heads), 1.0, 0.0).astype(BF)
    for ref, out in ((s.dt_bias, s.bias_c), (s.a_log, s.a_log_c)):
        rows = jnp.broadcast_to(ref[...][None], (8, 4 * heads))
        out[...] = exact(dot, rows, picked, 3)[0:1]
    head = lax.broadcasted_iota(jnp.int32, (2 * heads, width), 0)
    channel = lax.broadcasted_iota(jnp.int32, (2 * heads, width), 1) // s.head_dim
    spread = jnp.where(head == channel + s.core * heads, 1.0, 0.0).astype(BF)
    rows = jnp.broadcast_to(s.skip[...][None], (8, 2 * heads))
    s.skip_c[...] = exact(dot, rows, spread, 3)[0:1]
    for d in range(2):
        ones = head_map(d * heads, width, s.head_dim)
        s.maps[d, 0:LANES] = ones
        s.maps[d, LANES:] = ones
    row = lax.broadcasted_iota(jnp.int32, (BLOCK, BLOCK), 0)
    col = lax.broadcasted_iota(jnp.int32, (BLOCK, BLOCK), 1)
    s.tri[0:BLOCK] = jnp.where(row >= col, 1.0, 0.0).astype(BF)
    s.tri[BLOCK:] = jnp.where(row <= col, 1.0, 0.0).astype(BF)


def normalise(s, row):
    def norm(part):
        x = part.astype(F32)
        scale = lax.rsqrt(jnp.mean(x * x, axis=-1, keepdims=True) + EPSILON)
        return (x * scale * s.gain_c[...]).astype(BF)

    half = s.half
    s.normed[row, 0:HALO] = norm(s.halo[row])
    own = pl.multiple_of(HALO + s.core * half, HALO)
    other = pl.multiple_of(HALO + (1 - s.core) * half, HALO)
    s.normed[row, pl.ds(own, half)] = norm(s.tokens[row])
    s.normed[row, pl.ds(other, half)] = norm(s.tokens_other[row])


def front(s, row):
    heads, head_dim, state, width, span = s.heads, s.head_dim, s.state, s.width, s.span
    conv_width = s.conv_width
    projected = dot(s.normed[row], flat(s.w_pre))
    pre = projected[:, :conv_width].astype(BF)
    s.pre[row] = pre
    s.pre_f[...] = pre.astype(F32)
    raw = projected[HALO:, conv_width:].astype(BF).astype(F32)
    places = column_places(span, s.base)
    doc = doc_of(places, s.starts, row)
    valid = (places < s.row_len - s.pad_len[row]).astype(F32)
    summed = s.conv_b_c[...]
    for k in range(s.conv_len):
        back = s.conv_len - 1 - k
        ok = (doc_of(places - back, s.starts, row) == doc).astype(F32)
        summed = summed + s.pre_f[HALO - back : HALO - back + span] * s.conv_w_c[k : k + 1] * ok
    gate = 1.0 / (1.0 + jnp.exp(-summed))
    s.xbc[row] = (summed * gate * valid).astype(BF)
    s.dsil[row] = gate * (1.0 + summed * (1.0 - gate)) * valid
    forward = lax.broadcasted_iota(jnp.int32, (1, LANES), 1) < heads
    shifted_raw = raw + s.bias_c[...]
    step = jnp.maximum(shifted_raw, 0.0) + jnp.log1p(jnp.exp(-jnp.abs(shifted_raw)))
    slope = 1.0 / (1.0 + jnp.exp(-shifted_raw))
    logs = -step * jnp.exp(s.a_log_c[...])
    s.tab[row, 0] = step
    s.tab[row, 4] = slope
    blocks = s.blocks
    sums = running(s, logs)
    for b in range(blocks):
        at = block_rows(b)
        doc_b = doc[at]
        cum = jnp.where(forward, sums[b][0], sums[b][1])
        first_place = s.base + b * BLOCK
        end_f = doc_of(first_place + BLOCK - 1, s.starts, row)
        end_b = doc_of(first_place, s.starts, row)
        near_f = doc_of(first_place - 1, s.starts, row)
        near_b = doc_of(first_place + BLOCK, s.starts, row)
        final = jnp.where(forward, cum[BLOCK - 1 : BLOCK], cum[0:1])
        tail = jnp.exp(final - cum) * (doc_b == jnp.where(forward, end_f, end_b)).astype(F32)
        reach = jnp.exp(cum) * (doc_b == jnp.where(forward, near_f, near_b)).astype(F32)
        scaled = cum * LOG2E
        s.cumt[row, b] = scaled.T[: s.cumt.shape[2]]
        s.tab[row, 1, at] = scaled
        s.tab[row, 2, at] = tail
        s.tab[row, 3, at] = reach
        decay = jnp.broadcast_to(
            jnp.where(forward, reach[BLOCK - 1 : BLOCK], reach[0:1]), (8, LANES)
        )
        for d in range(2):
            s.decay[row, b, d] = exact(dot, decay, s.maps[d, 0:LANES], 3)
    u = s.xbc[row, :, :width].astype(F32)
    for d in range(2):
        stepped = expand(s, step, d) * u
        s.v[row, d] = stepped.astype(BF)
        tailed = (expand(s, s.tab[row, 2], d) * stepped).astype(BF)
        for b in range(blocks):
            at = block_rows(b)
            b_mat = s.xbc[row, at, width + d * state : width + (d + 1) * state]
            s.local[row, b, d] = dot_tn(b_mat, tailed[at])


def flat(ref, columns=slice(None)):
    if len(ref.shape) == 2:
        return ref[:, columns]
    value = ref[:, :, columns]
    return value.reshape(value.shape[0] * value.shape[1], value.shape[2])


def carried_rows(rate):
    coarse = rate.astype(BF)
    fine = (rate - coarse.astype(F32)).astype(BF)
    row = lax.broadcasted_iota(jnp.int32, (CARRY, rate.shape[1]), 0)
    return jnp.where(
        row == 0, coarse.astype(F32), jnp.where(row == 1, fine.astype(F32), 0.0)
    ).astype(BF)


def compose(received, place, count, state, up):
    total, rate = None, None
    for k in range(1, count):
        part = received[(k - 1) if up else (count - k - 1)]
        there = (place - k >= 0) if up else (place + k < count)
        there = there.astype(F32)
        term = part[0:state].astype(F32) * there
        total = term if total is None else total + rate * term
        hop = part[state : state + 1].astype(F32) + part[state + 1 : state + 2].astype(F32)
        rate = hop if rate is None else rate * hop
    return total


def run_through(s, row, d, now, terms, out, upward):
    for b in range(s.blocks) if upward else reversed(range(s.blocks)):
        here = terms[row, b, d]
        out[row, b, d] = now
        now = s.decay[row, b, d, 0:1] * now + here
    return now


def summarise(s, row, terms, send, downward):
    for d in range(2):
        upward = (d == 0) != downward
        total, rate = None, None
        for b in range(s.blocks) if upward else reversed(range(s.blocks)):
            own = s.decay[row, b, d, 0:1]
            total = terms[row, b, d] if total is None else own * total + terms[row, b, d]
            rate = own if rate is None else rate * own
        send[0 if upward else 1, row, 0 : s.state] = total.astype(BF)
        send[0 if upward else 1, row, s.state :] = carried_rows(rate)


def sent_states(s, row):
    summarise(s, row, s.local, s.send, False)


def back_states(s, row):
    summarise(s, row, s.enter, s.back_send, True)


def received_states(s, row):
    parts = [s.received[k, row] for k in range(s.count - 1)]
    for d in range(2):
        now = compose(parts, s.place, s.count, s.state, d == 0)
        run_through(s, row, d, now, s.local, s.inc, d == 0)


def returned_states(s, row):
    parts = [s.back_received[k, row] for k in range(s.count - 1)]
    for d in range(2):
        now = compose(parts, s.place, s.count, s.state, d == 1)
        run_through(s, row, d, now, s.enter, s.leaving, d == 1)


def pair_masks(first_place, starts, row):
    rest = BLOCK - LANES

    def mask(rows_from, count, cols_from, width, upper):
        rows = lax.broadcasted_iota(jnp.int32, (count, width), 0) + rows_from
        cols = lax.broadcasted_iota(jnp.int32, (count, width), 1) + cols_from
        doc_rows = doc_of(column_places(count, first_place + rows_from), starts, row)
        col_places = lax.broadcasted_iota(jnp.int32, (1, width), 1) + first_place + cols_from
        same = doc_rows == doc_of(col_places, starts, row)
        return jnp.where(same & ((rows < cols) if upper else (rows > cols)), 0.0, FAR)

    return (
        (mask(0, BLOCK, 0, LANES, False), mask(LANES, rest, LANES, rest, False)),
        (mask(0, LANES, 0, LANES, True), mask(0, BLOCK, LANES, rest, True)),
    )


def tile_rows(upper):
    return (slice(0, LANES), slice(0, BLOCK)) if upper else (slice(0, BLOCK), slice(LANES, BLOCK))


def tiles_nt(rows, cols, upper):
    first, second = tile_rows(upper)
    return dot_nt(rows[first], cols[:LANES]), dot_nt(rows[second], cols[LANES:])


def tiles_apply(tiles, values, upper):
    first, second = dot(tiles[0], values[:LANES]), dot(tiles[1], values[LANES:])
    if upper:
        return first + second[:LANES], second[LANES:]
    return first[:LANES], first[LANES:] + second


def tiles_turned(tiles, values, upper):
    first, second = tile_rows(upper)
    return dot_tn(tiles[0], values[first]), dot_tn(tiles[1], values[second])


def decays_of(s, row, block, lane, masks, upper, rows_first):
    rows = block_rows(block)
    by_row = s.tab[row, 1, rows, lane : lane + 1]
    by_col = s.cumt[row, block, lane : lane + 1, :]
    first, second = tile_rows(upper)
    gaps = by_row[first] - by_col[:, :LANES], by_row[second] - by_col[:, LANES:]
    if rows_first:
        return [jnp.exp2(mask - gap) for gap, mask in zip(gaps, masks)]
    return [jnp.exp2(gap + mask) for gap, mask in zip(gaps, masks)]


def block_mats(s, row, block, d):
    rows, width, state = block_rows(block), s.width, s.state
    b_mat = s.xbc[row, rows, width + d * state : width + (d + 1) * state]
    c_mat = s.xbc[row, rows, width + (2 + d) * state : width + (3 + d) * state]
    return b_mat, c_mat


def inner(s, row, block):
    heads, head_dim = s.heads, s.head_dim
    first = block * BLOCK
    parts = (slice(first, first + LANES), slice(first + LANES, first + BLOCK))
    masks = pair_masks(s.base + first, s.starts, row)
    low_half = lax.broadcasted_iota(jnp.int32, (1, LANES), 1) < head_dim
    for d in range(2):
        upper = d == 1
        b_mat, c_mat = block_mats(s, row, block, d)
        scores = tiles_nt(c_mat, b_mat, upper)
        for pair in range(heads // 2):
            at = slice(pair * LANES, (pair + 1) * LANES)
            values = s.v[row, d, block_rows(block), at]
            outs = []
            for h in (2 * pair, 2 * pair + 1):
                spread = decays_of(s, row, block, d * heads + h, masks[d], upper, False)
                mixing = [(a * b).astype(BF) for a, b in zip(spread, scores)]
                outs.append(tiles_apply(mixing, values, upper))
            for part, a, b in zip(parts, *outs):
                s.y[row, d, part, at] = jnp.where(low_half, a, b)


def gates(s, row):
    half, width = s.half, s.width
    s.z[row] = dot(s.normed[row, HALO:], flat(s.w_late, slice(0, width)))
    for cot, core in ((s.cot, s.core), (s.cot_other, 1 - s.core)):
        places = column_places(half, s.base + core * half)
        valid = (places < s.row_len - s.pad_len[row]).astype(F32)
        s.d_out[row, pl.ds(pl.multiple_of(core * half, HALO), half)] = (
            cot[row].astype(F32) * valid
        ).astype(BF)
    s.dg[row] = dot(s.d_out[row], flat(s.w_late, slice(width, None)))


def outer(s, row):
    heads, head_dim, state, width = s.heads, s.head_dim, s.state, s.width
    for d in range(2):
        reach = expand(s, s.tab[row, 3], d)
        for b in range(s.blocks):
            at = block_rows(b)
            c_mat = s.xbc[row, at, width + (2 + d) * state : width + (3 + d) * state]
            raw = dot(c_mat, s.inc[row, b, d].astype(BF))
            s.y[row, d, at] = s.y[row, d, at] + reach[at] * raw
    u = s.xbc[row, :, :width].astype(F32)
    y = s.y[row, 0] + s.skip_c[...] * u + s.y[row, 1]
    z = s.z[row]
    v = y * z * (1.0 / (1.0 + jnp.exp(-z)))
    lane = lax.broadcasted_iota(jnp.int32, (1, LANES), 1)
    squares = jnp.sum(v * v, axis=-1, keepdims=True)
    against = jnp.sum(s.dg[row] * s.gate_gain_c[...] * v, axis=-1, keepdims=True)
    s.sums[row] = jnp.where(lane == 0, squares, jnp.where(lane == 1, against, 0.0))


def turn(s, row):
    heads, head_dim, state, width = s.heads, s.head_dim, s.state, s.width
    blocks = s.blocks
    total = s.sums[row] + s.sums_other[row]
    scale = lax.rsqrt(total[:, 0:1] * (1.0 / s.inner_width) + EPSILON)
    against = total[:, 1:2]
    u = s.xbc[row, :, :width].astype(F32)
    y = s.y[row, 0] + s.skip_c[...] * u + s.y[row, 1]
    z = s.z[row]
    gate = 1.0 / (1.0 + jnp.exp(-z))
    silu = z * gate
    unit = y * silu * scale
    s.gated[row] = (unit * s.gate_gain_c[...]).astype(BF)
    d_gated = s.dg[row]
    d_v = scale * (d_gated * s.gate_gain_c[...]) - unit * (
        scale * scale * against * (1.0 / s.inner_width)
    )
    dy = (d_v * silu).astype(BF)
    s.dy[row] = dy
    s.dz[row] = (d_v * y * gate * (1.0 + z * (1.0 - gate))).astype(BF)
    dy_f = dy.astype(F32)
    gate_term = jnp.sum(d_gated * unit, axis=0, keepdims=True)
    skip_term = jnp.sum(dy_f * u, axis=0, keepdims=True)
    if row:
        gate_term, skip_term = gate_term + s.gate_sum[...], skip_term + s.skip_sum[...]
    s.gate_sum[...] = gate_term
    s.skip_sum[...] = skip_term
    for d in range(2):
        weighed = (expand(s, s.tab[row, 3], d) * dy_f).astype(BF)
        for b in range(blocks):
            at = block_rows(b)
            c_mat = s.xbc[row, at, width + (2 + d) * state : width + (3 + d) * state]
            s.enter[row, b, d] = dot_tn(c_mat, weighed[at])
            s.d_c[row, at, d * state : (d + 1) * state] = dot_nt(
                weighed[at], s.inc[row, b, d].astype(BF)
            )


def branches(s, row):
    s.branch[row] = dot_nt(s.gated[row], flat(s.w_late, slice(s.width, None))).astype(BF)


def weight_grad(s, out, lefts, rights):
    step = 8 * 2 * s.shard if len(out.shape) == 3 else s.model
    for first in range(0, s.model, step):
        total = None
        for left, right in zip(lefts, rights):
            term = dot_tn(left(slice(first, first + step)), right())
            total = term if total is None else total + term
        if len(out.shape) == 2:
            out[...] = total.astype(BF)
        else:
            per = out.shape[1]
            out[first // per : (first + step) // per] = (
                total.astype(BF).reshape(step // per, per, out.shape[2])
            )


def out_grads(s):
    rows = range(s.rows)
    weight_grad(
        s, s.grad_out,
        [lambda at, r=r: s.d_out[r, :, at] for r in rows], [lambda r=r: s.gated[r] for r in rows],
    )


def gate_grads(s):
    rows = range(s.rows)
    weight_grad(
        s, s.grad_gate,
        [lambda at, r=r: s.normed[r, HALO:, at] for r in rows], [lambda r=r: s.dz[r] for r in rows],
    )


def pre_grads(s):
    rows = range(s.rows)
    weight_grad(
        s, s.grad_pre,
        [lambda at, r=r: s.normed[r, :, at] for r in rows], [lambda r=r: s.d_all[r] for r in rows],
    )


def inner_back(s, row, block):
    heads, head_dim, state = s.heads, s.head_dim, s.state
    rows = block_rows(block)
    first = block * BLOCK
    parts = (slice(first, first + LANES), slice(first + LANES, first + BLOCK))
    masks = pair_masks(s.base + first, s.starts, row)
    low_half = lax.broadcasted_iota(jnp.int32, (1, LANES), 1) < head_dim
    dy_all = s.dy[row, rows].astype(F32)
    along = None
    for d in range(2):
        term = reduce(s, dy_all * s.y[row, d, rows], d, 2)
        along = term if along is None else along + term
        upper = d == 0
        b_mat, c_mat = block_mats(s, row, block, d)
        scores = tiles_nt(b_mat, c_mat, upper)
        d_scores = None
        for pair in range(heads // 2):
            at = slice(pair * LANES, (pair + 1) * LANES)
            values = s.v[row, d, rows, at]
            grads = s.dy[row, rows, at]
            outs = []
            for h in (2 * pair, 2 * pair + 1):
                spread = decays_of(s, row, block, d * heads + h, masks[1 - d], upper, True)
                mixing = [(a * b).astype(BF) for a, b in zip(spread, scores)]
                mine = low_half if h % 2 == 0 else ~low_half
                own = jnp.where(mine, grads, jnp.zeros_like(grads))
                terms = [a * b for a, b in zip(tiles_nt(values, own, upper), spread)]
                d_scores = terms if d_scores is None else [a + b for a, b in zip(d_scores, terms)]
                outs.append(tiles_apply(mixing, grads, upper))
            for part, a, b in zip(parts, *outs):
                s.y[row, d, part, at] = jnp.where(low_half, a, b)
        d_scores = [part.astype(BF) for part in d_scores]
        d_b = tiles_apply(d_scores, c_mat, upper)
        d_c = tiles_turned(d_scores, b_mat, upper)
        for part, b_part, c_part in zip(parts, d_b, d_c):
            s.dbc[row, part, d * state : (d + 1) * state] = b_part
            s.dbc[row, part, (2 + d) * state : (3 + d) * state] = (
                c_part + s.d_c[row, part, d * state : (d + 1) * state]
            )
    s.along[row, rows] = along


def back(s, row):
    heads, head_dim, state, width, span = s.heads, s.head_dim, s.state, s.width, s.span
    conv_width, conv_len, blocks = s.conv_width, s.conv_len, s.blocks
    forward = lax.broadcasted_iota(jnp.int32, (1, LANES), 1) < heads
    rate = jnp.exp(s.a_log_c[...])
    rows = lax.broadcasted_iota(jnp.int32, (BLOCK, 1), 0)
    row_id = lax.broadcasted_iota(jnp.int32, (8, width), 0)
    if row == 0:
        s.pad[0:HALO] = jnp.zeros((HALO, conv_width), F32)
        s.pad[HALO + span :] = jnp.zeros((s.pad.shape[0] - HALO - span, conv_width), F32)
    u = s.xbc[row, :, :width].astype(F32)
    step, tail, reach = s.tab[row, 0], s.tab[row, 2], s.tab[row, 3]
    d_u = s.skip_c[...] * s.dy[row].astype(F32)
    through, direct = None, None
    ended = [None] * blocks
    d_bc = []
    for d in range(2):
        v_d = s.v[row, d].astype(F32)
        leave = [s.leaving[row, b, d].astype(BF) for b in range(blocks)]
        tail_wide = expand(s, tail, d)
        tailed = (tail_wide * v_d).astype(BF)
        held = []
        for b in range(blocks):
            b_mat = s.xbc[row, block_rows(b), width + d * state : width + (d + 1) * state]
            held.append(dot(b_mat, leave[b]))
        dv_state = tail_wide * jnp.concatenate(held, axis=0)
        dv_all = s.y[row, d] + dv_state
        d_bc.append(
            jnp.concatenate([dot_nt(tailed[block_rows(b)], leave[b]) for b in range(blocks)], axis=0)
        )
        d_u = d_u + expand(s, step, d) * dv_all
        passed = v_d * dv_state
        for b in range(blocks):
            sides = jnp.where(
                row_id == 0,
                jnp.sum(passed[block_rows(b)], axis=0, keepdims=True),
                jnp.sum(s.leaving[row, b, d] * s.inc[row, b, d], axis=0, keepdims=True),
            )
            term = reduce(s, sides, d, 3)
            ended[b] = term if d == 0 else ended[b] + term
        terms = reduce(s, v_d * dv_all, d, 2), reduce(s, u * dv_all, d, 2)
        if d == 0:
            through, direct = terms
        else:
            through, direct = through + terms[0], direct + terms[1]
    ends = []
    for b in range(blocks):
        reach_b = reach[block_rows(b)]
        final = jnp.where(forward, reach_b[BLOCK - 1 : BLOCK], reach_b[0:1])
        at_end = jnp.where(
            forward, (rows == BLOCK - 1).astype(F32), (rows == 0).astype(F32)
        )
        ends.append(at_end * (ended[b][0:1] + ended[b][1:2] * final))
    d_cum = s.along[row] - through + jnp.concatenate(ends, axis=0)
    d_logs = jnp.concatenate(
        [jnp.where(forward, from_end, from_start) for from_start, from_end in running(s, d_cum)],
        axis=0,
    )
    d_raw = (direct - rate * d_logs) * s.tab[row, 4]
    s.d_all[row, HALO:, conv_width:] = d_raw.astype(BF)
    d_bias = jnp.sum(d_raw, axis=0, keepdims=True)
    d_rate = jnp.sum(-step * rate * d_logs, axis=0, keepdims=True)
    inside = slice(HALO, HALO + span)
    s.pad[inside, 0:width] = d_u * s.dsil[row, :, 0:width]
    s.pad[inside, width : width + 2 * state] = (
        s.dbc[row, :, : 2 * state] + jnp.concatenate(d_bc, axis=1)
    ) * s.dsil[row, :, width : width + 2 * state]
    s.pad[inside, width + 2 * state :] = (
        s.dbc[row, :, 2 * state :] * s.dsil[row, :, width + 2 * state :]
    )
    s.d_all[row, 0:HALO, conv_width:] = jnp.zeros((HALO, LANES), BF)
    s.pre_f[...] = s.pre[row].astype(F32)
    places = column_places(span, s.base)
    doc = doc_of(places, s.starts, row)
    outs = s.pad[HALO : HALO + span]
    conv_b_term = jnp.sum(outs, axis=0, keepdims=True)
    ext_places = column_places(HALO + span, s.base - HALO)
    ext_doc = doc_of(ext_places, s.starts, row)
    d_pre = None
    conv_w_terms = []
    for k in range(conv_len):
        ahead = conv_len - 1 - k
        ok = (doc_of(places - ahead, s.starts, row) == doc).astype(F32)
        conv_w_terms.append(
            jnp.sum(
                outs * ok * s.pre_f[HALO - ahead : HALO - ahead + span], axis=0, keepdims=True
            )
        )
        ok_ext = (doc_of(ext_places + ahead, s.starts, row) == ext_doc).astype(F32)
        term = s.pad[ahead : ahead + HALO + span] * ok_ext * s.conv_w_c[k : k + 1]
        d_pre = term if d_pre is None else d_pre + term
    s.d_all[row, :, 0:conv_width] = d_pre.astype(BF)
    conv_w_term = jnp.concatenate(conv_w_terms, axis=0)
    small_term = jnp.concatenate([d_bias, d_rate], axis=0)
    if row:
        conv_w_term = conv_w_term + s.sum_conv_w[...]
        conv_b_term = conv_b_term + s.sum_conv_b[...]
        small_term = small_term + s.small[0:2]
    s.sum_conv_w[...] = conv_w_term
    s.sum_conv_b[...] = conv_b_term
    s.small[0:2] = small_term


def d_norms(s, row):
    dn = dot_nt(s.d_all[row], flat(s.w_pre))
    s.dn[row, 0:HALO] = dn[0:HALO].astype(BF)
    s.dn[row, HALO:] = (
        dn[HALO:] + dot_nt(s.dz[row], flat(s.w_late, slice(0, s.width)))
    ).astype(BF)


def finish(s, row):
    half = s.half
    x = s.tokens[row].astype(F32)
    places = column_places(half, s.base + s.core * half)
    valid = (places < s.row_len - s.pad_len[row]).astype(F32)
    keep = pl.ds(pl.multiple_of(s.core * half, HALO), half)
    s.mixed[row] = (
        x + valid * (s.branch[row, keep].astype(F32) + s.branch_other[row].astype(F32))
    ).astype(BF)
    keep = pl.ds(pl.multiple_of(HALO + s.core * half, HALO), half)
    s.ds[...] = s.dn[row, keep].astype(F32) + s.dn_other[row].astype(F32)
    takes = ((s.core == 1) & (s.place + 1 < s.count)).astype(F32)
    s.ds[half - HALO :] += takes * (s.rims[0, row].astype(F32) + s.rims[1, row].astype(F32))
    d_normed = s.ds[...]
    scale = lax.rsqrt(jnp.mean(x * x, axis=-1, keepdims=True) + EPSILON)
    weighed = d_normed * s.norm_gain[...][None]
    along = jnp.mean(weighed * x, axis=-1, keepdims=True)
    dx = scale * weighed - x * (scale * scale * scale * along)
    s.tokens_grad[row] = (s.cot[row].astype(F32) + dx).astype(BF)
    term = jnp.sum(d_normed * x * scale, axis=0, keepdims=True)
    s.gain_sum[...] = term if row == 0 else s.gain_sum[...] + term


MESH = pl.DeviceIdType.MESH


def remote(src, dst, send_sem, recv_sem, device):
    return pltpu.make_async_remote_copy(
        src_ref=src, dst_ref=dst, send_sem=send_sem, recv_sem=recv_sem, device_id=device,
        device_id_type=MESH,
    )


class Sender:
    def __init__(self, send_sems, recv_sems):
        self.send_sems, self.recv_sems = send_sems, recv_sems
        self.sent = 0
        self.slots = 0
        self.pending = []

    def slot(self, count=1):
        self.slots += count
        return self.slots - count

    def send(self, src, dst, slot, device):
        copy = remote(src, dst, self.send_sems.at[self.sent], self.recv_sems.at[slot], device)
        self.sent += 1
        copy.start()
        self.pending.append(copy)

    def arrive(self, dst, slot, device):
        remote(dst, dst, self.send_sems.at[0], self.recv_sems.at[slot], device).wait_recv()

    def drain(self):
        for copy in self.pending:
            copy.wait_send()
        self.pending = []


class Place:
    def __init__(self, count):
        self.dp, self.seq, self.dir = (lax.axis_index(a) for a in ("dp", "seq", "dir"))
        self.count = count
        self.side = self.dp + 1 - 2 * (self.dp % 2)
        self.below = (self.dp + 2) % 4
        self.across = 3 - self.dp
        self.me = (self.dp, self.seq, self.dir)
        self.sibling = (self.dp, self.seq, 1 - self.dir)
        self.by_x = (self.side, self.seq, self.dir)
        self.by_y = (self.below, self.seq, self.dir)

    def along(self, k, crossed=False):
        core = 1 - self.dir if crossed else self.dir
        return (self.dp, (self.seq + k + self.count) % self.count, core)

    def at(self, k):
        return (self.seq + k + self.count) % self.count

    def chip(self, dp, k=0):
        return dp * self.count + self.at(k)

    def meet(self):
        barrier = pltpu.get_barrier_semaphore()
        others = [self.sibling, self.by_x, self.by_y]
        others += [self.along(k) for k in range(1, self.count)]
        others += [self.along(1, True), self.along(-1, True)]
        for device in others:
            pl.semaphore_signal(barrier, inc=1, device_id=device, device_id_type=MESH)
        pl.semaphore_wait(barrier, len(others))


class Spread:
    def __init__(self, place, sender, slab, cut):
        self.place, self.sender, self.slab, self.cut = place, sender, slab, cut
        count = place.count
        self.z, self.x, self.y, self.xd, self.yd = (sender.slot(count) for _ in range(5))
        self.hops = []
        z = place.seq
        low = (3 * count - 2 - 2 * z) // (2 * count)
        near = low * z + (1 - low) * (count - 1 - z)
        self.order = [(z, None)]
        for i in range(1, count):
            paired = (2 * near - i + 4 * count) // (4 * count)
            far = paired * ((i + 1) // 2) + (1 - paired) * (i - near)
            side = paired * (1 - 2 * (i % 2)) + (1 - paired) * (2 * low - 1)
            self.order.append((z + side * far, side))

    def block(self, dp, source):
        return self.slab.at[dp * self.place.count + source]

    def hop(self, source, step):
        here, to = self.place, self.sender
        spot = self.block(here.dp, source)
        sem = to.sent
        to.sent += 1
        there = here.seq + step
        copy = lambda: remote(
            spot, spot, to.send_sems.at[sem], to.recv_sems.at[self.z + source],
            (here.dp, there, here.dir),
        )
        inside = (there >= 0) & (there < here.count)

        @pl.when(inside)
        def _():
            copy().start()

        self.hops.append((inside, copy))

    def start_z(self):
        z = self.place.seq
        self.hop(z, 1)
        self.hop(z, -1)

    def both(self, source):
        here, to = self.place, self.sender
        spot = self.block(here.dp, source)
        to.send(spot, spot, self.x + source, here.by_x)
        to.send(spot, spot, self.y + source, here.by_y)

    def start_xy(self):
        self.both(self.place.seq)

    def relay(self, i):
        here, to = self.place, self.sender
        source, side = self.order[i]
        to.arrive(self.block(here.dp, source), self.z + source, here.by_x)
        self.hop(source, -side)
        self.both(source)

    def cross(self, i):
        here, to = self.place, self.sender
        source = self.order[i][0]
        from_x = self.block(here.side, source)
        to.arrive(from_x, self.x + source, here.by_x)
        part = from_x.at[:, : self.cut]
        to.send(part, part, self.yd + source, here.by_y)
        from_y = self.block(here.below, source)
        to.arrive(from_y, self.y + source, here.by_y)
        part = from_y.at[:, self.cut :]
        to.send(part, part, self.xd + source, here.by_x)

    def end(self, i):
        here, to = self.place, self.sender
        source = self.order[i][0]
        spot = self.block(here.across, source)
        to.arrive(spot.at[:, : self.cut], self.yd + source, here.by_y)
        to.arrive(spot.at[:, self.cut :], self.xd + source, here.by_x)

    def drain(self):
        for inside, copy in self.hops:
            @pl.when(inside)
            def _():
                copy().wait_send()


class Reduce:
    def __init__(self, place, sender, grad, cut, first, second, third, out_second, out_third, total):
        self.place, self.sender, self.grad, self.cut = place, sender, grad, cut
        self.first, self.second, self.third = first, second, third
        self.out_second, self.out_third, self.total = out_second, out_third, total
        count = place.count
        self.one = [[[sender.slot() for _ in range(count)] for _ in range(2)] for _ in range(2)]
        self.two = [[sender.slot() for _ in range(count)] for _ in range(2)]
        self.three = [None] + [sender.slot() for _ in range(1, count)]
        self.sides = (slice(0, cut), slice(cut, grad.shape[2]))

    def start(self, k):
        here, to = self.place, self.sender
        for side, device, targets in (
            (0, here.by_x, (here.side, here.across)),
            (1, here.by_y, (here.below, here.across)),
        ):
            at = self.sides[side]
            for q in (1, 0):
                to.send(
                    self.grad.at[here.chip(targets[q], k), :, at],
                    self.first.at[q, k, :, at],
                    self.one[side][q][k], device,
                )

    def pass_on(self, k):
        here, to = self.place, self.sender
        for side, came, device, target in (
            (0, here.by_x, here.by_y, here.below),
            (1, here.by_y, here.by_x, here.side),
        ):
            at = self.sides[side]
            to.arrive(self.first.at[1, k, :, at], self.one[side][1][k], came)
            self.out_second[k, :, at] = (
                self.grad[here.chip(target, k), :, at].astype(F32)
                + self.first[1, k, :, at].astype(F32)
            ).astype(BF)
            to.send(self.out_second.at[k, :, at], self.second.at[k, :, at], self.two[side][k], device)

    def along(self, k):
        here, to = self.place, self.sender
        for side, came, then in ((0, here.by_x, here.by_y), (1, here.by_y, here.by_x)):
            at = self.sides[side]
            to.arrive(self.first.at[0, k, :, at], self.one[side][0][k], came)
            to.arrive(self.second.at[k, :, at], self.two[side][k], then)
            summed = (
                self.grad[here.chip(here.dp, k), :, at].astype(F32)
                + self.first[0, k, :, at].astype(F32)
                + self.second[k, :, at].astype(F32)
            )
            if k == 0:
                self.total[:, at] = summed
            else:
                self.out_third[k - 1, :, at] = summed.astype(BF)
        if k:
            to.send(self.out_third.at[k - 1], self.third.at[k - 1], self.three[k], here.along(k))

    def end(self):
        here, to = self.place, self.sender
        for k in range(1, here.count):
            to.arrive(self.third.at[k - 1], self.three[k], here.along(-k))
            self.total[...] += self.third[k - 1].astype(F32)


def fill_columns(s, core, pre, late):
    width, heads, conv_width = s.width, s.heads, s.conv_width
    late_side = core == 1
    pick = lambda ref, at: jnp.where(
        late_side, ref[:, at + width : at + 2 * width], ref[:, at : at + width]
    )
    source = lax.broadcasted_iota(jnp.int32, (4 * heads, LANES), 0)
    lane = lax.broadcasted_iota(jnp.int32, (4 * heads, LANES), 1)
    column = jnp.where(lane < heads, lane, lane + heads) + core * heads
    ones = jnp.where((source == column) & (lane < 2 * heads), 1.0, 0.0).astype(BF)
    pre[:, 0:width] = pick(s.w_in, 2 * width).astype(pre.dtype)
    pre[:, width:conv_width] = s.w_in[:, 4 * width :].astype(pre.dtype)
    pre[:, conv_width:] = dot(s.w_dt[...], ones).astype(pre.dtype)
    late[:, 0:width] = pick(s.w_in, 0).astype(late.dtype)
    late[:, width:] = pick(s.w_out, 0).astype(late.dtype)


class Chain:
    def __init__(self, s, place, sender, upward, terms, out, landed, leaves):
        self.s, self.place, self.sender, self.upward = s, place, sender, upward
        self.terms, self.out, self.landed, self.leaves = terms, out, landed, leaves
        self.slots = [[sender.slot() for _ in range(2)] for _ in range(s.rows)]
        self.sems = [[sender.sent + 2 * row + d for d in range(2)] for row in range(s.rows)]
        sender.sent += 2 * s.rows

    def turn(self, d):
        here = self.place
        return here.seq if self.upward[d] else here.count - 1 - here.seq

    def copy(self, row, d):
        to = self.sender
        return remote(
            self.leaves.at[row, d], self.landed.at[row, d], to.send_sems.at[self.sems[row][d]],
            to.recv_sems.at[self.slots[row][d]], self.place.along(1 if self.upward[d] else -1),
        )

    def step(self, row, at):
        for d in range(2):
            @pl.when(self.turn(d) == at)
            def _():
                if at:
                    self.sender.arrive(
                        self.landed.at[row, d], self.slots[row][d],
                        self.place.along(-1 if self.upward[d] else 1),
                    )
                now = self.landed[row, d].astype(F32)
                now = run_through(self.s, row, d, now, self.terms, self.out, self.upward[d])
                if at < self.place.count - 1:
                    self.leaves[row, d] = now.astype(BF)
                    self.copy(row, d).start()

    def steps(self, level, last=None):
        for now in range(level, (level if last is None else last) + 1):
            for row in range(self.s.rows):
                if 0 <= now - row < self.place.count:
                    self.step(row, now - row)

    def drain(self):
        for row in range(self.s.rows):
            for d in range(2):
                @pl.when(self.turn(d) < self.place.count - 1)
                def _():
                    self.copy(row, d).wait_send()


def everything(sizes, names, *refs):
    s = Refs(sizes, names, refs).where()
    count, rows, half, width, heads = s.count, s.rows, s.half, s.width, s.heads
    conv_width, model, shard = s.conv_width, s.model, s.shard
    here = Place(count)
    to = Sender(s.send_sems, s.recv_sems)
    late_core = here.dir == 1
    fill_columns(s, 1 - here.dir, s.give_pre, s.give_late)
    s.chain_in[...] = jnp.zeros_like(s.chain_in)
    s.back_chain_in[...] = jnp.zeros_like(s.back_chain_in)
    here.meet()

    pair = [to.slot() for _ in range(5)]
    to.send(s.give_pre, s.got_pre, pair[0], here.sibling)
    to.send(s.tokens, s.tokens_other, pair[2], here.sibling)
    rim = s.tokens.at[:, pl.ds(half - HALO, HALO)]
    first_rim, second_rim = to.sent, to.sent + 1
    to.sent += 2

    def rims_out():
        return [
            remote(rim, s.halo, s.send_sems.at[sem], s.recv_sems.at[pair[4]], here.along(1, crossed))
            for sem, crossed in ((first_rim, False), (second_rim, True))
        ]

    @pl.when(late_core)
    def _():
        for copy in rims_out():
            copy.start()

    to.send(s.give_late, s.got_late, pair[1], here.sibling)
    to.send(s.cot, s.cot_other, pair[3], here.sibling)
    fill_columns(s, here.dir, s.pre_mine, s.late_mine)

    def joined(own, got):
        other = got[...].astype(F32)
        own = own[...]
        return jnp.where(
            late_core,
            jnp.concatenate([other, own], axis=0),
            jnp.concatenate([own, other], axis=0),
        ).astype(BF)

    me = here.chip(here.dp)
    spread_pre = Spread(here, to, s.w_pre, s.cuts[0])
    spread_late = Spread(here, to, s.w_late, s.cuts[1])
    to.arrive(s.got_pre, pair[0], here.sibling)
    s.w_pre[me] = joined(s.pre_mine, s.got_pre)
    spread_pre.start_z()
    spread_pre.start_xy()
    to.arrive(s.got_late, pair[1], here.sibling)
    s.w_late[me] = joined(s.late_mine, s.got_late)
    prepare(s)
    to.arrive(s.tokens_other, pair[2], here.sibling)
    to.arrive(s.halo, pair[4], here.along(-1))
    spread_pre.relay(1)
    spread_pre.cross(0)
    for row in range(rows):
        normalise(s, row)
    for k in range(2, count):
        spread_pre.relay(k)
        spread_pre.cross(k - 1)
    spread_late.start_z()
    spread_pre.cross(count - 1)
    spread_late.start_xy()
    spread_late.relay(1)
    for k in range(count):
        spread_pre.end(k)

    states = Chain(s, here, to, (True, False), s.local, s.inc, s.chain_in, s.chain_out)
    front(s, 0)
    states.steps(0)
    spread_late.cross(0)
    spread_late.relay(2)
    for row in range(1, rows):
        front(s, row)
        states.steps(row)
    spread_late.cross(1)
    spread_late.relay(3)
    units = [(row, block) for row in range(rows) for block in range(s.blocks)]
    for i, (row, block) in enumerate(units):
        inner(s, row, block)
        if i == 0:
            spread_late.cross(2)
        if block == s.blocks - 1:
            states.steps(rows + row)
        if i == 2:
            spread_late.cross(3)
    for k in range(count):
        spread_late.end(k)
    to.arrive(s.cot_other, pair[3], here.sibling)
    for row in range(rows):
        gates(s, row)
    states.steps(2 * rows, rows + count)
    sum_slots = [to.slot() for _ in range(rows)]
    for row in range(rows):
        outer(s, row)
        to.send(s.sums.at[row], s.sums_other.at[row], sum_slots[row], here.sibling)

    back_chain = Chain(
        s, here, to, (False, True), s.enter, s.leaving, s.back_chain_in, s.back_chain_out
    )
    for row in range(rows):
        to.arrive(s.sums_other.at[row], sum_slots[row], here.sibling)
        turn(s, row)
        back_chain.steps(row)
    grads = (s.grad_pre, s.grad_gate, s.grad_out)
    reduces = [Reduce(here, to, g, cut, *work) for g, cut, work in zip(grads, s.grad_cuts, s.works)]
    reduce_pre, reduce_late = reduces[0], reduces[1:]
    order = list(range(1, count)) + [0]
    gate_grads(s)
    for k in order[:2]:
        reduces[1].start(k)
    out_grads(s)
    for k in order[:2]:
        reduces[2].start(k)
    back_chain.steps(rows)
    for row in range(rows):
        branches(s, row)
    branch_slot, dn_slot, rim_own, rim_cross = (to.slot() for _ in range(4))
    give = pl.multiple_of((1 - here.dir) * half, HALO)
    to.send(s.branch.at[:, pl.ds(give, half)], s.branch_other, branch_slot, here.sibling)
    for i, (row, block) in enumerate(units):
        inner_back(s, row, block)
        if i == 0:
            back_chain.steps(rows + 1)
        if i == 1:
            back_chain.steps(rows + 2, rows + count)
        for reduce in reduce_late:
            if i + 2 < count:
                reduce.start(order[i + 2])
            if 1 <= i <= count:
                reduce.pass_on(order[i - 1])
    back(s, 0)
    for k in order[len(units) + 1 :]:
        for reduce in reduce_late:
            reduce.start(k)
    for k in order[len(units) - 1 :]:
        for reduce in reduce_late:
            reduce.pass_on(k)
    for k in order[:2]:
        for reduce in reduce_late:
            reduce.along(k)
    for row in range(1, rows):
        back(s, row)
    for k in order[2:]:
        for reduce in reduce_late:
            reduce.along(k)
    pre_grads(s)
    for k in order[:2]:
        reduce_pre.start(k)
    for row in range(rows):
        d_norms(s, row)
    to.send(s.dn.at[:, pl.ds(HALO + give, half)], s.dn_other, dn_slot, here.sibling)
    edge = s.dn.at[:, pl.ds(0, HALO)]
    rim_sem = to.sent
    to.sent += 1

    def edge_out(core):
        return remote(
            edge, s.rims.at[core], s.send_sems.at[rim_sem],
            s.recv_sems.at[(rim_cross, rim_own)[core]], here.along(-1, core == 0),
        )

    for core in range(2):
        @pl.when(here.dir == core)
        def _():
            edge_out(core).start()

    reduce_pre.pass_on(order[0])
    reduce_pre.start(order[2])
    to.arrive(s.branch_other, branch_slot, here.sibling)
    to.arrive(s.dn_other, dn_slot, here.sibling)

    @pl.when(late_core)
    def _():
        to.arrive(s.rims.at[1], rim_own, here.along(1))
        to.arrive(s.rims.at[0], rim_cross, here.along(1, True))

    @pl.when(here.dir == 0)
    def _():
        s.rims[...] = jnp.zeros_like(s.rims)

    for row in range(rows):
        finish(s, row)
    side = conv_width - width
    s.v_own[0:4] = s.sum_conv_w[...]
    s.v_own[4:5] = s.sum_conv_b[...]
    s.v_own[5:6] = jnp.concatenate([s.gate_sum[...], s.small[0:1], s.small[1:2]], axis=1)
    s.v_own[6:7] = jnp.concatenate([s.skip_sum[...], jnp.zeros((1, side), F32)], axis=1)
    s.v_own[7:8] = jnp.concatenate([s.gain_sum[...], jnp.zeros((1, side), F32)], axis=1)
    v_slots = [to.slot() for _ in range(2 + count)]
    to.send(s.v_own, s.v_x.at[0], v_slots[0], here.by_x)
    reduce_pre.pass_on(order[1])
    for k in order[3:]:
        reduce_pre.start(k)
    for reduce in reduce_late:
        reduce.end()
    reduce_pre.along(order[0])
    to.arrive(s.v_x.at[0], v_slots[0], here.by_x)
    s.v_x[1] = s.v_own[...] + s.v_x[0]
    to.send(s.v_x.at[1], s.v_y.at[0], v_slots[1], here.by_y)
    reduce_pre.pass_on(order[2])
    reduce_pre.along(order[1])
    to.arrive(s.v_y.at[0], v_slots[1], here.by_y)
    s.v_y[1] = s.v_x[1] + s.v_y[0]
    for k in range(1, count):
        to.send(s.v_y.at[1], s.v_z.at[k - 1], v_slots[1 + k], here.along(k))
    for k in order[3:]:
        reduce_pre.pass_on(k)
    for k in order[2:]:
        reduce_pre.along(k)
    swaps = []
    others = s.others
    back_rows = pl.ds(pl.multiple_of((1 - here.dir) * shard, 8), shard)
    own_rows = pl.ds(pl.multiple_of(here.dir * shard, 8), shard)
    for i in (1, 2, 0):
        slot = to.slot()
        if i == 0:
            reduce_pre.end()
        to.send(reduces[i].total.at[back_rows], others[i], slot, here.sibling)
        swaps.append((i, slot))
    total = s.v_y[1]
    for k in range(1, count):
        to.arrive(s.v_z.at[k - 1], v_slots[1 + k], here.along(-k))
        total = total + s.v_z[k - 1]
    s.v_x[0] = total
    to.send(s.v_x.at[0], s.v_other, v_slots[1 + count], here.sibling)
    parts = {}
    for i, slot in swaps:
        to.arrive(others[i], slot, here.sibling)
        own, got = reduces[i].total[own_rows], others[i][...]
        parts[i] = (jnp.where(late_core, got, own), jnp.where(late_core, own, got))
    (pre_a, pre_b), (gate_a, gate_b), (out_a, out_b) = (parts[i] for i in range(3))
    s.o_in[:, 0:width] = gate_a
    s.o_in[:, width : 2 * width] = gate_b
    s.o_in[:, 2 * width : 3 * width] = pre_a[:, :width]
    s.o_in[:, 3 * width : 4 * width] = pre_b[:, :width]
    s.o_in[:, 4 * width :] = pre_a[:, width:conv_width] + pre_b[:, width:conv_width]
    s.o_out[:, 0:width] = out_a
    s.o_out[:, width:] = out_b
    lane = lax.broadcasted_iota(jnp.int32, (LANES, 4 * heads), 0)
    column = lax.broadcasted_iota(jnp.int32, (LANES, 4 * heads), 1)
    first_lane = jnp.where(lane < heads, lane, jnp.where(lane < 2 * heads, lane + heads, -1))
    picks = [
        jnp.where((first_lane >= 0) & (column == first_lane + side_of * heads), 1.0, 0.0).astype(BF)
        for side_of in range(2)
    ]
    by_step = lambda a, b: exact(dot, a, picks[0], 3) + exact(dot, b, picks[1], 3)
    s.o_dt[...] = by_step(pre_a[:, conv_width:], pre_b[:, conv_width:])
    to.arrive(s.v_other, v_slots[1 + count], here.sibling)
    got = s.v_other[...]
    v_a, v_b = jnp.where(late_core, got, total), jnp.where(late_core, total, got)
    both = v_a + v_b
    s.o_conv_w[:, 0:width] = v_a[0:4, :width]
    s.o_conv_w[:, width : 2 * width] = v_b[0:4, :width]
    s.o_conv_w[:, 2 * width :] = both[0:4, width:]
    s.o_conv_b[...] = jnp.concatenate([v_a[4:5, :width], v_b[4:5, :width], both[4:5, width:]], axis=1)[0]
    s.o_gate[...] = jnp.concatenate([v_a[5:6, :width], v_b[5:6, :width]], axis=1)[0]
    steps = by_step(
        jnp.concatenate([v_a[5:6, width : width + LANES], v_a[5:6, width + LANES : width + 2 * LANES]] * 4, axis=0),
        jnp.concatenate([v_b[5:6, width : width + LANES], v_b[5:6, width + LANES : width + 2 * LANES]] * 4, axis=0),
    )
    s.o_bias[...] = steps[0]
    s.o_alog[...] = steps[1]
    head = lax.broadcasted_iota(jnp.int32, (width, 2 * heads), 1)
    channel = lax.broadcasted_iota(jnp.int32, (width, 2 * heads), 0) // s.head_dim
    skips = None
    for side_of, v_side in ((0, v_a), (1, v_b)):
        ones = jnp.where(head == channel + side_of * heads, 1.0, 0.0).astype(BF)
        term = exact(dot, jnp.broadcast_to(v_side[6:7, :width], (8, width)), ones, 3)
        skips = term if skips is None else skips + term
    s.o_skip[...] = skips[0]
    s.o_norm[...] = both[7:8, :model][0]
    to.drain()
    for waiting in (states, spread_pre, spread_late):
        waiting.drain()
    back_chain.drain()

    @pl.when(late_core)
    def _():
        for copy in rims_out():
            copy.wait_send()

    for core in range(2):
        @pl.when(here.dir == core)
        def _():
            edge_out(core).wait_send()

    assert (to.sent, to.slots) == (s.send_sems.shape[0], s.recv_sems.shape[0]), (to.sent, to.slots)


SMEM = pl.BlockSpec(memory_space=pltpu.SMEM)
VMEM = pl.BlockSpec(memory_space=pltpu.VMEM)


def call(body, ins, specs, out_shapes, scratch, name, collective_id=None):
    return pl.pallas_call(
        body,
        out_shape=out_shapes,
        in_specs=specs,
        out_specs=[VMEM] * len(out_shapes),
        scratch_shapes=scratch,
        compiler_params=pltpu.CompilerParams(
            vmem_limit_bytes=VMEM_BYTES, collective_id=collective_id,
            has_side_effects=collective_id is not None,
        ),
        name=name,
    )(*ins)


def shape_of(dtype, *dims):
    return jax.ShapeDtypeStruct(dims, dtype)


def buffers(z):
    rows, span, half, model, width, state = z[N.rows], z[N.span], z[N.half], z[N.model], z[N.width], z[N.state]
    blocks, conv_width, pre_width, count = z[N.blocks], z[N.conv_width], z[N.pre_width], z[N.count]
    ext, conv_len, heads = HALO + span, z[N.conv_len], z[N.heads]
    packed = 2 * heads + (-2 * heads) % 8
    carried = (state + CARRY, width)
    table = dict(
        conv_w_c=(F32, conv_len, conv_width), conv_b_c=(F32, 1, conv_width), bias_c=(F32, 1, LANES),
        a_log_c=(F32, 1, LANES), skip_c=(F32, 1, width), gate_gain_c=(F32, 1, width),
        gain_c=(F32, 1, model), halo=(BF, rows, HALO, model), tokens_other=(BF, rows, half, model),
        cot_other=(BF, rows, half, model), normed=(BF, rows, ext, model),
        pre=(BF, rows, ext, conv_width), pre_f=(F32, ext, conv_width),
        xbc=(BF, rows, span, conv_width), dsil=(F32, rows, span, conv_width),
        tab=(F32, rows, 5, span, LANES), cumt=(F32, rows, blocks, packed, BLOCK),
        v=(BF, rows, 2, span, width), local=(F32, rows, blocks, 2, state, width),
        decay=(F32, rows, blocks, 2, 8, width), send=(BF, 2, rows) + carried,
        received=(BF, count - 1, rows) + carried, y=(F32, rows, 2, span, width),
        inc=(F32, rows, blocks, 2, state, width), sums=(F32, rows, span, LANES),
        sums_other=(F32, rows, span, LANES), z=(F32, rows, span, width), dg=(F32, rows, span, width),
        d_out=(BF, rows, span, model), gated=(BF, rows, span, width), dy=(BF, rows, span, width),
        dz=(BF, rows, span, width), enter=(F32, rows, blocks, 2, state, width),
        back_send=(BF, 2, rows) + carried, back_received=(BF, count - 1, rows) + carried,
        maps=(BF, 2, 2 * LANES, width), tri=(BF, 2 * BLOCK, BLOCK), d_c=(F32, rows, span, 2 * state),
        leaving=(F32, rows, blocks, 2, state, width), branch=(BF, rows, span, model), grad_out=(BF, model, width), grad_gate=(BF, model, width),
        gate_sum=(F32, 1, width), skip_sum=(F32, 1, width), dbc=(F32, rows, span, 4 * state),
        along=(F32, rows, span, LANES), pad=(F32, ext + 8, conv_width),
        d_all=(BF, rows, ext, pre_width), grad_pre=(BF, model, pre_width),
        sum_conv_w=(F32, conv_len, conv_width), sum_conv_b=(F32, 1, conv_width), small=(F32, 8, LANES),
        dn=(BF, rows, ext, model), branch_other=(BF, rows, half, model),
        dn_other=(BF, rows, half, model), rims=(BF, 2, rows, HALO, model), ds=(F32, half, model),
        gain_sum=(F32, 1, model), mixed=(BF, rows, half, model), tokens_grad=(BF, rows, half, model),
    )
    return {name: shape_of(*shape) for name, shape in table.items()}


def together(z, args):
    count, shard, width, conv_width = z[N.count], z[N.shard], z[N.width], z[N.conv_width]
    pre_width, model, rows, half, heads = z[N.pre_width], z[N.model], z[N.rows], z[N.half], z[N.heads]
    chips, pair = 4 * count, 2 * shard
    table = buffers(z)
    for name in (N.grad_out, N.grad_gate, N.grad_pre):
        table[name] = shape_of(BF, chips, pair, table[name].shape[1])
    outs = dict(
        mixed=table.pop(N.mixed), tokens_grad=table.pop(N.tokens_grad), o_norm=shape_of(F32, model),
        o_in=shape_of(F32, shard, 4 * width + 4 * z[N.state]), o_dt=shape_of(F32, shard, 4 * heads),
        o_conv_w=shape_of(F32, z[N.conv_len], conv_width + width),
        o_conv_b=shape_of(F32, conv_width + width), o_bias=shape_of(F32, 4 * heads),
        o_alog=shape_of(F32, 4 * heads), o_skip=shape_of(F32, 2 * heads),
        o_gate=shape_of(F32, 2 * width), o_out=shape_of(F32, shard, 2 * width),
    )
    for name in (N.send, N.received, N.back_send, N.back_received):
        table.pop(name)
    aliases = {N.inc: N.local, N.leaving: N.enter}
    scratch = {
        name: pltpu.VMEM(value.shape, value.dtype)
        for name, value in table.items() if name not in aliases
    }
    scratch.update(
        w_pre=pltpu.VMEM((chips, pair, pre_width), BF), w_late=pltpu.VMEM((chips, pair, 2 * width), BF),
        give_pre=pltpu.VMEM((shard, pre_width), BF), give_late=pltpu.VMEM((shard, 2 * width), BF),
        got_pre=pltpu.VMEM((shard, pre_width), BF), got_late=pltpu.VMEM((shard, 2 * width), BF),
        pre_mine=pltpu.VMEM((shard, pre_width), F32), late_mine=pltpu.VMEM((shard, 2 * width), F32),
        **{
            name: pltpu.VMEM((rows, 2, z[N.state], width), BF)
            for name in (N.chain_in, N.chain_out, N.back_chain_in, N.back_chain_out)
        },
        v_own=pltpu.VMEM((8, conv_width), F32), v_x=pltpu.VMEM((2, 8, conv_width), F32),
        v_y=pltpu.VMEM((2, 8, conv_width), F32), v_z=pltpu.VMEM((count - 1, 8, conv_width), F32),
        v_other=pltpu.VMEM((8, conv_width), F32),
    )
    widths = dict(pre=pre_width, gate=width, out=width)
    work_names = []
    for name, size in widths.items():
        scratch[name, -1] = pltpu.VMEM((shard, size), F32)
        for i, shape in enumerate(
            ((2, count, pair), (count, pair), (count - 1, pair), (count, pair), (count - 1, pair))
        ):
            scratch[name, i] = pltpu.VMEM(shape + (size,), BF)
        scratch[name, 5] = pltpu.VMEM((pair, size), F32)
        work_names.append([(name, i) for i in range(6)])
    sent, landed = 32 * count + 13 + 5 * rows, 32 * count + 11 + 5 * rows
    scratch[N.send_sems] = pltpu.SemaphoreType.DMA((sent,))
    scratch[N.recv_sems] = pltpu.SemaphoreType.DMA((landed,))
    in_names = list(args)
    names = in_names + list(outs) + list(scratch)
    cut = pre_width // 256 * 128 + 128

    def body(*refs):
        sizes = dict(z, cuts=(cut, width), grad_cuts=(cut, width // 2, width // 2))
        by_name = dict(zip(names, refs))
        for name, of in aliases.items():
            by_name[name] = by_name[of]
        sizes[N.works] = [[by_name[n] for n in group] for group in work_names]
        sizes[N.others] = [by_name[name, -1] for name in widths]
        plain = {name: ref for name, ref in by_name.items() if isinstance(name, str)}
        everything(sizes, list(plain), *plain.values())

    specs = [SMEM if name in (N.starts, N.pad_len) else VMEM for name in in_names]
    out = call(
        body, list(args.values()), specs, list(outs.values()), list(scratch.values()), N.layer, 0
    )
    return dict(zip(outs, delivered(out)))


def delivered(arrays):
    count = len(arrays)

    def body(*refs):
        for source, target in zip(refs[:count], refs[count:]):
            target[...] = source[...]

    return call(
        body, arrays, [VMEM] * count, [shape_of(a.dtype, *a.shape) for a in arrays], (), N.deliver
    )


def swapped(value):
    return lax.ppermute(value, "dir", [(0, 1), (1, 0)])


def rotated_to(value, steps, cross):
    count = lax.axis_size("seq")
    pairs = []
    for i in range(count):
        for c in range(2):
            pairs.append((i * 2 + c, (i + steps) % count * 2 + (1 - c if cross else c)))
    return lax.ppermute(value, ("seq", "dir"), pairs)


def around(value):
    count, place = lax.axis_size("seq"), lax.axis_index("seq")
    out = []
    for k in range(1, count):
        chosen = jnp.where(place + k < count, value[0], value[1])
        out.append(rotated_to(chosen, k, False))
    return jnp.stack(out)


def stage(z, have, phase, ins, outs, scratch=(), units=None):
    table = buffers(z)
    ins = [N.starts, N.pad_len] + list(ins)
    names = ins + list(outs) + list(scratch)
    units = [(row,) for row in range(z[N.rows])] if units is None else units

    def body(*refs):
        s = Refs(z, names, refs).where()
        for unit in units:
            phase(s, *unit)

    results = call(
        body, [have[name] for name in ins],
        [SMEM if name in (N.starts, N.pad_len) else VMEM for name in ins],
        [table[name] for name in outs],
        [pltpu.VMEM(table[name].shape, table[name].dtype) for name in scratch],
        phase.__name__,
    )
    have.update(zip(outs, results))


def apart(z, args):
    heads, width, conv_width, count = z[N.heads], z[N.width], z[N.conv_width], z[N.count]
    half, shard = z[N.half], z[N.shard]
    have = dict(args)
    core = lax.axis_index("dir")
    is_late = core == 1
    w_in, w_dt, w_out, tokens = (args[n] for n in (N.w_in, N.w_dt, N.w_out, N.tokens))
    pad_dt = jnp.zeros((shard, LANES - 2 * heads), BF)

    def columns(c):
        own = slice(c * width, (c + 1) * width)
        return (
            jnp.concatenate(
                [
                    w_in[:, 2 * width :][:, own], w_in[:, 4 * width :],
                    w_dt[:, c * heads : (c + 1) * heads],
                    w_dt[:, (2 + c) * heads : (3 + c) * heads], pad_dt,
                ],
                axis=1,
            ),
            jnp.concatenate([w_in[:, own], w_out[:, own]], axis=1),
        )

    def ordered(own, other, axis):
        return jnp.where(
            is_late, jnp.concatenate([other, own], axis=axis), jnp.concatenate([own, other], axis=axis)
        )

    first, latter = columns(0), columns(1)

    def gathered(i):
        keep = jnp.where(is_late, latter[i], first[i])
        give = swapped(jnp.where(is_late, first[i], latter[i]))
        return lax.all_gather(ordered(keep, give, 0), ("dp", "seq"), axis=0, tiled=True)

    have[N.w_pre], have[N.w_late] = gathered(0), gathered(1)
    have[N.tokens_other], have[N.cot_other] = swapped(tokens), swapped(args[N.cot])
    rim = tokens[:, half - HALO :]
    have[N.halo] = jnp.where(is_late, rotated_to(rim, 1, False), rotated_to(rim, 1, True))
    small = [N.conv_w_c, N.conv_b_c, N.bias_c, N.a_log_c, N.skip_c, N.gate_gain_c, N.gain_c, N.maps, N.tri]
    stage(
        z, have, prepare,
        [N.conv_w, N.conv_b, N.dt_bias, N.a_log, N.skip, N.gate_gain, N.norm_gain], small, units=[()],
    )
    stage(z, have, normalise, [N.gain_c, N.halo, N.tokens, N.tokens_other], [N.normed])
    stage(
        z, have, front, [N.normed, N.w_pre, N.conv_w_c, N.conv_b_c, N.bias_c, N.a_log_c, N.maps, N.tri],
        [N.pre, N.xbc, N.dsil, N.tab, N.cumt, N.v, N.local, N.decay], [N.pre_f],
    )
    stage(z, have, sent_states, [N.local, N.decay], [N.send])
    have[N.received] = around(have[N.send])
    stage(z, have, received_states, [N.received, N.local, N.decay], [N.inc])
    units = [(row, block) for row in range(z[N.rows]) for block in range(z[N.blocks])]

    def forward(s):
        for unit in units:
            inner(s, *unit)
        for row in range(s.rows):
            gates(s, row)
            outer(s, row)

    stage(
        z, have, forward,
        [N.maps, N.xbc, N.tab, N.cumt, N.v, N.inc, N.normed, N.w_late, N.cot,
         N.cot_other, N.skip_c, N.gate_gain_c],
        [N.y, N.d_out, N.sums, N.z, N.dg], units=[()],
    )
    have[N.sums_other] = swapped(have[N.sums])

    def turned(s):
        for row in range(s.rows):
            turn(s, row)
            branches(s, row)
        out_grads(s)
        gate_grads(s)

    stage(
        z, have, turned,
        [N.sums, N.sums_other, N.xbc, N.y, N.z, N.dg, N.tab, N.inc, N.maps, N.skip_c, N.gate_gain_c, N.d_out,
         N.normed, N.w_late],
        [N.gated, N.dy, N.dz, N.gate_sum, N.skip_sum, N.enter, N.d_c, N.branch, N.grad_out,
         N.grad_gate],
        units=[()],
    )
    stage(z, have, back_states, [N.enter, N.decay], [N.back_send])
    have[N.back_received] = around(have[N.back_send])
    stage(z, have, returned_states, [N.back_received, N.enter, N.decay], [N.leaving])

    def backward(s):
        for row in range(s.rows):
            for block in range(s.blocks):
                for d in range(2):
                    at = block_rows(block)
                    s.y[row, d, at] = s.y_both[row, d, at]
                inner_back(s, row, block)
            back(s, row)
            d_norms(s, row)
        pre_grads(s)

    have[N.y_both] = have[N.y]
    stage(
        z, have, backward,
        [N.maps, N.tri, N.d_c, N.y_both, N.leaving, N.inc, N.xbc, N.tab, N.cumt, N.v, N.dy, N.dsil, N.pre,
         N.normed, N.dz, N.skip_c, N.a_log_c, N.conv_w_c, N.w_pre, N.w_late],
        [N.dn, N.d_all, N.grad_pre, N.sum_conv_w, N.sum_conv_b, N.small],
        [N.y, N.dbc, N.along, N.pad, N.pre_f], units=[()],
    )

    def give(values, first_row):
        return swapped(
            lax.dynamic_slice_in_dim(values, first_row + (1 - core) * half, half, axis=1)
        )

    edge = have[N.dn][:, :HALO]
    have[N.dn_other], have[N.branch_other] = give(have[N.dn], HALO), give(have[N.branch], 0)
    have[N.rims] = jnp.stack([rotated_to(edge, -1, True), rotated_to(edge, -1, False)])
    stage(
        z, have, finish,
        [N.tokens, N.cot, N.norm_gain, N.dn, N.dn_other, N.branch, N.branch_other, N.rims],
        [N.mixed, N.tokens_grad, N.gain_sum], [N.ds],
    )

    def placed(values):
        empty = jnp.zeros_like(values)
        return ordered(values, empty, -1)

    def sided(values):
        return jnp.concatenate([placed(values[:, :width]), values[:, width:]], axis=1)

    def reduced(name):
        value = lax.psum_scatter(have[name], ("dp", "seq"), scatter_dimension=0, tiled=True)
        own = lax.dynamic_slice_in_dim(value, core * shard, shard, axis=0)
        other = swapped(lax.dynamic_slice_in_dim(value, (1 - core) * shard, shard, axis=0))
        own, other = own.astype(F32), other.astype(F32)
        return jnp.where(is_late, other, own), jnp.where(is_late, own, other)

    def by_step(values):
        return jnp.concatenate(
            [placed(values[:, :heads]), placed(values[:, heads : 2 * heads])], axis=1
        )

    steps = by_step(have[N.small][:2])
    skips = placed(jnp.sum(have[N.skip_sum].reshape(1, heads, z[N.head_dim]), axis=-1))
    gain, all_conv_w, all_conv_b, steps, skips, gate_all = lax.psum(
        (
            have[N.gain_sum], sided(have[N.sum_conv_w]), sided(have[N.sum_conv_b]), steps, skips,
            placed(have[N.gate_sum]),
        ),
        ("dp", "seq", "dir"),
    )
    (pre_a, pre_b), (gate_a, gate_b), (out_a, out_b) = (
        reduced(name) for name in (N.grad_pre, N.grad_gate, N.grad_out)
    )
    last = conv_width
    return dict(
        mixed=have[N.mixed], tokens_grad=have[N.tokens_grad], o_norm=gain[0],
        o_in=jnp.concatenate(
            [
                gate_a, gate_b, pre_a[:, :width], pre_b[:, :width],
                pre_a[:, width:conv_width] + pre_b[:, width:conv_width],
            ],
            axis=1,
        ),
        o_dt=jnp.concatenate(
            [
                pre_a[:, last : last + heads], pre_b[:, last : last + heads],
                pre_a[:, last + heads : last + 2 * heads], pre_b[:, last + heads : last + 2 * heads],
            ],
            axis=1,
        ),
        o_conv_w=all_conv_w, o_conv_b=all_conv_b[0], o_bias=steps[0], o_alog=steps[1],
        o_skip=skips[0], o_gate=gate_all[0], o_out=jnp.concatenate([out_a, out_b], axis=1),
    )


def shards(tokens, starts, pad_len, norm_gain, w_in, w_dt, conv_w, conv_b, dt_bias, a_log, skip,
           gate_gain, w_out, cotangent):
    rows, half, model = tokens.shape
    span = 2 * half
    count = lax.axis_size("seq")
    inner_width = gate_gain.shape[0]
    heads = skip.shape[0] // 2
    width = inner_width // 2
    state = (conv_w.shape[1] - inner_width) // 4
    conv_width = width + 4 * state
    shard = w_in.shape[0]
    z = dict(
        rows=rows, half=half, model=model, span=span, count=count, row_len=span * count,
        blocks=span // BLOCK, inner_width=inner_width, heads=heads, head_dim=width // heads,
        width=width, state=state, conv_width=conv_width, conv_len=conv_w.shape[0],
        pre_width=conv_width + LANES, shard=shard,
    )
    args = dict(
        tokens=tokens, starts=starts, pad_len=pad_len, norm_gain=norm_gain, w_in=w_in, w_dt=w_dt,
        conv_w=conv_w, conv_b=conv_b, dt_bias=dt_bias, a_log=a_log, skip=skip, gate_gain=gate_gain,
        w_out=w_out, cot=cotangent,
    )
    direct = lax.axis_size("dp") == 4 and 2 * shard % 16 == 0 and model % (16 * shard) == 0
    out = together(z, args) if direct else apart(z, args)
    order = (
        N.mixed, N.tokens_grad, N.o_norm, N.o_in, N.o_dt, N.o_conv_w, N.o_conv_b, N.o_bias, N.o_alog,
        N.o_skip, N.o_gate, N.o_out,
    )
    return tuple(out[name] for name in order)


def solution(mesh):
    weight = P(("dp", "seq", "dir"), None)
    values = P("dp", ("seq", "dir"), None)
    return jax.shard_map(
        shards,
        mesh=mesh,
        in_specs=(
            values, P("dp", None), P("dp"), P(), weight, weight, P(), P(), P(), P(), P(), P(),
            weight, values,
        ),
        out_specs=(
            values, values, P(), weight, weight, P(), P(), P(), P(), P(), P(), weight,
        ),
        check_vma=False,
    )
```

```python
import jax
import jax.numpy as jnp
from jax import lax
from jax.experimental import pallas as pl
from jax.experimental.pallas import tpu as pltpu
from jax.sharding import PartitionSpec as P

BLOCK = 160
HALO = 16
LANES = 128
CARRY = 16
EPSILON = 1e-05
BF = jnp.bfloat16
F32 = jnp.float32
LOG2E = 1.4426950408889634
VMEM_BYTES = 62 * 1024 * 1024


class Names:
    def __getattr__(self, name):
        return name


N = Names()


def dot(a, b):
    return lax.dot_general(a, b, (((1,), (0,)), ((), ())), preferred_element_type=F32)


def dot_nt(a, b):
    return lax.dot_general(a, b, (((1,), (1,)), ((), ())), preferred_element_type=F32)


def dot_tn(a, b):
    return lax.dot_general(a, b, (((0,), (0,)), ((), ())), preferred_element_type=F32)


def pieces(values, count):
    parts = []
    for _ in range(count - 1):
        part = values.astype(BF)
        parts.append(part)
        values = values - part.astype(F32)
    parts.append(values.astype(BF))
    return parts


def exact(op, values, ones, count):
    total = None
    for part in pieces(values, count):
        term = op(part, ones)
        total = term if total is None else total + term
    return total


def head_map(first, width, head_dim):
    lane = lax.broadcasted_iota(jnp.int32, (LANES, width), 0)
    head = lax.broadcasted_iota(jnp.int32, (LANES, width), 1) // head_dim
    return jnp.where(lane == head + first, 1.0, 0.0).astype(BF)


def expand(s, values, d):
    return dot(jnp.concatenate(pieces(values, 2), axis=1), s.maps[d])


def reduce(s, values, d, count):
    return exact(dot_nt, values, s.maps[d, 0:LANES], count)


def running(s, values):
    parts = pieces(values, 3)
    blocks = range(values.shape[0] // BLOCK)
    wide = jnp.concatenate([part[block_rows(b)] for b in blocks for part in parts], axis=1)
    both = dot(s.tri[...], wide)
    result = []
    for b in blocks:
        first = 3 * b * LANES
        total = (
            both[:, first : first + LANES]
            + both[:, first + LANES : first + 2 * LANES]
            + both[:, first + 2 * LANES : first + 3 * LANES]
        )
        result.append((total[:BLOCK], total[BLOCK:]))
    return result


def doc_of(places, starts_ref, row):
    total = (starts_ref[row, 0] <= places).astype(jnp.int32)
    for j in range(1, starts_ref.shape[1]):
        total = total + (starts_ref[row, j] <= places).astype(jnp.int32)
    return total


def column_places(count, first):
    return lax.broadcasted_iota(jnp.int32, (count, 1), 0) + first


class Refs:
    def __init__(self, sizes, names, refs):
        self.__dict__.update(sizes)
        for name, ref in zip(names, refs):
            setattr(self, name, ref)

    def where(self):
        self.core = lax.axis_index("dir")
        self.place = lax.axis_index("seq")
        self.base = self.place * self.span
        return self


def block_rows(block):
    return slice(block * BLOCK, (block + 1) * BLOCK)


def prepare(s):
    late = s.core == 1
    width, heads = s.width, s.heads

    def mine(values, first, size):
        return jnp.where(
            late, values[:, first + size : first + 2 * size], values[:, first : first + size]
        )

    conv_w = s.conv_w[...]
    s.conv_w_c[:, 0:width] = mine(conv_w, 0, width)
    s.conv_w_c[:, width:] = conv_w[:, 2 * width :]
    conv_b = s.conv_b[...][None]
    s.conv_b_c[:, 0:width] = mine(conv_b, 0, width)
    s.conv_b_c[:, width:] = conv_b[:, 2 * width :]
    s.gate_gain_c[...] = mine(s.gate_gain[...][None], 0, width)
    s.gain_c[...] = s.norm_gain[...][None]
    source = lax.broadcasted_iota(jnp.int32, (4 * heads, LANES), 0)
    lane = lax.broadcasted_iota(jnp.int32, (4 * heads, LANES), 1)
    column = jnp.where(lane < heads, lane, lane + heads) + s.core * heads
    picked = jnp.where((source == column) & (lane < 2 * heads), 1.0, 0.0).astype(BF)
    for ref, out in ((s.dt_bias, s.bias_c), (s.a_log, s.a_log_c)):
        rows = jnp.broadcast_to(ref[...][None], (8, 4 * heads))
        out[...] = exact(dot, rows, picked, 3)[0:1]
    head = lax.broadcasted_iota(jnp.int32, (2 * heads, width), 0)
    channel = lax.broadcasted_iota(jnp.int32, (2 * heads, width), 1) // s.head_dim
    spread = jnp.where(head == channel + s.core * heads, 1.0, 0.0).astype(BF)
    rows = jnp.broadcast_to(s.skip[...][None], (8, 2 * heads))
    s.skip_c[...] = exact(dot, rows, spread, 3)[0:1]
    for d in range(2):
        ones = head_map(d * heads, width, s.head_dim)
        s.maps[d, 0:LANES] = ones
        s.maps[d, LANES:] = ones
    row = lax.broadcasted_iota(jnp.int32, (BLOCK, BLOCK), 0)
    col = lax.broadcasted_iota(jnp.int32, (BLOCK, BLOCK), 1)
    s.tri[0:BLOCK] = jnp.where(row >= col, 1.0, 0.0).astype(BF)
    s.tri[BLOCK:] = jnp.where(row <= col, 1.0, 0.0).astype(BF)


def normalise(s, row):
    def norm(part):
        x = part.astype(F32)
        scale = lax.rsqrt(jnp.mean(x * x, axis=-1, keepdims=True) + EPSILON)
        return (x * scale * s.gain_c[...]).astype(BF)

    half = s.half
    s.normed[row, 0:HALO] = norm(s.halo[row])
    own = pl.multiple_of(HALO + s.core * half, HALO)
    other = pl.multiple_of(HALO + (1 - s.core) * half, HALO)
    s.normed[row, pl.ds(own, half)] = norm(s.tokens[row])
    s.normed[row, pl.ds(other, half)] = norm(s.tokens_other[row])


def front(s, row):
    heads, head_dim, state, width, span = s.heads, s.head_dim, s.state, s.width, s.span
    conv_width = s.conv_width
    projected = dot(s.normed[row], flat(s.w_pre))
    pre = projected[:, :conv_width].astype(BF)
    s.pre[row] = pre
    s.pre_f[...] = pre.astype(F32)
    raw = projected[HALO:, conv_width:].astype(BF).astype(F32)
    places = column_places(span, s.base)
    doc = doc_of(places, s.starts, row)
    valid = (places < s.row_len - s.pad_len[row]).astype(F32)
    summed = s.conv_b_c[...]
    for k in range(s.conv_len):
        back = s.conv_len - 1 - k
        ok = (doc_of(places - back, s.starts, row) == doc).astype(F32)
        summed = summed + s.pre_f[HALO - back : HALO - back + span] * s.conv_w_c[k : k + 1] * ok
    gate = 1.0 / (1.0 + jnp.exp(-summed))
    s.xbc[row] = (summed * gate * valid).astype(BF)
    s.dsil[row] = gate * (1.0 + summed * (1.0 - gate)) * valid
    forward = lax.broadcasted_iota(jnp.int32, (1, LANES), 1) < heads
    shifted_raw = raw + s.bias_c[...]
    step = jnp.maximum(shifted_raw, 0.0) + jnp.log1p(jnp.exp(-jnp.abs(shifted_raw)))
    slope = 1.0 / (1.0 + jnp.exp(-shifted_raw))
    logs = -step * jnp.exp(s.a_log_c[...])
    s.tab[row, 0] = step
    s.tab[row, 4] = slope
    blocks = s.blocks
    sums = running(s, logs)
    for b in range(blocks):
        at = block_rows(b)
        doc_b = doc[at]
        cum = jnp.where(forward, sums[b][0], sums[b][1])
        first_place = s.base + b * BLOCK
        end_f = doc_of(first_place + BLOCK - 1, s.starts, row)
        end_b = doc_of(first_place, s.starts, row)
        near_f = doc_of(first_place - 1, s.starts, row)
        near_b = doc_of(first_place + BLOCK, s.starts, row)
        final = jnp.where(forward, cum[BLOCK - 1 : BLOCK], cum[0:1])
        tail = jnp.exp(final - cum) * (doc_b == jnp.where(forward, end_f, end_b)).astype(F32)
        reach = jnp.exp(cum) * (doc_b == jnp.where(forward, near_f, near_b)).astype(F32)
        scaled = cum * LOG2E
        s.cumt[row, b] = scaled.T[: s.cumt.shape[2]]
        s.tab[row, 1, at] = scaled
        s.tab[row, 2, at] = tail
        s.tab[row, 3, at] = reach
        decay = jnp.broadcast_to(
            jnp.where(forward, reach[BLOCK - 1 : BLOCK], reach[0:1]), (8, LANES)
        )
        for d in range(2):
            s.decay[row, b, d] = exact(dot, decay, s.maps[d, 0:LANES], 3)
    u = s.xbc[row, :, :width].astype(F32)
    for d in range(2):
        stepped = expand(s, step, d) * u
        s.v[row, d] = stepped.astype(BF)
        tailed = (expand(s, s.tab[row, 2], d) * stepped).astype(BF)
        for b in range(blocks):
            at = block_rows(b)
            b_mat = s.xbc[row, at, width + d * state : width + (d + 1) * state]
            s.local[row, b, d] = dot_tn(b_mat, tailed[at])


def flat(ref, columns=slice(None)):
    if len(ref.shape) == 2:
        return ref[:, columns]
    value = ref[:, :, columns]
    return value.reshape(value.shape[0] * value.shape[1], value.shape[2])


def carried_rows(rate):
    coarse = rate.astype(BF)
    fine = (rate - coarse.astype(F32)).astype(BF)
    row = lax.broadcasted_iota(jnp.int32, (CARRY, rate.shape[1]), 0)
    return jnp.where(
        row == 0, coarse.astype(F32), jnp.where(row == 1, fine.astype(F32), 0.0)
    ).astype(BF)


def compose(received, place, count, state, up):
    total, rate = None, None
    for k in range(1, count):
        part = received[(k - 1) if up else (count - k - 1)]
        there = (place - k >= 0) if up else (place + k < count)
        there = there.astype(F32)
        term = part[0:state].astype(F32) * there
        total = term if total is None else total + rate * term
        hop = part[state : state + 1].astype(F32) + part[state + 1 : state + 2].astype(F32)
        rate = hop if rate is None else rate * hop
    return total


def run_through(s, row, d, now, terms, out, upward):
    for b in range(s.blocks) if upward else reversed(range(s.blocks)):
        here = terms[row, b, d]
        out[row, b, d] = now
        now = s.decay[row, b, d, 0:1] * now + here
    return now


def summarise(s, row, terms, send, downward):
    for d in range(2):
        upward = (d == 0) != downward
        total, rate = None, None
        for b in range(s.blocks) if upward else reversed(range(s.blocks)):
            own = s.decay[row, b, d, 0:1]
            total = terms[row, b, d] if total is None else own * total + terms[row, b, d]
            rate = own if rate is None else rate * own
        send[0 if upward else 1, row, 0 : s.state] = total.astype(BF)
        send[0 if upward else 1, row, s.state :] = carried_rows(rate)


def sent_states(s, row):
    summarise(s, row, s.local, s.send, False)


def back_states(s, row):
    summarise(s, row, s.enter, s.back_send, True)


def received_states(s, row):
    parts = [s.received[k, row] for k in range(s.count - 1)]
    for d in range(2):
        now = compose(parts, s.place, s.count, s.state, d == 0)
        run_through(s, row, d, now, s.local, s.inc, d == 0)


def returned_states(s, row):
    parts = [s.back_received[k, row] for k in range(s.count - 1)]
    for d in range(2):
        now = compose(parts, s.place, s.count, s.state, d == 1)
        run_through(s, row, d, now, s.enter, s.leaving, d == 1)


def pair_masks(first_place, starts, row):
    rest = BLOCK - LANES

    def mask(rows_from, count, cols_from, width, upper):
        rows = lax.broadcasted_iota(jnp.int32, (count, width), 0) + rows_from
        cols = lax.broadcasted_iota(jnp.int32, (count, width), 1) + cols_from
        doc_rows = doc_of(column_places(count, first_place + rows_from), starts, row)
        col_places = lax.broadcasted_iota(jnp.int32, (1, width), 1) + first_place + cols_from
        same = doc_rows == doc_of(col_places, starts, row)
        return jnp.where(same & ((rows < cols) if upper else (rows > cols)), 1.0, 0.0)

    return (
        (mask(0, BLOCK, 0, LANES, False), mask(LANES, rest, LANES, rest, False)),
        (mask(0, LANES, 0, LANES, True), mask(0, BLOCK, LANES, rest, True)),
    )


def tile_rows(upper):
    return (slice(0, LANES), slice(0, BLOCK)) if upper else (slice(0, BLOCK), slice(LANES, BLOCK))


def tiles_nt(rows, cols, upper):
    first, second = tile_rows(upper)
    return dot_nt(rows[first], cols[:LANES]), dot_nt(rows[second], cols[LANES:])


def tiles_apply(tiles, values, upper):
    first, second = dot(tiles[0], values[:LANES]), dot(tiles[1], values[LANES:])
    if upper:
        return first + second[:LANES], second[LANES:]
    return first[:LANES], first[LANES:] + second


def tiles_turned(tiles, values, upper):
    first, second = tile_rows(upper)
    return dot_tn(tiles[0], values[first]), dot_tn(tiles[1], values[second])


def pair_apply(first, second, values, upper):
    wide = jnp.concatenate([first[0], second[0]], axis=1)
    tall = jnp.concatenate([part[:LANES] for part in values], axis=0)
    main = dot(wide, tall)
    rest = dot(first[1], values[0][LANES:]) + dot(second[1], values[1][LANES:])
    if upper:
        return main + rest[:LANES], rest[LANES:]
    return main[:LANES], main[LANES:] + rest


def pair_nt(rows, cols, upper):
    first, second = tile_rows(upper)
    main = dot_nt(rows[first], jnp.concatenate([part[:LANES] for part in cols], axis=0))
    return [
        (main[:, i * LANES : (i + 1) * LANES], dot_nt(rows[second], cols[i][LANES:]))
        for i in range(2)
    ]


def halves_of(values, head_dim):
    low = lax.broadcasted_iota(jnp.int32, (1, LANES), 1) < head_dim
    empty = jnp.zeros_like(values)
    return jnp.where(low, values, empty), jnp.where(low, empty, values)


def decays_of(s, row, block, lane, upper, rows_first):
    rows = block_rows(block)
    by_row = s.tab[row, 1, rows, lane : lane + 1]
    by_col = s.cumt[row, block, lane : lane + 1, :]
    first, second = tile_rows(upper)
    if rows_first:
        gaps = by_col[:, :LANES] - by_row[first], by_col[:, LANES:] - by_row[second]
    else:
        gaps = by_row[first] - by_col[:, :LANES], by_row[second] - by_col[:, LANES:]
    return [jnp.exp2(jnp.minimum(gap, 0.0)) for gap in gaps]


def block_mats(s, row, block, d):
    rows, width, state = block_rows(block), s.width, s.state
    b_mat = s.xbc[row, rows, width + d * state : width + (d + 1) * state]
    c_mat = s.xbc[row, rows, width + (2 + d) * state : width + (3 + d) * state]
    return b_mat, c_mat


def inner(s, row, block):
    heads, head_dim = s.heads, s.head_dim
    first = block * BLOCK
    parts = (slice(first, first + LANES), slice(first + LANES, first + BLOCK))
    masks = pair_masks(s.base + first, s.starts, row)
    for d in range(2):
        upper = d == 1
        b_mat, c_mat = block_mats(s, row, block, d)
        scores = [a * b for a, b in zip(tiles_nt(c_mat, b_mat, upper), masks[d])]
        for pair in range(heads // 2):
            at = slice(pair * LANES, (pair + 1) * LANES)
            values = halves_of(s.v[row, d, block_rows(block), at], head_dim)
            mixing = []
            for h in (2 * pair, 2 * pair + 1):
                spread = decays_of(s, row, block, d * heads + h, upper, False)
                mixing.append([(a * b).astype(BF) for a, b in zip(spread, scores)])
            for part, out in zip(parts, pair_apply(*mixing, values, upper)):
                s.y[row, d, part, at] = out


def gates(s, row):
    half, width = s.half, s.width
    s.z[row] = dot(s.normed[row, HALO:], flat(s.w_late, slice(0, width)))
    for cot, core in ((s.cot, s.core), (s.cot_other, 1 - s.core)):
        places = column_places(half, s.base + core * half)
        valid = (places < s.row_len - s.pad_len[row]).astype(F32)
        s.d_out[row, pl.ds(pl.multiple_of(core * half, HALO), half)] = (
            cot[row].astype(F32) * valid
        ).astype(BF)
    s.dg[row] = dot(s.d_out[row], flat(s.w_late, slice(width, None)))


def outer(s, row):
    heads, head_dim, state, width = s.heads, s.head_dim, s.state, s.width
    for d in range(2):
        reach = expand(s, s.tab[row, 3], d)
        for b in range(s.blocks):
            at = block_rows(b)
            c_mat = s.xbc[row, at, width + (2 + d) * state : width + (3 + d) * state]
            raw = dot(c_mat, s.inc[row, b, d].astype(BF))
            s.y[row, d, at] = s.y[row, d, at] + reach[at] * raw
    u = s.xbc[row, :, :width].astype(F32)
    y = s.y[row, 0] + s.skip_c[...] * u + s.y[row, 1]
    z = s.z[row]
    v = y * z * (1.0 / (1.0 + jnp.exp(-z)))
    lane = lax.broadcasted_iota(jnp.int32, (1, LANES), 1)
    squares = jnp.sum(v * v, axis=-1, keepdims=True)
    against = jnp.sum(s.dg[row] * s.gate_gain_c[...] * v, axis=-1, keepdims=True)
    s.sums[row] = jnp.where(lane == 0, squares, jnp.where(lane == 1, against, 0.0))


def turn(s, row):
    heads, head_dim, state, width = s.heads, s.head_dim, s.state, s.width
    blocks = s.blocks
    total = s.sums[row] + s.sums_other[row]
    scale = lax.rsqrt(total[:, 0:1] * (1.0 / s.inner_width) + EPSILON)
    against = total[:, 1:2]
    u = s.xbc[row, :, :width].astype(F32)
    y = s.y[row, 0] + s.skip_c[...] * u + s.y[row, 1]
    z = s.z[row]
    gate = 1.0 / (1.0 + jnp.exp(-z))
    silu = z * gate
    unit = y * silu * scale
    s.gated[row] = (unit * s.gate_gain_c[...]).astype(BF)
    d_gated = s.dg[row]
    d_v = scale * (d_gated * s.gate_gain_c[...]) - unit * (
        scale * scale * against * (1.0 / s.inner_width)
    )
    dy = (d_v * silu).astype(BF)
    s.dy[row] = dy
    s.dz[row] = (d_v * y * gate * (1.0 + z * (1.0 - gate))).astype(BF)
    dy_f = dy.astype(F32)
    gate_term = jnp.sum(d_gated * unit, axis=0, keepdims=True)
    skip_term = jnp.sum(dy_f * u, axis=0, keepdims=True)
    if row:
        gate_term, skip_term = gate_term + s.gate_sum[...], skip_term + s.skip_sum[...]
    s.gate_sum[...] = gate_term
    s.skip_sum[...] = skip_term
    for d in range(2):
        weighed = (expand(s, s.tab[row, 3], d) * dy_f).astype(BF)
        for b in range(blocks):
            at = block_rows(b)
            c_mat = s.xbc[row, at, width + (2 + d) * state : width + (3 + d) * state]
            s.enter[row, b, d] = dot_tn(c_mat, weighed[at])
            s.d_c[row, at, d * state : (d + 1) * state] = dot_nt(
                weighed[at], s.inc[row, b, d].astype(BF)
            )


def branches(s, row):
    s.branch[row] = dot_nt(s.gated[row], flat(s.w_late, slice(s.width, None))).astype(BF)


def turned(s, row):
    s.normed_t[row] = s.normed[row].T


def weight_grad(s, out, lefts, rights, columns=slice(None), product=dot):
    step = 8 * 2 * s.shard if len(out.shape) == 3 else s.model
    for first in range(0, s.model, step):
        total = None
        for left, right in zip(lefts, rights):
            term = product(left(slice(first, first + step)), right(columns))
            total = term if total is None else total + term
        if len(out.shape) == 2:
            out[:, columns] = total.astype(BF)
        else:
            per = out.shape[1]
            out[first // per : (first + step) // per, :, columns] = (
                total.astype(BF).reshape(step // per, per, total.shape[1])
            )


def out_grads(s):
    rows = range(s.rows)
    weight_grad(
        s, s.grad_out, [lambda at, r=r: s.d_out[r, :, at] for r in rows],
        [lambda at, r=r: s.gated[r, :, at] for r in rows], product=dot_tn,
    )


def gate_grads(s):
    rows = range(s.rows)
    weight_grad(
        s, s.grad_gate, [lambda at, r=r: s.normed_t[r, at, HALO:] for r in rows],
        [lambda at, r=r: s.dz[r, :, at] for r in rows],
    )


def pre_grads(s, columns=slice(None)):
    rows = range(s.rows)
    weight_grad(
        s, s.grad_pre, [lambda at, r=r: s.normed_t[r, at] for r in rows],
        [lambda at, r=r: s.d_all[r, :, at] for r in rows], columns,
    )


def inner_back(s, row, block):
    heads, head_dim, state = s.heads, s.head_dim, s.state
    rows = block_rows(block)
    first = block * BLOCK
    parts = (slice(first, first + LANES), slice(first + LANES, first + BLOCK))
    masks = pair_masks(s.base + first, s.starts, row)
    dy_all = s.dy[row, rows].astype(F32)
    along = None
    for d in range(2):
        term = reduce(s, dy_all * s.y[row, d, rows], d, 2)
        along = term if along is None else along + term
        upper = d == 0
        b_mat, c_mat = block_mats(s, row, block, d)
        scores = [a * b for a, b in zip(tiles_nt(b_mat, c_mat, upper), masks[1 - d])]
        d_scores = None
        for pair in range(heads // 2):
            at = slice(pair * LANES, (pair + 1) * LANES)
            grads = halves_of(s.dy[row, rows, at], head_dim)
            d_mixing = pair_nt(s.v[row, d, rows, at], grads, upper)
            mixing = []
            for i in range(2):
                spread = decays_of(s, row, block, d * heads + 2 * pair + i, upper, True)
                mixing.append([(a * b).astype(BF) for a, b in zip(spread, scores)])
                terms = [a * b for a, b in zip(d_mixing[i], spread)]
                d_scores = terms if d_scores is None else [a + b for a, b in zip(d_scores, terms)]
            for part, out in zip(parts, pair_apply(*mixing, grads, upper)):
                s.y[row, d, part, at] = out
        d_scores = [(a * b).astype(BF) for a, b in zip(d_scores, masks[1 - d])]
        d_b = tiles_apply(d_scores, c_mat, upper)
        d_c = tiles_turned(d_scores, b_mat, upper)
        for part, b_part, c_part in zip(parts, d_b, d_c):
            s.dbc[row, part, d * state : (d + 1) * state] = b_part
            s.dbc[row, part, (2 + d) * state : (3 + d) * state] = (
                c_part + s.d_c[row, part, d * state : (d + 1) * state]
            )
    s.along[row, rows] = along


def back(s, row):
    heads, head_dim, state, width, span = s.heads, s.head_dim, s.state, s.width, s.span
    conv_width, conv_len, blocks = s.conv_width, s.conv_len, s.blocks
    forward = lax.broadcasted_iota(jnp.int32, (1, LANES), 1) < heads
    rate = jnp.exp(s.a_log_c[...])
    rows = lax.broadcasted_iota(jnp.int32, (BLOCK, 1), 0)
    row_id = lax.broadcasted_iota(jnp.int32, (8, width), 0)
    if row == 0:
        s.pad[0:HALO] = jnp.zeros((HALO, conv_width), F32)
        s.pad[HALO + span :] = jnp.zeros((s.pad.shape[0] - HALO - span, conv_width), F32)
    u = s.xbc[row, :, :width].astype(F32)
    step, tail, reach = s.tab[row, 0], s.tab[row, 2], s.tab[row, 3]
    d_u = s.skip_c[...] * s.dy[row].astype(F32)
    through, direct = None, None
    ended = [None] * blocks
    d_bc = []
    for d in range(2):
        v_d = s.v[row, d].astype(F32)
        leave = [s.leaving[row, b, d].astype(BF) for b in range(blocks)]
        tail_wide = expand(s, tail, d)
        tailed = (tail_wide * v_d).astype(BF)
        held = []
        for b in range(blocks):
            b_mat = s.xbc[row, block_rows(b), width + d * state : width + (d + 1) * state]
            held.append(dot(b_mat, leave[b]))
        dv_state = tail_wide * jnp.concatenate(held, axis=0)
        dv_all = s.y[row, d] + dv_state
        d_bc.append(
            jnp.concatenate([dot_nt(tailed[block_rows(b)], leave[b]) for b in range(blocks)], axis=0)
        )
        d_u = d_u + expand(s, step, d) * dv_all
        passed = v_d * dv_state
        for b in range(blocks):
            sides = jnp.where(
                row_id == 0,
                jnp.sum(passed[block_rows(b)], axis=0, keepdims=True),
                jnp.sum(s.leaving[row, b, d] * s.inc[row, b, d], axis=0, keepdims=True),
            )
            term = reduce(s, sides, d, 3)
            ended[b] = term if d == 0 else ended[b] + term
        terms = reduce(s, v_d * dv_all, d, 2), reduce(s, u * dv_all, d, 2)
        if d == 0:
            through, direct = terms
        else:
            through, direct = through + terms[0], direct + terms[1]
    ends = []
    for b in range(blocks):
        reach_b = reach[block_rows(b)]
        final = jnp.where(forward, reach_b[BLOCK - 1 : BLOCK], reach_b[0:1])
        at_end = jnp.where(
            forward, (rows == BLOCK - 1).astype(F32), (rows == 0).astype(F32)
        )
        ends.append(at_end * (ended[b][0:1] + ended[b][1:2] * final))
    d_cum = s.along[row] - through + jnp.concatenate(ends, axis=0)
    d_logs = jnp.concatenate(
        [jnp.where(forward, from_end, from_start) for from_start, from_end in running(s, d_cum)],
        axis=0,
    )
    d_raw = (direct - rate * d_logs) * s.tab[row, 4]
    s.d_all[row, HALO:, conv_width:] = d_raw.astype(BF)
    d_bias = jnp.sum(d_raw, axis=0, keepdims=True)
    d_rate = jnp.sum(-step * rate * d_logs, axis=0, keepdims=True)
    inside = slice(HALO, HALO + span)
    s.pad[inside, 0:width] = d_u * s.dsil[row, :, 0:width]
    s.pad[inside, width : width + 2 * state] = (
        s.dbc[row, :, : 2 * state] + jnp.concatenate(d_bc, axis=1)
    ) * s.dsil[row, :, width : width + 2 * state]
    s.pad[inside, width + 2 * state :] = (
        s.dbc[row, :, 2 * state :] * s.dsil[row, :, width + 2 * state :]
    )
    s.d_all[row, 0:HALO, conv_width:] = jnp.zeros((HALO, LANES), BF)
    s.pre_f[...] = s.pre[row].astype(F32)
    places = column_places(span, s.base)
    doc = doc_of(places, s.starts, row)
    outs = s.pad[HALO : HALO + span]
    conv_b_term = jnp.sum(outs, axis=0, keepdims=True)
    ext_places = column_places(HALO + span, s.base - HALO)
    ext_doc = doc_of(ext_places, s.starts, row)
    d_pre = None
    conv_w_terms = []
    for k in range(conv_len):
        ahead = conv_len - 1 - k
        ok = (doc_of(places - ahead, s.starts, row) == doc).astype(F32)
        conv_w_terms.append(
            jnp.sum(
                outs * ok * s.pre_f[HALO - ahead : HALO - ahead + span], axis=0, keepdims=True
            )
        )
        ok_ext = (doc_of(ext_places + ahead, s.starts, row) == ext_doc).astype(F32)
        term = s.pad[ahead : ahead + HALO + span] * ok_ext * s.conv_w_c[k : k + 1]
        d_pre = term if d_pre is None else d_pre + term
    s.d_all[row, :, 0:conv_width] = d_pre.astype(BF)
    conv_w_term = jnp.concatenate(conv_w_terms, axis=0)
    small_term = jnp.concatenate([d_bias, d_rate], axis=0)
    if row:
        conv_w_term = conv_w_term + s.sum_conv_w[...]
        conv_b_term = conv_b_term + s.sum_conv_b[...]
        small_term = small_term + s.small[0:2]
    s.sum_conv_w[...] = conv_w_term
    s.sum_conv_b[...] = conv_b_term
    s.small[0:2] = small_term


def d_norms(s, row):
    dn = dot_nt(s.d_all[row], flat(s.w_pre))
    s.dn[row, 0:HALO] = dn[0:HALO].astype(BF)
    s.dn[row, HALO:] = (
        dn[HALO:] + dot_nt(s.dz[row], flat(s.w_late, slice(0, s.width)))
    ).astype(BF)


def finish(s, row):
    half = s.half
    x = s.tokens[row].astype(F32)
    places = column_places(half, s.base + s.core * half)
    valid = (places < s.row_len - s.pad_len[row]).astype(F32)
    keep = pl.ds(pl.multiple_of(s.core * half, HALO), half)
    s.mixed[row] = (
        x + valid * (s.branch[row, keep].astype(F32) + s.branch_other[row].astype(F32))
    ).astype(BF)
    keep = pl.ds(pl.multiple_of(HALO + s.core * half, HALO), half)
    s.ds[...] = s.dn[row, keep].astype(F32) + s.dn_other[row].astype(F32)
    takes = ((s.core == 1) & (s.place + 1 < s.count)).astype(F32)
    s.ds[half - HALO :] += takes * (s.rims[0, row].astype(F32) + s.rims[1, row].astype(F32))
    d_normed = s.ds[...]
    scale = lax.rsqrt(jnp.mean(x * x, axis=-1, keepdims=True) + EPSILON)
    weighed = d_normed * s.norm_gain[...][None]
    along = jnp.mean(weighed * x, axis=-1, keepdims=True)
    dx = scale * weighed - x * (scale * scale * scale * along)
    s.tokens_grad[row] = (s.cot[row].astype(F32) + dx).astype(BF)
    term = jnp.sum(d_normed * x * scale, axis=0, keepdims=True)
    s.gain_sum[...] = term if row == 0 else s.gain_sum[...] + term


MESH = pl.DeviceIdType.MESH


def remote(src, dst, send_sem, recv_sem, device):
    return pltpu.make_async_remote_copy(
        src_ref=src, dst_ref=dst, send_sem=send_sem, recv_sem=recv_sem, device_id=device,
        device_id_type=MESH,
    )


class Sender:
    def __init__(self, send_sems, recv_sems):
        self.send_sems, self.recv_sems = send_sems, recv_sems
        self.sent = 0
        self.slots = 0
        self.pending = []

    def slot(self, count=1):
        self.slots += count
        return self.slots - count

    def send(self, src, dst, slot, device):
        copy = remote(src, dst, self.send_sems.at[self.sent], self.recv_sems.at[slot], device)
        self.sent += 1
        copy.start()
        self.pending.append(copy)

    def arrive(self, dst, slot, device):
        remote(dst, dst, self.send_sems.at[0], self.recv_sems.at[slot], device).wait_recv()

    def drain(self):
        for copy in self.pending:
            copy.wait_send()
        self.pending = []


class Place:
    def __init__(self, count):
        self.dp, self.seq, self.dir = (lax.axis_index(a) for a in ("dp", "seq", "dir"))
        self.count = count
        self.side = self.dp + 1 - 2 * (self.dp % 2)
        self.below = (self.dp + 2) % 4
        self.across = 3 - self.dp
        self.me = (self.dp, self.seq, self.dir)
        self.sibling = (self.dp, self.seq, 1 - self.dir)
        self.by_x = (self.side, self.seq, self.dir)
        self.by_y = (self.below, self.seq, self.dir)

    def along(self, k, crossed=False):
        core = 1 - self.dir if crossed else self.dir
        return (self.dp, (self.seq + k + self.count) % self.count, core)

    def at(self, k):
        return (self.seq + k + self.count) % self.count

    def chip(self, dp, k=0):
        return dp * self.count + self.at(k)

    def meet(self):
        barrier = pltpu.get_barrier_semaphore()
        others = [self.sibling, self.by_x, self.by_y]
        others += [self.along(k) for k in range(1, self.count)]
        others += [self.along(1, True), self.along(-1, True)]
        for device in others:
            pl.semaphore_signal(barrier, inc=1, device_id=device, device_id_type=MESH)
        pl.semaphore_wait(barrier, len(others))


class Spread:
    def __init__(self, place, sender, slab, cut):
        self.place, self.sender, self.slab, self.cut = place, sender, slab, cut
        count = place.count
        self.z, self.x, self.y, self.xd, self.yd = (sender.slot(count) for _ in range(5))
        self.hops = []
        z = place.seq
        low = (3 * count - 2 - 2 * z) // (2 * count)
        near = low * z + (1 - low) * (count - 1 - z)
        self.order = [(z, None)]
        for i in range(1, count):
            paired = (2 * near - i + 4 * count) // (4 * count)
            far = paired * ((i + 1) // 2) + (1 - paired) * (i - near)
            side = paired * (1 - 2 * (i % 2)) + (1 - paired) * (2 * low - 1)
            self.order.append((z + side * far, side))

    def block(self, dp, source):
        return self.slab.at[dp * self.place.count + source]

    def hop(self, source, step):
        here, to = self.place, self.sender
        spot = self.block(here.dp, source)
        sem = to.sent
        to.sent += 1
        there = here.seq + step
        copy = lambda: remote(
            spot, spot, to.send_sems.at[sem], to.recv_sems.at[self.z + source],
            (here.dp, there, here.dir),
        )
        inside = (there >= 0) & (there < here.count)

        @pl.when(inside)
        def _():
            copy().start()

        self.hops.append((inside, copy))

    def start_z(self):
        z = self.place.seq
        self.hop(z, 1)
        self.hop(z, -1)

    def both(self, source):
        here, to = self.place, self.sender
        spot = self.block(here.dp, source)
        to.send(spot, spot, self.x + source, here.by_x)
        to.send(spot, spot, self.y + source, here.by_y)

    def start_xy(self):
        self.both(self.place.seq)

    def relay(self, i):
        here, to = self.place, self.sender
        source, side = self.order[i]
        to.arrive(self.block(here.dp, source), self.z + source, here.by_x)
        self.hop(source, -side)
        self.both(source)

    def cross(self, i):
        here, to = self.place, self.sender
        source = self.order[i][0]
        from_x = self.block(here.side, source)
        to.arrive(from_x, self.x + source, here.by_x)
        part = from_x.at[:, : self.cut]
        to.send(part, part, self.yd + source, here.by_y)
        from_y = self.block(here.below, source)
        to.arrive(from_y, self.y + source, here.by_y)
        part = from_y.at[:, self.cut :]
        to.send(part, part, self.xd + source, here.by_x)

    def end(self, i):
        here, to = self.place, self.sender
        source = self.order[i][0]
        spot = self.block(here.across, source)
        to.arrive(spot.at[:, : self.cut], self.yd + source, here.by_y)
        to.arrive(spot.at[:, self.cut :], self.xd + source, here.by_x)

    def drain(self):
        for inside, copy in self.hops:
            @pl.when(inside)
            def _():
                copy().wait_send()


class Reduce:
    def __init__(self, place, sender, grad, cut, first, second, third, out_second, out_third, total):
        self.place, self.sender, self.grad, self.cut = place, sender, grad, cut
        self.first, self.second, self.third = first, second, third
        self.out_second, self.out_third, self.total = out_second, out_third, total
        count = place.count
        self.one = [[[sender.slot() for _ in range(count)] for _ in range(2)] for _ in range(2)]
        self.two = [[sender.slot() for _ in range(count)] for _ in range(2)]
        self.three = [None] + [sender.slot() for _ in range(1, count)]
        self.sides = (slice(0, cut), slice(cut, grad.shape[2]))

    def start(self, k, sides=(0, 1)):
        here, to = self.place, self.sender
        for side, device, targets in (
            (0, here.by_x, (here.side, here.across)),
            (1, here.by_y, (here.below, here.across)),
        ):
            if side not in sides:
                continue
            at = self.sides[side]
            for q in (1, 0):
                to.send(
                    self.grad.at[here.chip(targets[q], k), :, at],
                    self.first.at[q, k, :, at],
                    self.one[side][q][k], device,
                )

    def pass_on(self, k):
        here, to = self.place, self.sender
        for side, came, device, target in (
            (0, here.by_x, here.by_y, here.below),
            (1, here.by_y, here.by_x, here.side),
        ):
            at = self.sides[side]
            to.arrive(self.first.at[1, k, :, at], self.one[side][1][k], came)
            self.out_second[k, :, at] = (
                self.grad[here.chip(target, k), :, at].astype(F32)
                + self.first[1, k, :, at].astype(F32)
            ).astype(BF)
            to.send(self.out_second.at[k, :, at], self.second.at[k, :, at], self.two[side][k], device)

    def along(self, k):
        here, to = self.place, self.sender
        for side, came, then in ((0, here.by_x, here.by_y), (1, here.by_y, here.by_x)):
            at = self.sides[side]
            to.arrive(self.first.at[0, k, :, at], self.one[side][0][k], came)
            to.arrive(self.second.at[k, :, at], self.two[side][k], then)
            summed = (
                self.grad[here.chip(here.dp, k), :, at].astype(F32)
                + self.first[0, k, :, at].astype(F32)
                + self.second[k, :, at].astype(F32)
            )
            if k == 0:
                self.total[:, at] = summed
            else:
                self.out_third[k - 1, :, at] = summed.astype(BF)
        if k:
            to.send(self.out_third.at[k - 1], self.third.at[k - 1], self.three[k], here.along(k))

    def end(self):
        here, to = self.place, self.sender
        for k in range(1, here.count):
            to.arrive(self.third.at[k - 1], self.three[k], here.along(-k))
            self.total[...] += self.third[k - 1].astype(F32)


def fill_columns(s, core, pre, late):
    width, heads, conv_width = s.width, s.heads, s.conv_width
    late_side = core == 1
    pick = lambda ref, at: jnp.where(
        late_side, ref[:, at + width : at + 2 * width], ref[:, at : at + width]
    )
    source = lax.broadcasted_iota(jnp.int32, (4 * heads, LANES), 0)
    lane = lax.broadcasted_iota(jnp.int32, (4 * heads, LANES), 1)
    column = jnp.where(lane < heads, lane, lane + heads) + core * heads
    ones = jnp.where((source == column) & (lane < 2 * heads), 1.0, 0.0).astype(BF)
    pre[:, 0:width] = pick(s.w_in, 2 * width).astype(pre.dtype)
    pre[:, width:conv_width] = s.w_in[:, 4 * width :].astype(pre.dtype)
    pre[:, conv_width:] = dot(s.w_dt[...], ones).astype(pre.dtype)
    late[:, 0:width] = pick(s.w_in, 0).astype(late.dtype)
    late[:, width:] = pick(s.w_out, 0).astype(late.dtype)


class Chain:
    def __init__(self, s, place, sender, upward, terms, out, landed, leaves):
        self.s, self.place, self.sender, self.upward = s, place, sender, upward
        self.terms, self.out, self.landed, self.leaves = terms, out, landed, leaves
        self.slots = [[sender.slot() for _ in range(2)] for _ in range(s.rows)]
        self.sems = [[sender.sent + 2 * row + d for d in range(2)] for row in range(s.rows)]
        sender.sent += 2 * s.rows

    def turn(self, d):
        here = self.place
        return here.seq if self.upward[d] else here.count - 1 - here.seq

    def copy(self, row, d):
        to = self.sender
        return remote(
            self.leaves.at[row, d], self.landed.at[row, d], to.send_sems.at[self.sems[row][d]],
            to.recv_sems.at[self.slots[row][d]], self.place.along(1 if self.upward[d] else -1),
        )

    def step(self, row, at):
        for d in range(2):
            @pl.when(self.turn(d) == at)
            def _():
                if at:
                    self.sender.arrive(
                        self.landed.at[row, d], self.slots[row][d],
                        self.place.along(-1 if self.upward[d] else 1),
                    )
                now = self.landed[row, d].astype(F32)
                now = run_through(self.s, row, d, now, self.terms, self.out, self.upward[d])
                if at < self.place.count - 1:
                    self.leaves[row, d] = now.astype(BF)
                    self.copy(row, d).start()

    def steps(self, level, last=None):
        for now in range(level, (level if last is None else last) + 1):
            for row in range(self.s.rows):
                if 0 <= now - row < self.place.count:
                    self.step(row, now - row)

    def drain(self):
        for row in range(self.s.rows):
            for d in range(2):
                @pl.when(self.turn(d) < self.place.count - 1)
                def _():
                    self.copy(row, d).wait_send()


def everything(sizes, names, *refs):
    s = Refs(sizes, names, refs).where()
    count, rows, half, width, heads = s.count, s.rows, s.half, s.width, s.heads
    conv_width, model, shard = s.conv_width, s.model, s.shard
    here = Place(count)
    to = Sender(s.send_sems, s.recv_sems)
    late_core = here.dir == 1
    brought = [
        pltpu.make_async_copy(source, target, s.own_sems.at[i])
        for i, (source, target) in enumerate(((s.tokens_in, s.tokens), (s.cot_in, s.cot)))
    ]
    for copy in brought:
        copy.start()
    fill_columns(s, 1 - here.dir, s.give_pre, s.give_late)
    s.chain_in[...] = jnp.zeros_like(s.chain_in)
    s.back_chain_in[...] = jnp.zeros_like(s.back_chain_in)
    here.meet()

    pair = [to.slot() for _ in range(5)]
    to.send(s.give_pre, s.got_pre, pair[0], here.sibling)
    brought[0].wait()
    to.send(s.tokens, s.tokens_other, pair[2], here.sibling)
    rim = s.tokens.at[:, pl.ds(half - HALO, HALO)]
    first_rim, second_rim = to.sent, to.sent + 1
    to.sent += 2

    def rims_out():
        return [
            remote(rim, s.halo, s.send_sems.at[sem], s.recv_sems.at[pair[4]], here.along(1, crossed))
            for sem, crossed in ((first_rim, False), (second_rim, True))
        ]

    @pl.when(late_core)
    def _():
        for copy in rims_out():
            copy.start()

    to.send(s.give_late, s.got_late, pair[1], here.sibling)
    brought[1].wait()
    to.send(s.cot, s.cot_other, pair[3], here.sibling)
    fill_columns(s, here.dir, s.pre_mine, s.late_mine)

    def joined(own, got):
        other = got[...].astype(F32)
        own = own[...]
        return jnp.where(
            late_core,
            jnp.concatenate([other, own], axis=0),
            jnp.concatenate([own, other], axis=0),
        ).astype(BF)

    me = here.chip(here.dp)
    spread_pre = Spread(here, to, s.w_pre, s.cuts[0])
    spread_late = Spread(here, to, s.w_late, s.cuts[1])
    to.arrive(s.got_pre, pair[0], here.sibling)
    s.w_pre[me] = joined(s.pre_mine, s.got_pre)
    spread_pre.start_z()
    spread_pre.start_xy()
    to.arrive(s.got_late, pair[1], here.sibling)
    s.w_late[me] = joined(s.late_mine, s.got_late)
    prepare(s)
    to.arrive(s.tokens_other, pair[2], here.sibling)
    to.arrive(s.halo, pair[4], here.along(-1))
    spread_pre.relay(1)
    spread_pre.cross(0)
    for row in range(rows):
        normalise(s, row)
        turned(s, row)
    for k in range(2, count):
        spread_pre.relay(k)
        spread_pre.cross(k - 1)
    spread_late.start_z()
    spread_pre.cross(count - 1)
    spread_late.start_xy()
    spread_late.relay(1)
    for k in range(count):
        spread_pre.end(k)

    states = Chain(s, here, to, (True, False), s.local, s.inc, s.chain_in, s.chain_out)
    front(s, 0)
    states.steps(0)
    spread_late.cross(0)
    spread_late.relay(2)
    for row in range(1, rows):
        front(s, row)
        states.steps(row)
    spread_late.cross(1)
    spread_late.relay(3)
    units = [(row, block) for row in range(rows) for block in range(s.blocks)]
    for i, (row, block) in enumerate(units):
        inner(s, row, block)
        if i == 0:
            spread_late.cross(2)
        if block == s.blocks - 1:
            states.steps(rows + row)
        if i == 2:
            spread_late.cross(3)
    for k in range(count):
        spread_late.end(k)
    to.arrive(s.cot_other, pair[3], here.sibling)
    for row in range(rows):
        gates(s, row)
    states.steps(2 * rows, rows + count)
    sum_slots = [to.slot() for _ in range(rows)]
    for row in range(rows):
        outer(s, row)
        to.send(s.sums.at[row], s.sums_other.at[row], sum_slots[row], here.sibling)

    back_chain = Chain(
        s, here, to, (False, True), s.enter, s.leaving, s.back_chain_in, s.back_chain_out
    )
    for row in range(rows):
        to.arrive(s.sums_other.at[row], sum_slots[row], here.sibling)
        turn(s, row)
        back_chain.steps(row)
    grads = (s.grad_pre, s.grad_gate, s.grad_out)
    reduces = [Reduce(here, to, g, cut, *work) for g, cut, work in zip(grads, s.grad_cuts, s.works)]
    reduce_pre, reduce_late = reduces[0], reduces[1:]
    order = list(range(1, count)) + [0]
    gate_grads(s)
    for k in order[:2]:
        reduces[1].start(k)
    out_grads(s)
    for k in order[:2]:
        reduces[2].start(k)
    back_chain.steps(rows)
    branch_slot, dn_slot, rim_own, rim_cross = (to.slot() for _ in range(4))
    give = pl.multiple_of((1 - here.dir) * half, HALO)
    for i, (row, block) in enumerate(units):
        inner_back(s, row, block)
        if i == 0:
            back_chain.steps(rows + 1)
        if i == 1:
            back_chain.steps(rows + 2, rows + count)
        for reduce in reduce_late:
            if i + 2 < count:
                reduce.start(order[i + 2])
            if 1 <= i <= count:
                reduce.pass_on(order[i - 1])
    back(s, 0)
    for k in order[len(units) + 1 :]:
        for reduce in reduce_late:
            reduce.start(k)
    for k in order[len(units) - 1 :]:
        for reduce in reduce_late:
            reduce.pass_on(k)
    for k in order[:2]:
        for reduce in reduce_late:
            reduce.along(k)
    for row in range(1, rows):
        back(s, row)
    for k in order[2:]:
        for reduce in reduce_late:
            reduce.along(k)
    for side, columns in enumerate(reduce_pre.sides):
        pre_grads(s, columns)
        for k in order[:2]:
            reduce_pre.start(k, (side,))
    for row in range(rows):
        d_norms(s, row)
    to.send(s.dn.at[:, pl.ds(HALO + give, half)], s.dn_other, dn_slot, here.sibling)
    edge = s.dn.at[:, pl.ds(0, HALO)]
    rim_sem = to.sent
    to.sent += 1

    def edge_out(core):
        return remote(
            edge, s.rims.at[core], s.send_sems.at[rim_sem],
            s.recv_sems.at[(rim_cross, rim_own)[core]], here.along(-1, core == 0),
        )

    for core in range(2):
        @pl.when(here.dir == core)
        def _():
            edge_out(core).start()

    for row in range(rows):
        branches(s, row)
    to.send(s.branch.at[:, pl.ds(give, half)], s.branch_other, branch_slot, here.sibling)
    reduce_pre.pass_on(order[0])
    reduce_pre.start(order[2])
    to.arrive(s.branch_other, branch_slot, here.sibling)
    to.arrive(s.dn_other, dn_slot, here.sibling)

    @pl.when(late_core)
    def _():
        to.arrive(s.rims.at[1], rim_own, here.along(1))
        to.arrive(s.rims.at[0], rim_cross, here.along(1, True))

    @pl.when(here.dir == 0)
    def _():
        s.rims[...] = jnp.zeros_like(s.rims)

    for row in range(rows):
        finish(s, row)
    taken = [
        pltpu.make_async_copy(source, target, s.own_sems.at[2 + i])
        for i, (source, target) in enumerate(((s.mixed, s.o_mixed), (s.tokens_grad, s.o_tokens)))
    ]
    for copy in taken:
        copy.start()
    side = conv_width - width
    s.v_own[0:4] = s.sum_conv_w[...]
    s.v_own[4:5] = s.sum_conv_b[...]
    s.v_own[5:6] = jnp.concatenate([s.gate_sum[...], s.small[0:1], s.small[1:2]], axis=1)
    s.v_own[6:7] = jnp.concatenate([s.skip_sum[...], jnp.zeros((1, side), F32)], axis=1)
    s.v_own[7:8] = jnp.concatenate([s.gain_sum[...], jnp.zeros((1, side), F32)], axis=1)
    v_slots = [to.slot() for _ in range(2 + count)]
    to.send(s.v_own, s.v_x.at[0], v_slots[0], here.by_x)
    reduce_pre.pass_on(order[1])
    for k in order[3:]:
        reduce_pre.start(k)
    for reduce in reduce_late:
        reduce.end()
    reduce_pre.along(order[0])
    to.arrive(s.v_x.at[0], v_slots[0], here.by_x)
    s.v_x[1] = s.v_own[...] + s.v_x[0]
    to.send(s.v_x.at[1], s.v_y.at[0], v_slots[1], here.by_y)
    reduce_pre.pass_on(order[2])
    reduce_pre.along(order[1])
    to.arrive(s.v_y.at[0], v_slots[1], here.by_y)
    s.v_y[1] = s.v_x[1] + s.v_y[0]
    for k in range(1, count):
        to.send(s.v_y.at[1], s.v_z.at[k - 1], v_slots[1 + k], here.along(k))
    for k in order[3:]:
        reduce_pre.pass_on(k)
    for k in order[2:]:
        reduce_pre.along(k)
    swaps = []
    others = s.others
    back_rows = pl.ds(pl.multiple_of((1 - here.dir) * shard, 8), shard)
    own_rows = pl.ds(pl.multiple_of(here.dir * shard, 8), shard)
    for i in (1, 2, 0):
        slot = to.slot()
        if i == 0:
            reduce_pre.end()
        to.send(reduces[i].total.at[back_rows], others[i], slot, here.sibling)
        swaps.append((i, slot))
    total = s.v_y[1]
    for k in range(1, count):
        to.arrive(s.v_z.at[k - 1], v_slots[1 + k], here.along(-k))
        total = total + s.v_z[k - 1]
    s.v_x[0] = total
    to.send(s.v_x.at[0], s.v_other, v_slots[1 + count], here.sibling)
    parts = {}
    for i, slot in swaps:
        to.arrive(others[i], slot, here.sibling)
        own, got = reduces[i].total[own_rows], others[i][...]
        parts[i] = (jnp.where(late_core, got, own), jnp.where(late_core, own, got))
    (pre_a, pre_b), (gate_a, gate_b), (out_a, out_b) = (parts[i] for i in range(3))
    s.o_in[:, 0:width] = gate_a
    s.o_in[:, width : 2 * width] = gate_b
    s.o_in[:, 2 * width : 3 * width] = pre_a[:, :width]
    s.o_in[:, 3 * width : 4 * width] = pre_b[:, :width]
    s.o_in[:, 4 * width :] = pre_a[:, width:conv_width] + pre_b[:, width:conv_width]
    s.o_out[:, 0:width] = out_a
    s.o_out[:, width:] = out_b
    s.o_steps[0] = pre_a[:, conv_width:]
    s.o_steps[1] = pre_b[:, conv_width:]
    to.arrive(s.v_other, v_slots[1 + count], here.sibling)
    got = s.v_other[...]
    s.o_small[0] = jnp.where(late_core, got, total)
    s.o_small[1] = jnp.where(late_core, total, got)
    for copy in taken:
        copy.wait()
    to.drain()
    for waiting in (states, spread_pre, spread_late):
        waiting.drain()
    back_chain.drain()

    @pl.when(late_core)
    def _():
        for copy in rims_out():
            copy.wait_send()

    for core in range(2):
        @pl.when(here.dir == core)
        def _():
            edge_out(core).wait_send()

    assert (to.sent, to.slots) == (s.send_sems.shape[0], s.recv_sems.shape[0]), (to.sent, to.slots)


SMEM = pl.BlockSpec(memory_space=pltpu.SMEM)
VMEM = pl.BlockSpec(memory_space=pltpu.VMEM)
ANY = pl.BlockSpec(memory_space=pl.ANY)


def call(body, ins, specs, out_shapes, scratch, name, collective_id=None, out_specs=None):
    return pl.pallas_call(
        body,
        out_shape=out_shapes,
        in_specs=specs,
        out_specs=out_specs or [VMEM] * len(out_shapes),
        scratch_shapes=scratch,
        compiler_params=pltpu.CompilerParams(
            vmem_limit_bytes=VMEM_BYTES, collective_id=collective_id,
            has_side_effects=collective_id is not None,
        ),
        name=name,
    )(*ins)


def shape_of(dtype, *dims):
    return jax.ShapeDtypeStruct(dims, dtype)


def buffers(z):
    rows, span, half, model, width, state = z[N.rows], z[N.span], z[N.half], z[N.model], z[N.width], z[N.state]
    blocks, conv_width, pre_width, count = z[N.blocks], z[N.conv_width], z[N.pre_width], z[N.count]
    ext, conv_len, heads = HALO + span, z[N.conv_len], z[N.heads]
    packed = 2 * heads + (-2 * heads) % 8
    carried = (state + CARRY, width)
    table = dict(
        conv_w_c=(F32, conv_len, conv_width), conv_b_c=(F32, 1, conv_width), bias_c=(F32, 1, LANES),
        a_log_c=(F32, 1, LANES), skip_c=(F32, 1, width), gate_gain_c=(F32, 1, width),
        gain_c=(F32, 1, model), halo=(BF, rows, HALO, model), tokens_other=(BF, rows, half, model),
        cot_other=(BF, rows, half, model), normed=(BF, rows, ext, model),
        pre=(BF, rows, ext, conv_width), pre_f=(F32, ext, conv_width),
        xbc=(BF, rows, span, conv_width), dsil=(F32, rows, span, conv_width),
        tab=(F32, rows, 5, span, LANES), cumt=(F32, rows, blocks, packed, BLOCK),
        v=(BF, rows, 2, span, width), local=(F32, rows, blocks, 2, state, width),
        decay=(F32, rows, blocks, 2, 8, width), send=(BF, 2, rows) + carried,
        received=(BF, count - 1, rows) + carried, y=(F32, rows, 2, span, width),
        inc=(F32, rows, blocks, 2, state, width), sums=(F32, rows, span, LANES),
        sums_other=(F32, rows, span, LANES), z=(F32, rows, span, width), dg=(F32, rows, span, width),
        d_out=(BF, rows, span, model), normed_t=(BF, rows, model, ext), gated=(BF, rows, span, width), dy=(BF, rows, span, width),
        dz=(BF, rows, span, width), enter=(F32, rows, blocks, 2, state, width),
        back_send=(BF, 2, rows) + carried, back_received=(BF, count - 1, rows) + carried,
        maps=(BF, 2, 2 * LANES, width), tri=(BF, 2 * BLOCK, BLOCK), d_c=(F32, rows, span, 2 * state),
        leaving=(F32, rows, blocks, 2, state, width), branch=(BF, rows, span, model), grad_out=(BF, model, width), grad_gate=(BF, model, width),
        gate_sum=(F32, 1, width), skip_sum=(F32, 1, width), dbc=(F32, rows, span, 4 * state),
        along=(F32, rows, span, LANES), pad=(F32, ext + 8, conv_width),
        d_all=(BF, rows, ext, pre_width), grad_pre=(BF, model, pre_width),
        sum_conv_w=(F32, conv_len, conv_width), sum_conv_b=(F32, 1, conv_width), small=(F32, 8, LANES),
        dn=(BF, rows, ext, model), branch_other=(BF, rows, half, model),
        dn_other=(BF, rows, half, model), rims=(BF, 2, rows, HALO, model), ds=(F32, half, model),
        gain_sum=(F32, 1, model), mixed=(BF, rows, half, model), tokens_grad=(BF, rows, half, model),
    )
    return {name: shape_of(*shape) for name, shape in table.items()}


def together(z, args):
    count, shard, width, conv_width = z[N.count], z[N.shard], z[N.width], z[N.conv_width]
    pre_width, model, rows, half, heads = z[N.pre_width], z[N.model], z[N.rows], z[N.half], z[N.heads]
    chips, pair = 4 * count, 2 * shard
    table = buffers(z)
    for name in (N.grad_out, N.grad_gate, N.grad_pre):
        table[name] = shape_of(BF, chips, pair, table[name].shape[1])
    outs = dict(
        o_mixed=table[N.mixed], o_tokens=table[N.tokens_grad],
        o_in=shape_of(F32, shard, 4 * width + 4 * z[N.state]), o_out=shape_of(F32, shard, 2 * width),
        o_steps=shape_of(F32, 2, shard, LANES), o_small=shape_of(F32, 2, 8, conv_width),
    )
    args = dict(args, tokens_in=args[N.tokens], cot_in=args[N.cot])
    for name in (N.tokens, N.cot):
        value = args.pop(name)
        table[name] = shape_of(value.dtype, *value.shape)
    for name in (N.send, N.received, N.back_send, N.back_received):
        table.pop(name)
    aliases = {N.inc: N.local, N.leaving: N.enter}
    views = {
        N.dbc: (N.z, 0, 4 * z[N.state]), N.along: (N.z, 4 * z[N.state], LANES),
        N.d_c: (N.dg, 0, 2 * z[N.state]),
    }
    scratch = {
        name: pltpu.VMEM(value.shape, value.dtype)
        for name, value in table.items() if name not in aliases and name not in views
    }
    scratch.update(
        w_pre=pltpu.VMEM((chips, pair, pre_width), BF), w_late=pltpu.VMEM((chips, pair, 2 * width), BF),
        give_pre=pltpu.VMEM((shard, pre_width), BF), give_late=pltpu.VMEM((shard, 2 * width), BF),
        got_pre=pltpu.VMEM((shard, pre_width), BF), got_late=pltpu.VMEM((shard, 2 * width), BF),
        pre_mine=pltpu.VMEM((shard, pre_width), F32), late_mine=pltpu.VMEM((shard, 2 * width), F32),
        **{
            name: pltpu.VMEM((rows, 2, z[N.state], width), BF)
            for name in (N.chain_in, N.chain_out, N.back_chain_in, N.back_chain_out)
        },
        v_own=pltpu.VMEM((8, conv_width), F32), v_x=pltpu.VMEM((2, 8, conv_width), F32),
        v_y=pltpu.VMEM((2, 8, conv_width), F32), v_z=pltpu.VMEM((count - 1, 8, conv_width), F32),
        v_other=pltpu.VMEM((8, conv_width), F32),
    )
    widths = dict(pre=pre_width, gate=width, out=width)
    work_names = []
    for name, size in widths.items():
        scratch[name, -1] = pltpu.VMEM((shard, size), F32)
        for i, shape in enumerate(
            ((2, count, pair), (count, pair), (count - 1, pair), (count, pair), (count - 1, pair))
        ):
            scratch[name, i] = pltpu.VMEM(shape + (size,), BF)
        scratch[name, 5] = pltpu.VMEM((pair, size), F32)
        work_names.append([(name, i) for i in range(6)])
    sent, landed = 32 * count + 13 + 5 * rows, 32 * count + 11 + 5 * rows
    scratch[N.own_sems] = pltpu.SemaphoreType.DMA((4,))
    scratch[N.send_sems] = pltpu.SemaphoreType.DMA((sent,))
    scratch[N.recv_sems] = pltpu.SemaphoreType.DMA((landed,))
    in_names = list(args)
    names = in_names + list(outs) + list(scratch)
    cut = pre_width // 256 * 128 + 128

    def body(*refs):
        sizes = dict(z, cuts=(cut, width), grad_cuts=(cut, width // 2, width // 2))
        by_name = dict(zip(names, refs))
        for name, of in aliases.items():
            by_name[name] = by_name[of]
        for name, (of, first, lanes) in views.items():
            by_name[name] = by_name[of].at[:, :, pl.ds(first, lanes)]
        sizes[N.works] = [[by_name[n] for n in group] for group in work_names]
        sizes[N.others] = [by_name[name, -1] for name in widths]
        plain = {name: ref for name, ref in by_name.items() if isinstance(name, str)}
        everything(sizes, list(plain), *plain.values())

    places = {N.starts: SMEM, N.pad_len: SMEM, N.tokens_in: ANY, N.cot_in: ANY}
    specs = [places.get(name, VMEM) for name in in_names]
    out = call(
        body, list(args.values()), specs, list(outs.values()), list(scratch.values()), N.layer, 0,
        [ANY, ANY] + [VMEM] * (len(outs) - 2),
    )
    return delivered(z, out)


def deliver(z, mixed, tokens_grad, d_in, d_out, parts, small, o_mixed, o_tokens, o_in, o_out, o_norm,
            o_dt, o_conv_w, o_conv_b, o_bias, o_alog, o_skip, o_gate):
    heads, width = z[N.heads], z[N.width]
    for source, target in ((mixed, o_mixed), (tokens_grad, o_tokens), (d_in, o_in), (d_out, o_out)):
        target[...] = source[...]
    lane = lax.broadcasted_iota(jnp.int32, (LANES, 4 * heads), 0)
    column = lax.broadcasted_iota(jnp.int32, (LANES, 4 * heads), 1)
    first_lane = jnp.where(lane < heads, lane, jnp.where(lane < 2 * heads, lane + heads, -1))
    picks = [
        jnp.where((first_lane >= 0) & (column == first_lane + side_of * heads), 1.0, 0.0).astype(BF)
        for side_of in range(2)
    ]
    by_step = lambda a, b: exact(dot, a, picks[0], 3) + exact(dot, b, picks[1], 3)
    o_dt[...] = by_step(parts[0], parts[1])
    v_a, v_b = small[0], small[1]
    both = v_a + v_b
    o_conv_w[:, 0:width] = v_a[0:4, :width]
    o_conv_w[:, width : 2 * width] = v_b[0:4, :width]
    o_conv_w[:, 2 * width :] = both[0:4, width:]
    o_conv_b[...] = jnp.concatenate([v_a[4:5, :width], v_b[4:5, :width], both[4:5, width:]], axis=1)[0]
    o_gate[...] = jnp.concatenate([v_a[5:6, :width], v_b[5:6, :width]], axis=1)[0]
    steps = by_step(
        jnp.concatenate([v_a[5:6, width : width + LANES], v_a[5:6, width + LANES : width + 2 * LANES]] * 4, axis=0),
        jnp.concatenate([v_b[5:6, width : width + LANES], v_b[5:6, width + LANES : width + 2 * LANES]] * 4, axis=0),
    )
    o_bias[...] = steps[0]
    o_alog[...] = steps[1]
    head = lax.broadcasted_iota(jnp.int32, (width, 2 * heads), 1)
    channel = lax.broadcasted_iota(jnp.int32, (width, 2 * heads), 0) // z[N.head_dim]
    skips = None
    for side_of, v_side in ((0, v_a), (1, v_b)):
        ones = jnp.where(head == channel + side_of * heads, 1.0, 0.0).astype(BF)
        term = exact(dot, jnp.broadcast_to(v_side[6:7, :width], (8, width)), ones, 3)
        skips = term if skips is None else skips + term
    o_skip[...] = skips[0]
    o_norm[...] = both[7:8, : z[N.model]][0]


def delivered(z, arrays):
    heads, width, conv_width = z[N.heads], z[N.width], z[N.conv_width]
    outs = dict(
        mixed=arrays[0], tokens_grad=arrays[1], o_in=arrays[2], o_out=arrays[3],
        o_norm=shape_of(F32, z[N.model]), o_dt=shape_of(F32, z[N.shard], 4 * heads),
        o_conv_w=shape_of(F32, z[N.conv_len], conv_width + width),
        o_conv_b=shape_of(F32, conv_width + width), o_bias=shape_of(F32, 4 * heads),
        o_alog=shape_of(F32, 4 * heads), o_skip=shape_of(F32, 2 * heads),
        o_gate=shape_of(F32, 2 * width),
    )
    results = call(
        lambda *refs: deliver(z, *refs), arrays, [VMEM] * len(arrays),
        [shape_of(a.dtype, *a.shape) for a in outs.values()], (), N.deliver,
    )
    return dict(zip(outs, results))


def swapped(value):
    return lax.ppermute(value, "dir", [(0, 1), (1, 0)])


def rotated_to(value, steps, cross):
    count = lax.axis_size("seq")
    pairs = []
    for i in range(count):
        for c in range(2):
            pairs.append((i * 2 + c, (i + steps) % count * 2 + (1 - c if cross else c)))
    return lax.ppermute(value, ("seq", "dir"), pairs)


def around(value):
    count, place = lax.axis_size("seq"), lax.axis_index("seq")
    out = []
    for k in range(1, count):
        chosen = jnp.where(place + k < count, value[0], value[1])
        out.append(rotated_to(chosen, k, False))
    return jnp.stack(out)


def stage(z, have, phase, ins, outs, scratch=(), units=None):
    table = buffers(z)
    ins = [N.starts, N.pad_len] + list(ins)
    names = ins + list(outs) + list(scratch)
    units = [(row,) for row in range(z[N.rows])] if units is None else units

    def body(*refs):
        s = Refs(z, names, refs).where()
        for unit in units:
            phase(s, *unit)

    results = call(
        body, [have[name] for name in ins],
        [SMEM if name in (N.starts, N.pad_len) else VMEM for name in ins],
        [table[name] for name in outs],
        [pltpu.VMEM(table[name].shape, table[name].dtype) for name in scratch],
        phase.__name__,
    )
    have.update(zip(outs, results))


def apart(z, args):
    heads, width, conv_width, count = z[N.heads], z[N.width], z[N.conv_width], z[N.count]
    half, shard = z[N.half], z[N.shard]
    have = dict(args)
    core = lax.axis_index("dir")
    is_late = core == 1
    w_in, w_dt, w_out, tokens = (args[n] for n in (N.w_in, N.w_dt, N.w_out, N.tokens))
    pad_dt = jnp.zeros((shard, LANES - 2 * heads), BF)

    def columns(c):
        own = slice(c * width, (c + 1) * width)
        return (
            jnp.concatenate(
                [
                    w_in[:, 2 * width :][:, own], w_in[:, 4 * width :],
                    w_dt[:, c * heads : (c + 1) * heads],
                    w_dt[:, (2 + c) * heads : (3 + c) * heads], pad_dt,
                ],
                axis=1,
            ),
            jnp.concatenate([w_in[:, own], w_out[:, own]], axis=1),
        )

    def ordered(own, other, axis):
        return jnp.where(
            is_late, jnp.concatenate([other, own], axis=axis), jnp.concatenate([own, other], axis=axis)
        )

    first, latter = columns(0), columns(1)

    def gathered(i):
        keep = jnp.where(is_late, latter[i], first[i])
        give = swapped(jnp.where(is_late, first[i], latter[i]))
        return lax.all_gather(ordered(keep, give, 0), ("dp", "seq"), axis=0, tiled=True)

    have[N.w_pre], have[N.w_late] = gathered(0), gathered(1)
    have[N.tokens_other], have[N.cot_other] = swapped(tokens), swapped(args[N.cot])
    rim = tokens[:, half - HALO :]
    have[N.halo] = jnp.where(is_late, rotated_to(rim, 1, False), rotated_to(rim, 1, True))
    small = [N.conv_w_c, N.conv_b_c, N.bias_c, N.a_log_c, N.skip_c, N.gate_gain_c, N.gain_c, N.maps, N.tri]
    stage(
        z, have, prepare,
        [N.conv_w, N.conv_b, N.dt_bias, N.a_log, N.skip, N.gate_gain, N.norm_gain], small, units=[()],
    )
    stage(z, have, normalise, [N.gain_c, N.halo, N.tokens, N.tokens_other], [N.normed])
    have[N.normed_t] = jnp.swapaxes(have[N.normed], 1, 2)
    stage(
        z, have, front, [N.normed, N.w_pre, N.conv_w_c, N.conv_b_c, N.bias_c, N.a_log_c, N.maps, N.tri],
        [N.pre, N.xbc, N.dsil, N.tab, N.cumt, N.v, N.local, N.decay], [N.pre_f],
    )
    stage(z, have, sent_states, [N.local, N.decay], [N.send])
    have[N.received] = around(have[N.send])
    stage(z, have, received_states, [N.received, N.local, N.decay], [N.inc])
    units = [(row, block) for row in range(z[N.rows]) for block in range(z[N.blocks])]

    def forward(s):
        for unit in units:
            inner(s, *unit)
        for row in range(s.rows):
            gates(s, row)
            outer(s, row)

    stage(
        z, have, forward,
        [N.maps, N.xbc, N.tab, N.cumt, N.v, N.inc, N.normed, N.w_late, N.cot,
         N.cot_other, N.skip_c, N.gate_gain_c],
        [N.y, N.d_out, N.sums, N.z, N.dg], units=[()],
    )
    have[N.sums_other] = swapped(have[N.sums])

    def turning(s):
        for row in range(s.rows):
            turn(s, row)
            branches(s, row)
        out_grads(s)
        gate_grads(s)

    stage(
        z, have, turning,
        [N.sums, N.sums_other, N.xbc, N.y, N.z, N.dg, N.tab, N.inc, N.maps, N.skip_c, N.gate_gain_c,
         N.d_out, N.normed_t, N.w_late],
        [N.gated, N.dy, N.dz, N.gate_sum, N.skip_sum, N.enter, N.d_c, N.branch, N.grad_out,
         N.grad_gate],
        units=[()],
    )
    stage(z, have, back_states, [N.enter, N.decay], [N.back_send])
    have[N.back_received] = around(have[N.back_send])
    stage(z, have, returned_states, [N.back_received, N.enter, N.decay], [N.leaving])

    def backward(s):
        for row in range(s.rows):
            for block in range(s.blocks):
                for d in range(2):
                    at = block_rows(block)
                    s.y[row, d, at] = s.y_both[row, d, at]
                inner_back(s, row, block)
            back(s, row)
            d_norms(s, row)
        pre_grads(s)

    have[N.y_both] = have[N.y]
    stage(
        z, have, backward,
        [N.maps, N.tri, N.d_c, N.y_both, N.leaving, N.inc, N.xbc, N.tab, N.cumt, N.v, N.dy, N.dsil, N.pre,
         N.normed_t, N.dz, N.skip_c, N.a_log_c, N.conv_w_c, N.w_pre, N.w_late],
        [N.dn, N.d_all, N.grad_pre, N.sum_conv_w, N.sum_conv_b, N.small],
        [N.y, N.dbc, N.along, N.pad, N.pre_f], units=[()],
    )

    def give(values, first_row):
        return swapped(
            lax.dynamic_slice_in_dim(values, first_row + (1 - core) * half, half, axis=1)
        )

    edge = have[N.dn][:, :HALO]
    have[N.dn_other], have[N.branch_other] = give(have[N.dn], HALO), give(have[N.branch], 0)
    have[N.rims] = jnp.stack([rotated_to(edge, -1, True), rotated_to(edge, -1, False)])
    stage(
        z, have, finish,
        [N.tokens, N.cot, N.norm_gain, N.dn, N.dn_other, N.branch, N.branch_other, N.rims],
        [N.mixed, N.tokens_grad, N.gain_sum], [N.ds],
    )

    def placed(values):
        empty = jnp.zeros_like(values)
        return ordered(values, empty, -1)

    def sided(values):
        return jnp.concatenate([placed(values[:, :width]), values[:, width:]], axis=1)

    def reduced(name):
        value = lax.psum_scatter(have[name], ("dp", "seq"), scatter_dimension=0, tiled=True)
        own = lax.dynamic_slice_in_dim(value, core * shard, shard, axis=0)
        other = swapped(lax.dynamic_slice_in_dim(value, (1 - core) * shard, shard, axis=0))
        own, other = own.astype(F32), other.astype(F32)
        return jnp.where(is_late, other, own), jnp.where(is_late, own, other)

    def by_step(values):
        return jnp.concatenate(
            [placed(values[:, :heads]), placed(values[:, heads : 2 * heads])], axis=1
        )

    steps = by_step(have[N.small][:2])
    skips = placed(jnp.sum(have[N.skip_sum].reshape(1, heads, z[N.head_dim]), axis=-1))
    gain, all_conv_w, all_conv_b, steps, skips, gate_all = lax.psum(
        (
            have[N.gain_sum], sided(have[N.sum_conv_w]), sided(have[N.sum_conv_b]), steps, skips,
            placed(have[N.gate_sum]),
        ),
        ("dp", "seq", "dir"),
    )
    (pre_a, pre_b), (gate_a, gate_b), (out_a, out_b) = (
        reduced(name) for name in (N.grad_pre, N.grad_gate, N.grad_out)
    )
    last = conv_width
    return dict(
        mixed=have[N.mixed], tokens_grad=have[N.tokens_grad], o_norm=gain[0],
        o_in=jnp.concatenate(
            [
                gate_a, gate_b, pre_a[:, :width], pre_b[:, :width],
                pre_a[:, width:conv_width] + pre_b[:, width:conv_width],
            ],
            axis=1,
        ),
        o_dt=jnp.concatenate(
            [
                pre_a[:, last : last + heads], pre_b[:, last : last + heads],
                pre_a[:, last + heads : last + 2 * heads], pre_b[:, last + heads : last + 2 * heads],
            ],
            axis=1,
        ),
        o_conv_w=all_conv_w, o_conv_b=all_conv_b[0], o_bias=steps[0], o_alog=steps[1],
        o_skip=skips[0], o_gate=gate_all[0], o_out=jnp.concatenate([out_a, out_b], axis=1),
    )


def shards(tokens, starts, pad_len, norm_gain, w_in, w_dt, conv_w, conv_b, dt_bias, a_log, skip,
           gate_gain, w_out, cotangent):
    rows, half, model = tokens.shape
    span = 2 * half
    count = lax.axis_size("seq")
    inner_width = gate_gain.shape[0]
    heads = skip.shape[0] // 2
    width = inner_width // 2
    state = (conv_w.shape[1] - inner_width) // 4
    conv_width = width + 4 * state
    shard = w_in.shape[0]
    z = dict(
        rows=rows, half=half, model=model, span=span, count=count, row_len=span * count,
        blocks=span // BLOCK, inner_width=inner_width, heads=heads, head_dim=width // heads,
        width=width, state=state, conv_width=conv_width, conv_len=conv_w.shape[0],
        pre_width=conv_width + LANES, shard=shard,
    )
    args = dict(
        tokens=tokens, starts=starts, pad_len=pad_len, norm_gain=norm_gain, w_in=w_in, w_dt=w_dt,
        conv_w=conv_w, conv_b=conv_b, dt_bias=dt_bias, a_log=a_log, skip=skip, gate_gain=gate_gain,
        w_out=w_out, cot=cotangent,
    )
    direct = lax.axis_size("dp") == 4 and 2 * shard % 16 == 0 and model % (16 * shard) == 0
    out = together(z, args) if direct else apart(z, args)
    order = (
        N.mixed, N.tokens_grad, N.o_norm, N.o_in, N.o_dt, N.o_conv_w, N.o_conv_b, N.o_bias, N.o_alog,
        N.o_skip, N.o_gate, N.o_out,
    )
    return tuple(out[name] for name in order)


def solution(mesh):
    weight = P(("dp", "seq", "dir"), None)
    values = P("dp", ("seq", "dir"), None)
    return jax.shard_map(
        shards,
        mesh=mesh,
        in_specs=(
            values, P("dp", None), P("dp"), P(), weight, weight, P(), P(), P(), P(), P(), P(),
            weight, values,
        ),
        out_specs=(
            values, values, P(), weight, weight, P(), P(), P(), P(), P(), P(), weight,
        ),
        check_vma=False,
    )
```

```python
import jax
import jax.numpy as jnp
from jax import lax
from jax.experimental import pallas as pl
from jax.experimental.pallas import tpu as pltpu
from jax.sharding import PartitionSpec as P

BLOCK = 160
HALO = 16
LANES = 128
CARRY = 16
EPSILON = 1e-05
BF = jnp.bfloat16
F32 = jnp.float32
LOG2E = 1.4426950408889634
VMEM_BYTES = 62 * 1024 * 1024


class Names:
    def __getattr__(self, name):
        return name


N = Names()


def dot(a, b):
    return lax.dot_general(a, b, (((1,), (0,)), ((), ())), preferred_element_type=F32)


def dot_nt(a, b):
    return lax.dot_general(a, b, (((1,), (1,)), ((), ())), preferred_element_type=F32)


def dot_tn(a, b):
    return lax.dot_general(a, b, (((0,), (0,)), ((), ())), preferred_element_type=F32)


def pieces(values, count):
    parts = []
    for _ in range(count - 1):
        part = values.astype(BF)
        parts.append(part)
        values = values - part.astype(F32)
    parts.append(values.astype(BF))
    return parts


def exact(op, values, ones, count):
    total = None
    for part in pieces(values, count):
        term = op(part, ones)
        total = term if total is None else total + term
    return total


def head_map(first, width, head_dim):
    lane = lax.broadcasted_iota(jnp.int32, (LANES, width), 0)
    head = lax.broadcasted_iota(jnp.int32, (LANES, width), 1) // head_dim
    return jnp.where(lane == head + first, 1.0, 0.0).astype(BF)


def expand(s, values, d):
    return dot(jnp.concatenate(pieces(values, 2), axis=1), s.maps[d])


def reduce(s, values, d, count):
    return exact(dot_nt, values, s.maps[d, 0:LANES], count)


def running(s, values):
    parts = pieces(values, 3)
    blocks = range(values.shape[0] // BLOCK)
    wide = jnp.concatenate([part[block_rows(b)] for b in blocks for part in parts], axis=1)
    both = dot(s.tri[...], wide)
    result = []
    for b in blocks:
        first = 3 * b * LANES
        total = (
            both[:, first : first + LANES]
            + both[:, first + LANES : first + 2 * LANES]
            + both[:, first + 2 * LANES : first + 3 * LANES]
        )
        result.append((total[:BLOCK], total[BLOCK:]))
    return result


def doc_of(places, starts_ref, row):
    total = (starts_ref[row, 0] <= places).astype(jnp.int32)
    for j in range(1, starts_ref.shape[1]):
        total = total + (starts_ref[row, j] <= places).astype(jnp.int32)
    return total


def column_places(count, first):
    return lax.broadcasted_iota(jnp.int32, (count, 1), 0) + first


class Refs:
    def __init__(self, sizes, names, refs):
        self.__dict__.update(sizes)
        for name, ref in zip(names, refs):
            setattr(self, name, ref)

    def where(self):
        self.core = lax.axis_index("dir")
        self.place = lax.axis_index("seq")
        self.base = self.place * self.span
        return self


def block_rows(block):
    return slice(block * BLOCK, (block + 1) * BLOCK)


def prepare(s):
    late = s.core == 1
    width, heads = s.width, s.heads

    def mine(values, first, size):
        return jnp.where(
            late, values[:, first + size : first + 2 * size], values[:, first : first + size]
        )

    conv_w = s.conv_w[...]
    s.conv_w_c[:, 0:width] = mine(conv_w, 0, width)
    s.conv_w_c[:, width:] = conv_w[:, 2 * width :]
    conv_b = s.conv_b[...][None]
    s.conv_b_c[:, 0:width] = mine(conv_b, 0, width)
    s.conv_b_c[:, width:] = conv_b[:, 2 * width :]
    s.gate_gain_c[...] = mine(s.gate_gain[...][None], 0, width)
    s.gain_c[...] = s.norm_gain[...][None]
    source = lax.broadcasted_iota(jnp.int32, (4 * heads, LANES), 0)
    lane = lax.broadcasted_iota(jnp.int32, (4 * heads, LANES), 1)
    column = jnp.where(lane < heads, lane, lane + heads) + s.core * heads
    picked = jnp.where((source == column) & (lane < 2 * heads), 1.0, 0.0).astype(BF)
    for ref, out in ((s.dt_bias, s.bias_c), (s.a_log, s.a_log_c)):
        rows = jnp.broadcast_to(ref[...][None], (8, 4 * heads))
        out[...] = exact(dot, rows, picked, 3)[0:1]
    head = lax.broadcasted_iota(jnp.int32, (2 * heads, width), 0)
    channel = lax.broadcasted_iota(jnp.int32, (2 * heads, width), 1) // s.head_dim
    spread = jnp.where(head == channel + s.core * heads, 1.0, 0.0).astype(BF)
    rows = jnp.broadcast_to(s.skip[...][None], (8, 2 * heads))
    s.skip_c[...] = exact(dot, rows, spread, 3)[0:1]
    for d in range(2):
        ones = head_map(d * heads, width, s.head_dim)
        s.maps[d, 0:LANES] = ones
        s.maps[d, LANES:] = ones
    row = lax.broadcasted_iota(jnp.int32, (BLOCK, BLOCK), 0)
    col = lax.broadcasted_iota(jnp.int32, (BLOCK, BLOCK), 1)
    s.tri[0:BLOCK] = jnp.where(row >= col, 1.0, 0.0).astype(BF)
    s.tri[BLOCK:] = jnp.where(row <= col, 1.0, 0.0).astype(BF)


def normalise(s, row):
    def norm(part):
        x = part.astype(F32)
        scale = lax.rsqrt(jnp.mean(x * x, axis=-1, keepdims=True) + EPSILON)
        return (x * scale * s.gain_c[...]).astype(BF)

    half = s.half
    s.normed[row, 0:HALO] = norm(s.halo[row])
    own = pl.multiple_of(HALO + s.core * half, HALO)
    other = pl.multiple_of(HALO + (1 - s.core) * half, HALO)
    s.normed[row, pl.ds(own, half)] = norm(s.tokens[row])
    s.normed[row, pl.ds(other, half)] = norm(s.tokens_other[row])


def front(s, row):
    heads, head_dim, state, width, span = s.heads, s.head_dim, s.state, s.width, s.span
    conv_width = s.conv_width
    projected = dot(s.normed[row], flat(s.w_pre))
    pre = projected[:, :conv_width].astype(BF)
    s.pre[row] = pre
    s.pre_f[...] = pre.astype(F32)
    raw = projected[HALO:, conv_width:].astype(BF).astype(F32)
    places = column_places(span, s.base)
    doc = doc_of(places, s.starts, row)
    valid = (places < s.row_len - s.pad_len[row]).astype(F32)
    summed = s.conv_b_c[...]
    for k in range(s.conv_len):
        back = s.conv_len - 1 - k
        ok = (doc_of(places - back, s.starts, row) == doc).astype(F32)
        summed = summed + s.pre_f[HALO - back : HALO - back + span] * s.conv_w_c[k : k + 1] * ok
    gate = 1.0 / (1.0 + jnp.exp(-summed))
    s.xbc[row] = (summed * gate * valid).astype(BF)
    s.dsil[row] = gate * (1.0 + summed * (1.0 - gate)) * valid
    forward = lax.broadcasted_iota(jnp.int32, (1, LANES), 1) < heads
    shifted_raw = raw + s.bias_c[...]
    step = jnp.maximum(shifted_raw, 0.0) + jnp.log1p(jnp.exp(-jnp.abs(shifted_raw)))
    slope = 1.0 / (1.0 + jnp.exp(-shifted_raw))
    logs = -step * jnp.exp(s.a_log_c[...])
    s.tab[row, 0] = step
    s.tab[row, 4] = slope
    blocks = s.blocks
    sums = running(s, logs)
    for b in range(blocks):
        at = block_rows(b)
        doc_b = doc[at]
        cum = jnp.where(forward, sums[b][0], sums[b][1])
        first_place = s.base + b * BLOCK
        end_f = doc_of(first_place + BLOCK - 1, s.starts, row)
        end_b = doc_of(first_place, s.starts, row)
        near_f = doc_of(first_place - 1, s.starts, row)
        near_b = doc_of(first_place + BLOCK, s.starts, row)
        final = jnp.where(forward, cum[BLOCK - 1 : BLOCK], cum[0:1])
        tail = jnp.exp(final - cum) * (doc_b == jnp.where(forward, end_f, end_b)).astype(F32)
        reach = jnp.exp(cum) * (doc_b == jnp.where(forward, near_f, near_b)).astype(F32)
        scaled = cum * LOG2E
        s.cumt[row, b] = scaled.T[: s.cumt.shape[2]]
        s.tab[row, 1, at] = scaled
        s.tab[row, 2, at] = tail
        s.tab[row, 3, at] = reach
        decay = jnp.broadcast_to(
            jnp.where(forward, reach[BLOCK - 1 : BLOCK], reach[0:1]), (8, LANES)
        )
        for d in range(2):
            s.decay[row, b, d] = exact(dot, decay, s.maps[d, 0:LANES], 3)
    u = s.xbc[row, :, :width].astype(F32)
    for d in range(2):
        stepped = expand(s, step, d) * u
        s.v[row, d] = stepped.astype(BF)
        tailed = (expand(s, s.tab[row, 2], d) * stepped).astype(BF)
        for b in range(blocks):
            at = block_rows(b)
            b_mat = s.xbc[row, at, width + d * state : width + (d + 1) * state]
            s.local[row, b, d] = dot_tn(b_mat, tailed[at])


def flat(ref, columns=slice(None)):
    if len(ref.shape) == 2:
        return ref[:, columns]
    value = ref[:, :, columns]
    return value.reshape(value.shape[0] * value.shape[1], value.shape[2])


def carried_rows(rate):
    coarse = rate.astype(BF)
    fine = (rate - coarse.astype(F32)).astype(BF)
    row = lax.broadcasted_iota(jnp.int32, (CARRY, rate.shape[1]), 0)
    return jnp.where(
        row == 0, coarse.astype(F32), jnp.where(row == 1, fine.astype(F32), 0.0)
    ).astype(BF)


def compose(received, place, count, state, up):
    total, rate = None, None
    for k in range(1, count):
        part = received[(k - 1) if up else (count - k - 1)]
        there = (place - k >= 0) if up else (place + k < count)
        there = there.astype(F32)
        term = part[0:state].astype(F32) * there
        total = term if total is None else total + rate * term
        hop = part[state : state + 1].astype(F32) + part[state + 1 : state + 2].astype(F32)
        rate = hop if rate is None else rate * hop
    return total


def run_through(s, row, d, now, terms, out, upward):
    for b in range(s.blocks) if upward else reversed(range(s.blocks)):
        here = terms[row, b, d]
        out[row, b, d] = now
        now = s.decay[row, b, d, 0:1] * now + here
    return now


def summarise(s, row, terms, send, downward):
    for d in range(2):
        upward = (d == 0) != downward
        total, rate = None, None
        for b in range(s.blocks) if upward else reversed(range(s.blocks)):
            own = s.decay[row, b, d, 0:1]
            total = terms[row, b, d] if total is None else own * total + terms[row, b, d]
            rate = own if rate is None else rate * own
        send[0 if upward else 1, row, 0 : s.state] = total.astype(BF)
        send[0 if upward else 1, row, s.state :] = carried_rows(rate)


def sent_states(s, row):
    summarise(s, row, s.local, s.send, False)


def back_states(s, row):
    summarise(s, row, s.enter, s.back_send, True)


def received_states(s, row):
    parts = [s.received[k, row] for k in range(s.count - 1)]
    for d in range(2):
        now = compose(parts, s.place, s.count, s.state, d == 0)
        run_through(s, row, d, now, s.local, s.inc, d == 0)


def returned_states(s, row):
    parts = [s.back_received[k, row] for k in range(s.count - 1)]
    for d in range(2):
        now = compose(parts, s.place, s.count, s.state, d == 1)
        run_through(s, row, d, now, s.enter, s.leaving, d == 1)


def pair_masks(first_place, starts, row):
    rest = BLOCK - LANES

    def mask(rows_from, count, cols_from, width, upper):
        rows = lax.broadcasted_iota(jnp.int32, (count, width), 0) + rows_from
        cols = lax.broadcasted_iota(jnp.int32, (count, width), 1) + cols_from
        doc_rows = doc_of(column_places(count, first_place + rows_from), starts, row)
        col_places = lax.broadcasted_iota(jnp.int32, (1, width), 1) + first_place + cols_from
        same = doc_rows == doc_of(col_places, starts, row)
        return jnp.where(same & ((rows < cols) if upper else (rows > cols)), 1.0, 0.0)

    return (
        (mask(0, BLOCK, 0, LANES, False), mask(LANES, rest, LANES, rest, False)),
        (mask(0, LANES, 0, LANES, True), mask(0, BLOCK, LANES, rest, True)),
    )


def tile_rows(upper):
    return (slice(0, LANES), slice(0, BLOCK)) if upper else (slice(0, BLOCK), slice(LANES, BLOCK))


def tiles_nt(rows, cols, upper):
    first, second = tile_rows(upper)
    return dot_nt(rows[first], cols[:LANES]), dot_nt(rows[second], cols[LANES:])


def tiles_apply(tiles, values, upper):
    first, second = dot(tiles[0], values[:LANES]), dot(tiles[1], values[LANES:])
    if upper:
        return first + second[:LANES], second[LANES:]
    return first[:LANES], first[LANES:] + second


def tiles_turned(tiles, values, upper):
    first, second = tile_rows(upper)
    return dot_tn(tiles[0], values[first]), dot_tn(tiles[1], values[second])


def pair_apply(first, second, values, upper):
    wide = jnp.concatenate([first[0], second[0]], axis=1)
    tall = jnp.concatenate([part[:LANES] for part in values], axis=0)
    main = dot(wide, tall)
    rest = dot(first[1], values[0][LANES:]) + dot(second[1], values[1][LANES:])
    if upper:
        return main + rest[:LANES], rest[LANES:]
    return main[:LANES], main[LANES:] + rest


def pair_nt(rows, cols, upper):
    first, second = tile_rows(upper)
    main = dot_nt(rows[first], jnp.concatenate([part[:LANES] for part in cols], axis=0))
    return [
        (main[:, i * LANES : (i + 1) * LANES], dot_nt(rows[second], cols[i][LANES:]))
        for i in range(2)
    ]


def halves_of(values, head_dim):
    low = lax.broadcasted_iota(jnp.int32, (1, LANES), 1) < head_dim
    empty = jnp.zeros_like(values)
    return jnp.where(low, values, empty), jnp.where(low, empty, values)


def decays_of(s, row, block, lane, upper, rows_first):
    rows = block_rows(block)
    by_row = s.tab[row, 1, rows, lane : lane + 1]
    by_col = s.cumt[row, block, lane : lane + 1, :]
    first, second = tile_rows(upper)
    if rows_first:
        gaps = by_col[:, :LANES] - by_row[first], by_col[:, LANES:] - by_row[second]
    else:
        gaps = by_row[first] - by_col[:, :LANES], by_row[second] - by_col[:, LANES:]
    return [jnp.exp2(jnp.minimum(gap, 0.0)) for gap in gaps]


def block_mats(s, row, block, d):
    rows, width, state = block_rows(block), s.width, s.state
    b_mat = s.xbc[row, rows, width + d * state : width + (d + 1) * state]
    c_mat = s.xbc[row, rows, width + (2 + d) * state : width + (3 + d) * state]
    return b_mat, c_mat


def inner(s, row, block):
    heads, head_dim = s.heads, s.head_dim
    first = block * BLOCK
    parts = (slice(first, first + LANES), slice(first + LANES, first + BLOCK))
    masks = pair_masks(s.base + first, s.starts, row)
    for d in range(2):
        upper = d == 1
        b_mat, c_mat = block_mats(s, row, block, d)
        scores = [a * b for a, b in zip(tiles_nt(c_mat, b_mat, upper), masks[d])]
        for pair in range(heads // 2):
            at = slice(pair * LANES, (pair + 1) * LANES)
            values = halves_of(s.v[row, d, block_rows(block), at], head_dim)
            mixing = []
            for h in (2 * pair, 2 * pair + 1):
                spread = decays_of(s, row, block, d * heads + h, upper, False)
                mixing.append([(a * b).astype(BF) for a, b in zip(spread, scores)])
            for part, out in zip(parts, pair_apply(*mixing, values, upper)):
                s.y[row, d, part, at] = out


def gates(s, row):
    half, width = s.half, s.width
    s.z[row] = dot(s.normed[row, HALO:], flat(s.w_late, slice(0, width)))
    for cot, core in ((s.cot, s.core), (s.cot_other, 1 - s.core)):
        places = column_places(half, s.base + core * half)
        valid = (places < s.row_len - s.pad_len[row]).astype(F32)
        s.d_out[row, pl.ds(pl.multiple_of(core * half, HALO), half)] = (
            cot[row].astype(F32) * valid
        ).astype(BF)
    s.dg[row] = dot(s.d_out[row], flat(s.w_late, slice(width, None)))


def outer(s, row):
    heads, head_dim, state, width = s.heads, s.head_dim, s.state, s.width
    for d in range(2):
        reach = expand(s, s.tab[row, 3], d)
        for b in range(s.blocks):
            at = block_rows(b)
            c_mat = s.xbc[row, at, width + (2 + d) * state : width + (3 + d) * state]
            raw = dot(c_mat, s.inc[row, b, d].astype(BF))
            s.y[row, d, at] = s.y[row, d, at] + reach[at] * raw
    u = s.xbc[row, :, :width].astype(F32)
    y = s.y[row, 0] + s.skip_c[...] * u + s.y[row, 1]
    z = s.z[row]
    v = y * z * (1.0 / (1.0 + jnp.exp(-z)))
    lane = lax.broadcasted_iota(jnp.int32, (1, LANES), 1)
    squares = jnp.sum(v * v, axis=-1, keepdims=True)
    against = jnp.sum(s.dg[row] * s.gate_gain_c[...] * v, axis=-1, keepdims=True)
    s.sums[row] = jnp.where(lane == 0, squares, jnp.where(lane == 1, against, 0.0))


def turn(s, row):
    heads, head_dim, state, width = s.heads, s.head_dim, s.state, s.width
    blocks = s.blocks
    total = s.sums[row] + s.sums_other[row]
    scale = lax.rsqrt(total[:, 0:1] * (1.0 / s.inner_width) + EPSILON)
    against = total[:, 1:2]
    u = s.xbc[row, :, :width].astype(F32)
    y = s.y[row, 0] + s.skip_c[...] * u + s.y[row, 1]
    z = s.z[row]
    gate = 1.0 / (1.0 + jnp.exp(-z))
    silu = z * gate
    unit = y * silu * scale
    s.gated[row] = (unit * s.gate_gain_c[...]).astype(BF)
    d_gated = s.dg[row]
    d_v = scale * (d_gated * s.gate_gain_c[...]) - unit * (
        scale * scale * against * (1.0 / s.inner_width)
    )
    dy = (d_v * silu).astype(BF)
    s.dy[row] = dy
    s.dz[row] = (d_v * y * gate * (1.0 + z * (1.0 - gate))).astype(BF)
    dy_f = dy.astype(F32)
    gate_term = jnp.sum(d_gated * unit, axis=0, keepdims=True)
    skip_term = jnp.sum(dy_f * u, axis=0, keepdims=True)
    if row:
        gate_term, skip_term = gate_term + s.gate_sum[...], skip_term + s.skip_sum[...]
    s.gate_sum[...] = gate_term
    s.skip_sum[...] = skip_term
    for d in range(2):
        weighed = (expand(s, s.tab[row, 3], d) * dy_f).astype(BF)
        for b in range(blocks):
            at = block_rows(b)
            c_mat = s.xbc[row, at, width + (2 + d) * state : width + (3 + d) * state]
            s.enter[row, b, d] = dot_tn(c_mat, weighed[at])
            s.d_c[row, at, d * state : (d + 1) * state] = dot_nt(
                weighed[at], s.inc[row, b, d].astype(BF)
            )


def branches(s, row):
    s.branch[row] = dot_nt(s.gated[row], flat(s.w_late, slice(s.width, None))).astype(BF)


def turned(s, row):
    s.normed_t[row] = s.normed[row].T


def weight_grad(s, out, lefts, rights, columns=slice(None), product=dot):
    step = 8 * 2 * s.shard if len(out.shape) == 3 else s.model
    for first in range(0, s.model, step):
        total = None
        for left, right in zip(lefts, rights):
            term = product(left(slice(first, first + step)), right(columns))
            total = term if total is None else total + term
        if len(out.shape) == 2:
            out[:, columns] = total.astype(BF)
        else:
            per = out.shape[1]
            out[first // per : (first + step) // per, :, columns] = (
                total.astype(BF).reshape(step // per, per, total.shape[1])
            )


def out_grads(s):
    rows = range(s.rows)
    weight_grad(
        s, s.grad_out, [lambda at, r=r: s.d_out[r, :, at] for r in rows],
        [lambda at, r=r: s.gated[r, :, at] for r in rows], product=dot_tn,
    )


def gate_grads(s):
    rows = range(s.rows)
    weight_grad(
        s, s.grad_gate, [lambda at, r=r: s.normed_t[r, at, HALO:] for r in rows],
        [lambda at, r=r: s.dz[r, :, at] for r in rows],
    )


def pre_grads(s, columns=slice(None)):
    rows = range(s.rows)
    weight_grad(
        s, s.grad_pre, [lambda at, r=r: s.normed_t[r, at] for r in rows],
        [lambda at, r=r: s.d_all[r, :, at] for r in rows], columns,
    )


def inner_back(s, row, block):
    heads, head_dim, state = s.heads, s.head_dim, s.state
    rows = block_rows(block)
    first = block * BLOCK
    parts = (slice(first, first + LANES), slice(first + LANES, first + BLOCK))
    masks = pair_masks(s.base + first, s.starts, row)
    dy_all = s.dy[row, rows].astype(F32)
    along = None
    for d in range(2):
        term = reduce(s, dy_all * s.y[row, d, rows], d, 2)
        along = term if along is None else along + term
        upper = d == 0
        b_mat, c_mat = block_mats(s, row, block, d)
        scores = [a * b for a, b in zip(tiles_nt(b_mat, c_mat, upper), masks[1 - d])]
        d_scores = None
        for pair in range(heads // 2):
            at = slice(pair * LANES, (pair + 1) * LANES)
            grads = halves_of(s.dy[row, rows, at], head_dim)
            d_mixing = pair_nt(s.v[row, d, rows, at], grads, upper)
            mixing = []
            for i in range(2):
                spread = decays_of(s, row, block, d * heads + 2 * pair + i, upper, True)
                mixing.append([(a * b).astype(BF) for a, b in zip(spread, scores)])
                terms = [a * b for a, b in zip(d_mixing[i], spread)]
                d_scores = terms if d_scores is None else [a + b for a, b in zip(d_scores, terms)]
            for part, out in zip(parts, pair_apply(*mixing, grads, upper)):
                s.y[row, d, part, at] = out
        d_scores = [(a * b).astype(BF) for a, b in zip(d_scores, masks[1 - d])]
        d_b = tiles_apply(d_scores, c_mat, upper)
        d_c = tiles_turned(d_scores, b_mat, upper)
        for part, b_part, c_part in zip(parts, d_b, d_c):
            s.dbc[row, part, d * state : (d + 1) * state] = b_part
            s.dbc[row, part, (2 + d) * state : (3 + d) * state] = (
                c_part + s.d_c[row, part, d * state : (d + 1) * state]
            )
    s.along[row, rows] = along


def back(s, row):
    heads, head_dim, state, width, span = s.heads, s.head_dim, s.state, s.width, s.span
    conv_width, conv_len, blocks = s.conv_width, s.conv_len, s.blocks
    forward = lax.broadcasted_iota(jnp.int32, (1, LANES), 1) < heads
    rate = jnp.exp(s.a_log_c[...])
    rows = lax.broadcasted_iota(jnp.int32, (BLOCK, 1), 0)
    row_id = lax.broadcasted_iota(jnp.int32, (8, width), 0)
    if row == 0:
        s.pad[0:HALO] = jnp.zeros((HALO, conv_width), F32)
        s.pad[HALO + span :] = jnp.zeros((s.pad.shape[0] - HALO - span, conv_width), F32)
    u = s.xbc[row, :, :width].astype(F32)
    step, tail, reach = s.tab[row, 0], s.tab[row, 2], s.tab[row, 3]
    d_u = s.skip_c[...] * s.dy[row].astype(F32)
    through, direct = None, None
    ended = [None] * blocks
    d_bc = []
    for d in range(2):
        v_d = s.v[row, d].astype(F32)
        leave = [s.leaving[row, b, d].astype(BF) for b in range(blocks)]
        tail_wide = expand(s, tail, d)
        tailed = (tail_wide * v_d).astype(BF)
        held = []
        for b in range(blocks):
            b_mat = s.xbc[row, block_rows(b), width + d * state : width + (d + 1) * state]
            held.append(dot(b_mat, leave[b]))
        dv_state = tail_wide * jnp.concatenate(held, axis=0)
        dv_all = s.y[row, d] + dv_state
        d_bc.append(
            jnp.concatenate([dot_nt(tailed[block_rows(b)], leave[b]) for b in range(blocks)], axis=0)
        )
        d_u = d_u + expand(s, step, d) * dv_all
        passed = v_d * dv_state
        for b in range(blocks):
            sides = jnp.where(
                row_id == 0,
                jnp.sum(passed[block_rows(b)], axis=0, keepdims=True),
                jnp.sum(s.leaving[row, b, d] * s.inc[row, b, d], axis=0, keepdims=True),
            )
            term = reduce(s, sides, d, 3)
            ended[b] = term if d == 0 else ended[b] + term
        terms = reduce(s, v_d * dv_all, d, 2), reduce(s, u * dv_all, d, 2)
        if d == 0:
            through, direct = terms
        else:
            through, direct = through + terms[0], direct + terms[1]
    ends = []
    for b in range(blocks):
        reach_b = reach[block_rows(b)]
        final = jnp.where(forward, reach_b[BLOCK - 1 : BLOCK], reach_b[0:1])
        at_end = jnp.where(
            forward, (rows == BLOCK - 1).astype(F32), (rows == 0).astype(F32)
        )
        ends.append(at_end * (ended[b][0:1] + ended[b][1:2] * final))
    d_cum = s.along[row] - through + jnp.concatenate(ends, axis=0)
    d_logs = jnp.concatenate(
        [jnp.where(forward, from_end, from_start) for from_start, from_end in running(s, d_cum)],
        axis=0,
    )
    d_raw = (direct - rate * d_logs) * s.tab[row, 4]
    s.d_all[row, HALO:, conv_width:] = d_raw.astype(BF)
    d_bias = jnp.sum(d_raw, axis=0, keepdims=True)
    d_rate = jnp.sum(-step * rate * d_logs, axis=0, keepdims=True)
    inside = slice(HALO, HALO + span)
    s.pad[inside, 0:width] = d_u * s.dsil[row, :, 0:width]
    s.pad[inside, width : width + 2 * state] = (
        s.dbc[row, :, : 2 * state] + jnp.concatenate(d_bc, axis=1)
    ) * s.dsil[row, :, width : width + 2 * state]
    s.pad[inside, width + 2 * state :] = (
        s.dbc[row, :, 2 * state :] * s.dsil[row, :, width + 2 * state :]
    )
    s.d_all[row, 0:HALO, conv_width:] = jnp.zeros((HALO, LANES), BF)
    s.pre_f[...] = s.pre[row].astype(F32)
    places = column_places(span, s.base)
    doc = doc_of(places, s.starts, row)
    outs = s.pad[HALO : HALO + span]
    conv_b_term = jnp.sum(outs, axis=0, keepdims=True)
    ext_places = column_places(HALO + span, s.base - HALO)
    ext_doc = doc_of(ext_places, s.starts, row)
    d_pre = None
    conv_w_terms = []
    for k in range(conv_len):
        ahead = conv_len - 1 - k
        ok = (doc_of(places - ahead, s.starts, row) == doc).astype(F32)
        conv_w_terms.append(
            jnp.sum(
                outs * ok * s.pre_f[HALO - ahead : HALO - ahead + span], axis=0, keepdims=True
            )
        )
        ok_ext = (doc_of(ext_places + ahead, s.starts, row) == ext_doc).astype(F32)
        term = s.pad[ahead : ahead + HALO + span] * ok_ext * s.conv_w_c[k : k + 1]
        d_pre = term if d_pre is None else d_pre + term
    s.d_all[row, :, 0:conv_width] = d_pre.astype(BF)
    conv_w_term = jnp.concatenate(conv_w_terms, axis=0)
    small_term = jnp.concatenate([d_bias, d_rate], axis=0)
    if row:
        conv_w_term = conv_w_term + s.sum_conv_w[...]
        conv_b_term = conv_b_term + s.sum_conv_b[...]
        small_term = small_term + s.small[0:2]
    s.sum_conv_w[...] = conv_w_term
    s.sum_conv_b[...] = conv_b_term
    s.small[0:2] = small_term


def d_norms(s, row):
    dn = dot_nt(s.d_all[row], flat(s.w_pre))
    s.dn[row, 0:HALO] = dn[0:HALO].astype(BF)
    s.dn[row, HALO:] = (
        dn[HALO:] + dot_nt(s.dz[row], flat(s.w_late, slice(0, s.width)))
    ).astype(BF)


def finish(s, row):
    half = s.half
    x = s.tokens[row].astype(F32)
    places = column_places(half, s.base + s.core * half)
    valid = (places < s.row_len - s.pad_len[row]).astype(F32)
    keep = pl.ds(pl.multiple_of(s.core * half, HALO), half)
    s.mixed[row] = (
        x + valid * (s.branch[row, keep].astype(F32) + s.branch_other[row].astype(F32))
    ).astype(BF)
    keep = pl.ds(pl.multiple_of(HALO + s.core * half, HALO), half)
    s.ds[...] = s.dn[row, keep].astype(F32) + s.dn_other[row].astype(F32)
    takes = ((s.core == 1) & (s.place + 1 < s.count)).astype(F32)
    s.ds[half - HALO :] += takes * (s.rims[0, row].astype(F32) + s.rims[1, row].astype(F32))
    d_normed = s.ds[...]
    scale = lax.rsqrt(jnp.mean(x * x, axis=-1, keepdims=True) + EPSILON)
    weighed = d_normed * s.norm_gain[...][None]
    along = jnp.mean(weighed * x, axis=-1, keepdims=True)
    dx = scale * weighed - x * (scale * scale * scale * along)
    s.tokens_grad[row] = (s.cot[row].astype(F32) + dx).astype(BF)
    term = jnp.sum(d_normed * x * scale, axis=0, keepdims=True)
    s.gain_sum[...] = term if row == 0 else s.gain_sum[...] + term


MESH = pl.DeviceIdType.MESH


def remote(src, dst, send_sem, recv_sem, device):
    return pltpu.make_async_remote_copy(
        src_ref=src, dst_ref=dst, send_sem=send_sem, recv_sem=recv_sem, device_id=device,
        device_id_type=MESH,
    )


class Sender:
    def __init__(self, send_sems, recv_sems):
        self.send_sems, self.recv_sems = send_sems, recv_sems
        self.sent = 0
        self.slots = 0
        self.pending = []

    def slot(self, count=1):
        self.slots += count
        return self.slots - count

    def send(self, src, dst, slot, device):
        copy = remote(src, dst, self.send_sems.at[self.sent], self.recv_sems.at[slot], device)
        self.sent += 1
        copy.start()
        self.pending.append(copy)

    def arrive(self, dst, slot, device):
        remote(dst, dst, self.send_sems.at[0], self.recv_sems.at[slot], device).wait_recv()

    def drain(self):
        for copy in self.pending:
            copy.wait_send()
        self.pending = []


class Place:
    def __init__(self, count):
        self.dp, self.seq, self.dir = (lax.axis_index(a) for a in ("dp", "seq", "dir"))
        self.count = count
        self.side = self.dp + 1 - 2 * (self.dp % 2)
        self.below = (self.dp + 2) % 4
        self.across = 3 - self.dp
        self.me = (self.dp, self.seq, self.dir)
        self.sibling = (self.dp, self.seq, 1 - self.dir)
        self.by_x = (self.side, self.seq, self.dir)
        self.by_y = (self.below, self.seq, self.dir)

    def along(self, k, crossed=False):
        core = 1 - self.dir if crossed else self.dir
        return (self.dp, (self.seq + k + self.count) % self.count, core)

    def at(self, k):
        return (self.seq + k + self.count) % self.count

    def chip(self, dp, k=0):
        return dp * self.count + self.at(k)

    def meet(self):
        barrier = pltpu.get_barrier_semaphore()
        others = [self.sibling, self.by_x, self.by_y]
        others += [self.along(k) for k in range(1, self.count)]
        others += [self.along(1, True), self.along(-1, True)]
        for device in others:
            pl.semaphore_signal(barrier, inc=1, device_id=device, device_id_type=MESH)
        pl.semaphore_wait(barrier, len(others))


class Spread:
    def __init__(self, place, sender, slab, cut):
        self.place, self.sender, self.slab, self.cut = place, sender, slab, cut
        count = place.count
        self.z, self.x, self.y, self.xd, self.yd = (sender.slot(count) for _ in range(5))
        self.hops = []
        z = place.seq
        low = (3 * count - 2 - 2 * z) // (2 * count)
        near = low * z + (1 - low) * (count - 1 - z)
        self.order = [(z, None)]
        for i in range(1, count):
            paired = (2 * near - i + 4 * count) // (4 * count)
            far = paired * ((i + 1) // 2) + (1 - paired) * (i - near)
            side = paired * (1 - 2 * (i % 2)) + (1 - paired) * (2 * low - 1)
            self.order.append((z + side * far, side))

    def block(self, dp, source):
        return self.slab.at[dp * self.place.count + source]

    def hop(self, source, step):
        here, to = self.place, self.sender
        spot = self.block(here.dp, source)
        sem = to.sent
        to.sent += 1
        there = here.seq + step
        copy = lambda: remote(
            spot, spot, to.send_sems.at[sem], to.recv_sems.at[self.z + source],
            (here.dp, there, here.dir),
        )
        inside = (there >= 0) & (there < here.count)

        @pl.when(inside)
        def _():
            copy().start()

        self.hops.append((inside, copy))

    def start_z(self):
        z = self.place.seq
        self.hop(z, 1)
        self.hop(z, -1)

    def both(self, source):
        here, to = self.place, self.sender
        spot = self.block(here.dp, source)
        to.send(spot, spot, self.x + source, here.by_x)
        to.send(spot, spot, self.y + source, here.by_y)

    def start_xy(self):
        self.both(self.place.seq)

    def relay(self, i):
        here, to = self.place, self.sender
        source, side = self.order[i]
        to.arrive(self.block(here.dp, source), self.z + source, here.by_x)
        self.hop(source, -side)
        self.both(source)

    def cross(self, i):
        here, to = self.place, self.sender
        source = self.order[i][0]
        from_x = self.block(here.side, source)
        to.arrive(from_x, self.x + source, here.by_x)
        part = from_x.at[:, : self.cut]
        to.send(part, part, self.yd + source, here.by_y)
        from_y = self.block(here.below, source)
        to.arrive(from_y, self.y + source, here.by_y)
        part = from_y.at[:, self.cut :]
        to.send(part, part, self.xd + source, here.by_x)

    def end(self, i):
        here, to = self.place, self.sender
        source = self.order[i][0]
        spot = self.block(here.across, source)
        to.arrive(spot.at[:, : self.cut], self.yd + source, here.by_y)
        to.arrive(spot.at[:, self.cut :], self.xd + source, here.by_x)

    def drain(self):
        for inside, copy in self.hops:
            @pl.when(inside)
            def _():
                copy().wait_send()


class Reduce:
    def __init__(self, place, sender, grad, cut, first, second, third, out_second, out_third, total):
        self.place, self.sender, self.grad, self.cut = place, sender, grad, cut
        self.first, self.second, self.third = first, second, third
        self.out_second, self.out_third, self.total = out_second, out_third, total
        count = place.count
        self.one = [[[sender.slot() for _ in range(count)] for _ in range(2)] for _ in range(2)]
        self.two = [[sender.slot() for _ in range(count)] for _ in range(2)]
        self.three = [None] + [sender.slot() for _ in range(1, count)]
        self.sides = (slice(0, cut), slice(cut, grad.shape[2]))

    def start(self, k, sides=(0, 1)):
        here, to = self.place, self.sender
        for side, device, targets in (
            (0, here.by_x, (here.side, here.across)),
            (1, here.by_y, (here.below, here.across)),
        ):
            if side not in sides:
                continue
            at = self.sides[side]
            for q in (1, 0):
                to.send(
                    self.grad.at[here.chip(targets[q], k), :, at],
                    self.first.at[q, k, :, at],
                    self.one[side][q][k], device,
                )

    def pass_on(self, k):
        here, to = self.place, self.sender
        for side, came, device, target in (
            (0, here.by_x, here.by_y, here.below),
            (1, here.by_y, here.by_x, here.side),
        ):
            at = self.sides[side]
            to.arrive(self.first.at[1, k, :, at], self.one[side][1][k], came)
            self.out_second[k, :, at] = (
                self.grad[here.chip(target, k), :, at].astype(F32)
                + self.first[1, k, :, at].astype(F32)
            ).astype(BF)
            to.send(self.out_second.at[k, :, at], self.second.at[k, :, at], self.two[side][k], device)

    def along(self, k):
        here, to = self.place, self.sender
        for side, came, then in ((0, here.by_x, here.by_y), (1, here.by_y, here.by_x)):
            at = self.sides[side]
            to.arrive(self.first.at[0, k, :, at], self.one[side][0][k], came)
            to.arrive(self.second.at[k, :, at], self.two[side][k], then)
            summed = (
                self.grad[here.chip(here.dp, k), :, at].astype(F32)
                + self.first[0, k, :, at].astype(F32)
                + self.second[k, :, at].astype(F32)
            )
            if k == 0:
                self.total[:, at] = summed
            else:
                self.out_third[k - 1, :, at] = summed.astype(BF)
        if k:
            to.send(self.out_third.at[k - 1], self.third.at[k - 1], self.three[k], here.along(k))

    def end(self):
        here, to = self.place, self.sender
        for k in range(1, here.count):
            to.arrive(self.third.at[k - 1], self.three[k], here.along(-k))
            self.total[...] += self.third[k - 1].astype(F32)


def fill_columns(s, core, pre, late):
    width, heads, conv_width = s.width, s.heads, s.conv_width
    late_side = core == 1
    pick = lambda ref, at: jnp.where(
        late_side, ref[:, at + width : at + 2 * width], ref[:, at : at + width]
    )
    source = lax.broadcasted_iota(jnp.int32, (4 * heads, LANES), 0)
    lane = lax.broadcasted_iota(jnp.int32, (4 * heads, LANES), 1)
    column = jnp.where(lane < heads, lane, lane + heads) + core * heads
    ones = jnp.where((source == column) & (lane < 2 * heads), 1.0, 0.0).astype(BF)
    pre[:, 0:width] = pick(s.w_in, 2 * width).astype(pre.dtype)
    pre[:, width:conv_width] = s.w_in[:, 4 * width :].astype(pre.dtype)
    pre[:, conv_width:] = dot(s.w_dt[...], ones).astype(pre.dtype)
    late[:, 0:width] = pick(s.w_in, 0).astype(late.dtype)
    late[:, width:] = pick(s.w_out, 0).astype(late.dtype)


class Chain:
    def __init__(self, s, place, sender, upward, terms, out, landed, leaves):
        self.s, self.place, self.sender, self.upward = s, place, sender, upward
        self.terms, self.out, self.landed, self.leaves = terms, out, landed, leaves
        self.slots = [[sender.slot() for _ in range(2)] for _ in range(s.rows)]
        self.sems = [[sender.sent + 2 * row + d for d in range(2)] for row in range(s.rows)]
        sender.sent += 2 * s.rows

    def turn(self, d):
        here = self.place
        return here.seq if self.upward[d] else here.count - 1 - here.seq

    def copy(self, row, d):
        to = self.sender
        return remote(
            self.leaves.at[row, d], self.landed.at[row, d], to.send_sems.at[self.sems[row][d]],
            to.recv_sems.at[self.slots[row][d]], self.place.along(1 if self.upward[d] else -1),
        )

    def step(self, row, at):
        for d in range(2):
            @pl.when(self.turn(d) == at)
            def _():
                if at:
                    self.sender.arrive(
                        self.landed.at[row, d], self.slots[row][d],
                        self.place.along(-1 if self.upward[d] else 1),
                    )
                now = self.landed[row, d].astype(F32)
                now = run_through(self.s, row, d, now, self.terms, self.out, self.upward[d])
                if at < self.place.count - 1:
                    self.leaves[row, d] = now.astype(BF)
                    self.copy(row, d).start()

    def steps(self, level, last=None):
        for now in range(level, (level if last is None else last) + 1):
            for row in range(self.s.rows):
                if 0 <= now - row < self.place.count:
                    self.step(row, now - row)

    def drain(self):
        for row in range(self.s.rows):
            for d in range(2):
                @pl.when(self.turn(d) < self.place.count - 1)
                def _():
                    self.copy(row, d).wait_send()


def everything(sizes, names, *refs):
    s = Refs(sizes, names, refs).where()
    count, rows, half, width, heads = s.count, s.rows, s.half, s.width, s.heads
    conv_width, model, shard = s.conv_width, s.model, s.shard
    here = Place(count)
    to = Sender(s.send_sems, s.recv_sems)
    late_core = here.dir == 1
    brought = [
        pltpu.make_async_copy(source, target, s.own_sems.at[i])
        for i, (source, target) in enumerate(((s.tokens_in, s.tokens), (s.cot_in, s.cot)))
    ]
    for copy in brought:
        copy.start()
    fill_columns(s, 1 - here.dir, s.give_pre, s.give_late)
    s.chain_in[...] = jnp.zeros_like(s.chain_in)
    s.back_chain_in[...] = jnp.zeros_like(s.back_chain_in)
    here.meet()

    pair = [to.slot() for _ in range(5)]
    to.send(s.give_pre, s.got_pre, pair[0], here.sibling)
    brought[0].wait()
    to.send(s.tokens, s.tokens_other, pair[2], here.sibling)
    rim = s.tokens.at[:, pl.ds(half - HALO, HALO)]
    first_rim, second_rim = to.sent, to.sent + 1
    to.sent += 2

    def rims_out():
        return [
            remote(rim, s.halo, s.send_sems.at[sem], s.recv_sems.at[pair[4]], here.along(1, crossed))
            for sem, crossed in ((first_rim, False), (second_rim, True))
        ]

    @pl.when(late_core)
    def _():
        for copy in rims_out():
            copy.start()

    to.send(s.give_late, s.got_late, pair[1], here.sibling)
    brought[1].wait()
    to.send(s.cot, s.cot_other, pair[3], here.sibling)
    fill_columns(s, here.dir, s.pre_mine, s.late_mine)

    def joined(own, got):
        other = got[...].astype(F32)
        own = own[...]
        return jnp.where(
            late_core,
            jnp.concatenate([other, own], axis=0),
            jnp.concatenate([own, other], axis=0),
        ).astype(BF)

    me = here.chip(here.dp)
    spread_pre = Spread(here, to, s.w_pre, s.cuts[0])
    spread_late = Spread(here, to, s.w_late, s.cuts[1])
    to.arrive(s.got_pre, pair[0], here.sibling)
    s.w_pre[me] = joined(s.pre_mine, s.got_pre)
    spread_pre.start_z()
    spread_pre.start_xy()
    to.arrive(s.got_late, pair[1], here.sibling)
    s.w_late[me] = joined(s.late_mine, s.got_late)
    prepare(s)
    to.arrive(s.tokens_other, pair[2], here.sibling)
    to.arrive(s.halo, pair[4], here.along(-1))
    spread_pre.relay(1)
    spread_pre.cross(0)
    for row in range(rows):
        normalise(s, row)
        turned(s, row)
    for k in range(2, count):
        spread_pre.relay(k)
        spread_pre.cross(k - 1)
    spread_late.start_z()
    spread_pre.cross(count - 1)
    spread_late.start_xy()
    spread_late.relay(1)
    for k in range(count):
        spread_pre.end(k)

    states = Chain(s, here, to, (True, False), s.local, s.inc, s.chain_in, s.chain_out)
    front(s, 0)
    states.steps(0)
    spread_late.cross(0)
    spread_late.relay(2)
    for row in range(1, rows):
        front(s, row)
        states.steps(row)
    spread_late.cross(1)
    spread_late.relay(3)
    units = [(row, block) for row in range(rows) for block in range(s.blocks)]
    for i, (row, block) in enumerate(units):
        inner(s, row, block)
        if i == 0:
            spread_late.cross(2)
        if block == s.blocks - 1:
            states.steps(rows + row)
        if i == 2:
            spread_late.cross(3)
    for k in range(count):
        spread_late.end(k)
    to.arrive(s.cot_other, pair[3], here.sibling)
    for row in range(rows):
        gates(s, row)
    states.steps(2 * rows, rows + count)
    sum_slots = [to.slot() for _ in range(rows)]
    for row in range(rows):
        outer(s, row)
        to.send(s.sums.at[row], s.sums_other.at[row], sum_slots[row], here.sibling)

    back_chain = Chain(
        s, here, to, (False, True), s.enter, s.leaving, s.back_chain_in, s.back_chain_out
    )
    for row in range(rows):
        to.arrive(s.sums_other.at[row], sum_slots[row], here.sibling)
        turn(s, row)
        back_chain.steps(row)
    grads = (s.grad_pre, s.grad_gate, s.grad_out)
    reduces = [Reduce(here, to, g, cut, *work) for g, cut, work in zip(grads, s.grad_cuts, s.works)]
    reduce_pre, reduce_late = reduces[0], reduces[1:]
    order = list(range(1, count)) + [0]
    gate_grads(s)
    for k in order[:2]:
        reduces[1].start(k)
    out_grads(s)
    for k in order[:2]:
        reduces[2].start(k)
    back_chain.steps(rows)
    branch_slot, dn_slot, rim_own, rim_cross = (to.slot() for _ in range(4))
    give = pl.multiple_of((1 - here.dir) * half, HALO)
    for i, (row, block) in enumerate(units):
        inner_back(s, row, block)
        if i == 0:
            back_chain.steps(rows + 1)
        if i == 1:
            back_chain.steps(rows + 2, rows + count)
        for reduce in reduce_late:
            if i + 2 < count:
                reduce.start(order[i + 2])
            if 1 <= i <= count:
                reduce.pass_on(order[i - 1])
    back(s, 0)
    for k in order[len(units) + 1 :]:
        for reduce in reduce_late:
            reduce.start(k)
    for k in order[len(units) - 1 :]:
        for reduce in reduce_late:
            reduce.pass_on(k)
    for k in order[:2]:
        for reduce in reduce_late:
            reduce.along(k)
    for row in range(1, rows):
        back(s, row)
    for k in order[2:]:
        for reduce in reduce_late:
            reduce.along(k)
    for side, columns in enumerate(reduce_pre.sides):
        pre_grads(s, columns)
        for k in order[:2]:
            reduce_pre.start(k, (side,))
    for row in range(rows):
        d_norms(s, row)
    to.send(s.dn.at[:, pl.ds(HALO + give, half)], s.dn_other, dn_slot, here.sibling)
    edge = s.dn.at[:, pl.ds(0, HALO)]
    rim_sem = to.sent
    to.sent += 1

    def edge_out(core):
        return remote(
            edge, s.rims.at[core], s.send_sems.at[rim_sem],
            s.recv_sems.at[(rim_cross, rim_own)[core]], here.along(-1, core == 0),
        )

    for core in range(2):
        @pl.when(here.dir == core)
        def _():
            edge_out(core).start()

    for row in range(rows):
        branches(s, row)
    to.send(s.branch.at[:, pl.ds(give, half)], s.branch_other, branch_slot, here.sibling)
    reduce_pre.pass_on(order[0])
    reduce_pre.start(order[2])
    to.arrive(s.branch_other, branch_slot, here.sibling)
    to.arrive(s.dn_other, dn_slot, here.sibling)

    @pl.when(late_core)
    def _():
        to.arrive(s.rims.at[1], rim_own, here.along(1))
        to.arrive(s.rims.at[0], rim_cross, here.along(1, True))

    @pl.when(here.dir == 0)
    def _():
        s.rims[...] = jnp.zeros_like(s.rims)

    for row in range(rows):
        finish(s, row)
    taken = [
        pltpu.make_async_copy(source, target, s.own_sems.at[2 + i])
        for i, (source, target) in enumerate(((s.mixed, s.o_mixed), (s.tokens_grad, s.o_tokens)))
    ]
    for copy in taken:
        copy.start()
    side = conv_width - width
    s.v_own[0:4] = s.sum_conv_w[...]
    s.v_own[4:5] = s.sum_conv_b[...]
    s.v_own[5:6] = jnp.concatenate([s.gate_sum[...], s.small[0:1], s.small[1:2]], axis=1)
    s.v_own[6:7] = jnp.concatenate([s.skip_sum[...], jnp.zeros((1, side), F32)], axis=1)
    s.v_own[7:8] = jnp.concatenate([s.gain_sum[...], jnp.zeros((1, side), F32)], axis=1)
    v_slots = [to.slot() for _ in range(2 + count)]
    to.send(s.v_own, s.v_x.at[0], v_slots[0], here.by_x)
    reduce_pre.pass_on(order[1])
    for k in order[3:]:
        reduce_pre.start(k)
    others = s.others
    swap_slots = [to.slot() for _ in range(3)]
    back_rows = pl.ds(pl.multiple_of((1 - here.dir) * shard, 8), shard)
    own_rows = pl.ds(pl.multiple_of(here.dir * shard, 8), shard)
    for i in (1, 2):
        reduces[i].end()
        to.send(reduces[i].total.at[back_rows], others[i], swap_slots[i], here.sibling)
    reduce_pre.along(order[0])
    to.arrive(s.v_x.at[0], v_slots[0], here.by_x)
    s.v_x[1] = s.v_own[...] + s.v_x[0]
    to.send(s.v_x.at[1], s.v_y.at[0], v_slots[1], here.by_y)
    reduce_pre.pass_on(order[2])
    reduce_pre.along(order[1])
    to.arrive(s.v_y.at[0], v_slots[1], here.by_y)
    s.v_y[1] = s.v_x[1] + s.v_y[0]
    for k in range(1, count):
        to.send(s.v_y.at[1], s.v_z.at[k - 1], v_slots[1 + k], here.along(k))
    for k in order[3:]:
        reduce_pre.pass_on(k)
    for k in order[2:]:
        reduce_pre.along(k)
    total = s.v_y[1]
    for k in range(1, count):
        to.arrive(s.v_z.at[k - 1], v_slots[1 + k], here.along(-k))
        total = total + s.v_z[k - 1]
    s.v_x[0] = total
    to.send(s.v_x.at[0], s.v_other, v_slots[1 + count], here.sibling)
    parts = {}

    def take(i):
        to.arrive(others[i], swap_slots[i], here.sibling)
        own, got = reduces[i].total[own_rows], others[i][...]
        parts[i] = (jnp.where(late_core, got, own), jnp.where(late_core, own, got))

    for i in (1, 2):
        take(i)
    (gate_a, gate_b), (out_a, out_b) = parts[1], parts[2]
    s.o_in[:, 0:width] = gate_a
    s.o_in[:, width : 2 * width] = gate_b
    s.o_out[:, 0:width] = out_a
    s.o_out[:, width:] = out_b
    reduce_pre.end()
    to.send(reduce_pre.total.at[back_rows], others[0], swap_slots[0], here.sibling)
    take(0)
    pre_a, pre_b = parts[0]
    s.o_in[:, 2 * width : 3 * width] = pre_a[:, :width]
    s.o_in[:, 3 * width : 4 * width] = pre_b[:, :width]
    s.o_in[:, 4 * width :] = pre_a[:, width:conv_width] + pre_b[:, width:conv_width]
    s.o_steps[0] = pre_a[:, conv_width:]
    s.o_steps[1] = pre_b[:, conv_width:]
    to.arrive(s.v_other, v_slots[1 + count], here.sibling)
    got = s.v_other[...]
    s.o_small[0] = jnp.where(late_core, got, total)
    s.o_small[1] = jnp.where(late_core, total, got)
    for copy in taken:
        copy.wait()
    to.drain()
    for waiting in (states, spread_pre, spread_late):
        waiting.drain()
    back_chain.drain()

    @pl.when(late_core)
    def _():
        for copy in rims_out():
            copy.wait_send()

    for core in range(2):
        @pl.when(here.dir == core)
        def _():
            edge_out(core).wait_send()

    assert (to.sent, to.slots) == (s.send_sems.shape[0], s.recv_sems.shape[0]), (to.sent, to.slots)


SMEM = pl.BlockSpec(memory_space=pltpu.SMEM)
VMEM = pl.BlockSpec(memory_space=pltpu.VMEM)
ANY = pl.BlockSpec(memory_space=pl.ANY)


def call(body, ins, specs, out_shapes, scratch, name, collective_id=None, out_specs=None):
    return pl.pallas_call(
        body,
        out_shape=out_shapes,
        in_specs=specs,
        out_specs=out_specs or [VMEM] * len(out_shapes),
        scratch_shapes=scratch,
        compiler_params=pltpu.CompilerParams(
            vmem_limit_bytes=VMEM_BYTES, collective_id=collective_id,
            has_side_effects=collective_id is not None,
        ),
        name=name,
    )(*ins)


def shape_of(dtype, *dims):
    return jax.ShapeDtypeStruct(dims, dtype)


def buffers(z):
    rows, span, half, model, width, state = z[N.rows], z[N.span], z[N.half], z[N.model], z[N.width], z[N.state]
    blocks, conv_width, pre_width, count = z[N.blocks], z[N.conv_width], z[N.pre_width], z[N.count]
    ext, conv_len, heads = HALO + span, z[N.conv_len], z[N.heads]
    packed = 2 * heads + (-2 * heads) % 8
    carried = (state + CARRY, width)
    table = dict(
        conv_w_c=(F32, conv_len, conv_width), conv_b_c=(F32, 1, conv_width), bias_c=(F32, 1, LANES),
        a_log_c=(F32, 1, LANES), skip_c=(F32, 1, width), gate_gain_c=(F32, 1, width),
        gain_c=(F32, 1, model), halo=(BF, rows, HALO, model), tokens_other=(BF, rows, half, model),
        cot_other=(BF, rows, half, model), normed=(BF, rows, ext, model),
        pre=(BF, rows, ext, conv_width), pre_f=(F32, ext, conv_width),
        xbc=(BF, rows, span, conv_width), dsil=(F32, rows, span, conv_width),
        tab=(F32, rows, 5, span, LANES), cumt=(F32, rows, blocks, packed, BLOCK),
        v=(BF, rows, 2, span, width), local=(F32, rows, blocks, 2, state, width),
        decay=(F32, rows, blocks, 2, 8, width), send=(BF, 2, rows) + carried,
        received=(BF, count - 1, rows) + carried, y=(F32, rows, 2, span, width),
        inc=(F32, rows, blocks, 2, state, width), sums=(F32, rows, span, LANES),
        sums_other=(F32, rows, span, LANES), z=(F32, rows, span, width), dg=(F32, rows, span, width),
        d_out=(BF, rows, span, model), normed_t=(BF, rows, model, ext), gated=(BF, rows, span, width), dy=(BF, rows, span, width),
        dz=(BF, rows, span, width), enter=(F32, rows, blocks, 2, state, width),
        back_send=(BF, 2, rows) + carried, back_received=(BF, count - 1, rows) + carried,
        maps=(BF, 2, 2 * LANES, width), tri=(BF, 2 * BLOCK, BLOCK), d_c=(F32, rows, span, 2 * state),
        leaving=(F32, rows, blocks, 2, state, width), branch=(BF, rows, span, model), grad_out=(BF, model, width), grad_gate=(BF, model, width),
        gate_sum=(F32, 1, width), skip_sum=(F32, 1, width), dbc=(F32, rows, span, 4 * state),
        along=(F32, rows, span, LANES), pad=(F32, ext + 8, conv_width),
        d_all=(BF, rows, ext, pre_width), grad_pre=(BF, model, pre_width),
        sum_conv_w=(F32, conv_len, conv_width), sum_conv_b=(F32, 1, conv_width), small=(F32, 8, LANES),
        dn=(BF, rows, ext, model), branch_other=(BF, rows, half, model),
        dn_other=(BF, rows, half, model), rims=(BF, 2, rows, HALO, model), ds=(F32, half, model),
        gain_sum=(F32, 1, model), mixed=(BF, rows, half, model), tokens_grad=(BF, rows, half, model),
    )
    return {name: shape_of(*shape) for name, shape in table.items()}


def together(z, args):
    count, shard, width, conv_width = z[N.count], z[N.shard], z[N.width], z[N.conv_width]
    pre_width, model, rows, half, heads = z[N.pre_width], z[N.model], z[N.rows], z[N.half], z[N.heads]
    chips, pair = 4 * count, 2 * shard
    table = buffers(z)
    for name in (N.grad_out, N.grad_gate, N.grad_pre):
        table[name] = shape_of(BF, chips, pair, table[name].shape[1])
    outs = dict(
        o_mixed=table[N.mixed], o_tokens=table[N.tokens_grad],
        o_in=shape_of(F32, shard, 4 * width + 4 * z[N.state]), o_out=shape_of(F32, shard, 2 * width),
        o_steps=shape_of(F32, 2, shard, LANES), o_small=shape_of(F32, 2, 8, conv_width),
    )
    args = dict(args, tokens_in=args[N.tokens], cot_in=args[N.cot])
    for name in (N.tokens, N.cot):
        value = args.pop(name)
        table[name] = shape_of(value.dtype, *value.shape)
    for name in (N.send, N.received, N.back_send, N.back_received):
        table.pop(name)
    aliases = {N.inc: N.local, N.leaving: N.enter}
    views = {
        N.dbc: (N.z, 0, 4 * z[N.state]), N.along: (N.z, 4 * z[N.state], LANES),
        N.d_c: (N.dg, 0, 2 * z[N.state]),
    }
    scratch = {
        name: pltpu.VMEM(value.shape, value.dtype)
        for name, value in table.items() if name not in aliases and name not in views
    }
    scratch.update(
        w_pre=pltpu.VMEM((chips, pair, pre_width), BF), w_late=pltpu.VMEM((chips, pair, 2 * width), BF),
        give_pre=pltpu.VMEM((shard, pre_width), BF), give_late=pltpu.VMEM((shard, 2 * width), BF),
        got_pre=pltpu.VMEM((shard, pre_width), BF), got_late=pltpu.VMEM((shard, 2 * width), BF),
        pre_mine=pltpu.VMEM((shard, pre_width), F32), late_mine=pltpu.VMEM((shard, 2 * width), F32),
        **{
            name: pltpu.VMEM((rows, 2, z[N.state], width), BF)
            for name in (N.chain_in, N.chain_out, N.back_chain_in, N.back_chain_out)
        },
        v_own=pltpu.VMEM((8, conv_width), F32), v_x=pltpu.VMEM((2, 8, conv_width), F32),
        v_y=pltpu.VMEM((2, 8, conv_width), F32), v_z=pltpu.VMEM((count - 1, 8, conv_width), F32),
        v_other=pltpu.VMEM((8, conv_width), F32),
    )
    widths = dict(pre=pre_width, gate=width, out=width)
    work_names = []
    for name, size in widths.items():
        scratch[name, -1] = pltpu.VMEM((shard, size), F32)
        for i, shape in enumerate(
            ((2, count, pair), (count, pair), (count - 1, pair), (count, pair), (count - 1, pair))
        ):
            scratch[name, i] = pltpu.VMEM(shape + (size,), BF)
        scratch[name, 5] = pltpu.VMEM((pair, size), F32)
        work_names.append([(name, i) for i in range(6)])
    sent, landed = 32 * count + 13 + 5 * rows, 32 * count + 11 + 5 * rows
    scratch[N.own_sems] = pltpu.SemaphoreType.DMA((4,))
    scratch[N.send_sems] = pltpu.SemaphoreType.DMA((sent,))
    scratch[N.recv_sems] = pltpu.SemaphoreType.DMA((landed,))
    in_names = list(args)
    names = in_names + list(outs) + list(scratch)
    cut = pre_width // 256 * 128 + 128

    def body(*refs):
        sizes = dict(z, cuts=(cut, width), grad_cuts=(cut, width // 2, width // 2))
        by_name = dict(zip(names, refs))
        for name, of in aliases.items():
            by_name[name] = by_name[of]
        for name, (of, first, lanes) in views.items():
            by_name[name] = by_name[of].at[:, :, pl.ds(first, lanes)]
        sizes[N.works] = [[by_name[n] for n in group] for group in work_names]
        sizes[N.others] = [by_name[name, -1] for name in widths]
        plain = {name: ref for name, ref in by_name.items() if isinstance(name, str)}
        everything(sizes, list(plain), *plain.values())

    places = {N.starts: SMEM, N.pad_len: SMEM, N.tokens_in: ANY, N.cot_in: ANY}
    specs = [places.get(name, VMEM) for name in in_names]
    out = call(
        body, list(args.values()), specs, list(outs.values()), list(scratch.values()), N.layer, 0,
        [ANY, ANY] + [VMEM] * (len(outs) - 2),
    )
    return delivered(z, out)


def deliver(z, mixed, tokens_grad, d_in, d_out, parts, small, o_mixed, o_tokens, o_in, o_out, o_norm,
            o_dt, o_conv_w, o_conv_b, o_bias, o_alog, o_skip, o_gate):
    heads, width = z[N.heads], z[N.width]
    for source, target in ((mixed, o_mixed), (tokens_grad, o_tokens), (d_in, o_in), (d_out, o_out)):
        target[...] = source[...]
    lane = lax.broadcasted_iota(jnp.int32, (LANES, 4 * heads), 0)
    column = lax.broadcasted_iota(jnp.int32, (LANES, 4 * heads), 1)
    first_lane = jnp.where(lane < heads, lane, jnp.where(lane < 2 * heads, lane + heads, -1))
    picks = [
        jnp.where((first_lane >= 0) & (column == first_lane + side_of * heads), 1.0, 0.0).astype(BF)
        for side_of in range(2)
    ]
    by_step = lambda a, b: exact(dot, a, picks[0], 3) + exact(dot, b, picks[1], 3)
    o_dt[...] = by_step(parts[0], parts[1])
    v_a, v_b = small[0], small[1]
    both = v_a + v_b
    o_conv_w[:, 0:width] = v_a[0:4, :width]
    o_conv_w[:, width : 2 * width] = v_b[0:4, :width]
    o_conv_w[:, 2 * width :] = both[0:4, width:]
    o_conv_b[...] = jnp.concatenate([v_a[4:5, :width], v_b[4:5, :width], both[4:5, width:]], axis=1)[0]
    o_gate[...] = jnp.concatenate([v_a[5:6, :width], v_b[5:6, :width]], axis=1)[0]
    steps = by_step(
        jnp.concatenate([v_a[5:6, width : width + LANES], v_a[5:6, width + LANES : width + 2 * LANES]] * 4, axis=0),
        jnp.concatenate([v_b[5:6, width : width + LANES], v_b[5:6, width + LANES : width + 2 * LANES]] * 4, axis=0),
    )
    o_bias[...] = steps[0]
    o_alog[...] = steps[1]
    head = lax.broadcasted_iota(jnp.int32, (width, 2 * heads), 1)
    channel = lax.broadcasted_iota(jnp.int32, (width, 2 * heads), 0) // z[N.head_dim]
    skips = None
    for side_of, v_side in ((0, v_a), (1, v_b)):
        ones = jnp.where(head == channel + side_of * heads, 1.0, 0.0).astype(BF)
        term = exact(dot, jnp.broadcast_to(v_side[6:7, :width], (8, width)), ones, 3)
        skips = term if skips is None else skips + term
    o_skip[...] = skips[0]
    o_norm[...] = both[7:8, : z[N.model]][0]


def delivered(z, arrays):
    heads, width, conv_width = z[N.heads], z[N.width], z[N.conv_width]
    outs = dict(
        mixed=arrays[0], tokens_grad=arrays[1], o_in=arrays[2], o_out=arrays[3],
        o_norm=shape_of(F32, z[N.model]), o_dt=shape_of(F32, z[N.shard], 4 * heads),
        o_conv_w=shape_of(F32, z[N.conv_len], conv_width + width),
        o_conv_b=shape_of(F32, conv_width + width), o_bias=shape_of(F32, 4 * heads),
        o_alog=shape_of(F32, 4 * heads), o_skip=shape_of(F32, 2 * heads),
        o_gate=shape_of(F32, 2 * width),
    )
    results = call(
        lambda *refs: deliver(z, *refs), arrays, [VMEM] * len(arrays),
        [shape_of(a.dtype, *a.shape) for a in outs.values()], (), N.deliver,
    )
    return dict(zip(outs, results))


def swapped(value):
    return lax.ppermute(value, "dir", [(0, 1), (1, 0)])


def rotated_to(value, steps, cross):
    count = lax.axis_size("seq")
    pairs = []
    for i in range(count):
        for c in range(2):
            pairs.append((i * 2 + c, (i + steps) % count * 2 + (1 - c if cross else c)))
    return lax.ppermute(value, ("seq", "dir"), pairs)


def around(value):
    count, place = lax.axis_size("seq"), lax.axis_index("seq")
    out = []
    for k in range(1, count):
        chosen = jnp.where(place + k < count, value[0], value[1])
        out.append(rotated_to(chosen, k, False))
    return jnp.stack(out)


def stage(z, have, phase, ins, outs, scratch=(), units=None):
    table = buffers(z)
    ins = [N.starts, N.pad_len] + list(ins)
    names = ins + list(outs) + list(scratch)
    units = [(row,) for row in range(z[N.rows])] if units is None else units

    def body(*refs):
        s = Refs(z, names, refs).where()
        for unit in units:
            phase(s, *unit)

    results = call(
        body, [have[name] for name in ins],
        [SMEM if name in (N.starts, N.pad_len) else VMEM for name in ins],
        [table[name] for name in outs],
        [pltpu.VMEM(table[name].shape, table[name].dtype) for name in scratch],
        phase.__name__,
    )
    have.update(zip(outs, results))


def apart(z, args):
    heads, width, conv_width, count = z[N.heads], z[N.width], z[N.conv_width], z[N.count]
    half, shard = z[N.half], z[N.shard]
    have = dict(args)
    core = lax.axis_index("dir")
    is_late = core == 1
    w_in, w_dt, w_out, tokens = (args[n] for n in (N.w_in, N.w_dt, N.w_out, N.tokens))
    pad_dt = jnp.zeros((shard, LANES - 2 * heads), BF)

    def columns(c):
        own = slice(c * width, (c + 1) * width)
        return (
            jnp.concatenate(
                [
                    w_in[:, 2 * width :][:, own], w_in[:, 4 * width :],
                    w_dt[:, c * heads : (c + 1) * heads],
                    w_dt[:, (2 + c) * heads : (3 + c) * heads], pad_dt,
                ],
                axis=1,
            ),
            jnp.concatenate([w_in[:, own], w_out[:, own]], axis=1),
        )

    def ordered(own, other, axis):
        return jnp.where(
            is_late, jnp.concatenate([other, own], axis=axis), jnp.concatenate([own, other], axis=axis)
        )

    first, latter = columns(0), columns(1)

    def gathered(i):
        keep = jnp.where(is_late, latter[i], first[i])
        give = swapped(jnp.where(is_late, first[i], latter[i]))
        return lax.all_gather(ordered(keep, give, 0), ("dp", "seq"), axis=0, tiled=True)

    have[N.w_pre], have[N.w_late] = gathered(0), gathered(1)
    have[N.tokens_other], have[N.cot_other] = swapped(tokens), swapped(args[N.cot])
    rim = tokens[:, half - HALO :]
    have[N.halo] = jnp.where(is_late, rotated_to(rim, 1, False), rotated_to(rim, 1, True))
    small = [N.conv_w_c, N.conv_b_c, N.bias_c, N.a_log_c, N.skip_c, N.gate_gain_c, N.gain_c, N.maps, N.tri]
    stage(
        z, have, prepare,
        [N.conv_w, N.conv_b, N.dt_bias, N.a_log, N.skip, N.gate_gain, N.norm_gain], small, units=[()],
    )
    stage(z, have, normalise, [N.gain_c, N.halo, N.tokens, N.tokens_other], [N.normed])
    have[N.normed_t] = jnp.swapaxes(have[N.normed], 1, 2)
    stage(
        z, have, front, [N.normed, N.w_pre, N.conv_w_c, N.conv_b_c, N.bias_c, N.a_log_c, N.maps, N.tri],
        [N.pre, N.xbc, N.dsil, N.tab, N.cumt, N.v, N.local, N.decay], [N.pre_f],
    )
    stage(z, have, sent_states, [N.local, N.decay], [N.send])
    have[N.received] = around(have[N.send])
    stage(z, have, received_states, [N.received, N.local, N.decay], [N.inc])
    units = [(row, block) for row in range(z[N.rows]) for block in range(z[N.blocks])]

    def forward(s):
        for unit in units:
            inner(s, *unit)
        for row in range(s.rows):
            gates(s, row)
            outer(s, row)

    stage(
        z, have, forward,
        [N.maps, N.xbc, N.tab, N.cumt, N.v, N.inc, N.normed, N.w_late, N.cot,
         N.cot_other, N.skip_c, N.gate_gain_c],
        [N.y, N.d_out, N.sums, N.z, N.dg], units=[()],
    )
    have[N.sums_other] = swapped(have[N.sums])

    def turning(s):
        for row in range(s.rows):
            turn(s, row)
            branches(s, row)
        out_grads(s)
        gate_grads(s)

    stage(
        z, have, turning,
        [N.sums, N.sums_other, N.xbc, N.y, N.z, N.dg, N.tab, N.inc, N.maps, N.skip_c, N.gate_gain_c,
         N.d_out, N.normed_t, N.w_late],
        [N.gated, N.dy, N.dz, N.gate_sum, N.skip_sum, N.enter, N.d_c, N.branch, N.grad_out,
         N.grad_gate],
        units=[()],
    )
    stage(z, have, back_states, [N.enter, N.decay], [N.back_send])
    have[N.back_received] = around(have[N.back_send])
    stage(z, have, returned_states, [N.back_received, N.enter, N.decay], [N.leaving])

    def backward(s):
        for row in range(s.rows):
            for block in range(s.blocks):
                for d in range(2):
                    at = block_rows(block)
                    s.y[row, d, at] = s.y_both[row, d, at]
                inner_back(s, row, block)
            back(s, row)
            d_norms(s, row)
        pre_grads(s)

    have[N.y_both] = have[N.y]
    stage(
        z, have, backward,
        [N.maps, N.tri, N.d_c, N.y_both, N.leaving, N.inc, N.xbc, N.tab, N.cumt, N.v, N.dy, N.dsil, N.pre,
         N.normed_t, N.dz, N.skip_c, N.a_log_c, N.conv_w_c, N.w_pre, N.w_late],
        [N.dn, N.d_all, N.grad_pre, N.sum_conv_w, N.sum_conv_b, N.small],
        [N.y, N.dbc, N.along, N.pad, N.pre_f], units=[()],
    )

    def give(values, first_row):
        return swapped(
            lax.dynamic_slice_in_dim(values, first_row + (1 - core) * half, half, axis=1)
        )

    edge = have[N.dn][:, :HALO]
    have[N.dn_other], have[N.branch_other] = give(have[N.dn], HALO), give(have[N.branch], 0)
    have[N.rims] = jnp.stack([rotated_to(edge, -1, True), rotated_to(edge, -1, False)])
    stage(
        z, have, finish,
        [N.tokens, N.cot, N.norm_gain, N.dn, N.dn_other, N.branch, N.branch_other, N.rims],
        [N.mixed, N.tokens_grad, N.gain_sum], [N.ds],
    )

    def placed(values):
        empty = jnp.zeros_like(values)
        return ordered(values, empty, -1)

    def sided(values):
        return jnp.concatenate([placed(values[:, :width]), values[:, width:]], axis=1)

    def reduced(name):
        value = lax.psum_scatter(have[name], ("dp", "seq"), scatter_dimension=0, tiled=True)
        own = lax.dynamic_slice_in_dim(value, core * shard, shard, axis=0)
        other = swapped(lax.dynamic_slice_in_dim(value, (1 - core) * shard, shard, axis=0))
        own, other = own.astype(F32), other.astype(F32)
        return jnp.where(is_late, other, own), jnp.where(is_late, own, other)

    def by_step(values):
        return jnp.concatenate(
            [placed(values[:, :heads]), placed(values[:, heads : 2 * heads])], axis=1
        )

    steps = by_step(have[N.small][:2])
    skips = placed(jnp.sum(have[N.skip_sum].reshape(1, heads, z[N.head_dim]), axis=-1))
    gain, all_conv_w, all_conv_b, steps, skips, gate_all = lax.psum(
        (
            have[N.gain_sum], sided(have[N.sum_conv_w]), sided(have[N.sum_conv_b]), steps, skips,
            placed(have[N.gate_sum]),
        ),
        ("dp", "seq", "dir"),
    )
    (pre_a, pre_b), (gate_a, gate_b), (out_a, out_b) = (
        reduced(name) for name in (N.grad_pre, N.grad_gate, N.grad_out)
    )
    last = conv_width
    return dict(
        mixed=have[N.mixed], tokens_grad=have[N.tokens_grad], o_norm=gain[0],
        o_in=jnp.concatenate(
            [
                gate_a, gate_b, pre_a[:, :width], pre_b[:, :width],
                pre_a[:, width:conv_width] + pre_b[:, width:conv_width],
            ],
            axis=1,
        ),
        o_dt=jnp.concatenate(
            [
                pre_a[:, last : last + heads], pre_b[:, last : last + heads],
                pre_a[:, last + heads : last + 2 * heads], pre_b[:, last + heads : last + 2 * heads],
            ],
            axis=1,
        ),
        o_conv_w=all_conv_w, o_conv_b=all_conv_b[0], o_bias=steps[0], o_alog=steps[1],
        o_skip=skips[0], o_gate=gate_all[0], o_out=jnp.concatenate([out_a, out_b], axis=1),
    )


def shards(tokens, starts, pad_len, norm_gain, w_in, w_dt, conv_w, conv_b, dt_bias, a_log, skip,
           gate_gain, w_out, cotangent):
    rows, half, model = tokens.shape
    span = 2 * half
    count = lax.axis_size("seq")
    inner_width = gate_gain.shape[0]
    heads = skip.shape[0] // 2
    width = inner_width // 2
    state = (conv_w.shape[1] - inner_width) // 4
    conv_width = width + 4 * state
    shard = w_in.shape[0]
    z = dict(
        rows=rows, half=half, model=model, span=span, count=count, row_len=span * count,
        blocks=span // BLOCK, inner_width=inner_width, heads=heads, head_dim=width // heads,
        width=width, state=state, conv_width=conv_width, conv_len=conv_w.shape[0],
        pre_width=conv_width + LANES, shard=shard,
    )
    args = dict(
        tokens=tokens, starts=starts, pad_len=pad_len, norm_gain=norm_gain, w_in=w_in, w_dt=w_dt,
        conv_w=conv_w, conv_b=conv_b, dt_bias=dt_bias, a_log=a_log, skip=skip, gate_gain=gate_gain,
        w_out=w_out, cot=cotangent,
    )
    direct = lax.axis_size("dp") == 4 and 2 * shard % 16 == 0 and model % (16 * shard) == 0
    out = together(z, args) if direct else apart(z, args)
    order = (
        N.mixed, N.tokens_grad, N.o_norm, N.o_in, N.o_dt, N.o_conv_w, N.o_conv_b, N.o_bias, N.o_alog,
        N.o_skip, N.o_gate, N.o_out,
    )
    return tuple(out[name] for name in order)


def solution(mesh):
    weight = P(("dp", "seq", "dir"), None)
    values = P("dp", ("seq", "dir"), None)
    return jax.shard_map(
        shards,
        mesh=mesh,
        in_specs=(
            values, P("dp", None), P("dp"), P(), weight, weight, P(), P(), P(), P(), P(), P(),
            weight, values,
        ),
        out_specs=(
            values, values, P(), weight, weight, P(), P(), P(), P(), P(), P(), weight,
        ),
        check_vma=False,
    )
```
